32 devices in a mesh: aperture: 8 (over y, x, core), beam: 4 (over z).
Axes of the slice: x: 2, y: 2, z: 4, core: 2. Of those that a mesh axis runs over, the one named last changes fastest.
Arguments:
- subimages: bfloat16 [8, 2, 1024, 512], P('aperture', None, 'beam'), may hold values from -6 to 6
- range_kernel: bfloat16 [8, 2, 512, 512], P('aperture'), may hold values from -0.1875 to 0.1875
- weights0: bfloat16 [8, 16, 2, 128, 320], P('aperture', 'beam'), may hold values from -0.25 to 0.25
- starts0: int32 [8, 16], P(None, 'beam'), may hold values from -6 to 28, as said below
- weights1: bfloat16 [8, 32, 2, 128, 320], P('aperture', 'beam'), may hold values from -0.25 to 0.25
- starts1: int32 [8, 32], P(None, 'beam'), may hold values from -6 to 60, as said below
- owners: int32 [8, 64, 1], P('aperture', 'beam'), may hold values from 0 to 3; in each aligned block of 16 rows (0 to 15, 16 to 31, ..., all dimensions but the last counted through in order) at most 8 rows name the same one
Outputs:
- merged: bfloat16 [8, 128, 2, 64, 128], P('aperture', 'beam')
The draws below stay inside these ranges and needn't reach their ends.
Inputs may be any that keep to these rules, and one draw needn't show every extreme that they name: starts0[s, p] = 2p - (10 - 2) // 2 + e with -2 <= e <= 2; both ends of e occur. starts1[s, p] = 2p - (10 - 2) // 2 + e with -2 <= e <= 2; both ends of e occur. `owners`: among the 16 sectors homed on one beam device (aligned blocks of 16 rows of one subaperture row), at most 8 name the same owner, a bound that some block reaches.
All inputs are finite; a program needn't handle non-finite values.
Results may differ from the reference program's by a relative error of at most 0.0072.
Values may be sent and summed in bfloat16 or wider, within the bound.
No kernel may reach another device: no remote copies, remote signals or barrier semaphores. Data moves between devices by JAX's collectives and lax.ppermute only.
A program may use at most 64 MiB of HBM per device.

```python
import math
import jax
import jax.numpy as jnp
import numpy as np
from jax import lax

BLK = 32
NW = 10
REACH = 2
BDEV_BLK = 8
RNG = 512
S = 8
PS = 128
OS = 64
WIN = 320
CB0 = 1024
NSEC0 = 16
NSEC1 = 32
ODEV = 16
ONS = 64
CAP = 8
SLOTS = 128
HALF = 256
QUART = 128
N_BEAM = 4


def start_table(key, row_count, sectors, per_device):
    subkeys = jax.random.split(key, 7)
    offset = jax.random.randint(subkeys[0], (row_count, sectors), -REACH, REACH + 1)
    low_row = jax.random.randint(subkeys[1], (), 0, row_count)
    low_device = jax.random.randint(subkeys[2], (), 0, sectors // per_device)
    high_row = jax.random.randint(subkeys[3], (), 0, row_count)
    high_device = jax.random.randint(subkeys[4], (), 0, sectors // per_device)
    first_row = jax.random.randint(subkeys[5], (), 0, row_count)
    last_row = jax.random.randint(subkeys[6], (), 0, row_count)
    row_index = jnp.arange(row_count, dtype=jnp.int32)[:, None]
    sector_index = jnp.arange(sectors, dtype=jnp.int32)[None, :]
    offset = jnp.where((row_index == low_row) & (sector_index == low_device * per_device), -REACH, offset)
    offset = jnp.where((row_index == high_row) & (sector_index == high_device * per_device + per_device - 1), REACH, offset)
    offset = jnp.where((row_index == first_row) & (sector_index == 0), -REACH, offset)
    offset = jnp.where((row_index == last_row) & (sector_index == sectors - 1), REACH, offset)
    return (2 * sector_index - (NW - 2) // 2 + offset).astype(jnp.int32)


def draw_starts0(key, part):
    return start_table(jax.random.fold_in(key, 11), S, NSEC0, BDEV_BLK // 2)


def draw_starts1(key, part):
    return start_table(jax.random.fold_in(key, 23), S, NSEC1, BDEV_BLK)


def level_of(stream_key, shape, cuts, least, top_value):
    def one(position, parts):
        heights = jax.random.uniform(jax.random.fold_in(jax.random.fold_in(stream_key, 6), position), (parts,), jnp.float32, least / len(cuts), top_value / len(cuts))
        return jnp.repeat(jnp.exp(heights), shape[position] // parts).reshape((-1,) + (1,) * (len(shape) - position - 1))

    factor_of = one(*cuts[0])
    for cut in cuts[1:]:
        factor_of = factor_of * one(*cut)
    return factor_of


def deal_out(stream_key, own, number, rows, count, top, bound, slope):
    ranking = jax.random.permutation(stream_key, count)
    packed, common = portions_of(count, rows * top, bound, slope, True), portions_of(count, rows * top, bound, slope, False)
    places = jnp.arange(count)

    def named(sizes, offset_by):
        used = int((sizes > 0).sum())
        fixed = max(1, used // 4)
        shifted = fixed + (places - fixed + offset_by * (used - fixed)) % max(1, count - fixed)
        return jnp.zeros((count,), jnp.int32).at[ranking[jnp.where(places < fixed, places, shifted)]].set(jnp.asarray(sizes, jnp.int32))

    sizes = jnp.where(number % 4 == 0, named(packed, number // 4), named(common, number - number // 4 - 1))
    mixed = jax.random.permutation(jax.random.fold_in(own, 3), count)
    source_of, taker = mixed[0:count // 2 * 2:2], mixed[1:count // 2 * 2:2]
    slack = jnp.minimum(sizes[source_of] - 1, bound - sizes[taker]) // 2
    slack = jnp.where((source_of == ranking[0]) | (taker == ranking[0]) | (sizes[taker] == 0), 0, jnp.maximum(slack, 0))
    shifted = jax.random.randint(jax.random.fold_in(own, 4), (count // 2,), 0, 1 << 20) % (slack + 1)
    sizes = sizes.at[source_of].add(-shifted).at[taker].add(shifted)
    items = jnp.searchsorted(jnp.cumsum(sizes), jnp.arange(rows * top), side="right").astype(jnp.int32)
    grid = items.reshape(top, rows).T
    grid = grid[jax.random.permutation(jax.random.fold_in(own, 1), rows)]
    offset_by = jax.random.randint(jax.random.fold_in(own, 2), (rows, 1), 0, top)
    return jnp.take_along_axis(grid, (jnp.arange(top)[None, :] + offset_by) % top, axis=1)


def portions_of(amount, total, limit, slope, full):
    loads = [(1 << 20) // math.isqrt(rank ** slope) + 1 for rank in range(1, amount + 1)]
    largest = limit if full else min(limit, max(-(-total // amount), total * loads[0] // sum(loads)))
    least = 1 if total - largest >= amount - 1 else 0
    holding, surplus = [largest] + [least] * (amount - 1), total - largest - least * (amount - 1)
    while surplus > 0:
        candidates = [i for i in range(1, amount) if holding[i] < largest] or [i for i in range(1, amount) if holding[i] < limit]
        mass, left = sum([loads[i] for i in candidates]), surplus
        for i in candidates:
            extra = min(limit - holding[i], max(1, left * loads[i] // mass), surplus)
            holding[i] = holding[i] + extra
            surplus = surplus - extra
    return np.array(holding)


def gaussian(stream_key, dims, width, reach, shards=(), held_as=jnp.bfloat16):
    level = level_of(stream_key, dims, shards, -0.22, 0.18) if shards else 1.0
    result = jax.random.normal(stream_key, dims, jnp.float32) * width * level
    return jnp.minimum(jnp.maximum(result, -reach), reach).astype(held_as)


def setup_inputs(seed: int = 0) -> dict:
    splits = jax.random.split(jax.random.key(seed), 8)
    subimages = gaussian(splits[0], (S, 2, CB0, RNG), 1.0, 6.0, ((0, 8), (2, 4)))
    range_kernel = gaussian(splits[1], (S, 2, RNG, RNG), (2 * RNG) ** -0.5, 0.1875, ((0, 8),))
    weights0 = gaussian(splits[2], (S, NSEC0, 2, PS, WIN), (2 * WIN) ** -0.5, 0.25, ((0, 8), (1, 4)))
    starts0 = draw_starts0(jax.random.fold_in(splits[7], 71), 0)
    weights1 = gaussian(splits[4], (S, NSEC1, 2, PS, WIN), (2 * WIN) ** -0.5, 0.25, ((0, 8), (1, 4)))
    starts1 = draw_starts1(jax.random.fold_in(splits[7], 71), 0)
    owners_keys = jax.random.split(jax.random.fold_in(splits[6], 1), S * ONS // ODEV)
    owners_turns = jax.random.permutation(jax.random.fold_in(splits[6], 3), S * ONS // ODEV)
    owners = jax.vmap(lambda own, number: deal_out(jax.random.fold_in(splits[6], 2), own, number, ODEV, N_BEAM, 1, CAP, 2))(owners_keys, owners_turns).reshape((S, ONS, 1))
    return {"subimages": subimages, "range_kernel": range_kernel, "weights0": weights0, "starts0": starts0, "weights1": weights1, "starts1": starts1, "owners": owners}


def complex_dot(left_real, left_imag, right_real, right_imag):
    real_part = jnp.dot(left_real, right_real, preferred_element_type=jnp.float32) - jnp.dot(left_imag, right_imag, preferred_element_type=jnp.float32)
    imag_part = jnp.dot(left_real, right_imag, preferred_element_type=jnp.float32) + jnp.dot(left_imag, right_real, preferred_element_type=jnp.float32)
    return jnp.stack([real_part, imag_part])


def resample(operands):
    subimage, kernel = operands
    return complex_dot(subimage[0], subimage[1], kernel[0], kernel[1]).astype(jnp.bfloat16)


def interp(operands):
    child, weights, starts = operands
    margin = ((NW - 2) // 2 + REACH) * BLK
    padded = jnp.pad(child, ((0, 0), (margin, margin), (0, 0)))

    def one_sector(sector_operands):
        matrix, first_block = sector_operands
        window = lax.dynamic_slice_in_dim(padded, (first_block * BLK + margin).astype(jnp.int32), NW * BLK, 1)
        return complex_dot(matrix[0], matrix[1], window[0], window[1])

    sectors = lax.map(one_sector, (weights, starts))
    sector_count = sectors.shape[0]
    joined = jnp.transpose(sectors, (1, 0, 2, 3)).reshape(2, sector_count * sectors.shape[2], child.shape[2])
    return joined.astype(jnp.bfloat16)


def reference(subimages, range_kernel, weights0, starts0, weights1, starts1, owners):
    resampled = lax.map(resample, (subimages, range_kernel))
    beams_first = lax.map(interp, (resampled, weights0, starts0))
    level_one = (beams_first[0::2].astype(jnp.float32) + beams_first[1::2].astype(jnp.float32)).astype(jnp.bfloat16)
    width_one = level_one.shape[2]
    halves = level_one.reshape(S // 2, 2, width_one, 2, HALF).transpose(0, 3, 1, 2, 4).reshape(S, 2, width_one, HALF)
    beams_second = lax.map(interp, (halves, weights1, starts1))
    width_two = beams_second.shape[2]
    grouped = beams_second.astype(jnp.float32).reshape(S // 4, 2, 2, 2, width_two, HALF)
    summed = (grouped[:, 0] + grouped[:, 1]).astype(jnp.bfloat16)
    quarters = summed.reshape(S // 4, 2, 2, width_two, 2, QUART).transpose(0, 4, 1, 2, 3, 5).reshape(S, 2, width_two, QUART)
    by_sector = jnp.transpose(quarters.reshape(S, 2, ONS, OS, QUART), (0, 2, 1, 3, 4))
    target = owners[:, :, 0]
    one_hot = (target[:, :, None] == jnp.arange(N_BEAM, dtype=jnp.int32)[None, None, :]).astype(jnp.int32)
    grouped_hot = one_hot.reshape(S, N_BEAM, ODEV, N_BEAM)
    earlier = jnp.cumsum(grouped_hot, axis=2) - grouped_hot
    slot_rank = jnp.sum(earlier * grouped_hot, axis=3).reshape(S, ONS)
    home_device = jnp.arange(ONS, dtype=jnp.int32) // ODEV
    slot_index = (target * (N_BEAM * CAP) + home_device[None, :] * CAP + slot_rank).astype(jnp.int32)
    row_index = jnp.arange(S, dtype=jnp.int32)[:, None] * jnp.ones((1, ONS), jnp.int32)
    merged = jnp.zeros((S, SLOTS, 2, OS, QUART), jnp.bfloat16).at[row_index, slot_index].set(by_sector)
    return merged
```

```python
import functools

import jax
import jax.numpy as jnp
from jax import lax
from jax.experimental import pallas as pl
from jax.experimental.pallas import tpu as pltpu
from jax.sharding import PartitionSpec as P

BLK = 32
NW = 10
REACH = 2
OS = 64
MARGIN_BLOCKS = (NW - 2) // 2 + REACH
VMEM_LIMIT = 24 * 1024 * 1024
ANY = pl.BlockSpec(memory_space=pl.ANY)
VMEM = pl.BlockSpec(memory_space=pltpu.VMEM)
SMEM = pl.BlockSpec(memory_space=pltpu.SMEM)


def params():
    return pltpu.CompilerParams(vmem_limit_bytes=VMEM_LIMIT)


def cost(macs, moved):
    return pl.CostEstimate(flops=2 * macs, bytes_accessed=moved, transcendentals=0)


def swap_route(count, first):
    route = []
    for low in range(first, count - 1, 2):
        route += [(low, low + 1), (low + 1, low)]
    return route


def exchange_edges(cells, axis, width):
    count = lax.axis_size(axis)
    even = lax.axis_index(axis) % 2 == 0
    rows = cells.shape[1]
    tail_start = jnp.where(even, rows - width, 0)
    head_start = jnp.where(even, 0, rows - width)
    first = lax.dynamic_slice_in_dim(cells, tail_start, width, 1)
    second = lax.dynamic_slice_in_dim(cells, head_start, width, 1)
    return (
        lax.ppermute(first, axis, swap_route(count, 0)),
        lax.ppermute(second, axis, swap_route(count, 1)),
    )


def partner(block, axis, distance):
    count = lax.axis_size(axis)
    route = []
    for low in range(count):
        high = low | 1 << distance
        if high != low and high < count:
            route += [(low, high), (high, low)]
    return lax.ppermute(block, axis, route)


def dot(left, right):
    return jnp.dot(left, right, preferred_element_type=jnp.float32)


def resample_into(out_ref, out_start, rows, child_ref, kernel_ref):
    real, imag = child_ref[0], child_ref[1]
    k_real, k_imag = kernel_ref[0], kernel_ref[1]
    place = pl.ds(out_start, rows)
    out_ref[0, place, :] = (dot(real, k_real) - dot(imag, k_imag)).astype(jnp.bfloat16)
    out_ref[1, place, :] = (dot(real, k_imag) + dot(imag, k_real)).astype(jnp.bfloat16)


def resample_kernel(child_ref, kernel_ref, out_ref):
    resample_into(out_ref, 0, child_ref.shape[1], child_ref, kernel_ref)


def resample(child, kernel):
    return pl.pallas_call(
        resample_kernel,
        out_shape=jax.ShapeDtypeStruct((2, child.shape[1], kernel.shape[2]), jnp.bfloat16),
        in_specs=[VMEM, VMEM],
        out_specs=VMEM,
        compiler_params=params(),
        cost_estimate=cost(4 * child.shape[1] * kernel.shape[1] * kernel.shape[2], 2**21),
        name="resample_own",
    )(child, kernel)


def complex_window(weights_ref, sector, real, imag):
    beams = weights_ref.shape[1] // 2
    with_real = dot(weights_ref[sector], real)
    with_imag = dot(weights_ref[sector], imag)
    return (
        (with_real[:beams] - with_imag[beams:]).astype(jnp.bfloat16),
        (with_imag[:beams] + with_real[beams:]).astype(jnp.bfloat16),
    )


def first_level_kernel(
    starts_ref, side_ref, own_ref, first_ref, second_ref, kernel_ref, weights_ref,
    keep_ref, send_ref, padded,
):
    margin = first_ref.shape[1]
    rows = own_ref.shape[1]
    sectors, stacked, window = weights_ref.shape
    beams = stacked // 2
    even, half = side_ref[0], side_ref[1]
    width = keep_ref.shape[2]
    padded[:, margin : margin + rows, :] = own_ref[...]
    far = margin + rows
    first_at = pl.multiple_of(even * far, BLK)
    second_at = pl.multiple_of((1 - even) * far, BLK)
    resample_into(padded, first_at, margin, first_ref, kernel_ref)
    resample_into(padded, second_at, margin, second_ref, kernel_ref)
    for sector in range(sectors):
        place = pl.ds(pl.multiple_of(starts_ref[sector] * BLK, BLK), window)
        out = pl.ds(sector * beams, beams)
        for ref, side in ((send_ref, 1 - half), (keep_ref, half)):
            columns = pl.ds(pl.multiple_of(side * width, 128), width)
            real, imag = complex_window(
                weights_ref, sector, padded[0, place, columns], padded[1, place, columns]
            )
            ref[0, out, :] = real
            ref[1, out, :] = imag


def first_level(starts, side, own, first, second, kernel, weights):
    sectors, stacked, window = weights.shape
    rng = own.shape[2]
    margin, rows = first.shape[1], own.shape[1]
    shape = jax.ShapeDtypeStruct((2, sectors * stacked // 2, rng // 2), jnp.bfloat16)
    return pl.pallas_call(
        first_level_kernel,
        out_shape=(shape, shape),
        in_specs=[SMEM, SMEM] + [VMEM] * 5,
        out_specs=(VMEM, VMEM),
        scratch_shapes=[pltpu.VMEM((2, rows + 2 * margin, rng), jnp.bfloat16)],
        compiler_params=params(),
        cost_estimate=cost(sectors * 2 * stacked * window * rng + 8 * margin * rng * rng, 2**22),
        name="first_level",
    )(starts, side, own, first, second, kernel, weights)


def second_level_kernel(
    starts_ref, side_ref, own_ref, first_ref, second_ref, weights_ref,
    keep_ref, send_ref, padded,
):
    margin = first_ref.shape[1]
    rows = own_ref.shape[1]
    sectors, stacked, window = weights_ref.shape
    beams = stacked // 2
    even, quarter = side_ref[0], side_ref[1]
    width = keep_ref.shape[3]
    padded[:, margin : margin + rows, :] = own_ref[...]
    far = margin + rows
    padded[:, pl.ds(pl.multiple_of(even * far, BLK), margin), :] = first_ref[...]
    padded[:, pl.ds(pl.multiple_of((1 - even) * far, BLK), margin), :] = second_ref[...]
    per = beams // OS
    for sector in range(sectors):
        place = pl.ds(pl.multiple_of(starts_ref[sector] * BLK, BLK), window)
        parts = complex_window(weights_ref, sector, padded[0, place, :], padded[1, place, :])

        def store(swapped):
            for ref, column in ((keep_ref, swapped), (send_ref, 1 - swapped)):
                for part in range(2):
                    for piece in range(per):
                        ref[sector * per + piece, part] = parts[part][
                            piece * OS : (piece + 1) * OS, column * width : (column + 1) * width
                        ]

        pl.when(quarter == 0)(functools.partial(store, 0))
        pl.when(quarter == 1)(functools.partial(store, 1))


def second_level(starts, side, own, first, second, weights):
    sectors, stacked, window = weights.shape
    rng = own.shape[2]
    margin, rows = first.shape[1], own.shape[1]
    shape = jax.ShapeDtypeStruct(
        (sectors * stacked // 2 // OS, 2, OS, rng // 2), jnp.bfloat16
    )
    return pl.pallas_call(
        second_level_kernel,
        out_shape=(shape, shape),
        in_specs=[SMEM, SMEM] + [VMEM] * 4,
        out_specs=(VMEM, VMEM),
        scratch_shapes=[pltpu.VMEM((2, rows + 2 * margin, rng), jnp.bfloat16)],
        compiler_params=params(),
        cost_estimate=cost(sectors * 2 * stacked * window * rng, 2**22),
        name="second_level",
    )(starts, side, own, first, second, weights)


def slots_kernel(slot_ref, keep_ref, other_ref, out_ref):
    out_ref[...] = jnp.zeros_like(out_ref)
    for sector in range(keep_ref.shape[0]):
        total = keep_ref[sector].astype(jnp.float32) + other_ref[sector].astype(jnp.float32)
        out_ref[slot_ref[sector]] = total.astype(jnp.bfloat16)


def fill_slots(slot, keep, other, slots):
    return pl.pallas_call(
        slots_kernel,
        out_shape=jax.ShapeDtypeStruct((slots,) + keep.shape[1:], jnp.bfloat16),
        in_specs=[SMEM, VMEM, VMEM],
        out_specs=VMEM,
        compiler_params=params(),
        cost_estimate=cost(0, 2**21),
        name="fill_slots",
    )(slot, keep, other)


def stacked_weights(weights):
    return weights[0].reshape(weights.shape[1], -1, weights.shape[4])


def table_row(table, row_number):
    return lax.dynamic_index_in_dim(table, row_number, 0, keepdims=False)


def local(subimages, range_kernel, weights0, starts0, weights1, starts1, owners):
    aper_index = lax.axis_index("aperture")
    beam_index = lax.axis_index("beam")
    beam_count = lax.axis_size("beam")
    margin = MARGIN_BLOCKS * BLK
    subimage = subimages[0]
    kernel = range_kernel[0]
    local_blocks = subimage.shape[1] // BLK
    even = (beam_index % 2 == 0).astype(jnp.int32)

    first, second = exchange_edges(subimage, "beam", margin)
    own = resample(subimage, kernel)
    begin0 = table_row(starts0, aper_index) - (beam_index * local_blocks - MARGIN_BLOCKS)
    side0 = jnp.stack([even, aper_index % 2])
    keep, send = first_level(
        begin0, side0, own, first, second, kernel, stacked_weights(weights0)
    )
    other = partner(send, "aperture", 0)
    level_one = (keep.astype(jnp.float32) + other.astype(jnp.float32)).astype(jnp.bfloat16)

    first, second = exchange_edges(level_one, "beam", margin)
    begin1 = table_row(starts1, aper_index) - (beam_index * 2 * local_blocks - MARGIN_BLOCKS)
    side1 = jnp.stack([even, aper_index // 2 % 2])
    keep, send = second_level(
        begin1, side1, level_one, first, second, stacked_weights(weights1)
    )
    other = partner(send, "aperture", 1)

    sector_count = owners.shape[1]
    capacity = max(2, 2 * sector_count // beam_count)
    target = owners[0, :, 0]
    one_hot = (target[:, None] == jnp.arange(beam_count, dtype=jnp.int32)[None, :]).astype(
        jnp.int32
    )
    earlier = jnp.cumsum(one_hot, axis=0) - one_hot
    slot_rank = jnp.sum(earlier * one_hot, axis=1)
    slot_index = target * capacity + slot_rank
    outgoing = fill_slots(slot_index, keep, other, beam_count * capacity)
    received = lax.all_to_all(outgoing, "beam", split_axis=0, concat_axis=0, tiled=True)
    return received[None]


def solution(mesh):
    return jax.shard_map(
        local,
        mesh=mesh,
        in_specs=(
            P("aperture", None, "beam", None),
            P("aperture", None, None, None),
            P("aperture", "beam", None, None, None),
            P(None, "beam"),
            P("aperture", "beam", None, None, None),
            P(None, "beam"),
            P("aperture", "beam", None),
        ),
        out_specs=P("aperture", "beam", None, None, None),
        check_vma=False,
    )
```

```python
import functools

import jax
import jax.numpy as jnp
from jax import lax
from jax.experimental import pallas as pl
from jax.experimental.pallas import tpu as pltpu
from jax.sharding import PartitionSpec as P

BLK = 32
NW = 10
REACH = 2
OS = 64
MARGIN_BLOCKS = (NW - 2) // 2 + REACH
VMEM_LIMIT = 8 * 1024 * 1024
ANY = pl.BlockSpec(memory_space=pl.ANY)
VMEM = pl.BlockSpec(memory_space=pltpu.VMEM)
SMEM = pl.BlockSpec(memory_space=pltpu.SMEM)


def params():
    return pltpu.CompilerParams(vmem_limit_bytes=VMEM_LIMIT)


def cost(macs, moved):
    return pl.CostEstimate(flops=2 * macs, bytes_accessed=moved, transcendentals=0)


def swap_route(count, first):
    route = []
    for low in range(first, count - 1, 2):
        route += [(low, low + 1), (low + 1, low)]
    return route


def trade_edges(first, second, axis):
    count = lax.axis_size(axis)
    return (
        lax.ppermute(first, axis, swap_route(count, 0)),
        lax.ppermute(second, axis, swap_route(count, 1)),
    )


def partner(block, axis, distance):
    count = lax.axis_size(axis)
    route = []
    for low in range(count):
        high = low | 1 << distance
        if high != low and high < count:
            route += [(low, high), (high, low)]
    return lax.ppermute(block, axis, route)


def dot(left, right):
    return jnp.dot(left, right, preferred_element_type=jnp.float32)


def resample_kernel(side_ref, child_hbm, kernel_hbm, own_ref, first_ref, second_ref, child, kernel, sems):
    even, half, quarter = side_ref[0], side_ref[1], side_ref[2]
    rng = child.shape[2]
    piece = rng // 4
    copies = [pltpu.make_async_copy(child_hbm, child, sems.at[4])]
    for place in range(4):
        source = (half ^ (place // 2)) * 2 + (quarter ^ (place % 2))
        copies.append(
            pltpu.make_async_copy(
                kernel_hbm.at[:, :, pl.ds(pl.multiple_of(source * piece, 128), piece)],
                kernel.at[:, :, place * piece : (place + 1) * piece],
                sems.at[place],
            )
        )
    for copy in copies:
        copy.start()
    for copy in copies:
        copy.wait()
    real, imag = child[0], child[1]
    k_real, k_imag = kernel[0], kernel[1]
    own_ref[0] = (dot(real, k_real) - dot(imag, k_imag)).astype(jnp.bfloat16)
    own_ref[1] = (dot(real, k_imag) + dot(imag, k_real)).astype(jnp.bfloat16)
    rows, margin = own_ref.shape[1], first_ref.shape[1]
    tail = pl.multiple_of(even * (rows - margin), BLK)
    head = pl.multiple_of((1 - even) * (rows - margin), BLK)
    first_ref[...] = own_ref[:, pl.ds(tail, margin), :]
    second_ref[...] = own_ref[:, pl.ds(head, margin), :]


def resample(side, child, kernel, margin):
    rows, rng = child.shape[1:]
    shapes = [
        jax.ShapeDtypeStruct((2, count, rng), jnp.bfloat16) for count in (rows, margin, margin)
    ]
    return pl.pallas_call(
        resample_kernel,
        out_shape=shapes,
        in_specs=[SMEM, ANY, ANY],
        out_specs=[VMEM] * 3,
        scratch_shapes=[
            pltpu.VMEM(child.shape, jnp.bfloat16),
            pltpu.VMEM(kernel.shape, jnp.bfloat16),
            pltpu.SemaphoreType.DMA((5,)),
        ],
        compiler_params=params(),
        cost_estimate=cost(4 * rows * rng * rng, 2**21),
        name="resample",
    )(side, child, kernel)


def complex_window(weights_ref, sector, real, imag):
    beams = weights_ref.shape[1] // 2
    with_real = dot(weights_ref[sector], real)
    with_imag = dot(weights_ref[sector], imag)
    return (
        (with_real[:beams] - with_imag[beams:]).astype(jnp.bfloat16),
        (with_imag[:beams] + with_real[beams:]).astype(jnp.bfloat16),
    )


def pad_with(padded, even, own_ref, first_ref, second_ref):
    margin, rows = first_ref.shape[1], own_ref.shape[1]
    far = margin + rows
    padded[:, margin:far, :] = own_ref[...]
    padded[:, pl.ds(pl.multiple_of(even * far, BLK), margin), :] = first_ref[...]
    padded[:, pl.ds(pl.multiple_of((1 - even) * far, BLK), margin), :] = second_ref[...]


def first_level_kernel(
    starts_ref, side_ref, own_ref, first_ref, second_ref, weights_ref, keep_ref, send_ref, padded
):
    sectors, stacked, window = weights_ref.shape
    beams = stacked // 2
    width = keep_ref.shape[2]
    pad_with(padded, side_ref[0], own_ref, first_ref, second_ref)
    for sector in range(sectors):
        place = pl.ds(pl.multiple_of(starts_ref[sector] * BLK, BLK), window)
        parts = complex_window(weights_ref, sector, padded[0, place, :], padded[1, place, :])
        out = pl.ds(sector * beams, beams)
        for part in range(2):
            keep_ref[part, out, :] = parts[part][:, :width]
            send_ref[part, out, :] = parts[part][:, width:]


def first_level(starts, side, own, first, second, weights):
    sectors, stacked, window = weights.shape
    rng = own.shape[2]
    margin, rows = first.shape[1], own.shape[1]
    shape = jax.ShapeDtypeStruct((2, sectors * stacked // 2, rng // 2), jnp.bfloat16)
    return pl.pallas_call(
        first_level_kernel,
        out_shape=(shape, shape),
        in_specs=[SMEM, SMEM] + [VMEM] * 4,
        out_specs=(VMEM, VMEM),
        scratch_shapes=[pltpu.VMEM((2, rows + 2 * margin, rng), jnp.bfloat16)],
        compiler_params=params(),
        cost_estimate=cost(sectors * 2 * stacked * window * rng, 2**22),
        name="first_level",
    )(starts, side, own, first, second, weights)


def second_level_kernel(
    starts_ref, side_ref, own_at_ref, other_at_ref, own_ref, first_ref, second_ref, weights_ref,
    keep_ref, *refs,
):
    send_refs, (padded, send) = refs[:-2], refs[-2:]
    sectors, stacked, window = weights_ref.shape
    beams = stacked // 2
    width = keep_ref.shape[3]
    pad_with(padded, side_ref[0], own_ref, first_ref, second_ref)
    per = beams // OS
    for sector in range(sectors):
        place = pl.ds(pl.multiple_of(starts_ref[sector] * BLK, BLK), window)
        parts = complex_window(weights_ref, sector, padded[0, place, :], padded[1, place, :])
        for piece in range(per):
            own_at = own_at_ref[sector * per + piece]
            other_at = other_at_ref[sector * per + piece]
            rows = slice(piece * OS, (piece + 1) * OS)
            for part in range(2):
                keep_ref[own_at, part] = parts[part][rows, :width]
                send[other_at, part] = parts[part][rows, width:]
    done = 0
    for ref in send_refs:
        ref[...] = send[done : done + ref.shape[0]]
        done += ref.shape[0]


def second_level(starts, side, own_at, other_at, own, first, second, weights, chunks):
    sectors, stacked, window = weights.shape
    rng = own.shape[2]
    margin, rows = first.shape[1], own.shape[1]
    count = sectors * stacked // 2 // OS
    block = (2, OS, rng // 2)
    shapes = [jax.ShapeDtypeStruct((n,) + block, jnp.bfloat16) for n in (count,) + chunks]
    return pl.pallas_call(
        second_level_kernel,
        out_shape=shapes,
        in_specs=[SMEM] * 4 + [VMEM] * 4,
        out_specs=[VMEM] * len(shapes),
        scratch_shapes=[
            pltpu.VMEM((2, rows + 2 * margin, rng), jnp.bfloat16),
            pltpu.VMEM((count,) + block, jnp.bfloat16),
        ],
        compiler_params=params(),
        cost_estimate=cost(sectors * 2 * stacked * window * rng, 2**22),
        name="second_level",
    )(starts, side, own_at, other_at, own, first, second, weights)


def plan_kernel(own_ref, other_ref, own_at_ref, other_at_ref, target_ref, rank_ref, taken, filled):
    count = own_ref.shape[0]
    for owners_ref, at_ref in ((other_ref, other_at_ref), (own_ref, own_at_ref)):
        for target in range(taken.shape[0]):
            taken[target] = 0
        for rank in range(filled.shape[0]):
            filled[rank] = 0
        for sector in range(count):
            target = owners_ref[sector]
            rank = taken[target]
            taken[target] = rank + 1
            filled[rank + 1] = filled[rank + 1] + 1
            at_ref[sector] = rank
        for rank in range(1, filled.shape[0]):
            filled[rank] = filled[rank] + filled[rank - 1]
        for sector in range(count):
            rank = at_ref[sector]
            place = filled[rank]
            filled[rank] = place + 1
            at_ref[sector] = place
            if at_ref is own_at_ref:
                target_ref[place] = owners_ref[sector]
                rank_ref[place] = rank


def plan(own, other, beam_count):
    count = own.shape[0]
    shape = jax.ShapeDtypeStruct((count,), jnp.int32)
    return pl.pallas_call(
        plan_kernel,
        out_shape=[shape] * 4,
        in_specs=[SMEM, SMEM],
        out_specs=[SMEM] * 4,
        scratch_shapes=[pltpu.SMEM((beam_count,), jnp.int32), pltpu.SMEM((count + 1,), jnp.int32)],
        compiler_params=params(),
        name="plan",
    )(own, other)


def wires_kernel(low, high, me_ref, target_ref, rank_ref, keep_ref, *refs):
    wires = refs[-1]
    spare = wires.shape[0] - 1
    beam_count = spare // (high - low)
    other_refs, out_refs = refs[: -1 - beam_count], refs[-1 - beam_count : -1]
    wires[...] = jnp.zeros_like(wires)
    me = me_ref[0]
    place = 0
    for other_ref in other_refs:
        for row in range(other_ref.shape[0]):
            rank = rank_ref[place]
            wanted = jnp.logical_and(rank >= low, rank < high)
            at = jnp.where(wanted, (target_ref[place] ^ me) * (high - low) + rank - low, spare)
            total = keep_ref[place].astype(jnp.float32) + other_ref[row].astype(jnp.float32)
            wires[at] = total.astype(jnp.bfloat16)
            place += 1
    for distance, ref in enumerate(out_refs):
        ref[...] = wires[distance * (high - low) : (distance + 1) * (high - low)]


def wires(low, high, beam_count, me, target, rank, keep, *others):
    block = keep.shape[1:]
    shape = jax.ShapeDtypeStruct((high - low,) + block, jnp.bfloat16)
    return pl.pallas_call(
        functools.partial(wires_kernel, low, high),
        out_shape=[shape] * beam_count,
        in_specs=[SMEM] * 3 + [VMEM] * (1 + len(others)),
        out_specs=[VMEM] * beam_count,
        scratch_shapes=[pltpu.VMEM(((high - low) * beam_count + 1,) + block, jnp.bfloat16)],
        compiler_params=params(),
        cost_estimate=cost(0, 2**21),
        name=f"wires_{low}",
    )(me, target, rank, keep, *others)


def collect_kernel(bounds, me_ref, *refs):
    sems = refs[-1]
    out_ref = refs[-2]
    groups = len(bounds)
    beam_count = (len(refs) - 2) // groups
    capacity = bounds[-1][1]
    copies = []
    for group, (low, high) in enumerate(bounds):
        for distance in range(beam_count):
            place = group * beam_count + distance
            start = (me_ref[0] ^ distance) * capacity + low
            copies.append(
                pltpu.make_async_copy(
                    refs[place], out_ref.at[pl.ds(start, high - low)], sems.at[place]
                )
            )
    for copy in copies:
        copy.start()
    for copy in copies:
        copy.wait()


def collect(bounds, me, received):
    beam_count = len(received[0])
    flat = [array for group in received for array in group]
    shape = (beam_count * bounds[-1][1],) + flat[0].shape[1:]
    return pl.pallas_call(
        functools.partial(collect_kernel, bounds),
        out_shape=jax.ShapeDtypeStruct(shape, jnp.bfloat16),
        in_specs=[SMEM] + [ANY] * len(flat),
        out_specs=ANY,
        scratch_shapes=[pltpu.SemaphoreType.DMA((len(flat),))],
        compiler_params=params(),
        cost_estimate=cost(0, 2**21),
        name="collect",
    )(me, *flat)


def spread(group, axis):
    count = lax.axis_size(axis)
    received = {0: group[0]}
    for distance in reversed(range(1, count)):
        route = [(place, place ^ distance) for place in range(count)]
        received[distance] = lax.ppermute(group[distance], axis, route)
    return [received[distance] for distance in range(count)]


def stacked_weights(weights):
    return weights[0].reshape(weights.shape[1], -1, weights.shape[4])


def table_row(table, row_number):
    return lax.dynamic_index_in_dim(table, row_number, 0, keepdims=False)


def local(subimages, range_kernel, weights0, starts0, weights1, starts1, owners):
    aper_index = lax.axis_index("aperture")
    beam_index = lax.axis_index("beam")
    beam_count = lax.axis_size("beam")
    margin = MARGIN_BLOCKS * BLK
    local_blocks = subimages.shape[2] // BLK
    even = (beam_index % 2 == 0).astype(jnp.int32)
    side = jnp.stack([even, aper_index % 2, aper_index // 2 % 2])
    me = beam_index.reshape(1)

    sector_count = owners.shape[1]
    capacity = max(2, 2 * sector_count // beam_count)
    early = sector_count // 2 // beam_count
    paired = beam_count & (beam_count - 1) == 0
    if early and paired:
        chunks = (sector_count // 2, sector_count - sector_count // 2)
        bounds = ((0, early), (early, capacity))
    else:
        chunks = (sector_count,)
        bounds = ((0, capacity),)

    own, first, second = resample(side, subimages[0], range_kernel[0], margin)
    first, second = trade_edges(first, second, "beam")
    own_owners = owners[0, :, 0]
    other_owners = partner(owners, "aperture", 1)[0, :, 0]
    own_at, other_at, target, rank = plan(own_owners, other_owners, beam_count)
    begin0 = table_row(starts0, aper_index) - (beam_index * local_blocks - MARGIN_BLOCKS)
    keep, send = first_level(begin0, side, own, first, second, stacked_weights(weights0))
    other = partner(send, "aperture", 0)
    level_one = (keep.astype(jnp.float32) + other.astype(jnp.float32)).astype(jnp.bfloat16)

    rows = level_one.shape[1]
    first = lax.dynamic_slice_in_dim(level_one, even * (rows - margin), margin, 1)
    second = lax.dynamic_slice_in_dim(level_one, (1 - even) * (rows - margin), margin, 1)
    first, second = trade_edges(first, second, "beam")
    begin1 = table_row(starts1, aper_index) - (beam_index * 2 * local_blocks - MARGIN_BLOCKS)
    keep, *sends = second_level(
        begin1, side, own_at, other_at, level_one, first, second, stacked_weights(weights1), chunks
    )
    others = [partner(send, "aperture", 1) for send in sends]

    if len(bounds) == 1 or not paired:
        outgoing = wires(0, capacity, beam_count, me, target, rank, keep, *others)
        outgoing = jnp.stack([outgoing[0]] + list(outgoing[1:]))
        order = jnp.arange(beam_count) ^ beam_index
        outgoing = jnp.take(outgoing, order, axis=0)
        received = lax.all_to_all(outgoing, "beam", split_axis=0, concat_axis=0, tiled=True)
        return received.reshape((1, beam_count * capacity) + keep.shape[1:])
    received = []
    for number, (low, high) in enumerate(bounds):
        group = wires(low, high, beam_count, me, target, rank, keep, *others[: number + 1])
        received.append(spread(group, "beam"))
    return collect(bounds, me, received)[None]


def solution(mesh):
    return jax.shard_map(
        local,
        mesh=mesh,
        in_specs=(
            P("aperture", None, "beam", None),
            P("aperture", None, None, None),
            P("aperture", "beam", None, None, None),
            P(None, "beam"),
            P("aperture", "beam", None, None, None),
            P(None, "beam"),
            P("aperture", "beam", None),
        ),
        out_specs=P("aperture", "beam", None, None, None),
        check_vma=False,
    )
```

```python
import functools

import jax
import jax.numpy as jnp
from jax import lax
from jax.experimental import pallas as pl
from jax.experimental.pallas import tpu as pltpu
from jax.sharding import PartitionSpec as P

BLK = 32
NW = 10
REACH = 2
OS = 64
MARGIN_BLOCKS = (NW - 2) // 2 + REACH
VMEM_LIMIT = 8 * 1024 * 1024
WHOLE_VMEM = 60 * 1024 * 1024
ANY = pl.BlockSpec(memory_space=pl.ANY)
VMEM = pl.BlockSpec(memory_space=pltpu.VMEM)
SMEM = pl.BlockSpec(memory_space=pltpu.SMEM)


def params(limit=VMEM_LIMIT):
    return pltpu.CompilerParams(vmem_limit_bytes=limit)


def cost(macs, moved):
    return pl.CostEstimate(flops=2 * macs, bytes_accessed=moved, transcendentals=0)


def trade_edges(first, second):
    count = lax.axis_size("beam")
    received = []
    for order, block in enumerate((first, second)):
        route = []
        for aper in range(lax.axis_size("aperture")):
            for low in range((aper + order) % 2, count - 1, 2):
                place = aper * count + low
                route += [(place, place + 1), (place + 1, place)]
        received.append(lax.ppermute(block, ("aperture", "beam"), route))
    return received


def partner(block, axis, distance):
    count = lax.axis_size(axis)
    route = []
    for low in range(count):
        high = low | 1 << distance
        if high != low and high < count:
            route += [(low, high), (high, low)]
    return lax.ppermute(block, axis, route)


def dot(left, right):
    return jnp.dot(left, right, preferred_element_type=jnp.float32)


def resample_kernel(side_ref, child_hbm, kernel_hbm, own_ref, first_ref, second_ref, child, kernel, sems):
    even, half, quarter = side_ref[0], side_ref[1], side_ref[2]
    rng = child.shape[2]
    piece = rng // 4
    copies = [pltpu.make_async_copy(child_hbm, child, sems.at[4])]
    for place in range(4):
        source = (half ^ (place // 2)) * 2 + (quarter ^ (place % 2))
        copies.append(
            pltpu.make_async_copy(
                kernel_hbm.at[:, :, pl.ds(pl.multiple_of(source * piece, 128), piece)],
                kernel.at[:, :, place * piece : (place + 1) * piece],
                sems.at[place],
            )
        )
    for copy in copies:
        copy.start()
    for copy in copies:
        copy.wait()
    real, imag = child[0], child[1]
    k_real, k_imag = kernel[0], kernel[1]
    own_ref[0] = (dot(real, k_real) - dot(imag, k_imag)).astype(jnp.bfloat16)
    own_ref[1] = (dot(real, k_imag) + dot(imag, k_real)).astype(jnp.bfloat16)
    rows, margin = own_ref.shape[1], first_ref.shape[1]
    tail = pl.multiple_of(even * (rows - margin), BLK)
    head = pl.multiple_of((1 - even) * (rows - margin), BLK)
    first_ref[...] = own_ref[:, pl.ds(tail, margin), :]
    second_ref[...] = own_ref[:, pl.ds(head, margin), :]


def resample(side, child, kernel, margin):
    rows, rng = child.shape[1:]
    shapes = [
        jax.ShapeDtypeStruct((2, count, rng), jnp.bfloat16) for count in (rows, margin, margin)
    ]
    return pl.pallas_call(
        resample_kernel,
        out_shape=shapes,
        in_specs=[SMEM, ANY, ANY],
        out_specs=[VMEM] * 3,
        scratch_shapes=[
            pltpu.VMEM(child.shape, jnp.bfloat16),
            pltpu.VMEM(kernel.shape, jnp.bfloat16),
            pltpu.SemaphoreType.DMA((5,)),
        ],
        compiler_params=params(WHOLE_VMEM),
        cost_estimate=cost(4 * rows * rng * rng, 2**21),
        name="resample",
    )(side, child, kernel)


def complex_window(weights_ref, sector, real, imag):
    beams = weights_ref.shape[1] // 2
    with_real = dot(weights_ref[sector], real)
    with_imag = dot(weights_ref[sector], imag)
    return (
        (with_real[:beams] - with_imag[beams:]).astype(jnp.bfloat16),
        (with_imag[:beams] + with_real[beams:]).astype(jnp.bfloat16),
    )


def pad_with(padded, even, own_ref, first_ref, second_ref):
    margin, rows = first_ref.shape[1], own_ref.shape[1]
    far = margin + rows
    padded[:, margin:far, :] = own_ref[...]
    padded[:, pl.ds(pl.multiple_of(even * far, BLK), margin), :] = first_ref[...]
    padded[:, pl.ds(pl.multiple_of((1 - even) * far, BLK), margin), :] = second_ref[...]


def first_level_kernel(
    starts_ref, side_ref, own_ref, first_ref, second_ref, weights_ref, keep_ref, send_ref, padded
):
    sectors, stacked, window = weights_ref.shape
    beams = stacked // 2
    width = keep_ref.shape[2]
    pad_with(padded, side_ref[0], own_ref, first_ref, second_ref)
    for sector in range(sectors):
        place = pl.ds(pl.multiple_of(starts_ref[sector] * BLK, BLK), window)
        parts = complex_window(weights_ref, sector, padded[0, place, :], padded[1, place, :])
        out = pl.ds(sector * beams, beams)
        for part in range(2):
            keep_ref[part, out, :] = parts[part][:, :width]
            send_ref[part, out, :] = parts[part][:, width:]


def first_level(starts, side, own, first, second, weights):
    sectors, stacked, window = weights.shape
    rng = own.shape[2]
    margin, rows = first.shape[1], own.shape[1]
    shape = jax.ShapeDtypeStruct((2, sectors * stacked // 2, rng // 2), jnp.bfloat16)
    return pl.pallas_call(
        first_level_kernel,
        out_shape=(shape, shape),
        in_specs=[SMEM, SMEM] + [VMEM] * 4,
        out_specs=(VMEM, VMEM),
        scratch_shapes=[pltpu.VMEM((2, rows + 2 * margin, rng), jnp.bfloat16)],
        compiler_params=params(),
        cost_estimate=cost(sectors * 2 * stacked * window * rng, 2**22),
        name="first_level",
    )(starts, side, own, first, second, weights)


def second_level_kernel(
    starts_ref, side_ref, own_at_ref, other_at_ref, own_ref, first_ref, second_ref, weights_ref,
    keep_ref, *refs,
):
    send_refs, (padded, send) = refs[:-2], refs[-2:]
    sectors, stacked, window = weights_ref.shape
    beams = stacked // 2
    width = keep_ref.shape[3]
    pad_with(padded, side_ref[0], own_ref, first_ref, second_ref)
    per = beams // OS
    for sector in range(sectors):
        place = pl.ds(pl.multiple_of(starts_ref[sector] * BLK, BLK), window)
        parts = complex_window(weights_ref, sector, padded[0, place, :], padded[1, place, :])
        for piece in range(per):
            own_at = own_at_ref[sector * per + piece]
            other_at = other_at_ref[sector * per + piece]
            rows = slice(piece * OS, (piece + 1) * OS)
            for part in range(2):
                keep_ref[own_at, part] = parts[part][rows, :width]
                send[other_at, part] = parts[part][rows, width:]
    done = 0
    for ref in send_refs:
        ref[...] = send[done : done + ref.shape[0]]
        done += ref.shape[0]


def second_level(starts, side, own_at, other_at, own, first, second, weights, chunks):
    sectors, stacked, window = weights.shape
    rng = own.shape[2]
    margin, rows = first.shape[1], own.shape[1]
    count = sectors * stacked // 2 // OS
    block = (2, OS, rng // 2)
    shapes = [jax.ShapeDtypeStruct((n,) + block, jnp.bfloat16) for n in (count,) + chunks]
    return pl.pallas_call(
        second_level_kernel,
        out_shape=shapes,
        in_specs=[SMEM] * 4 + [VMEM] * 4,
        out_specs=[VMEM] * len(shapes),
        scratch_shapes=[
            pltpu.VMEM((2, rows + 2 * margin, rng), jnp.bfloat16),
            pltpu.VMEM((count,) + block, jnp.bfloat16),
        ],
        compiler_params=params(),
        cost_estimate=cost(sectors * 2 * stacked * window * rng, 2**22),
        name="second_level",
    )(starts, side, own_at, other_at, own, first, second, weights)


def plan_kernel(
    me_ref, own_ref, other_ref, own_at_ref, other_at_ref, target_ref, rank_ref, taken, filled
):
    count = own_ref.shape[0]
    far_bit = taken.shape[0] // 2
    for owners_ref, at_ref in ((other_ref, other_at_ref), (own_ref, own_at_ref)):
        for target in range(taken.shape[0]):
            taken[target] = 0
        for bucket in range(filled.shape[0]):
            filled[bucket] = 0
        for sector in range(count):
            target = owners_ref[sector]
            rank = taken[target]
            taken[target] = rank + 1
            near = jnp.where(((target ^ me_ref[0]) & far_bit) == 0, count, 0)
            at_ref[sector] = rank + near
            filled[rank + near + 1] = filled[rank + near + 1] + 1
        for bucket in range(1, filled.shape[0]):
            filled[bucket] = filled[bucket] + filled[bucket - 1]
        for sector in range(count):
            bucket = at_ref[sector]
            place = filled[bucket]
            filled[bucket] = place + 1
            at_ref[sector] = place
            if at_ref is own_at_ref:
                target_ref[place] = owners_ref[sector]
                rank_ref[place] = jnp.where(bucket >= count, bucket - count, bucket)


def plan(me, own, other, beam_count):
    count = own.shape[0]
    shape = jax.ShapeDtypeStruct((count,), jnp.int32)
    return pl.pallas_call(
        plan_kernel,
        out_shape=[shape] * 4,
        in_specs=[SMEM] * 3,
        out_specs=[SMEM] * 4,
        scratch_shapes=[
            pltpu.SMEM((beam_count,), jnp.int32),
            pltpu.SMEM((2 * count + 1,), jnp.int32),
        ],
        compiler_params=params(),
        name="plan",
    )(me, own, other)


def wires_kernel(spans, me_ref, target_ref, rank_ref, keep_ref, *refs):
    wires = refs[-1]
    spare = wires.shape[0] - 1
    out_refs = refs[-1 - len(spans) : -1]
    other_ref, *summed_refs = refs[: -1 - len(spans)]
    wires[...] = jnp.zeros_like(wires)
    me = me_ref[0]
    early = all(low == 0 for _, low, _ in spans)

    def lay(place, total):
        rank = rank_ref[place]
        distance = target_ref[place] ^ me
        at = spare
        start = 0
        for number, low, high in spans:
            wanted = (distance == number) & (rank >= low) & (rank < high)
            at = jnp.where(wanted, start + rank - low, at)
            start += high - low
        wires[at] = total

    before = 0
    if not early:
        before = summed_refs[0].shape[0]
        for row in range(before):
            lay(row, summed_refs[0][row])
    for row in range(other_ref.shape[0]):
        place = before + row
        total = keep_ref[place].astype(jnp.float32) + other_ref[row].astype(jnp.float32)
        total = total.astype(jnp.bfloat16)
        lay(place, total)
        if early:
            summed_refs[0][row] = total
    start = 0
    for (_, low, high), ref in zip(spans, out_refs):
        ref[...] = wires[start : start + high - low]
        start += high - low


def wires(spans, me, target, rank, keep, other, summed=None):
    block = keep.shape[1:]
    sizes = [high - low for _, low, high in spans]
    inputs = [me, target, rank, keep, other]
    if summed is None:
        sizes = [other.shape[0]] + sizes
    else:
        inputs.append(summed)
    shapes = [jax.ShapeDtypeStruct((size,) + block, jnp.bfloat16) for size in sizes]
    total = sum(high - low for _, low, high in spans)
    return pl.pallas_call(
        functools.partial(wires_kernel, spans),
        out_shape=shapes,
        in_specs=[SMEM] * 3 + [VMEM] * (len(inputs) - 3),
        out_specs=[VMEM] * len(shapes),
        scratch_shapes=[pltpu.VMEM((total + 1,) + block, jnp.bfloat16)],
        compiler_params=params(),
        cost_estimate=cost(0, 2**21),
        name="early_wires" if summed is None else "late_wires",
    )(*inputs)


def collect_kernel(spans, capacity, me_ref, *refs):
    sems = refs[-1]
    out_ref = refs[-2]
    copies = []
    for number, (distance, low, high) in enumerate(spans):
        start = (me_ref[0] ^ distance) * capacity + low
        copies.append(
            pltpu.make_async_copy(
                refs[number], out_ref.at[pl.ds(start, high - low)], sems.at[number]
            )
        )
    for copy in copies:
        copy.start()
    for copy in copies:
        copy.wait()


def collect(spans, capacity, beam_count, me, received):
    shape = (beam_count * capacity,) + received[0].shape[1:]
    return pl.pallas_call(
        functools.partial(collect_kernel, spans, capacity),
        out_shape=jax.ShapeDtypeStruct(shape, jnp.bfloat16),
        in_specs=[SMEM] + [ANY] * len(received),
        out_specs=ANY,
        scratch_shapes=[pltpu.SemaphoreType.DMA((len(received),))],
        compiler_params=params(),
        cost_estimate=cost(0, 2**21),
        name="collect",
    )(me, *received)


def spread(spans, group):
    count = lax.axis_size("beam")
    received = []
    for (distance, _, _), wire in zip(spans, group):
        route = [(place, place ^ distance) for place in range(count)]
        received.append(lax.ppermute(wire, "beam", route) if distance else wire)
    return received


def stacked_weights(weights):
    return weights[0].reshape(weights.shape[1], -1, weights.shape[4])


def table_row(table, row_number):
    return lax.dynamic_index_in_dim(table, row_number, 0, keepdims=False)


def local(subimages, range_kernel, weights0, starts0, weights1, starts1, owners):
    aper_index = lax.axis_index("aperture")
    beam_index = lax.axis_index("beam")
    beam_count = lax.axis_size("beam")
    margin = MARGIN_BLOCKS * BLK
    local_blocks = subimages.shape[2] // BLK
    even = ((beam_index + aper_index) % 2 == 0).astype(jnp.int32)
    side = jnp.stack([even, aper_index % 2, aper_index // 2 % 2])
    me = beam_index.reshape(1)

    sector_count = owners.shape[1]
    capacity = max(2, 2 * sector_count // beam_count)
    early = max(1, 3 * capacity // 8)
    far = beam_count // 2
    chunks = (early * far, sector_count - early * far)
    distances = list(reversed(range(beam_count)))
    early_spans = tuple((distance, 0, early) for distance in distances if distance >= far)
    late_spans = tuple(
        (distance, early if distance >= far else 0, capacity) for distance in distances
    )

    own, first, second = resample(side, subimages[0], range_kernel[0], margin)
    first, second = trade_edges(first, second)
    own_owners = owners[0, :, 0]
    other_owners = partner(owners, "aperture", 1)[0, :, 0]
    own_at, other_at, target, rank = plan(me, own_owners, other_owners, beam_count)
    begin0 = table_row(starts0, aper_index) - (beam_index * local_blocks - MARGIN_BLOCKS)
    first, own_at, other_at, target, rank = lax.optimization_barrier(
        (first, own_at, other_at, target, rank)
    )
    keep, send = first_level(begin0, side, own, first, second, stacked_weights(weights0))
    other = partner(send, "aperture", 0)
    level_one = (keep.astype(jnp.float32) + other.astype(jnp.float32)).astype(jnp.bfloat16)

    rows = level_one.shape[1]
    first = lax.dynamic_slice_in_dim(level_one, even * (rows - margin), margin, 1)
    second = lax.dynamic_slice_in_dim(level_one, (1 - even) * (rows - margin), margin, 1)
    first, second = trade_edges(first, second)
    begin1 = table_row(starts1, aper_index) - (beam_index * 2 * local_blocks - MARGIN_BLOCKS)
    keep, *sends = second_level(
        begin1, side, own_at, other_at, level_one, first, second, stacked_weights(weights1), chunks
    )
    other = partner(sends[0], "aperture", 1)

    other, late = lax.optimization_barrier((other, sends[1]))
    late = partner(late, "aperture", 1)
    summed, *group = wires(early_spans, me, target, rank, keep, other)
    received = spread(early_spans, group)
    late, *received = lax.optimization_barrier((late, *received))
    group = wires(late_spans, me, target, rank, keep, late, summed)
    received += spread(late_spans, group)
    return collect(early_spans + late_spans, capacity, beam_count, me, received)[None]


def solution(mesh):
    return jax.shard_map(
        local,
        mesh=mesh,
        in_specs=(
            P("aperture", None, "beam", None),
            P("aperture", None, None, None),
            P("aperture", "beam", None, None, None),
            P(None, "beam"),
            P("aperture", "beam", None, None, None),
            P(None, "beam"),
            P("aperture", "beam", None),
        ),
        out_specs=P("aperture", "beam", None, None, None),
        check_vma=False,
    )
```

```python
import functools

import jax
import jax.numpy as jnp
from jax import lax
from jax.experimental import pallas as pl
from jax.experimental.pallas import tpu as pltpu
from jax.sharding import PartitionSpec as P

BLK = 32
NW = 10
REACH = 2
OS = 64
MARGIN_BLOCKS = (NW - 2) // 2 + REACH
VMEM_LIMIT = 8 * 1024 * 1024
MOST_VMEM = 53 * 1024 * 1024
ANY = pl.BlockSpec(memory_space=pl.ANY)
VMEM = pl.BlockSpec(memory_space=pltpu.VMEM)
SMEM = pl.BlockSpec(memory_space=pltpu.SMEM)


def params(limit=VMEM_LIMIT):
    return pltpu.CompilerParams(vmem_limit_bytes=limit)


def cost(macs, moved):
    return pl.CostEstimate(flops=2 * macs, bytes_accessed=moved, transcendentals=0)


def trade_edges(first, second):
    count = lax.axis_size("beam")
    received = []
    for order, block in enumerate((first, second)):
        route = []
        for aper in range(lax.axis_size("aperture")):
            for low in range((aper + order) % 2, count - 1, 2):
                place = aper * count + low
                route += [(place, place + 1), (place + 1, place)]
        received.append(lax.ppermute(block, ("aperture", "beam"), route))
    return received


def partner(block, axis, distance):
    count = lax.axis_size(axis)
    route = []
    for low in range(count):
        high = low | 1 << distance
        if high != low and high < count:
            route += [(low, high), (high, low)]
    return lax.ppermute(block, axis, route)


def dot(left, right):
    return jnp.dot(left, right, preferred_element_type=jnp.float32)


def resample_kernel(child_hbm, kernel_hbm, first_ref, second_ref, child, kernel, own, sems):
    aper, beam = lax.axis_index("aperture"), lax.axis_index("beam")
    half, quarter = aper & 1, (aper >> 1) & 1
    even = 1 - ((aper + beam) & 1)
    rows, rng = child.shape[1:]
    piece = rng // 4
    child_copy = pltpu.make_async_copy(child_hbm, child, sems.at[4])
    copies = []
    for place in range(4):
        source = (half ^ (place // 2)) * 2 + (quarter ^ (place % 2))
        copies.append(
            pltpu.make_async_copy(
                kernel_hbm.at[:, :, pl.ds(pl.multiple_of(source * piece, 128), piece)],
                kernel.at[:, :, place * piece : (place + 1) * piece],
                sems.at[place],
            )
        )
    child_copy.start()
    for copy in copies:
        copy.start()
    child_copy.wait()
    real, imag = child[0], child[1]
    margin = first_ref.shape[1]
    tail = pl.ds(pl.multiple_of(even * (rows - margin), BLK), margin)
    head = pl.ds(pl.multiple_of((1 - even) * (rows - margin), BLK), margin)
    for side in range(2):
        columns = slice(side * 2 * piece, (side + 1) * 2 * piece)
        copies[2 * side].wait()
        copies[2 * side + 1].wait()
        k_real, k_imag = kernel[0, :, columns], kernel[1, :, columns]
        own[0, :, columns] = (dot(real, k_real) - dot(imag, k_imag)).astype(jnp.bfloat16)
        own[1, :, columns] = (dot(real, k_imag) + dot(imag, k_real)).astype(jnp.bfloat16)
        for part in range(2):
            first_ref[part, :, columns] = own[part, tail, columns]
            second_ref[part, :, columns] = own[part, head, columns]


def resample(child, kernel, margin):
    rows, rng = child.shape[1:]
    shape = jax.ShapeDtypeStruct((2, margin, rng), jnp.bfloat16)
    return pl.pallas_call(
        resample_kernel,
        out_shape=(shape, shape),
        in_specs=[ANY, ANY],
        out_specs=(VMEM, VMEM),
        scratch_shapes=[
            pltpu.VMEM(child.shape, jnp.bfloat16),
            pltpu.VMEM(kernel.shape, jnp.bfloat16),
            pltpu.VMEM(child.shape, jnp.bfloat16),
            pltpu.SemaphoreType.DMA((5,)),
        ],
        compiler_params=params(MOST_VMEM),
        cost_estimate=cost(4 * rows * rng * rng, 2**21),
        name="resample",
    )(child, kernel)


def complex_window(weights, real, imag):
    beams = weights.shape[0] // 2
    with_real = dot(weights, real)
    with_imag = dot(weights, imag)
    return (
        (with_real[:beams] - with_imag[beams:]).astype(jnp.bfloat16),
        (with_imag[:beams] + with_real[beams:]).astype(jnp.bfloat16),
    )


def place_halos(padded, even, rows, first, second):
    margin = first.shape[1]
    far = margin + rows
    padded[:, pl.ds(pl.multiple_of(even * far, BLK), margin), :] = first
    padded[:, pl.ds(pl.multiple_of((1 - even) * far, BLK), margin), :] = second


def first_level_kernel(
    column, rows, starts_ref, side_ref, sent_first_ref, sent_second_ref, first_ref, second_ref,
    weights_ref, out_ref, padded,
):
    sectors, stacked, window = weights_ref.shape
    beams = stacked // 2
    margin = first_ref.shape[1]
    columns = slice(column, column + out_ref.shape[2])
    even = side_ref[0]
    tail = pl.multiple_of(margin + even * (rows - margin), BLK)
    head = pl.multiple_of(margin + (1 - even) * (rows - margin), BLK)
    padded[:, pl.ds(tail, margin), :] = sent_first_ref[:, :, columns]
    padded[:, pl.ds(head, margin), :] = sent_second_ref[:, :, columns]
    place_halos(padded, even, rows, first_ref[:, :, columns], second_ref[:, :, columns])
    for sector in range(sectors):
        place = pl.ds(pl.multiple_of(starts_ref[sector] * BLK, BLK), window)
        parts = complex_window(weights_ref[sector], padded[0, place, :], padded[1, place, :])
        for part in range(2):
            out_ref[part, sector * beams : (sector + 1) * beams, :] = parts[part]


def first_level(column, rows, starts, side, sent, halos, weights):
    sectors, stacked, window = weights.shape
    margin, rng = sent[0].shape[1:]
    assert 2 * margin >= rows
    width = rng // 2
    return pl.pallas_call(
        functools.partial(first_level_kernel, column, rows),
        out_shape=jax.ShapeDtypeStruct((2, sectors * stacked // 2, width), jnp.bfloat16),
        in_specs=[SMEM, SMEM] + [VMEM] * 5,
        out_specs=VMEM,
        scratch_shapes=[pltpu.VMEM((2, rows + 2 * margin, width), jnp.bfloat16)],
        compiler_params=params(),
        cost_estimate=cost(sectors * 2 * stacked * window * width, 2**21),
        name="first_level",
    )(starts, side, *sent, *halos, weights)


def second_level_early_kernel(
    starts_ref, side_ref, sector_ref, own_ref, first_ref, second_ref, weights_ref, send_ref, padded
):
    _, stacked, window = weights_ref.shape
    per = stacked // 2 // OS
    margin, rows = first_ref.shape[1], own_ref.shape[1]
    columns = slice(send_ref.shape[3], 2 * send_ref.shape[3])
    padded[:, margin : margin + rows, :] = own_ref[:, :, columns]
    place_halos(padded, side_ref[0], rows, first_ref[:, :, columns], second_ref[:, :, columns])
    for place in range(send_ref.shape[0]):
        sector = sector_ref[place] // per
        piece = pl.multiple_of(sector_ref[place] % per * OS, OS)
        window_rows = pl.ds(pl.multiple_of(starts_ref[sector] * BLK, BLK), window)
        weights = jnp.concatenate(
            [
                weights_ref[sector, pl.ds(piece, OS), :],
                weights_ref[sector, pl.ds(pl.multiple_of(piece + stacked // 2, OS), OS), :],
            ]
        )
        parts = complex_window(weights, padded[0, window_rows, :], padded[1, window_rows, :])
        for part in range(2):
            send_ref[place, part] = parts[part]


def second_level_kernel(
    starts_ref, side_ref, own_at_ref, other_at_ref, own_ref, first_ref, second_ref, weights_ref,
    keep_ref, send_ref, padded, send,
):
    sectors, stacked, window = weights_ref.shape
    beams = stacked // 2
    width = keep_ref.shape[3]
    margin, rows = first_ref.shape[1], own_ref.shape[1]
    padded[:, margin : margin + rows, :] = own_ref[...]
    place_halos(padded, side_ref[0], rows, first_ref[...], second_ref[...])
    per = beams // OS
    for sector in range(sectors):
        place = pl.ds(pl.multiple_of(starts_ref[sector] * BLK, BLK), window)
        parts = complex_window(weights_ref[sector], padded[0, place, :], padded[1, place, :])
        for piece in range(per):
            own_at = own_at_ref[sector * per + piece]
            other_at = other_at_ref[sector * per + piece]
            taken = slice(piece * OS, (piece + 1) * OS)
            for part in range(2):
                keep_ref[own_at, part] = parts[part][taken, :width]
                send[other_at, part] = parts[part][taken, width:]
    send_ref[...] = send[send.shape[0] - send_ref.shape[0] :]


def second_level(starts, side, planned, own, halos, weights, early):
    sectors, stacked, window = weights.shape
    margin, rows, rng = halos[0].shape[1], own.shape[1], own.shape[2]
    count = sectors * stacked // 2 // OS
    block = (2, OS, rng // 2)
    own_at, other_at, other_sector = planned
    early_send = pl.pallas_call(
        second_level_early_kernel,
        out_shape=jax.ShapeDtypeStruct((early,) + block, jnp.bfloat16),
        in_specs=[SMEM] * 3 + [VMEM] * 4,
        out_specs=VMEM,
        scratch_shapes=[pltpu.VMEM((2, rows + 2 * margin, rng // 2), jnp.bfloat16)],
        compiler_params=params(),
        cost_estimate=cost(early * 2 * 2 * OS * window * rng // 2, 2**20),
        name="second_level_early",
    )(starts, side, other_sector, own, *halos, weights)
    shapes = [jax.ShapeDtypeStruct((n,) + block, jnp.bfloat16) for n in (count, count - early)]
    keep, late_send = pl.pallas_call(
        second_level_kernel,
        out_shape=shapes,
        in_specs=[SMEM] * 4 + [VMEM] * 4,
        out_specs=[VMEM] * 2,
        scratch_shapes=[
            pltpu.VMEM((2, rows + 2 * margin, rng), jnp.bfloat16),
            pltpu.VMEM((count,) + block, jnp.bfloat16),
        ],
        compiler_params=params(),
        cost_estimate=cost(sectors * 2 * stacked * window * rng, 2**22),
        name="second_level",
    )(starts, side, own_at, other_at, own, *halos, weights)
    return keep, early_send, late_send


def plan_kernel(
    me_ref, own_ref, other_ref, own_at_ref, other_at_ref, other_sector_ref, target_ref, rank_ref,
    taken, filled,
):
    count = own_ref.shape[0]
    far_bit = taken.shape[0] // 2
    for owners_ref, at_ref in ((other_ref, other_at_ref), (own_ref, own_at_ref)):
        for target in range(taken.shape[0]):
            taken[target] = 0
        for bucket in range(filled.shape[0]):
            filled[bucket] = 0
        for sector in range(count):
            target = owners_ref[sector]
            rank = taken[target]
            taken[target] = rank + 1
            near = jnp.where(((target ^ me_ref[0]) & far_bit) == 0, count, 0)
            at_ref[sector] = rank + near
            filled[rank + near + 1] = filled[rank + near + 1] + 1
        for bucket in range(1, filled.shape[0]):
            filled[bucket] = filled[bucket] + filled[bucket - 1]
        for sector in range(count):
            bucket = at_ref[sector]
            place = filled[bucket]
            filled[bucket] = place + 1
            at_ref[sector] = place
            if at_ref is own_at_ref:
                target_ref[place] = owners_ref[sector]
                rank_ref[place] = jnp.where(bucket >= count, bucket - count, bucket)
            else:
                other_sector_ref[place] = sector


def plan(me, own, other, beam_count):
    count = own.shape[0]
    shape = jax.ShapeDtypeStruct((count,), jnp.int32)
    return pl.pallas_call(
        plan_kernel,
        out_shape=[shape] * 5,
        in_specs=[SMEM] * 3,
        out_specs=[SMEM] * 5,
        scratch_shapes=[
            pltpu.SMEM((beam_count,), jnp.int32),
            pltpu.SMEM((2 * count + 1,), jnp.int32),
        ],
        compiler_params=params(),
        name="plan",
    )(me, own, other)


def wires_kernel(spans, me_ref, target_ref, rank_ref, keep_ref, *refs):
    wires = refs[-1]
    spare = wires.shape[0] - 1
    out_refs = refs[-1 - len(spans) : -1]
    other_ref, *summed_refs = refs[: -1 - len(spans)]
    wires[...] = jnp.zeros_like(wires)
    me = me_ref[0]
    early = all(low == 0 for _, low, _ in spans)

    def lay(place, total):
        rank = rank_ref[place]
        distance = target_ref[place] ^ me
        at = spare
        start = 0
        for number, low, high in spans:
            wanted = (distance == number) & (rank >= low) & (rank < high)
            at = jnp.where(wanted, start + rank - low, at)
            start += high - low
        wires[at] = total

    before = 0
    if not early:
        before = summed_refs[0].shape[0]
        for row in range(before):
            lay(row, summed_refs[0][row])
    for row in range(other_ref.shape[0]):
        place = before + row
        total = keep_ref[place].astype(jnp.float32) + other_ref[row].astype(jnp.float32)
        total = total.astype(jnp.bfloat16)
        lay(place, total)
        if early:
            summed_refs[0][row] = total
    start = 0
    for (_, low, high), ref in zip(spans, out_refs):
        ref[...] = wires[start : start + high - low]
        start += high - low


def wires(spans, me, target, rank, keep, other, summed=None):
    block = keep.shape[1:]
    sizes = [high - low for _, low, high in spans]
    inputs = [me, target, rank, keep, other]
    if summed is None:
        sizes = [other.shape[0]] + sizes
    else:
        inputs.append(summed)
    shapes = [jax.ShapeDtypeStruct((size,) + block, jnp.bfloat16) for size in sizes]
    total = sum(high - low for _, low, high in spans)
    return pl.pallas_call(
        functools.partial(wires_kernel, spans),
        out_shape=shapes,
        in_specs=[SMEM] * 3 + [VMEM] * (len(inputs) - 3),
        out_specs=[VMEM] * len(shapes),
        scratch_shapes=[pltpu.VMEM((total + 1,) + block, jnp.bfloat16)],
        compiler_params=params(),
        cost_estimate=cost(0, 2**21),
        name="early_wires" if summed is None else "late_wires",
    )(*inputs)


def collect_kernel(spans, capacity, me_ref, *refs):
    sems = refs[-1]
    out_ref = refs[-2]
    copies = []
    for number, (distance, low, high) in enumerate(spans):
        start = (me_ref[0] ^ distance) * capacity + low
        copies.append(
            pltpu.make_async_copy(
                refs[number], out_ref.at[pl.ds(start, high - low)], sems.at[number]
            )
        )
    for copy in copies:
        copy.start()
    for copy in copies:
        copy.wait()


def collect(spans, capacity, beam_count, me, received):
    shape = (beam_count * capacity,) + received[0].shape[1:]
    return pl.pallas_call(
        functools.partial(collect_kernel, spans, capacity),
        out_shape=jax.ShapeDtypeStruct(shape, jnp.bfloat16),
        in_specs=[SMEM] + [ANY] * len(received),
        out_specs=ANY,
        scratch_shapes=[pltpu.SemaphoreType.DMA((len(received),))],
        compiler_params=params(),
        cost_estimate=cost(0, 2**21),
        name="collect",
    )(me, *received)


def spread(spans, group):
    count = lax.axis_size("beam")
    received = []
    for (distance, _, _), wire in zip(spans, group):
        route = [(place, place ^ distance) for place in range(count)]
        received.append(lax.ppermute(wire, "beam", route) if distance else wire)
    return received


def stacked_weights(weights):
    return weights[0].reshape(weights.shape[1], -1, weights.shape[4])


def table_row(table, row_number):
    return lax.dynamic_index_in_dim(table, row_number, 0, keepdims=False)


def local(subimages, range_kernel, weights0, starts0, weights1, starts1, owners):
    aper_index = lax.axis_index("aperture")
    beam_index = lax.axis_index("beam")
    beam_count = lax.axis_size("beam")
    margin = MARGIN_BLOCKS * BLK
    rows = subimages.shape[2]
    local_blocks = rows // BLK
    even = ((beam_index + aper_index) % 2 == 0).astype(jnp.int32)
    side = even.reshape(1)
    me = beam_index.reshape(1)

    sector_count = owners.shape[1]
    capacity = max(2, 2 * sector_count // beam_count)
    early = max(1, 3 * capacity // 8)
    far = beam_count // 2
    distances = list(reversed(range(beam_count)))
    early_spans = tuple((distance, 0, early) for distance in distances if distance >= far)
    late_spans = tuple(
        (distance, early if distance >= far else 0, capacity) for distance in distances
    )

    sent = resample(subimages[0], range_kernel[0], margin)
    halos = trade_edges(*sent)
    own_owners = owners[0, :, 0]
    other_owners = partner(owners, "aperture", 1)[0, :, 0]
    planned = plan(me, own_owners, other_owners, beam_count)
    begin0 = table_row(starts0, aper_index) - (beam_index * local_blocks - MARGIN_BLOCKS)
    halos, planned = lax.optimization_barrier((halos, planned))
    *planned, target, rank = planned
    width = range_kernel.shape[3] // 2
    weights = stacked_weights(weights0)
    send = first_level(width, rows, begin0, side, sent, halos, weights)
    other = partner(send, "aperture", 0)
    keep = first_level(0, rows, begin0, side, sent, halos, weights)
    level_one = (keep.astype(jnp.float32) + other.astype(jnp.float32)).astype(jnp.bfloat16)

    beams = level_one.shape[1]
    first = lax.dynamic_slice_in_dim(level_one, even * (beams - margin), margin, 1)
    second = lax.dynamic_slice_in_dim(level_one, (1 - even) * (beams - margin), margin, 1)
    halos = trade_edges(first, second)
    begin1 = table_row(starts1, aper_index) - (beam_index * 2 * local_blocks - MARGIN_BLOCKS)
    keep, send, late = second_level(
        begin1, side, planned, level_one, halos, stacked_weights(weights1), early * far
    )
    other = partner(send, "aperture", 1)
    other, late = lax.optimization_barrier((other, late))
    late = partner(late, "aperture", 1)
    summed, *group = wires(early_spans, me, target, rank, keep, other)
    received = spread(early_spans, group)
    late, *received = lax.optimization_barrier((late, *received))
    group = wires(late_spans, me, target, rank, keep, late, summed)
    received += spread(late_spans, group)
    return collect(early_spans + late_spans, capacity, beam_count, me, received)[None]


def solution(mesh):
    return jax.shard_map(
        local,
        mesh=mesh,
        in_specs=(
            P("aperture", None, "beam", None),
            P("aperture", None, None, None),
            P("aperture", "beam", None, None, None),
            P(None, "beam"),
            P("aperture", "beam", None, None, None),
            P(None, "beam"),
            P("aperture", "beam", None),
        ),
        out_specs=P("aperture", "beam", None, None, None),
        check_vma=False,
    )
```

```python
import functools

import jax
import jax.numpy as jnp
from jax import lax
from jax.experimental import pallas as pl
from jax.experimental.pallas import tpu as pltpu
from jax.sharding import PartitionSpec as P

BLK = 32
NW = 10
REACH = 2
OS = 64
MARGIN_BLOCKS = (NW - 2) // 2 + REACH
VMEM_LIMIT = 8 * 1024 * 1024
MOST_VMEM = 53 * 1024 * 1024
ANY = pl.BlockSpec(memory_space=pl.ANY)
VMEM = pl.BlockSpec(memory_space=pltpu.VMEM)
SMEM = pl.BlockSpec(memory_space=pltpu.SMEM)


def params(limit=VMEM_LIMIT):
    return pltpu.CompilerParams(vmem_limit_bytes=limit)


def cost(macs, moved):
    return pl.CostEstimate(flops=2 * macs, bytes_accessed=moved, transcendentals=0)


def trade_edges(first, second):
    count = lax.axis_size("beam")
    received = []
    for order, block in enumerate((first, second)):
        route = [(place, place) for place in range(count)]
        for low in range(order, count - 1, 2):
            route[low], route[low + 1] = (low, low + 1), (low + 1, low)
        received.append(lax.ppermute(block, "beam", route))
    return received


def partner(block, axis, distance):
    count = lax.axis_size(axis)
    route = []
    for low in range(count):
        high = low | 1 << distance
        if high != low and high < count:
            route += [(low, high), (high, low)]
    return lax.ppermute(block, axis, route)


def dot(left, right):
    return jnp.dot(left, right, preferred_element_type=jnp.float32)


def resample_kernel(child_hbm, kernel_hbm, first_ref, second_ref, child, kernel, own, sems):
    aper, beam = lax.axis_index("aperture"), lax.axis_index("beam")
    half, quarter = aper & 1, (aper >> 1) & 1
    even = 1 - (beam & 1)
    rows, rng = child.shape[1:]
    piece = rng // 4
    child_copy = pltpu.make_async_copy(child_hbm, child, sems.at[4])
    copies = []
    for place in range(4):
        source = (half ^ (place // 2)) * 2 + (quarter ^ (place % 2))
        copies.append(
            pltpu.make_async_copy(
                kernel_hbm.at[:, :, pl.ds(pl.multiple_of(source * piece, 128), piece)],
                kernel.at[:, :, place * piece : (place + 1) * piece],
                sems.at[place],
            )
        )
    child_copy.start()
    for copy in copies:
        copy.start()
    child_copy.wait()
    real, imag = child[0], child[1]
    margin = first_ref.shape[1]
    tail = pl.ds(pl.multiple_of(even * (rows - margin), BLK), margin)
    head = pl.ds(pl.multiple_of((1 - even) * (rows - margin), BLK), margin)
    for side in range(2):
        columns = slice(side * 2 * piece, (side + 1) * 2 * piece)
        copies[2 * side].wait()
        copies[2 * side + 1].wait()
        k_real, k_imag = kernel[0, :, columns], kernel[1, :, columns]
        own[0, :, columns] = (dot(real, k_real) - dot(imag, k_imag)).astype(jnp.bfloat16)
        own[1, :, columns] = (dot(real, k_imag) + dot(imag, k_real)).astype(jnp.bfloat16)
        for part in range(2):
            first_ref[part, :, columns] = own[part, tail, columns]
            second_ref[part, :, columns] = own[part, head, columns]


def resample(child, kernel, margin):
    rows, rng = child.shape[1:]
    shape = jax.ShapeDtypeStruct((2, margin, rng), jnp.bfloat16)
    return pl.pallas_call(
        resample_kernel,
        out_shape=(shape, shape),
        in_specs=[ANY, ANY],
        out_specs=(VMEM, VMEM),
        scratch_shapes=[
            pltpu.VMEM(child.shape, jnp.bfloat16),
            pltpu.VMEM(kernel.shape, jnp.bfloat16),
            pltpu.VMEM(child.shape, jnp.bfloat16),
            pltpu.SemaphoreType.DMA((5,)),
        ],
        compiler_params=params(MOST_VMEM),
        cost_estimate=cost(4 * rows * rng * rng, 2**21),
        name="resample",
    )(child, kernel)


def complex_window(weights, real, imag):
    beams = weights.shape[0] // 2
    with_real = dot(weights, real)
    with_imag = dot(weights, imag)
    return (
        (with_real[:beams] - with_imag[beams:]).astype(jnp.bfloat16),
        (with_imag[:beams] + with_real[beams:]).astype(jnp.bfloat16),
    )


def place_halos(padded, side_ref, rows, first, second):
    even, lowest, highest = side_ref[0], side_ref[1], side_ref[2]
    margin = first.shape[1]
    far = margin + rows
    padded[:, pl.ds(pl.multiple_of(even * far, BLK), margin), :] = first
    padded[:, pl.ds(pl.multiple_of((1 - even) * far, BLK), margin), :] = second
    zeros = jnp.zeros_like(first)

    @pl.when(lowest == 1)
    def _():
        padded[:, :margin, :] = zeros

    @pl.when(highest == 1)
    def _():
        padded[:, far:, :] = zeros


def first_level_kernel(
    column, rows, starts_ref, side_ref, sent_first_ref, sent_second_ref, first_ref, second_ref,
    weights_ref, out_ref, padded,
):
    sectors, stacked, window = weights_ref.shape
    beams = stacked // 2
    margin = first_ref.shape[1]
    columns = slice(column, column + out_ref.shape[2])
    even = side_ref[0]
    tail = pl.multiple_of(margin + even * (rows - margin), BLK)
    head = pl.multiple_of(margin + (1 - even) * (rows - margin), BLK)
    padded[:, pl.ds(tail, margin), :] = sent_first_ref[:, :, columns]
    padded[:, pl.ds(head, margin), :] = sent_second_ref[:, :, columns]
    place_halos(padded, side_ref, rows, first_ref[:, :, columns], second_ref[:, :, columns])
    for sector in range(sectors):
        place = pl.ds(pl.multiple_of(starts_ref[sector] * BLK, BLK), window)
        parts = complex_window(weights_ref[sector], padded[0, place, :], padded[1, place, :])
        for part in range(2):
            out_ref[part, sector * beams : (sector + 1) * beams, :] = parts[part]


def first_level(column, rows, starts, side, sent, halos, weights):
    sectors, stacked, window = weights.shape
    margin, rng = sent[0].shape[1:]
    assert 2 * margin >= rows
    width = rng // 2
    return pl.pallas_call(
        functools.partial(first_level_kernel, column, rows),
        out_shape=jax.ShapeDtypeStruct((2, sectors * stacked // 2, width), jnp.bfloat16),
        in_specs=[SMEM, SMEM] + [VMEM] * 5,
        out_specs=VMEM,
        scratch_shapes=[pltpu.VMEM((2, rows + 2 * margin, width), jnp.bfloat16)],
        compiler_params=params(),
        cost_estimate=cost(sectors * 2 * stacked * window * width, 2**21),
        name="first_level",
    )(starts, side, *sent, *halos, weights)


def second_level_early_kernel(
    starts_ref, side_ref, sector_ref, own_ref, first_ref, second_ref, weights_ref, send_ref, padded
):
    _, stacked, window = weights_ref.shape
    per = stacked // 2 // OS
    margin, rows = first_ref.shape[1], own_ref.shape[1]
    columns = slice(send_ref.shape[3], 2 * send_ref.shape[3])
    padded[:, margin : margin + rows, :] = own_ref[:, :, columns]
    place_halos(padded, side_ref, rows, first_ref[:, :, columns], second_ref[:, :, columns])
    for place in range(send_ref.shape[0]):
        sector = sector_ref[place] // per
        piece = pl.multiple_of(sector_ref[place] % per * OS, OS)
        window_rows = pl.ds(pl.multiple_of(starts_ref[sector] * BLK, BLK), window)
        weights = jnp.concatenate(
            [
                weights_ref[sector, pl.ds(piece, OS), :],
                weights_ref[sector, pl.ds(pl.multiple_of(piece + stacked // 2, OS), OS), :],
            ]
        )
        parts = complex_window(weights, padded[0, window_rows, :], padded[1, window_rows, :])
        for part in range(2):
            send_ref[place, part] = parts[part]


def second_level_kernel(
    starts_ref, side_ref, own_at_ref, other_at_ref, own_ref, first_ref, second_ref, weights_ref,
    keep_ref, send_ref, padded, send,
):
    sectors, stacked, window = weights_ref.shape
    beams = stacked // 2
    width = keep_ref.shape[3]
    margin, rows = first_ref.shape[1], own_ref.shape[1]
    padded[:, margin : margin + rows, :] = own_ref[...]
    place_halos(padded, side_ref, rows, first_ref[...], second_ref[...])
    per = beams // OS
    for sector in range(sectors):
        place = pl.ds(pl.multiple_of(starts_ref[sector] * BLK, BLK), window)
        parts = complex_window(weights_ref[sector], padded[0, place, :], padded[1, place, :])
        for piece in range(per):
            own_at = own_at_ref[sector * per + piece]
            other_at = other_at_ref[sector * per + piece]
            taken = slice(piece * OS, (piece + 1) * OS)
            for part in range(2):
                keep_ref[own_at, part] = parts[part][taken, :width]
                send[other_at, part] = parts[part][taken, width:]
    send_ref[...] = send[send.shape[0] - send_ref.shape[0] :]


def second_level(starts, side, planned, own, halos, weights, early):
    sectors, stacked, window = weights.shape
    margin, rows, rng = halos[0].shape[1], own.shape[1], own.shape[2]
    count = sectors * stacked // 2 // OS
    block = (2, OS, rng // 2)
    own_at, other_at, other_sector = planned
    early_send = pl.pallas_call(
        second_level_early_kernel,
        out_shape=jax.ShapeDtypeStruct((early,) + block, jnp.bfloat16),
        in_specs=[SMEM] * 3 + [VMEM] * 4,
        out_specs=VMEM,
        scratch_shapes=[pltpu.VMEM((2, rows + 2 * margin, rng // 2), jnp.bfloat16)],
        compiler_params=params(),
        cost_estimate=cost(early * 2 * 2 * OS * window * rng // 2, 2**20),
        name="second_level_early",
    )(starts, side, other_sector, own, *halos, weights)
    shapes = [jax.ShapeDtypeStruct((n,) + block, jnp.bfloat16) for n in (count, count - early)]
    keep, late_send = pl.pallas_call(
        second_level_kernel,
        out_shape=shapes,
        in_specs=[SMEM] * 4 + [VMEM] * 4,
        out_specs=[VMEM] * 2,
        scratch_shapes=[
            pltpu.VMEM((2, rows + 2 * margin, rng), jnp.bfloat16),
            pltpu.VMEM((count,) + block, jnp.bfloat16),
        ],
        compiler_params=params(),
        cost_estimate=cost(sectors * 2 * stacked * window * rng, 2**22),
        name="second_level",
    )(starts, side, own_at, other_at, own, *halos, weights)
    return keep, early_send, late_send


def plan_kernel(
    shift, me_ref, own_ref, other_ref, own_at_ref, other_at_ref, other_sector_ref, target_ref, rank_ref,
    taken, filled,
):
    count = own_ref.shape[0]
    far_bit = taken.shape[0] // 2

    def delay(target):
        distance = target ^ me_ref[0]
        return jnp.where((distance & far_bit) == 0, 2 * count, (distance & 1) * shift)

    for owners_ref, at_ref in ((other_ref, other_at_ref), (own_ref, own_at_ref)):
        for target in range(taken.shape[0]):
            taken[target] = 0
        for bucket in range(filled.shape[0]):
            filled[bucket] = 0
        for sector in range(count):
            target = owners_ref[sector]
            rank = taken[target]
            taken[target] = rank + 1
            bucket = rank + delay(target)
            at_ref[sector] = bucket
            filled[bucket + 1] = filled[bucket + 1] + 1
        for bucket in range(1, filled.shape[0]):
            filled[bucket] = filled[bucket] + filled[bucket - 1]
        for sector in range(count):
            bucket = at_ref[sector]
            place = filled[bucket]
            filled[bucket] = place + 1
            at_ref[sector] = place
            if at_ref is own_at_ref:
                target_ref[place] = owners_ref[sector]
                rank_ref[place] = bucket - delay(owners_ref[sector])
            else:
                other_sector_ref[place] = sector


def plan(shift, me, own, other, beam_count):
    count = own.shape[0]
    shape = jax.ShapeDtypeStruct((count,), jnp.int32)
    return pl.pallas_call(
        functools.partial(plan_kernel, shift),
        out_shape=[shape] * 5,
        in_specs=[SMEM] * 3,
        out_specs=[SMEM] * 5,
        scratch_shapes=[
            pltpu.SMEM((beam_count,), jnp.int32),
            pltpu.SMEM((3 * count + 1,), jnp.int32),
        ],
        compiler_params=params(),
        name="plan",
    )(me, own, other)


def wires_kernel(spans, early, me_ref, target_ref, rank_ref, keep_ref, *refs):
    wires = refs[-1]
    spare = wires.shape[0] - 1
    out_refs = refs[-1 - len(spans) : -1]
    other_ref, *summed_refs = refs[: -1 - len(spans)]
    wires[...] = jnp.zeros_like(wires)
    me = me_ref[0]

    def lay(place, total):
        rank = rank_ref[place]
        distance = target_ref[place] ^ me
        at = spare
        start = 0
        for number, low, high in spans:
            wanted = (distance == number) & (rank >= low) & (rank < high)
            at = jnp.where(wanted, start + rank - low, at)
            start += high - low
        wires[at] = total

    before = 0
    if not early:
        before = summed_refs[0].shape[0]
        for row in range(before):
            lay(row, summed_refs[0][row])
    for row in range(other_ref.shape[0]):
        place = before + row
        total = keep_ref[place].astype(jnp.float32) + other_ref[row].astype(jnp.float32)
        total = total.astype(jnp.bfloat16)
        lay(place, total)
        if early:
            summed_refs[0][row] = total
    start = 0
    for (_, low, high), ref in zip(spans, out_refs):
        ref[...] = wires[start : start + high - low]
        start += high - low


def wires(spans, me, target, rank, keep, other, summed=None):
    block = keep.shape[1:]
    sizes = [high - low for _, low, high in spans]
    inputs = [me, target, rank, keep, other]
    if summed is None:
        sizes = [other.shape[0]] + sizes
    else:
        inputs.append(summed)
    shapes = [jax.ShapeDtypeStruct((size,) + block, jnp.bfloat16) for size in sizes]
    total = sum(high - low for _, low, high in spans)
    return pl.pallas_call(
        functools.partial(wires_kernel, spans, summed is None),
        out_shape=shapes,
        in_specs=[SMEM] * 3 + [VMEM] * (len(inputs) - 3),
        out_specs=[VMEM] * len(shapes),
        scratch_shapes=[pltpu.VMEM((total + 1,) + block, jnp.bfloat16)],
        compiler_params=params(),
        cost_estimate=cost(0, 2**21),
        name="early_wires" if summed is None else "late_wires",
    )(*inputs)


def collect_kernel(spans, capacity, me_ref, *refs):
    sems = refs[-1]
    out_ref = refs[-2]
    copies = []
    for number, (distance, low, high) in enumerate(spans):
        start = (me_ref[0] ^ distance) * capacity + low
        copies.append(
            pltpu.make_async_copy(
                refs[number], out_ref.at[pl.ds(start, high - low)], sems.at[number]
            )
        )
    for copy in copies:
        copy.start()
    for copy in copies:
        copy.wait()


def collect(spans, capacity, beam_count, me, received):
    shape = (beam_count * capacity,) + received[0].shape[1:]
    return pl.pallas_call(
        functools.partial(collect_kernel, spans, capacity),
        out_shape=jax.ShapeDtypeStruct(shape, jnp.bfloat16),
        in_specs=[SMEM] + [ANY] * len(received),
        out_specs=ANY,
        scratch_shapes=[pltpu.SemaphoreType.DMA((len(received),))],
        compiler_params=params(),
        cost_estimate=cost(0, 2**21),
        name="collect",
    )(me, *received)


def spread(spans, group):
    count = lax.axis_size("beam")
    received = []
    for (distance, _, _), wire in zip(spans, group):
        route = [(place, place ^ distance) for place in range(count)]
        received.append(lax.ppermute(wire, "beam", route) if distance else wire)
    return received


def stacked_weights(weights):
    return weights[0].reshape(weights.shape[1], -1, weights.shape[4])


def table_row(table, row_number):
    return lax.dynamic_index_in_dim(table, row_number, 0, keepdims=False)


def local(subimages, range_kernel, weights0, starts0, weights1, starts1, owners):
    aper_index = lax.axis_index("aperture")
    beam_index = lax.axis_index("beam")
    beam_count = lax.axis_size("beam")
    margin = MARGIN_BLOCKS * BLK
    rows = subimages.shape[2]
    local_blocks = rows // BLK
    even = (beam_index + 1) % 2
    ends = (beam_index == 0, beam_index == beam_count - 1)
    side = jnp.stack([even] + [end.astype(jnp.int32) for end in ends])
    me = beam_index.reshape(1)

    sector_count = owners.shape[1]
    capacity = max(2, 2 * sector_count // beam_count)
    shorter, longer = max(1, capacity // 4), max(1, capacity // 2)
    far = range(beam_count // 2, beam_count)
    odd = [distance for distance in far if distance % 2]
    others = [distance for distance in far if distance % 2 == 0]
    early = len(odd) * shorter + len(others) * longer
    early_spans = [(distance, 0, shorter) for distance in odd]
    early_spans += [(distance, 0, longer) for distance in others]
    late_spans = [(distance, shorter, capacity) for distance in odd]
    for distance in range(1, beam_count // 2):
        late_spans += [(distance, 0, capacity // 2), (distance, capacity // 2, capacity)]
    late_spans.append((0, 0, capacity))
    last_spans = [(distance, longer, capacity) for distance in others]

    sent = resample(subimages[0], range_kernel[0], margin)
    halos = trade_edges(*sent)
    own_owners = owners[0, :, 0]
    other_owners = partner(owners, "aperture", 1)[0, :, 0]
    planned = plan(longer - shorter, me, own_owners, other_owners, beam_count)
    begin0 = table_row(starts0, aper_index) - (beam_index * local_blocks - MARGIN_BLOCKS)
    halos, planned = lax.optimization_barrier((halos, planned))
    *planned, target, rank = planned
    width = range_kernel.shape[3] // 2
    weights = stacked_weights(weights0)
    send = first_level(width, rows, begin0, side, sent, halos, weights)
    other = partner(send, "aperture", 0)
    keep = first_level(0, rows, begin0, side, sent, halos, weights)
    level_one = (keep.astype(jnp.float32) + other.astype(jnp.float32)).astype(jnp.bfloat16)

    beams = level_one.shape[1]
    first = lax.dynamic_slice_in_dim(level_one, even * (beams - margin), margin, 1)
    second = lax.dynamic_slice_in_dim(level_one, (1 - even) * (beams - margin), margin, 1)
    halos = trade_edges(first, second)
    begin1 = table_row(starts1, aper_index) - (beam_index * 2 * local_blocks - MARGIN_BLOCKS)
    keep, send, late = second_level(
        begin1, side, planned, level_one, halos, stacked_weights(weights1), early
    )
    other = partner(send, "aperture", 1)
    other, late = lax.optimization_barrier((other, late))
    late = partner(late, "aperture", 1)
    summed, *group = wires(early_spans, me, target, rank, keep, other)
    received = spread(early_spans, group)
    from_odd, from_others = received[: len(odd)], received[len(odd) :]
    ready, from_odd = lax.optimization_barrier((late, from_odd))
    group = wires(late_spans, me, target, rank, keep, ready, summed)
    received = from_odd + spread(late_spans, group)
    ready, from_others = lax.optimization_barrier((late, from_others))
    group = wires(last_spans, me, target, rank, keep, ready, summed)
    received += from_others + spread(last_spans, group)
    spans = early_spans[: len(odd)] + late_spans + early_spans[len(odd) :] + last_spans
    return collect(spans, capacity, beam_count, me, received)[None]


def solution(mesh):
    return jax.shard_map(
        local,
        mesh=mesh,
        in_specs=(
            P("aperture", None, "beam", None),
            P("aperture", None, None, None),
            P("aperture", "beam", None, None, None),
            P(None, "beam"),
            P("aperture", "beam", None, None, None),
            P(None, "beam"),
            P("aperture", "beam", None),
        ),
        out_specs=P("aperture", "beam", None, None, None),
        check_vma=False,
    )
```

```python
import functools

import jax
import jax.numpy as jnp
from jax import lax
from jax.experimental import pallas as pl
from jax.experimental.pallas import tpu as pltpu
from jax.sharding import PartitionSpec as P

BLK = 32
NW = 10
REACH = 2
OS = 64
MARGIN_BLOCKS = (NW - 2) // 2 + REACH
VMEM_LIMIT = 8 * 1024 * 1024
MOST_VMEM = 53 * 1024 * 1024
ANY = pl.BlockSpec(memory_space=pl.ANY)
VMEM = pl.BlockSpec(memory_space=pltpu.VMEM)
SMEM = pl.BlockSpec(memory_space=pltpu.SMEM)


def params(limit=VMEM_LIMIT):
    return pltpu.CompilerParams(vmem_limit_bytes=limit)


def cost(macs, moved):
    return pl.CostEstimate(flops=2 * macs, bytes_accessed=moved, transcendentals=0)


def trade_edges(first, second):
    count, apertures = lax.axis_size("beam"), lax.axis_size("aperture")
    received = []
    for order, block in enumerate((first, second)):
        route = []
        for aper in range(apertures):
            for place in range(count):
                other = place + 1 if (place - order) % 2 == 0 else place - 1
                if 0 <= other < count:
                    to = aper * count + other
                else:
                    to = min(aper ^ 1, apertures - 1) * count + place
                route.append((aper * count + place, to))
        received.append(lax.ppermute(block, ("aperture", "beam"), route))
    return received


def partner(block, axis, distance):
    count = lax.axis_size(axis)
    route = []
    for low in range(count):
        high = low | 1 << distance
        if high != low and high < count:
            route += [(low, high), (high, low)]
    return lax.ppermute(block, axis, route)


def dot(left, right):
    return jnp.dot(left, right, preferred_element_type=jnp.float32)


def resample_kernel(child_hbm, kernel_hbm, first_ref, second_ref, child, kernel, own, sems):
    aper, beam = lax.axis_index("aperture"), lax.axis_index("beam")
    half, quarter = aper & 1, (aper >> 1) & 1
    even = 1 - (beam & 1)
    rows, rng = child.shape[1:]
    piece = rng // 4
    child_copy = pltpu.make_async_copy(child_hbm, child, sems.at[4])
    copies = []
    for place in range(4):
        source = (half ^ (place // 2)) * 2 + (quarter ^ (place % 2))
        copies.append(
            pltpu.make_async_copy(
                kernel_hbm.at[:, :, pl.ds(pl.multiple_of(source * piece, 128), piece)],
                kernel.at[:, :, place * piece : (place + 1) * piece],
                sems.at[place],
            )
        )
    child_copy.start()
    for copy in copies:
        copy.start()
    child_copy.wait()
    real, imag = child[0], child[1]
    margin = first_ref.shape[1]
    tail = pl.ds(pl.multiple_of(even * (rows - margin), BLK), margin)
    head = pl.ds(pl.multiple_of((1 - even) * (rows - margin), BLK), margin)
    for side in range(2):
        columns = slice(side * 2 * piece, (side + 1) * 2 * piece)
        copies[2 * side].wait()
        copies[2 * side + 1].wait()
        k_real, k_imag = kernel[0, :, columns], kernel[1, :, columns]
        own[0, :, columns] = (dot(real, k_real) - dot(imag, k_imag)).astype(jnp.bfloat16)
        own[1, :, columns] = (dot(real, k_imag) + dot(imag, k_real)).astype(jnp.bfloat16)
        for part in range(2):
            first_ref[part, :, columns] = own[part, tail, columns]
            second_ref[part, :, columns] = own[part, head, columns]


def resample(child, kernel, margin):
    rows, rng = child.shape[1:]
    shape = jax.ShapeDtypeStruct((2, margin, rng), jnp.bfloat16)
    return pl.pallas_call(
        resample_kernel,
        out_shape=(shape, shape),
        in_specs=[ANY, ANY],
        out_specs=(VMEM, VMEM),
        scratch_shapes=[
            pltpu.VMEM(child.shape, jnp.bfloat16),
            pltpu.VMEM(kernel.shape, jnp.bfloat16),
            pltpu.VMEM(child.shape, jnp.bfloat16),
            pltpu.SemaphoreType.DMA((5,)),
        ],
        compiler_params=params(MOST_VMEM),
        cost_estimate=cost(4 * rows * rng * rng, 2**21),
        name="resample",
    )(child, kernel)


def complex_window(weights, real, imag):
    beams = weights.shape[0] // 2
    with_real = dot(weights, real)
    with_imag = dot(weights, imag)
    return (
        (with_real[:beams] - with_imag[beams:]).astype(jnp.bfloat16),
        (with_imag[:beams] + with_real[beams:]).astype(jnp.bfloat16),
    )


def place_halos(padded, side_ref, rows, first, second):
    even, lowest, highest = side_ref[0], side_ref[1], side_ref[2]
    margin = first.shape[1]
    far = margin + rows
    padded[:, pl.ds(pl.multiple_of(even * far, BLK), margin), :] = first
    padded[:, pl.ds(pl.multiple_of((1 - even) * far, BLK), margin), :] = second
    zeros = jnp.zeros_like(first)

    @pl.when(lowest == 1)
    def _():
        padded[:, :margin, :] = zeros

    @pl.when(highest == 1)
    def _():
        padded[:, far:, :] = zeros


def first_level_kernel(
    column, rows, starts_ref, side_ref, sent_first_ref, sent_second_ref, first_ref, second_ref,
    weights_ref, out_ref, padded,
):
    sectors, stacked, window = weights_ref.shape
    beams = stacked // 2
    margin = first_ref.shape[1]
    columns = slice(column, column + out_ref.shape[2])
    even = side_ref[0]
    tail = pl.multiple_of(margin + even * (rows - margin), BLK)
    head = pl.multiple_of(margin + (1 - even) * (rows - margin), BLK)
    padded[:, pl.ds(tail, margin), :] = sent_first_ref[:, :, columns]
    padded[:, pl.ds(head, margin), :] = sent_second_ref[:, :, columns]
    place_halos(padded, side_ref, rows, first_ref[:, :, columns], second_ref[:, :, columns])
    for sector in range(sectors):
        place = pl.ds(pl.multiple_of(starts_ref[sector] * BLK, BLK), window)
        parts = complex_window(weights_ref[sector], padded[0, place, :], padded[1, place, :])
        for part in range(2):
            out_ref[part, sector * beams : (sector + 1) * beams, :] = parts[part]


def first_level(column, rows, starts, side, sent, halos, weights):
    sectors, stacked, window = weights.shape
    margin, rng = sent[0].shape[1:]
    assert 2 * margin >= rows
    width = rng // 2
    return pl.pallas_call(
        functools.partial(first_level_kernel, column, rows),
        out_shape=jax.ShapeDtypeStruct((2, sectors * stacked // 2, width), jnp.bfloat16),
        in_specs=[SMEM, SMEM] + [VMEM] * 5,
        out_specs=VMEM,
        scratch_shapes=[pltpu.VMEM((2, rows + 2 * margin, width), jnp.bfloat16)],
        compiler_params=params(),
        cost_estimate=cost(sectors * 2 * stacked * window * width, 2**21),
        name="first_level",
    )(starts, side, *sent, *halos, weights)


def second_level_early_kernel(
    starts_ref, side_ref, sector_ref, own_ref, first_ref, second_ref, weights_ref, send_ref, padded
):
    _, stacked, window = weights_ref.shape
    per = stacked // 2 // OS
    margin, rows = first_ref.shape[1], own_ref.shape[1]
    columns = slice(send_ref.shape[3], 2 * send_ref.shape[3])
    padded[:, margin : margin + rows, :] = own_ref[:, :, columns]
    place_halos(padded, side_ref, rows, first_ref[:, :, columns], second_ref[:, :, columns])
    for place in range(send_ref.shape[0]):
        sector = sector_ref[place] // per
        piece = pl.multiple_of(sector_ref[place] % per * OS, OS)
        window_rows = pl.ds(pl.multiple_of(starts_ref[sector] * BLK, BLK), window)
        weights = jnp.concatenate(
            [
                weights_ref[sector, pl.ds(piece, OS), :],
                weights_ref[sector, pl.ds(pl.multiple_of(piece + stacked // 2, OS), OS), :],
            ]
        )
        parts = complex_window(weights, padded[0, window_rows, :], padded[1, window_rows, :])
        for part in range(2):
            send_ref[place, part] = parts[part]


def second_level_kernel(
    starts_ref, side_ref, own_at_ref, other_at_ref, own_ref, first_ref, second_ref, weights_ref,
    keep_ref, send_ref, padded, send,
):
    sectors, stacked, window = weights_ref.shape
    beams = stacked // 2
    width = keep_ref.shape[3]
    margin, rows = first_ref.shape[1], own_ref.shape[1]
    padded[:, margin : margin + rows, :] = own_ref[...]
    place_halos(padded, side_ref, rows, first_ref[...], second_ref[...])
    per = beams // OS
    for sector in range(sectors):
        place = pl.ds(pl.multiple_of(starts_ref[sector] * BLK, BLK), window)
        parts = complex_window(weights_ref[sector], padded[0, place, :], padded[1, place, :])
        for piece in range(per):
            own_at = own_at_ref[sector * per + piece]
            other_at = other_at_ref[sector * per + piece]
            taken = slice(piece * OS, (piece + 1) * OS)
            for part in range(2):
                keep_ref[own_at, part] = parts[part][taken, :width]
                send[other_at, part] = parts[part][taken, width:]
    send_ref[...] = send[send.shape[0] - send_ref.shape[0] :]


def second_level(starts, side, planned, own, halos, weights, early):
    sectors, stacked, window = weights.shape
    margin, rows, rng = halos[0].shape[1], own.shape[1], own.shape[2]
    count = sectors * stacked // 2 // OS
    block = (2, OS, rng // 2)
    own_at, other_at, other_sector = planned
    early_send = pl.pallas_call(
        second_level_early_kernel,
        out_shape=jax.ShapeDtypeStruct((early,) + block, jnp.bfloat16),
        in_specs=[SMEM] * 3 + [VMEM] * 4,
        out_specs=VMEM,
        scratch_shapes=[pltpu.VMEM((2, rows + 2 * margin, rng // 2), jnp.bfloat16)],
        compiler_params=params(),
        cost_estimate=cost(early * 2 * 2 * OS * window * rng // 2, 2**20),
        name="second_level_early",
    )(starts, side, other_sector, own, *halos, weights)
    shapes = [jax.ShapeDtypeStruct((n,) + block, jnp.bfloat16) for n in (count, count - early)]
    keep, late_send = pl.pallas_call(
        second_level_kernel,
        out_shape=shapes,
        in_specs=[SMEM] * 4 + [VMEM] * 4,
        out_specs=[VMEM] * 2,
        scratch_shapes=[
            pltpu.VMEM((2, rows + 2 * margin, rng), jnp.bfloat16),
            pltpu.VMEM((count,) + block, jnp.bfloat16),
        ],
        compiler_params=params(),
        cost_estimate=cost(sectors * 2 * stacked * window * rng, 2**22),
        name="second_level",
    )(starts, side, own_at, other_at, own, *halos, weights)
    return keep, early_send, late_send


def plan_kernel(
    shift, me_ref, own_ref, other_ref, own_at_ref, other_at_ref, other_sector_ref, target_ref, rank_ref,
    taken, filled,
):
    count = own_ref.shape[0]
    far_bit = taken.shape[0] // 2

    def delay(target):
        distance = target ^ me_ref[0]
        return jnp.where((distance & far_bit) == 0, 2 * count, (distance & 1) * shift)

    for owners_ref, at_ref in ((other_ref, other_at_ref), (own_ref, own_at_ref)):
        for target in range(taken.shape[0]):
            taken[target] = 0
        for bucket in range(filled.shape[0]):
            filled[bucket] = 0
        for sector in range(count):
            target = owners_ref[sector]
            rank = taken[target]
            taken[target] = rank + 1
            bucket = rank + delay(target)
            at_ref[sector] = bucket
            filled[bucket + 1] = filled[bucket + 1] + 1
        for bucket in range(1, filled.shape[0]):
            filled[bucket] = filled[bucket] + filled[bucket - 1]
        for sector in range(count):
            bucket = at_ref[sector]
            place = filled[bucket]
            filled[bucket] = place + 1
            at_ref[sector] = place
            if at_ref is own_at_ref:
                target_ref[place] = owners_ref[sector]
                rank_ref[place] = bucket - delay(owners_ref[sector])
            else:
                other_sector_ref[place] = sector


def plan(shift, me, own, other, beam_count):
    count = own.shape[0]
    shape = jax.ShapeDtypeStruct((count,), jnp.int32)
    return pl.pallas_call(
        functools.partial(plan_kernel, shift),
        out_shape=[shape] * 5,
        in_specs=[SMEM] * 3,
        out_specs=[SMEM] * 5,
        scratch_shapes=[
            pltpu.SMEM((beam_count,), jnp.int32),
            pltpu.SMEM((3 * count + 1,), jnp.int32),
        ],
        compiler_params=params(),
        name="plan",
    )(me, own, other)


def wires_kernel(spans, early, me_ref, target_ref, rank_ref, keep_ref, *refs):
    wires = refs[-1]
    spare = wires.shape[0] - 1
    out_refs = refs[-1 - len(spans) : -1]
    other_ref, *summed_refs = refs[: -1 - len(spans)]
    wires[...] = jnp.zeros_like(wires)
    me = me_ref[0]

    def lay(place, total):
        rank = rank_ref[place]
        distance = target_ref[place] ^ me
        at = spare
        start = 0
        for number, low, high in spans:
            wanted = (distance == number) & (rank >= low) & (rank < high)
            at = jnp.where(wanted, start + rank - low, at)
            start += high - low
        wires[at] = total

    before = 0
    if not early:
        before = summed_refs[0].shape[0]
        for row in range(before):
            lay(row, summed_refs[0][row])
    for row in range(other_ref.shape[0]):
        place = before + row
        total = keep_ref[place].astype(jnp.float32) + other_ref[row].astype(jnp.float32)
        total = total.astype(jnp.bfloat16)
        lay(place, total)
        if early:
            summed_refs[0][row] = total
    start = 0
    for (_, low, high), ref in zip(spans, out_refs):
        ref[...] = wires[start : start + high - low]
        start += high - low


def wires(spans, me, target, rank, keep, other, summed=None):
    block = keep.shape[1:]
    sizes = [high - low for _, low, high in spans]
    inputs = [me, target, rank, keep, other]
    if summed is None:
        sizes = [other.shape[0]] + sizes
    else:
        inputs.append(summed)
    shapes = [jax.ShapeDtypeStruct((size,) + block, jnp.bfloat16) for size in sizes]
    total = sum(high - low for _, low, high in spans)
    return pl.pallas_call(
        functools.partial(wires_kernel, spans, summed is None),
        out_shape=shapes,
        in_specs=[SMEM] * 3 + [VMEM] * (len(inputs) - 3),
        out_specs=[VMEM] * len(shapes),
        scratch_shapes=[pltpu.VMEM((total + 1,) + block, jnp.bfloat16)],
        compiler_params=params(),
        cost_estimate=cost(0, 2**21),
        name="early_wires" if summed is None else "late_wires",
    )(*inputs)


def collect_kernel(spans, capacity, me_ref, *refs):
    sems = refs[-1]
    out_ref = refs[-2]
    copies = []
    for number, (distance, low, high) in enumerate(spans):
        start = (me_ref[0] ^ distance) * capacity + low
        copies.append(
            pltpu.make_async_copy(
                refs[number], out_ref.at[pl.ds(start, high - low)], sems.at[number]
            )
        )
    for copy in copies:
        copy.start()
    for copy in copies:
        copy.wait()


def collect(spans, capacity, beam_count, me, received):
    shape = (beam_count * capacity,) + received[0].shape[1:]
    return pl.pallas_call(
        functools.partial(collect_kernel, spans, capacity),
        out_shape=jax.ShapeDtypeStruct(shape, jnp.bfloat16),
        in_specs=[SMEM] + [ANY] * len(received),
        out_specs=ANY,
        scratch_shapes=[pltpu.SemaphoreType.DMA((len(received),))],
        compiler_params=params(),
        cost_estimate=cost(0, 2**21),
        name="collect",
    )(me, *received)


def spread(spans, group):
    count = lax.axis_size("beam")
    received = []
    for (distance, _, _), wire in zip(spans, group):
        route = [(place, place ^ distance) for place in range(count)]
        received.append(lax.ppermute(wire, "beam", route) if distance else wire)
    return received


def stacked_weights(weights):
    return weights[0].reshape(weights.shape[1], -1, weights.shape[4])


def table_row(table, row_number):
    return lax.dynamic_index_in_dim(table, row_number, 0, keepdims=False)


def local(subimages, range_kernel, weights0, starts0, weights1, starts1, owners):
    aper_index = lax.axis_index("aperture")
    beam_index = lax.axis_index("beam")
    beam_count = lax.axis_size("beam")
    margin = MARGIN_BLOCKS * BLK
    rows = subimages.shape[2]
    local_blocks = rows // BLK
    even = (beam_index + 1) % 2
    ends = (beam_index == 0, beam_index == beam_count - 1)
    side = jnp.stack([even] + [end.astype(jnp.int32) for end in ends])
    me = beam_index.reshape(1)

    sector_count = owners.shape[1]
    capacity = max(2, 2 * sector_count // beam_count)
    shorter, longer = max(1, capacity // 4), max(1, capacity // 2)
    far = range(beam_count // 2, beam_count)
    odd = [distance for distance in far if distance % 2]
    others = [distance for distance in far if distance % 2 == 0]
    early = len(odd) * shorter + len(others) * longer
    early_spans = [(distance, 0, shorter) for distance in odd]
    early_spans += [(distance, 0, longer) for distance in others]
    late_spans = [(distance, shorter, capacity) for distance in odd]
    for distance in range(1, beam_count // 2):
        late_spans += [(distance, 0, capacity // 2), (distance, capacity // 2, capacity)]
    late_spans.append((0, 0, capacity))
    last_spans = [(distance, longer, capacity) for distance in others]

    sent = resample(subimages[0], range_kernel[0], margin)
    halos = trade_edges(*sent)
    own_owners = owners[0, :, 0]
    other_owners = partner(owners, "aperture", 1)[0, :, 0]
    planned = plan(longer - shorter, me, own_owners, other_owners, beam_count)
    begin0 = table_row(starts0, aper_index) - (beam_index * local_blocks - MARGIN_BLOCKS)
    halos, planned = lax.optimization_barrier((halos, planned))
    *planned, target, rank = planned
    width = range_kernel.shape[3] // 2
    weights = stacked_weights(weights0)
    send = first_level(width, rows, begin0, side, sent, halos, weights)
    other = partner(send, "aperture", 0)
    keep = first_level(0, rows, begin0, side, sent, halos, weights)
    level_one = (keep.astype(jnp.float32) + other.astype(jnp.float32)).astype(jnp.bfloat16)

    beams = level_one.shape[1]
    first = lax.dynamic_slice_in_dim(level_one, even * (beams - margin), margin, 1)
    second = lax.dynamic_slice_in_dim(level_one, (1 - even) * (beams - margin), margin, 1)
    halos = trade_edges(first, second)
    begin1 = table_row(starts1, aper_index) - (beam_index * 2 * local_blocks - MARGIN_BLOCKS)
    keep, send, late = second_level(
        begin1, side, planned, level_one, halos, stacked_weights(weights1), early
    )
    other = partner(send, "aperture", 1)
    other, late = lax.optimization_barrier((other, late))
    late = partner(late, "aperture", 1)
    summed, *group = wires(early_spans, me, target, rank, keep, other)
    received = spread(early_spans, group)
    from_odd, from_others = received[: len(odd)], received[len(odd) :]
    ready, from_odd = lax.optimization_barrier((late, from_odd))
    group = wires(late_spans, me, target, rank, keep, ready, summed)
    received = from_odd + spread(late_spans, group)
    ready, from_others = lax.optimization_barrier((late, from_others))
    group = wires(last_spans, me, target, rank, keep, ready, summed)
    received += from_others + spread(last_spans, group)
    spans = early_spans[: len(odd)] + late_spans + early_spans[len(odd) :] + last_spans
    return collect(spans, capacity, beam_count, me, received)[None]


def solution(mesh):
    return jax.shard_map(
        local,
        mesh=mesh,
        in_specs=(
            P("aperture", None, "beam", None),
            P("aperture", None, None, None),
            P("aperture", "beam", None, None, None),
            P(None, "beam"),
            P("aperture", "beam", None, None, None),
            P(None, "beam"),
            P("aperture", "beam", None),
        ),
        out_specs=P("aperture", "beam", None, None, None),
        check_vma=False,
    )
```

```python
import functools

import jax
import jax.numpy as jnp
from jax import lax
from jax.experimental import pallas as pl
from jax.experimental.pallas import tpu as pltpu
from jax.sharding import PartitionSpec as P

BLK = 32
NW = 10
REACH = 2
OS = 64
MARGIN_BLOCKS = (NW - 2) // 2 + REACH
VMEM_LIMIT = 8 * 1024 * 1024
MOST_VMEM = 53 * 1024 * 1024
ANY = pl.BlockSpec(memory_space=pl.ANY)
VMEM = pl.BlockSpec(memory_space=pltpu.VMEM)
SMEM = pl.BlockSpec(memory_space=pltpu.SMEM)


def params(limit=VMEM_LIMIT):
    return pltpu.CompilerParams(vmem_limit_bytes=limit)


def cost(macs, moved):
    return pl.CostEstimate(flops=2 * macs, bytes_accessed=moved, transcendentals=0)


def trade_edges(first, second):
    count, apertures = lax.axis_size("beam"), lax.axis_size("aperture")
    received = []
    for order, block in enumerate((first, second)):
        route = []
        for aper in range(apertures):
            for place in range(count):
                other = place + 1 if (place - order) % 2 == 0 else place - 1
                if 0 <= other < count:
                    to = aper * count + other
                else:
                    to = min(aper ^ 1, apertures - 1) * count + place
                route.append((aper * count + place, to))
        received.append(lax.ppermute(block, ("aperture", "beam"), route))
    return received


def partner(block, axis, distance):
    count = lax.axis_size(axis)
    route = []
    for low in range(count):
        high = low | 1 << distance
        if high != low and high < count:
            route += [(low, high), (high, low)]
    return lax.ppermute(block, axis, route)


def dot(left, right):
    return jnp.dot(left, right, preferred_element_type=jnp.float32)


def edges_kernel(child_hbm, first_ref, second_ref, sems):
    even = 1 - (lax.axis_index("beam") & 1)
    margin = first_ref.shape[1]
    spare = child_hbm.shape[1] - margin
    copies = []
    for number, (start, ref) in enumerate(((even * spare, first_ref), ((1 - even) * spare, second_ref))):
        rows = pl.ds(pl.multiple_of(start, BLK), margin)
        copies.append(pltpu.make_async_copy(child_hbm.at[:, rows, :], ref, sems.at[number]))
    for copy in copies:
        copy.start()
    for copy in copies:
        copy.wait()


def edges(child, margin):
    shape = jax.ShapeDtypeStruct((2, margin, child.shape[2]), child.dtype)
    return pl.pallas_call(
        edges_kernel,
        out_shape=(shape, shape),
        in_specs=[ANY],
        out_specs=(VMEM, VMEM),
        scratch_shapes=[pltpu.SemaphoreType.DMA((2,))],
        compiler_params=params(MOST_VMEM),
        cost_estimate=cost(0, 2**20),
        name="edges",
    )(child)


def complex_product(real, imag, k_real, k_imag):
    return (
        (dot(real, k_real) - dot(imag, k_imag)).astype(jnp.bfloat16),
        (dot(real, k_imag) + dot(imag, k_real)).astype(jnp.bfloat16),
    )


def resample_kernel(child_ref, kernel_hbm, own_ref, kernel_ref, sems):
    aper = lax.axis_index("aperture")
    half, quarter = aper & 1, (aper >> 1) & 1
    piece = kernel_ref.shape[2] // 4
    copies = []
    for place in range(4):
        source = (half ^ (place // 2)) * 2 + (quarter ^ (place % 2))
        copies.append(
            pltpu.make_async_copy(
                kernel_hbm.at[:, :, pl.ds(pl.multiple_of(source * piece, 128), piece)],
                kernel_ref.at[:, :, place * piece : (place + 1) * piece],
                sems.at[place],
            )
        )
    for copy in copies:
        copy.start()
    for copy in copies:
        copy.wait()
    own_ref[0], own_ref[1] = complex_product(
        child_ref[0], child_ref[1], kernel_ref[0], kernel_ref[1]
    )


def resample(child, kernel):
    rows, rng = child.shape[1:]
    return pl.pallas_call(
        resample_kernel,
        out_shape=(
            jax.ShapeDtypeStruct(child.shape, jnp.bfloat16),
            jax.ShapeDtypeStruct(kernel.shape, kernel.dtype),
        ),
        in_specs=[VMEM, ANY],
        out_specs=(VMEM, VMEM),
        scratch_shapes=[pltpu.SemaphoreType.DMA((4,))],
        compiler_params=params(),
        cost_estimate=cost(4 * rows * rng * rng, 2**21),
        name="resample",
    )(child, kernel)


def complex_window(weights, real, imag):
    beams = weights.shape[0] // 2
    with_real = dot(weights, real)
    with_imag = dot(weights, imag)
    return (
        (with_real[:beams] - with_imag[beams:]).astype(jnp.bfloat16),
        (with_imag[:beams] + with_real[beams:]).astype(jnp.bfloat16),
    )


def place_halos(padded, side_ref, rows, first, second):
    even, lowest, highest = side_ref[0], side_ref[1], side_ref[2]
    margin = first.shape[1]
    far = margin + rows
    padded[:, pl.ds(pl.multiple_of(even * far, BLK), margin), :] = first
    padded[:, pl.ds(pl.multiple_of((1 - even) * far, BLK), margin), :] = second
    zeros = jnp.zeros_like(first)

    @pl.when(lowest == 1)
    def _():
        padded[:, :margin, :] = zeros

    @pl.when(highest == 1)
    def _():
        padded[:, far:, :] = zeros


def first_level_kernel(
    column, starts_ref, side_ref, own_ref, first_ref, second_ref, kernel_ref, weights_ref,
    out_ref, padded,
):
    sectors, stacked, window = weights_ref.shape
    beams = stacked // 2
    margin, rows = first_ref.shape[1], own_ref.shape[1]
    columns = slice(column, column + out_ref.shape[2])
    k_real, k_imag = kernel_ref[0, :, columns], kernel_ref[1, :, columns]
    padded[:, margin : margin + rows, :] = own_ref[:, :, columns]
    first = complex_product(first_ref[0], first_ref[1], k_real, k_imag)
    second = complex_product(second_ref[0], second_ref[1], k_real, k_imag)
    place_halos(padded, side_ref, rows, jnp.stack(first), jnp.stack(second))
    for sector in range(sectors):
        place = pl.ds(pl.multiple_of(starts_ref[sector] * BLK, BLK), window)
        parts = complex_window(weights_ref[sector], padded[0, place, :], padded[1, place, :])
        for part in range(2):
            out_ref[part, sector * beams : (sector + 1) * beams, :] = parts[part]


def first_level(column, starts, side, own, halos, kernel, weights):
    sectors, stacked, window = weights.shape
    margin, rows, rng = halos[0].shape[1], own.shape[1], own.shape[2]
    width = rng // 2
    macs = sectors * 2 * stacked * window * width + 8 * margin * rng * width
    return pl.pallas_call(
        functools.partial(first_level_kernel, column),
        out_shape=jax.ShapeDtypeStruct((2, sectors * stacked // 2, width), jnp.bfloat16),
        in_specs=[SMEM, SMEM] + [VMEM] * 5,
        out_specs=VMEM,
        scratch_shapes=[pltpu.VMEM((2, rows + 2 * margin, width), jnp.bfloat16)],
        compiler_params=params(),
        cost_estimate=cost(macs, 2**21),
        name="first_level",
    )(starts, side, own, *halos, kernel, weights)


def second_level_early_kernel(
    starts_ref, side_ref, sector_ref, own_ref, first_ref, second_ref, weights_ref, send_ref, padded
):
    _, stacked, window = weights_ref.shape
    per = stacked // 2 // OS
    margin, rows = first_ref.shape[1], own_ref.shape[1]
    columns = slice(send_ref.shape[3], 2 * send_ref.shape[3])
    padded[:, margin : margin + rows, :] = own_ref[:, :, columns]
    place_halos(padded, side_ref, rows, first_ref[:, :, columns], second_ref[:, :, columns])
    for place in range(send_ref.shape[0]):
        sector = sector_ref[place] // per
        piece = pl.multiple_of(sector_ref[place] % per * OS, OS)
        window_rows = pl.ds(pl.multiple_of(starts_ref[sector] * BLK, BLK), window)
        weights = jnp.concatenate(
            [
                weights_ref[sector, pl.ds(piece, OS), :],
                weights_ref[sector, pl.ds(pl.multiple_of(piece + stacked // 2, OS), OS), :],
            ]
        )
        parts = complex_window(weights, padded[0, window_rows, :], padded[1, window_rows, :])
        for part in range(2):
            send_ref[place, part] = parts[part]


def second_level_kernel(
    starts_ref, side_ref, own_at_ref, other_at_ref, own_ref, first_ref, second_ref, weights_ref,
    keep_ref, send_ref, padded, send,
):
    sectors, stacked, window = weights_ref.shape
    beams = stacked // 2
    width = keep_ref.shape[3]
    margin, rows = first_ref.shape[1], own_ref.shape[1]
    padded[:, margin : margin + rows, :] = own_ref[...]
    place_halos(padded, side_ref, rows, first_ref[...], second_ref[...])
    per = beams // OS
    for sector in range(sectors):
        place = pl.ds(pl.multiple_of(starts_ref[sector] * BLK, BLK), window)
        parts = complex_window(weights_ref[sector], padded[0, place, :], padded[1, place, :])
        for piece in range(per):
            own_at = own_at_ref[sector * per + piece]
            other_at = other_at_ref[sector * per + piece]
            taken = slice(piece * OS, (piece + 1) * OS)
            for part in range(2):
                keep_ref[own_at, part] = parts[part][taken, :width]
                send[other_at, part] = parts[part][taken, width:]
    send_ref[...] = send[send.shape[0] - send_ref.shape[0] :]


def second_level(starts, side, planned, own, halos, weights, early):
    sectors, stacked, window = weights.shape
    margin, rows, rng = halos[0].shape[1], own.shape[1], own.shape[2]
    count = sectors * stacked // 2 // OS
    block = (2, OS, rng // 2)
    own_at, other_at, other_sector = planned
    early_send = pl.pallas_call(
        second_level_early_kernel,
        out_shape=jax.ShapeDtypeStruct((early,) + block, jnp.bfloat16),
        in_specs=[SMEM] * 3 + [VMEM] * 4,
        out_specs=VMEM,
        scratch_shapes=[pltpu.VMEM((2, rows + 2 * margin, rng // 2), jnp.bfloat16)],
        compiler_params=params(),
        cost_estimate=cost(early * 2 * 2 * OS * window * rng // 2, 2**20),
        name="second_level_early",
    )(starts, side, other_sector, own, *halos, weights)
    shapes = [jax.ShapeDtypeStruct((n,) + block, jnp.bfloat16) for n in (count, count - early)]
    keep, late_send = pl.pallas_call(
        second_level_kernel,
        out_shape=shapes,
        in_specs=[SMEM] * 4 + [VMEM] * 4,
        out_specs=[VMEM] * 2,
        scratch_shapes=[
            pltpu.VMEM((2, rows + 2 * margin, rng), jnp.bfloat16),
            pltpu.VMEM((count,) + block, jnp.bfloat16),
        ],
        compiler_params=params(),
        cost_estimate=cost(sectors * 2 * stacked * window * rng, 2**22),
        name="second_level",
    )(starts, side, own_at, other_at, own, *halos, weights)
    return keep, early_send, late_send


def plan_kernel(
    shift, me_ref, own_ref, other_ref, own_at_ref, other_at_ref, other_sector_ref, target_ref, rank_ref,
    taken, filled,
):
    count = own_ref.shape[0]
    far_bit = taken.shape[0] // 2

    def delay(target):
        distance = target ^ me_ref[0]
        return jnp.where((distance & far_bit) == 0, 2 * count, (distance & 1) * shift)

    for owners_ref, at_ref in ((other_ref, other_at_ref), (own_ref, own_at_ref)):
        for target in range(taken.shape[0]):
            taken[target] = 0
        for bucket in range(filled.shape[0]):
            filled[bucket] = 0
        for sector in range(count):
            target = owners_ref[sector]
            rank = taken[target]
            taken[target] = rank + 1
            bucket = rank + delay(target)
            at_ref[sector] = bucket
            filled[bucket + 1] = filled[bucket + 1] + 1
        for bucket in range(1, filled.shape[0]):
            filled[bucket] = filled[bucket] + filled[bucket - 1]
        for sector in range(count):
            bucket = at_ref[sector]
            place = filled[bucket]
            filled[bucket] = place + 1
            at_ref[sector] = place
            if at_ref is own_at_ref:
                target_ref[place] = owners_ref[sector]
                rank_ref[place] = bucket - delay(owners_ref[sector])
            else:
                other_sector_ref[place] = sector


def plan(shift, me, own, other, beam_count):
    count = own.shape[0]
    shape = jax.ShapeDtypeStruct((count,), jnp.int32)
    return pl.pallas_call(
        functools.partial(plan_kernel, shift),
        out_shape=[shape] * 5,
        in_specs=[SMEM] * 3,
        out_specs=[SMEM] * 5,
        scratch_shapes=[
            pltpu.SMEM((beam_count,), jnp.int32),
            pltpu.SMEM((3 * count + 1,), jnp.int32),
        ],
        compiler_params=params(),
        name="plan",
    )(me, own, other)


def wires_kernel(spans, early, me_ref, target_ref, rank_ref, keep_ref, *refs):
    wires = refs[-1]
    spare = wires.shape[0] - 1
    out_refs = refs[-1 - len(spans) : -1]
    other_ref, *summed_refs = refs[: -1 - len(spans)]
    wires[...] = jnp.zeros_like(wires)
    me = me_ref[0]

    def lay(place, total):
        rank = rank_ref[place]
        distance = target_ref[place] ^ me
        at = spare
        start = 0
        for number, low, high in spans:
            wanted = (distance == number) & (rank >= low) & (rank < high)
            at = jnp.where(wanted, start + rank - low, at)
            start += high - low
        wires[at] = total

    before = 0
    if not early:
        before = summed_refs[0].shape[0]
        for row in range(before):
            lay(row, summed_refs[0][row])
    for row in range(other_ref.shape[0]):
        place = before + row
        total = keep_ref[place].astype(jnp.float32) + other_ref[row].astype(jnp.float32)
        total = total.astype(jnp.bfloat16)
        lay(place, total)
        if early:
            summed_refs[0][row] = total
    start = 0
    for (_, low, high), ref in zip(spans, out_refs):
        ref[...] = wires[start : start + high - low]
        start += high - low


def wires(spans, me, target, rank, keep, other, summed=None):
    block = keep.shape[1:]
    sizes = [high - low for _, low, high in spans]
    inputs = [me, target, rank, keep, other]
    if summed is None:
        sizes = [other.shape[0]] + sizes
    else:
        inputs.append(summed)
    shapes = [jax.ShapeDtypeStruct((size,) + block, jnp.bfloat16) for size in sizes]
    total = sum(high - low for _, low, high in spans)
    return pl.pallas_call(
        functools.partial(wires_kernel, spans, summed is None),
        out_shape=shapes,
        in_specs=[SMEM] * 3 + [VMEM] * (len(inputs) - 3),
        out_specs=[VMEM] * len(shapes),
        scratch_shapes=[pltpu.VMEM((total + 1,) + block, jnp.bfloat16)],
        compiler_params=params(),
        cost_estimate=cost(0, 2**21),
        name="early_wires" if summed is None else "late_wires",
    )(*inputs)


def collect_kernel(spans, capacity, me_ref, *refs):
    sems = refs[-1]
    out_ref = refs[-2]
    copies = []
    for number, (distance, low, high) in enumerate(spans):
        start = (me_ref[0] ^ distance) * capacity + low
        copies.append(
            pltpu.make_async_copy(
                refs[number], out_ref.at[pl.ds(start, high - low)], sems.at[number]
            )
        )
    for copy in copies:
        copy.start()
    for copy in copies:
        copy.wait()


def collect(spans, capacity, beam_count, me, received):
    shape = (beam_count * capacity,) + received[0].shape[1:]
    return pl.pallas_call(
        functools.partial(collect_kernel, spans, capacity),
        out_shape=jax.ShapeDtypeStruct(shape, jnp.bfloat16),
        in_specs=[SMEM] + [ANY] * len(received),
        out_specs=ANY,
        scratch_shapes=[pltpu.SemaphoreType.DMA((len(received),))],
        compiler_params=params(),
        cost_estimate=cost(0, 2**21),
        name="collect",
    )(me, *received)


def spread(spans, group):
    count = lax.axis_size("beam")
    received = []
    for (distance, _, _), wire in zip(spans, group):
        route = [(place, place ^ distance) for place in range(count)]
        received.append(lax.ppermute(wire, "beam", route) if distance else wire)
    return received


def stacked_weights(weights):
    return weights[0].reshape(weights.shape[1], -1, weights.shape[4])


def table_row(table, row_number):
    return lax.dynamic_index_in_dim(table, row_number, 0, keepdims=False)


def local(subimages, range_kernel, weights0, starts0, weights1, starts1, owners):
    aper_index = lax.axis_index("aperture")
    beam_index = lax.axis_index("beam")
    beam_count = lax.axis_size("beam")
    margin = MARGIN_BLOCKS * BLK
    local_blocks = subimages.shape[2] // BLK
    even = (beam_index + 1) % 2
    ends = (beam_index == 0, beam_index == beam_count - 1)
    side = jnp.stack([even] + [end.astype(jnp.int32) for end in ends])
    me = beam_index.reshape(1)

    sector_count = owners.shape[1]
    capacity = max(2, 2 * sector_count // beam_count)
    shorter, longer = max(1, capacity // 4), max(1, capacity // 2)
    far = range(beam_count // 2, beam_count)
    odd = [distance for distance in far if distance % 2]
    others = [distance for distance in far if distance % 2 == 0]
    early = len(odd) * shorter + len(others) * longer
    early_spans = [(distance, 0, shorter) for distance in odd]
    early_spans += [(distance, 0, longer) for distance in others]
    late_spans = [(distance, shorter, capacity) for distance in odd]
    for distance in range(1, beam_count // 2):
        cut = (5 * capacity + 4) // 8
        late_spans += [(distance, 0, cut), (distance, cut, capacity)]
    late_spans.append((0, 0, capacity))
    last_spans = [(distance, longer, capacity) for distance in others]

    halos = trade_edges(*edges(subimages[0], margin))
    own, kernel = resample(subimages[0], range_kernel[0])
    own_owners = owners[0, :, 0]
    other_owners = partner(owners, "aperture", 1)[0, :, 0]
    planned = plan(longer - shorter, me, own_owners, other_owners, beam_count)
    begin0 = table_row(starts0, aper_index) - (beam_index * local_blocks - MARGIN_BLOCKS)
    halos, own, planned = lax.optimization_barrier((halos, own, planned))
    *planned, target, rank = planned
    width = range_kernel.shape[3] // 2
    weights = stacked_weights(weights0)
    send = first_level(width, begin0, side, own, halos, kernel, weights)
    other = partner(send, "aperture", 0)
    keep = first_level(0, begin0, side, own, halos, kernel, weights)
    level_one = (keep.astype(jnp.float32) + other.astype(jnp.float32)).astype(jnp.bfloat16)

    beams = level_one.shape[1]
    first = lax.dynamic_slice_in_dim(level_one, even * (beams - margin), margin, 1)
    second = lax.dynamic_slice_in_dim(level_one, (1 - even) * (beams - margin), margin, 1)
    halos = trade_edges(first, second)
    begin1 = table_row(starts1, aper_index) - (beam_index * 2 * local_blocks - MARGIN_BLOCKS)
    keep, send, late = second_level(
        begin1, side, planned, level_one, halos, stacked_weights(weights1), early
    )
    other = partner(send, "aperture", 1)
    other, late = lax.optimization_barrier((other, late))
    late = partner(late, "aperture", 1)
    summed, *group = wires(early_spans, me, target, rank, keep, other)
    received = spread(early_spans, group)
    from_odd, from_others = received[: len(odd)], received[len(odd) :]
    ready, from_odd = lax.optimization_barrier((late, from_odd))
    group = wires(late_spans, me, target, rank, keep, ready, summed)
    received = from_odd + spread(late_spans, group)
    ready, from_others = lax.optimization_barrier((late, from_others))
    group = wires(last_spans, me, target, rank, keep, ready, summed)
    received += from_others + spread(last_spans, group)
    spans = early_spans[: len(odd)] + late_spans + early_spans[len(odd) :] + last_spans
    return collect(spans, capacity, beam_count, me, received)[None]


def solution(mesh):
    return jax.shard_map(
        local,
        mesh=mesh,
        in_specs=(
            P("aperture", None, "beam", None),
            P("aperture", None, None, None),
            P("aperture", "beam", None, None, None),
            P(None, "beam"),
            P("aperture", "beam", None, None, None),
            P(None, "beam"),
            P("aperture", "beam", None),
        ),
        out_specs=P("aperture", "beam", None, None, None),
        check_vma=False,
    )
```

```python
import functools

import jax
import jax.numpy as jnp
from jax import lax
from jax.experimental import pallas as pl
from jax.experimental.pallas import tpu as pltpu
from jax.sharding import PartitionSpec as P

BLK = 32
NW = 10
REACH = 2
OS = 64
COPIES = 4
MARGIN_BLOCKS = (NW - 2) // 2 + REACH
VMEM_LIMIT = 8 * 1024 * 1024
MOST_VMEM = 53 * 1024 * 1024
ANY = pl.BlockSpec(memory_space=pl.ANY)
VMEM = pl.BlockSpec(memory_space=pltpu.VMEM)
SMEM = pl.BlockSpec(memory_space=pltpu.SMEM)


def params(limit=VMEM_LIMIT):
    return pltpu.CompilerParams(vmem_limit_bytes=limit)


def cost(macs, moved):
    return pl.CostEstimate(flops=2 * macs, bytes_accessed=moved, transcendentals=0)


def trade_edges(first, second):
    count, apertures = lax.axis_size("beam"), lax.axis_size("aperture")
    received = []
    for order, block in enumerate((first, second)):
        route = []
        for aper in range(apertures):
            for place in range(count):
                other = place + 1 if (place - order) % 2 == 0 else place - 1
                if 0 <= other < count:
                    to = aper * count + other
                else:
                    to = min(aper ^ 1, apertures - 1) * count + place
                route.append((aper * count + place, to))
        received.append(lax.ppermute(block, ("aperture", "beam"), route))
    return received


def partner(block, axis, distance):
    count = lax.axis_size(axis)
    route = []
    for low in range(count):
        high = low | 1 << distance
        if high != low and high < count:
            route += [(low, high), (high, low)]
    return lax.ppermute(block, axis, route)


def dot(left, right):
    return jnp.dot(left, right, preferred_element_type=jnp.float32)


def resample_kernel(
    child_hbm, kernel_hbm, first_ref, second_ref, child, kernel, own, child_sems, kernel_sems
):
    aper, beam = lax.axis_index("aperture"), lax.axis_index("beam")
    half, quarter = aper & 1, (aper >> 1) & 1
    even = 1 - (beam & 1)
    rows, rng = child.shape[1:]
    piece = rng // 4
    child_copies = []
    for part in range(2):
        for block in range(COPIES):
            taken = pl.ds(block * (rows // COPIES), rows // COPIES)
            child_copies.append(
                pltpu.make_async_copy(
                    child_hbm.at[part, taken, :],
                    child.at[part, taken, :],
                    child_sems.at[part, block],
                )
            )
    copies = []
    for place in range(4):
        source = (half ^ (place // 2)) * 2 + (quarter ^ (place % 2))
        columns = pl.ds(pl.multiple_of(source * piece, 128), piece)
        copies.append([])
        for part in range(2):
            for block in range(2):
                taken = pl.ds(block * (rng // 2), rng // 2)
                copies[place].append(
                    pltpu.make_async_copy(
                        kernel_hbm.at[part, taken, columns],
                        kernel.at[part, taken, place * piece : (place + 1) * piece],
                        kernel_sems.at[place, part, block],
                    )
                )
    for copy in child_copies + copies[0] + copies[1] + copies[2] + copies[3]:
        copy.start()
    for copy in child_copies:
        copy.wait()
    real, imag = child[0], child[1]
    margin = first_ref.shape[1]
    tail = pl.ds(pl.multiple_of(even * (rows - margin), BLK), margin)
    head = pl.ds(pl.multiple_of((1 - even) * (rows - margin), BLK), margin)
    for side in range(2):
        columns = slice(side * 2 * piece, (side + 1) * 2 * piece)
        for copy in copies[2 * side] + copies[2 * side + 1]:
            copy.wait()
        k_real, k_imag = kernel[0, :, columns], kernel[1, :, columns]
        own[0, :, columns] = (dot(real, k_real) - dot(imag, k_imag)).astype(jnp.bfloat16)
        own[1, :, columns] = (dot(real, k_imag) + dot(imag, k_real)).astype(jnp.bfloat16)
        for part in range(2):
            first_ref[part, :, columns] = own[part, tail, columns]
            second_ref[part, :, columns] = own[part, head, columns]


def resample(child, kernel, margin):
    rows, rng = child.shape[1:]
    shape = jax.ShapeDtypeStruct((2, margin, rng), jnp.bfloat16)
    return pl.pallas_call(
        resample_kernel,
        out_shape=(shape, shape),
        in_specs=[ANY, ANY],
        out_specs=(VMEM, VMEM),
        scratch_shapes=[
            pltpu.VMEM(child.shape, jnp.bfloat16),
            pltpu.VMEM(kernel.shape, jnp.bfloat16),
            pltpu.VMEM(child.shape, jnp.bfloat16),
            pltpu.SemaphoreType.DMA((2, COPIES)),
            pltpu.SemaphoreType.DMA((4, 2, 2)),
        ],
        compiler_params=params(MOST_VMEM),
        cost_estimate=cost(4 * rows * rng * rng, 2**21),
        name="resample",
    )(child, kernel)


def complex_window(weights, real, imag):
    beams = weights.shape[0] // 2
    with_real = dot(weights, real)
    with_imag = dot(weights, imag)
    return (
        (with_real[:beams] - with_imag[beams:]).astype(jnp.bfloat16),
        (with_imag[:beams] + with_real[beams:]).astype(jnp.bfloat16),
    )


def place_halos(padded, side_ref, rows, first, second):
    even, lowest, highest = side_ref[0], side_ref[1], side_ref[2]
    margin = first.shape[1]
    far = margin + rows
    padded[:, pl.ds(pl.multiple_of(even * far, BLK), margin), :] = first
    padded[:, pl.ds(pl.multiple_of((1 - even) * far, BLK), margin), :] = second
    zeros = jnp.zeros_like(first)

    @pl.when(lowest == 1)
    def _():
        padded[:, :margin, :] = zeros

    @pl.when(highest == 1)
    def _():
        padded[:, far:, :] = zeros


def first_level_kernel(
    column, rows, starts_ref, side_ref, sent_first_ref, sent_second_ref, first_ref, second_ref,
    weights_ref, out_ref, padded,
):
    sectors, stacked, window = weights_ref.shape
    beams = stacked // 2
    margin = first_ref.shape[1]
    columns = slice(column, column + out_ref.shape[2])
    even = side_ref[0]
    tail = pl.multiple_of(margin + even * (rows - margin), BLK)
    head = pl.multiple_of(margin + (1 - even) * (rows - margin), BLK)
    padded[:, pl.ds(tail, margin), :] = sent_first_ref[:, :, columns]
    padded[:, pl.ds(head, margin), :] = sent_second_ref[:, :, columns]
    place_halos(padded, side_ref, rows, first_ref[:, :, columns], second_ref[:, :, columns])
    for sector in range(sectors):
        place = pl.ds(pl.multiple_of(starts_ref[sector] * BLK, BLK), window)
        parts = complex_window(weights_ref[sector], padded[0, place, :], padded[1, place, :])
        for part in range(2):
            out_ref[part, sector * beams : (sector + 1) * beams, :] = parts[part]


def first_level(column, rows, starts, side, sent, halos, weights):
    sectors, stacked, window = weights.shape
    margin, rng = sent[0].shape[1:]
    assert 2 * margin >= rows
    width = rng // 2
    return pl.pallas_call(
        functools.partial(first_level_kernel, column, rows),
        out_shape=jax.ShapeDtypeStruct((2, sectors * stacked // 2, width), jnp.bfloat16),
        in_specs=[SMEM, SMEM] + [VMEM] * 5,
        out_specs=VMEM,
        scratch_shapes=[pltpu.VMEM((2, rows + 2 * margin, width), jnp.bfloat16)],
        compiler_params=params(),
        cost_estimate=cost(sectors * 2 * stacked * window * width, 2**21),
        name="first_level",
    )(starts, side, *sent, *halos, weights)


def second_level_early_kernel(
    starts_ref, side_ref, sector_ref, own_ref, first_ref, second_ref, weights_ref, send_ref, padded
):
    _, stacked, window = weights_ref.shape
    per = stacked // 2 // OS
    margin, rows = first_ref.shape[1], own_ref.shape[1]
    columns = slice(send_ref.shape[3], 2 * send_ref.shape[3])
    padded[:, margin : margin + rows, :] = own_ref[:, :, columns]
    place_halos(padded, side_ref, rows, first_ref[:, :, columns], second_ref[:, :, columns])
    for place in range(send_ref.shape[0]):
        sector = sector_ref[place] // per
        piece = pl.multiple_of(sector_ref[place] % per * OS, OS)
        window_rows = pl.ds(pl.multiple_of(starts_ref[sector] * BLK, BLK), window)
        weights = jnp.concatenate(
            [
                weights_ref[sector, pl.ds(piece, OS), :],
                weights_ref[sector, pl.ds(pl.multiple_of(piece + stacked // 2, OS), OS), :],
            ]
        )
        parts = complex_window(weights, padded[0, window_rows, :], padded[1, window_rows, :])
        for part in range(2):
            send_ref[place, part] = parts[part]


def second_level_kernel(
    starts_ref, side_ref, own_at_ref, other_at_ref, own_ref, first_ref, second_ref, weights_ref,
    keep_ref, send_ref, padded, send,
):
    sectors, stacked, window = weights_ref.shape
    beams = stacked // 2
    width = keep_ref.shape[3]
    margin, rows = first_ref.shape[1], own_ref.shape[1]
    padded[:, margin : margin + rows, :] = own_ref[...]
    place_halos(padded, side_ref, rows, first_ref[...], second_ref[...])
    per = beams // OS
    for sector in range(sectors):
        place = pl.ds(pl.multiple_of(starts_ref[sector] * BLK, BLK), window)
        parts = complex_window(weights_ref[sector], padded[0, place, :], padded[1, place, :])
        for piece in range(per):
            own_at = own_at_ref[sector * per + piece]
            other_at = other_at_ref[sector * per + piece]
            taken = slice(piece * OS, (piece + 1) * OS)
            for part in range(2):
                keep_ref[own_at, part] = parts[part][taken, :width]
                send[other_at, part] = parts[part][taken, width:]
    send_ref[...] = send[send.shape[0] - send_ref.shape[0] :]


def second_level(starts, side, planned, own, halos, weights, early):
    sectors, stacked, window = weights.shape
    margin, rows, rng = halos[0].shape[1], own.shape[1], own.shape[2]
    count = sectors * stacked // 2 // OS
    block = (2, OS, rng // 2)
    own_at, other_at, other_sector = planned
    early_send = pl.pallas_call(
        second_level_early_kernel,
        out_shape=jax.ShapeDtypeStruct((early,) + block, jnp.bfloat16),
        in_specs=[SMEM] * 3 + [VMEM] * 4,
        out_specs=VMEM,
        scratch_shapes=[pltpu.VMEM((2, rows + 2 * margin, rng // 2), jnp.bfloat16)],
        compiler_params=params(),
        cost_estimate=cost(early * 2 * 2 * OS * window * rng // 2, 2**20),
        name="second_level_early",
    )(starts, side, other_sector, own, *halos, weights)
    shapes = [jax.ShapeDtypeStruct((n,) + block, jnp.bfloat16) for n in (count, count - early)]
    keep, late_send = pl.pallas_call(
        second_level_kernel,
        out_shape=shapes,
        in_specs=[SMEM] * 4 + [VMEM] * 4,
        out_specs=[VMEM] * 2,
        scratch_shapes=[
            pltpu.VMEM((2, rows + 2 * margin, rng), jnp.bfloat16),
            pltpu.VMEM((count,) + block, jnp.bfloat16),
        ],
        compiler_params=params(),
        cost_estimate=cost(sectors * 2 * stacked * window * rng, 2**22),
        name="second_level",
    )(starts, side, own_at, other_at, own, *halos, weights)
    return keep, early_send, late_send


def plan_kernel(
    shift, me_ref, own_ref, other_ref, own_at_ref, other_at_ref, other_sector_ref, target_ref, rank_ref,
    taken, filled,
):
    count = own_ref.shape[0]
    far_bit = taken.shape[0] // 2

    def delay(target):
        distance = target ^ me_ref[0]
        return jnp.where((distance & far_bit) == 0, 2 * count, (distance & 1) * shift)

    for owners_ref, at_ref in ((other_ref, other_at_ref), (own_ref, own_at_ref)):
        for target in range(taken.shape[0]):
            taken[target] = 0
        for bucket in range(filled.shape[0]):
            filled[bucket] = 0
        for sector in range(count):
            target = owners_ref[sector]
            rank = taken[target]
            taken[target] = rank + 1
            bucket = rank + delay(target)
            at_ref[sector] = bucket
            filled[bucket + 1] = filled[bucket + 1] + 1
        for bucket in range(1, filled.shape[0]):
            filled[bucket] = filled[bucket] + filled[bucket - 1]
        for sector in range(count):
            bucket = at_ref[sector]
            place = filled[bucket]
            filled[bucket] = place + 1
            at_ref[sector] = place
            if at_ref is own_at_ref:
                target_ref[place] = owners_ref[sector]
                rank_ref[place] = bucket - delay(owners_ref[sector])
            else:
                other_sector_ref[place] = sector


def plan(shift, me, own, other, beam_count):
    count = own.shape[0]
    shape = jax.ShapeDtypeStruct((count,), jnp.int32)
    return pl.pallas_call(
        functools.partial(plan_kernel, shift),
        out_shape=[shape] * 5,
        in_specs=[SMEM] * 3,
        out_specs=[SMEM] * 5,
        scratch_shapes=[
            pltpu.SMEM((beam_count,), jnp.int32),
            pltpu.SMEM((3 * count + 1,), jnp.int32),
        ],
        compiler_params=params(),
        name="plan",
    )(me, own, other)


def wires_kernel(spans, early, me_ref, target_ref, rank_ref, keep_ref, *refs):
    wires = refs[-1]
    spare = wires.shape[0] - 1
    out_refs = refs[-1 - len(spans) : -1]
    other_ref, *summed_refs = refs[: -1 - len(spans)]
    wires[...] = jnp.zeros_like(wires)
    me = me_ref[0]

    def lay(place, total):
        rank = rank_ref[place]
        distance = target_ref[place] ^ me
        at = spare
        start = 0
        for number, low, high in spans:
            wanted = (distance == number) & (rank >= low) & (rank < high)
            at = jnp.where(wanted, start + rank - low, at)
            start += high - low
        wires[at] = total

    before = 0
    if not early:
        before = summed_refs[0].shape[0]
        for row in range(before):
            lay(row, summed_refs[0][row])
    for row in range(other_ref.shape[0]):
        place = before + row
        total = keep_ref[place].astype(jnp.float32) + other_ref[row].astype(jnp.float32)
        total = total.astype(jnp.bfloat16)
        lay(place, total)
        if early:
            summed_refs[0][row] = total
    start = 0
    for (_, low, high), ref in zip(spans, out_refs):
        ref[...] = wires[start : start + high - low]
        start += high - low


def wires(spans, me, target, rank, keep, other, summed=None):
    block = keep.shape[1:]
    sizes = [high - low for _, low, high in spans]
    inputs = [me, target, rank, keep, other]
    if summed is None:
        sizes = [other.shape[0]] + sizes
    else:
        inputs.append(summed)
    shapes = [jax.ShapeDtypeStruct((size,) + block, jnp.bfloat16) for size in sizes]
    total = sum(high - low for _, low, high in spans)
    return pl.pallas_call(
        functools.partial(wires_kernel, spans, summed is None),
        out_shape=shapes,
        in_specs=[SMEM] * 3 + [VMEM] * (len(inputs) - 3),
        out_specs=[VMEM] * len(shapes),
        scratch_shapes=[pltpu.VMEM((total + 1,) + block, jnp.bfloat16)],
        compiler_params=params(),
        cost_estimate=cost(0, 2**21),
        name="early_wires" if summed is None else "late_wires",
    )(*inputs)


def collect_kernel(spans, capacity, me_ref, *refs):
    sems = refs[-1]
    out_ref = refs[-2]
    copies = []
    for number, (distance, low, high) in enumerate(spans):
        start = (me_ref[0] ^ distance) * capacity
        for slot in range(low, high):
            copies.append(
                pltpu.make_async_copy(
                    refs[number].at[slot - low], out_ref.at[start + slot], sems.at[len(copies)]
                )
            )
    for copy in copies:
        copy.start()
    for copy in copies:
        copy.wait()


def collect(spans, capacity, beam_count, me, received):
    shape = (beam_count * capacity,) + received[0].shape[1:]
    return pl.pallas_call(
        functools.partial(collect_kernel, spans, capacity),
        out_shape=jax.ShapeDtypeStruct(shape, jnp.bfloat16),
        in_specs=[SMEM] + [ANY] * len(received),
        out_specs=ANY,
        scratch_shapes=[pltpu.SemaphoreType.DMA((shape[0],))],
        compiler_params=params(),
        cost_estimate=cost(0, 2**21),
        name="collect",
    )(me, *received)


def spread(spans, group):
    count = lax.axis_size("beam")
    received = []
    for (distance, _, _), wire in zip(spans, group):
        route = [(place, place ^ distance) for place in range(count)]
        received.append(lax.ppermute(wire, "beam", route) if distance else wire)
    return received


def stacked_weights(weights):
    return weights[0].reshape(weights.shape[1], -1, weights.shape[4])


def table_row(table, row_number):
    return lax.dynamic_index_in_dim(table, row_number, 0, keepdims=False)


def local(subimages, range_kernel, weights0, starts0, weights1, starts1, owners):
    aper_index = lax.axis_index("aperture")
    beam_index = lax.axis_index("beam")
    beam_count = lax.axis_size("beam")
    margin = MARGIN_BLOCKS * BLK
    rows = subimages.shape[2]
    local_blocks = rows // BLK
    even = (beam_index + 1) % 2
    ends = (beam_index == 0, beam_index == beam_count - 1)
    side = jnp.stack([even] + [end.astype(jnp.int32) for end in ends])
    me = beam_index.reshape(1)

    sector_count = owners.shape[1]
    capacity = max(2, 2 * sector_count // beam_count)
    shorter, longer = max(1, capacity // 4), max(1, capacity // 2)
    far = range(beam_count // 2, beam_count)
    odd = [distance for distance in far if distance % 2]
    others = [distance for distance in far if distance % 2 == 0]
    early = len(odd) * shorter + len(others) * longer
    early_spans = [(distance, 0, shorter) for distance in odd]
    early_spans += [(distance, 0, longer) for distance in others]
    late_spans = [(distance, shorter, capacity) for distance in odd]
    for distance in range(1, beam_count // 2):
        cut = (5 * capacity + 4) // 8
        late_spans += [(distance, 0, cut), (distance, cut, capacity)]
    late_spans.append((0, 0, capacity))
    last_spans = [(distance, longer, capacity) for distance in others]

    sent = resample(subimages[0], range_kernel[0], margin)
    halos = trade_edges(*sent)
    own_owners = owners[0, :, 0]
    other_owners = partner(owners, "aperture", 1)[0, :, 0]
    planned = plan(longer - shorter, me, own_owners, other_owners, beam_count)
    begin0 = table_row(starts0, aper_index) - (beam_index * local_blocks - MARGIN_BLOCKS)
    halos, planned = lax.optimization_barrier((halos, planned))
    *planned, target, rank = planned
    width = range_kernel.shape[3] // 2
    weights = stacked_weights(weights0)
    send = first_level(width, rows, begin0, side, sent, halos, weights)
    other = partner(send, "aperture", 0)
    keep = first_level(0, rows, begin0, side, sent, halos, weights)
    level_one = (keep.astype(jnp.float32) + other.astype(jnp.float32)).astype(jnp.bfloat16)

    beams = level_one.shape[1]
    first = lax.dynamic_slice_in_dim(level_one, even * (beams - margin), margin, 1)
    second = lax.dynamic_slice_in_dim(level_one, (1 - even) * (beams - margin), margin, 1)
    halos = trade_edges(first, second)
    begin1 = table_row(starts1, aper_index) - (beam_index * 2 * local_blocks - MARGIN_BLOCKS)
    keep, send, late = second_level(
        begin1, side, planned, level_one, halos, stacked_weights(weights1), early
    )
    other = partner(send, "aperture", 1)
    other, late = lax.optimization_barrier((other, late))
    late = partner(late, "aperture", 1)
    summed, *group = wires(early_spans, me, target, rank, keep, other)
    received = spread(early_spans, group)
    from_odd, from_others = received[: len(odd)], received[len(odd) :]
    ready, from_odd = lax.optimization_barrier((late, from_odd))
    group = wires(late_spans, me, target, rank, keep, ready, summed)
    received = from_odd + spread(late_spans, group)
    ready, from_others = lax.optimization_barrier((late, from_others))
    group = wires(last_spans, me, target, rank, keep, ready, summed)
    received += from_others + spread(last_spans, group)
    spans = early_spans[: len(odd)] + late_spans + early_spans[len(odd) :] + last_spans
    return collect(spans, capacity, beam_count, me, received)[None]


def solution(mesh):
    return jax.shard_map(
        local,
        mesh=mesh,
        in_specs=(
            P("aperture", None, "beam", None),
            P("aperture", None, None, None),
            P("aperture", "beam", None, None, None),
            P(None, "beam"),
            P("aperture", "beam", None, None, None),
            P(None, "beam"),
            P("aperture", "beam", None),
        ),
        out_specs=P("aperture", "beam", None, None, None),
        check_vma=False,
    )
```

```python
import functools

import jax
import jax.numpy as jnp
from jax import lax
from jax.experimental import pallas as pl
from jax.experimental.pallas import tpu as pltpu
from jax.sharding import PartitionSpec as P

BLK = 32
NW = 10
REACH = 2
OS = 64
MARGIN_BLOCKS = (NW - 2) // 2 + REACH
VMEM_LIMIT = 8 * 1024 * 1024
MOST_VMEM = 53 * 1024 * 1024
ANY = pl.BlockSpec(memory_space=pl.ANY)
VMEM = pl.BlockSpec(memory_space=pltpu.VMEM)
SMEM = pl.BlockSpec(memory_space=pltpu.SMEM)


def params(limit=VMEM_LIMIT):
    return pltpu.CompilerParams(vmem_limit_bytes=limit)


def cost(macs, moved):
    return pl.CostEstimate(flops=2 * macs, bytes_accessed=moved, transcendentals=0)


def trade_edges(first, second):
    count, apertures = lax.axis_size("beam"), lax.axis_size("aperture")
    received = []
    for order, block in enumerate((first, second)):
        route = []
        for aper in range(apertures):
            for place in range(count):
                other = place + 1 if (place - order) % 2 == 0 else place - 1
                if 0 <= other < count:
                    to = aper * count + other
                else:
                    to = min(aper ^ 1, apertures - 1) * count + place
                route.append((aper * count + place, to))
        received.append(lax.ppermute(block, ("aperture", "beam"), route))
    return received


def partner(block, axis, distance):
    count = lax.axis_size(axis)
    route = []
    for low in range(count):
        high = low | 1 << distance
        if high != low and high < count:
            route += [(low, high), (high, low)]
    return lax.ppermute(block, axis, route)


def dot(left, right):
    return jnp.dot(left, right, preferred_element_type=jnp.float32)


def resample_kernel(child_hbm, kernel_hbm, first_ref, second_ref, child, kernel, own, sems):
    aper, beam = lax.axis_index("aperture"), lax.axis_index("beam")
    half, quarter = aper & 1, (aper >> 1) & 1
    even = 1 - (beam & 1)
    rows, rng = child.shape[1:]
    piece = rng // 4
    child_copy = pltpu.make_async_copy(child_hbm, child, sems.at[4])
    copies = []
    for place in range(4):
        source = (half ^ (place // 2)) * 2 + (quarter ^ (place % 2))
        copies.append(
            pltpu.make_async_copy(
                kernel_hbm.at[:, :, pl.ds(pl.multiple_of(source * piece, 128), piece)],
                kernel.at[:, :, place * piece : (place + 1) * piece],
                sems.at[place],
            )
        )
    child_copy.start()
    for copy in copies:
        copy.start()
    child_copy.wait()
    real, imag = child[0], child[1]
    margin = first_ref.shape[1]
    tail = pl.ds(pl.multiple_of(even * (rows - margin), BLK), margin)
    head = pl.ds(pl.multiple_of((1 - even) * (rows - margin), BLK), margin)
    for side in range(2):
        columns = slice(side * 2 * piece, (side + 1) * 2 * piece)
        copies[2 * side].wait()
        copies[2 * side + 1].wait()
        k_real, k_imag = kernel[0, :, columns], kernel[1, :, columns]
        own[0, :, columns] = (dot(real, k_real) - dot(imag, k_imag)).astype(jnp.bfloat16)
        own[1, :, columns] = (dot(real, k_imag) + dot(imag, k_real)).astype(jnp.bfloat16)
        for part in range(2):
            first_ref[part, :, columns] = own[part, tail, columns]
            second_ref[part, :, columns] = own[part, head, columns]


def resample(child, kernel, margin):
    rows, rng = child.shape[1:]
    shape = jax.ShapeDtypeStruct((2, margin, rng), jnp.bfloat16)
    return pl.pallas_call(
        resample_kernel,
        out_shape=(shape, shape),
        in_specs=[ANY, ANY],
        out_specs=(VMEM, VMEM),
        scratch_shapes=[
            pltpu.VMEM(child.shape, jnp.bfloat16),
            pltpu.VMEM(kernel.shape, jnp.bfloat16),
            pltpu.VMEM(child.shape, jnp.bfloat16),
            pltpu.SemaphoreType.DMA((5,)),
        ],
        compiler_params=params(MOST_VMEM),
        cost_estimate=cost(4 * rows * rng * rng, 2**21),
        name="resample",
    )(child, kernel)


def complex_window(weights, real, imag):
    beams = weights.shape[0] // 2
    with_real = dot(weights, real)
    with_imag = dot(weights, imag)
    return (
        (with_real[:beams] - with_imag[beams:]).astype(jnp.bfloat16),
        (with_imag[:beams] + with_real[beams:]).astype(jnp.bfloat16),
    )


def place_halos(padded, side_ref, rows, first, second):
    even, lowest, highest = side_ref[0], side_ref[1], side_ref[2]
    margin = first.shape[1]
    far = margin + rows
    padded[:, pl.ds(pl.multiple_of(even * far, BLK), margin), :] = first
    padded[:, pl.ds(pl.multiple_of((1 - even) * far, BLK), margin), :] = second
    zeros = jnp.zeros_like(first)

    @pl.when(lowest == 1)
    def _():
        padded[:, :margin, :] = zeros

    @pl.when(highest == 1)
    def _():
        padded[:, far:, :] = zeros


def first_level_kernel(
    column, rows, starts_ref, side_ref, sent_first_ref, sent_second_ref, first_ref, second_ref,
    weights_ref, out_ref, padded,
):
    sectors, stacked, window = weights_ref.shape
    beams = stacked // 2
    margin = first_ref.shape[1]
    columns = slice(column, column + out_ref.shape[2])
    even = side_ref[0]
    tail = pl.multiple_of(margin + even * (rows - margin), BLK)
    head = pl.multiple_of(margin + (1 - even) * (rows - margin), BLK)
    padded[:, pl.ds(tail, margin), :] = sent_first_ref[:, :, columns]
    padded[:, pl.ds(head, margin), :] = sent_second_ref[:, :, columns]
    place_halos(padded, side_ref, rows, first_ref[:, :, columns], second_ref[:, :, columns])
    for sector in range(sectors):
        place = pl.ds(pl.multiple_of(starts_ref[sector] * BLK, BLK), window)
        parts = complex_window(weights_ref[sector], padded[0, place, :], padded[1, place, :])
        for part in range(2):
            out_ref[part, sector * beams : (sector + 1) * beams, :] = parts[part]


def first_level(column, rows, starts, side, sent, halos, weights):
    sectors, stacked, window = weights.shape
    margin, rng = sent[0].shape[1:]
    assert 2 * margin >= rows
    width = rng // 2
    return pl.pallas_call(
        functools.partial(first_level_kernel, column, rows),
        out_shape=jax.ShapeDtypeStruct((2, sectors * stacked // 2, width), jnp.bfloat16),
        in_specs=[SMEM, SMEM] + [VMEM] * 5,
        out_specs=VMEM,
        scratch_shapes=[pltpu.VMEM((2, rows + 2 * margin, width), jnp.bfloat16)],
        compiler_params=params(),
        cost_estimate=cost(sectors * 2 * stacked * window * width, 2**21),
        name="first_level",
    )(starts, side, *sent, *halos, weights)


def second_level_early_kernel(
    starts_ref, side_ref, sector_ref, own_ref, first_ref, second_ref, weights_ref, send_ref, padded
):
    _, stacked, window = weights_ref.shape
    per = stacked // 2 // OS
    margin, rows = first_ref.shape[1], own_ref.shape[1]
    columns = slice(send_ref.shape[3], 2 * send_ref.shape[3])
    padded[:, margin : margin + rows, :] = own_ref[:, :, columns]
    place_halos(padded, side_ref, rows, first_ref[:, :, columns], second_ref[:, :, columns])
    for place in range(send_ref.shape[0]):
        sector = sector_ref[place] // per
        piece = pl.multiple_of(sector_ref[place] % per * OS, OS)
        window_rows = pl.ds(pl.multiple_of(starts_ref[sector] * BLK, BLK), window)
        weights = jnp.concatenate(
            [
                weights_ref[sector, pl.ds(piece, OS), :],
                weights_ref[sector, pl.ds(pl.multiple_of(piece + stacked // 2, OS), OS), :],
            ]
        )
        parts = complex_window(weights, padded[0, window_rows, :], padded[1, window_rows, :])
        for part in range(2):
            send_ref[place, part] = parts[part]


def second_level_kernel(
    starts_ref, side_ref, own_at_ref, other_at_ref, own_ref, first_ref, second_ref, weights_ref,
    keep_ref, send_ref, padded, send,
):
    sectors, stacked, window = weights_ref.shape
    beams = stacked // 2
    width = keep_ref.shape[3]
    margin, rows = first_ref.shape[1], own_ref.shape[1]
    padded[:, margin : margin + rows, :] = own_ref[...]
    place_halos(padded, side_ref, rows, first_ref[...], second_ref[...])
    per = beams // OS
    for sector in range(sectors):
        place = pl.ds(pl.multiple_of(starts_ref[sector] * BLK, BLK), window)
        parts = complex_window(weights_ref[sector], padded[0, place, :], padded[1, place, :])
        for piece in range(per):
            own_at = own_at_ref[sector * per + piece]
            other_at = other_at_ref[sector * per + piece]
            taken = slice(piece * OS, (piece + 1) * OS)
            for part in range(2):
                keep_ref[own_at, part] = parts[part][taken, :width]
                send[other_at, part] = parts[part][taken, width:]
    send_ref[...] = send[send.shape[0] - send_ref.shape[0] :]


def second_level(starts, side, planned, own, halos, weights, early):
    sectors, stacked, window = weights.shape
    margin, rows, rng = halos[0].shape[1], own.shape[1], own.shape[2]
    count = sectors * stacked // 2 // OS
    block = (2, OS, rng // 2)
    own_at, other_at, other_sector = planned
    early_send = pl.pallas_call(
        second_level_early_kernel,
        out_shape=jax.ShapeDtypeStruct((early,) + block, jnp.bfloat16),
        in_specs=[SMEM] * 3 + [VMEM] * 4,
        out_specs=VMEM,
        scratch_shapes=[pltpu.VMEM((2, rows + 2 * margin, rng // 2), jnp.bfloat16)],
        compiler_params=params(),
        cost_estimate=cost(early * 2 * 2 * OS * window * rng // 2, 2**20),
        name="second_level_early",
    )(starts, side, other_sector, own, *halos, weights)
    shapes = [jax.ShapeDtypeStruct((n,) + block, jnp.bfloat16) for n in (count, count - early)]
    keep, late_send = pl.pallas_call(
        second_level_kernel,
        out_shape=shapes,
        in_specs=[SMEM] * 4 + [VMEM] * 4,
        out_specs=[VMEM] * 2,
        scratch_shapes=[
            pltpu.VMEM((2, rows + 2 * margin, rng), jnp.bfloat16),
            pltpu.VMEM((count,) + block, jnp.bfloat16),
        ],
        compiler_params=params(),
        cost_estimate=cost(sectors * 2 * stacked * window * rng, 2**22),
        name="second_level",
    )(starts, side, own_at, other_at, own, *halos, weights)
    return keep, early_send, late_send


def plan_kernel(
    shift, me_ref, own_ref, other_ref, own_at_ref, other_at_ref, other_sector_ref, target_ref, rank_ref,
    taken, filled,
):
    count = own_ref.shape[0]
    far_bit = taken.shape[0] // 2

    def delay(target):
        distance = target ^ me_ref[0]
        return jnp.where((distance & far_bit) == 0, 2 * count, (distance & 1) * shift)

    for owners_ref, at_ref in ((other_ref, other_at_ref), (own_ref, own_at_ref)):
        for target in range(taken.shape[0]):
            taken[target] = 0
        for bucket in range(filled.shape[0]):
            filled[bucket] = 0
        for sector in range(count):
            target = owners_ref[sector]
            rank = taken[target]
            taken[target] = rank + 1
            bucket = rank + delay(target)
            at_ref[sector] = bucket
            filled[bucket + 1] = filled[bucket + 1] + 1
        for bucket in range(1, filled.shape[0]):
            filled[bucket] = filled[bucket] + filled[bucket - 1]
        for sector in range(count):
            bucket = at_ref[sector]
            place = filled[bucket]
            filled[bucket] = place + 1
            at_ref[sector] = place
            if at_ref is own_at_ref:
                target_ref[place] = owners_ref[sector]
                rank_ref[place] = bucket - delay(owners_ref[sector])
            else:
                other_sector_ref[place] = sector


def plan(shift, me, own, other, beam_count):
    count = own.shape[0]
    shape = jax.ShapeDtypeStruct((count,), jnp.int32)
    return pl.pallas_call(
        functools.partial(plan_kernel, shift),
        out_shape=[shape] * 5,
        in_specs=[SMEM] * 3,
        out_specs=[SMEM] * 5,
        scratch_shapes=[
            pltpu.SMEM((beam_count,), jnp.int32),
            pltpu.SMEM((3 * count + 1,), jnp.int32),
        ],
        compiler_params=params(),
        name="plan",
    )(me, own, other)


def wires_kernel(spans, early, me_ref, target_ref, rank_ref, keep_ref, *refs):
    wires = refs[-1]
    spare = wires.shape[0] - 1
    out_refs = refs[-1 - len(spans) : -1]
    other_ref, *summed_refs = refs[: -1 - len(spans)]
    wires[...] = jnp.zeros_like(wires)
    me = me_ref[0]

    def lay(place, total):
        rank = rank_ref[place]
        distance = target_ref[place] ^ me
        at = spare
        start = 0
        for number, low, high in spans:
            wanted = (distance == number) & (rank >= low) & (rank < high)
            at = jnp.where(wanted, start + rank - low, at)
            start += high - low
        wires[at] = total

    before = 0
    if not early:
        before = summed_refs[0].shape[0]
        for row in range(before):
            lay(row, summed_refs[0][row])
    for row in range(other_ref.shape[0]):
        place = before + row
        total = keep_ref[place].astype(jnp.float32) + other_ref[row].astype(jnp.float32)
        total = total.astype(jnp.bfloat16)
        lay(place, total)
        if early:
            summed_refs[0][row] = total
    start = 0
    for (_, low, high), ref in zip(spans, out_refs):
        ref[...] = wires[start : start + high - low]
        start += high - low


def wires(spans, me, target, rank, keep, other, summed=None):
    block = keep.shape[1:]
    sizes = [high - low for _, low, high in spans]
    inputs = [me, target, rank, keep, other]
    if summed is None:
        sizes = [other.shape[0]] + sizes
    else:
        inputs.append(summed)
    shapes = [jax.ShapeDtypeStruct((size,) + block, jnp.bfloat16) for size in sizes]
    total = sum(high - low for _, low, high in spans)
    return pl.pallas_call(
        functools.partial(wires_kernel, spans, summed is None),
        out_shape=shapes,
        in_specs=[SMEM] * 3 + [VMEM] * (len(inputs) - 3),
        out_specs=[VMEM] * len(shapes),
        scratch_shapes=[pltpu.VMEM((total + 1,) + block, jnp.bfloat16)],
        compiler_params=params(),
        cost_estimate=cost(0, 2**21),
        name="early_wires" if summed is None else "late_wires",
    )(*inputs)


def collect_kernel(spans, capacity, me_ref, *refs):
    sems = refs[-1]
    out_ref = refs[-2]
    copies = []
    for number, (distance, low, high) in enumerate(spans):
        start = (me_ref[0] ^ distance) * capacity + low
        copies.append(
            pltpu.make_async_copy(
                refs[number], out_ref.at[pl.ds(start, high - low)], sems.at[number]
            )
        )
    for copy in copies:
        copy.start()
    for copy in copies:
        copy.wait()


def collect(spans, capacity, beam_count, me, received):
    shape = (beam_count * capacity,) + received[0].shape[1:]
    return pl.pallas_call(
        functools.partial(collect_kernel, spans, capacity),
        out_shape=jax.ShapeDtypeStruct(shape, jnp.bfloat16),
        in_specs=[SMEM] + [ANY] * len(received),
        out_specs=ANY,
        scratch_shapes=[pltpu.SemaphoreType.DMA((len(received),))],
        compiler_params=params(),
        cost_estimate=cost(0, 2**21),
        name="collect",
    )(me, *received)


def spread(spans, group):
    count = lax.axis_size("beam")
    received = []
    for (distance, _, _), wire in zip(spans, group):
        route = [(place, place ^ distance) for place in range(count)]
        received.append(lax.ppermute(wire, "beam", route) if distance else wire)
    return received


def stacked_weights(weights):
    return weights[0].reshape(weights.shape[1], -1, weights.shape[4])


def table_row(table, row_number):
    return lax.dynamic_index_in_dim(table, row_number, 0, keepdims=False)


def local(subimages, range_kernel, weights0, starts0, weights1, starts1, owners):
    aper_index = lax.axis_index("aperture")
    beam_index = lax.axis_index("beam")
    beam_count = lax.axis_size("beam")
    margin = MARGIN_BLOCKS * BLK
    rows = subimages.shape[2]
    local_blocks = rows // BLK
    even = (beam_index + 1) % 2
    ends = (beam_index == 0, beam_index == beam_count - 1)
    side = jnp.stack([even] + [end.astype(jnp.int32) for end in ends])
    me = beam_index.reshape(1)

    sector_count = owners.shape[1]
    capacity = max(2, 2 * sector_count // beam_count)
    shorter, longer = max(1, capacity // 4), max(1, capacity // 2)
    far = range(beam_count // 2, beam_count)
    odd = [distance for distance in far if distance % 2]
    others = [distance for distance in far if distance % 2 == 0]
    early = len(odd) * shorter + len(others) * longer
    early_spans = [(distance, 0, shorter) for distance in odd]
    early_spans += [(distance, 0, longer) for distance in others]
    late_spans = [(distance, shorter, capacity) for distance in odd]
    near_spans = [(distance, 0, capacity) for distance in reversed(range(beam_count // 2))]
    last_spans = [(distance, longer, capacity) for distance in others]

    sent = resample(subimages[0], range_kernel[0], margin)
    halos = trade_edges(*sent)
    own_owners = owners[0, :, 0]
    other_owners = partner(owners, "aperture", 1)[0, :, 0]
    planned = plan(longer - shorter, me, own_owners, other_owners, beam_count)
    begin0 = table_row(starts0, aper_index) - (beam_index * local_blocks - MARGIN_BLOCKS)
    halos, planned = lax.optimization_barrier((halos, planned))
    *planned, target, rank = planned
    width = range_kernel.shape[3] // 2
    weights = stacked_weights(weights0)
    send = first_level(width, rows, begin0, side, sent, halos, weights)
    other = partner(send, "aperture", 0)
    keep = first_level(0, rows, begin0, side, sent, halos, weights)
    level_one = (keep.astype(jnp.float32) + other.astype(jnp.float32)).astype(jnp.bfloat16)

    beams = level_one.shape[1]
    first = lax.dynamic_slice_in_dim(level_one, even * (beams - margin), margin, 1)
    second = lax.dynamic_slice_in_dim(level_one, (1 - even) * (beams - margin), margin, 1)
    halos = trade_edges(first, second)
    begin1 = table_row(starts1, aper_index) - (beam_index * 2 * local_blocks - MARGIN_BLOCKS)
    keep, send, late = second_level(
        begin1, side, planned, level_one, halos, stacked_weights(weights1), early
    )
    other = partner(send, "aperture", 1)
    other, late = lax.optimization_barrier((other, late))
    late = partner(late, "aperture", 1)
    summed, *group = wires(early_spans, me, target, rank, keep, other)
    received = spread(early_spans, group)
    from_odd, from_others = received[: len(odd)], received[len(odd) :]
    near = wires(near_spans, me, target, rank, keep, late, summed)
    ready, from_odd = lax.optimization_barrier((late, from_odd))
    from_near = spread(near_spans, near)
    group = wires(late_spans, me, target, rank, keep, ready, summed)
    from_late = spread(late_spans, group)
    ready, from_others = lax.optimization_barrier((late, from_others))
    group = wires(last_spans, me, target, rank, keep, ready, summed)
    received = from_odd + from_others + from_near + from_late + spread(last_spans, group)
    spans = early_spans + near_spans + late_spans + last_spans
    return collect(spans, capacity, beam_count, me, received)[None]


def solution(mesh):
    return jax.shard_map(
        local,
        mesh=mesh,
        in_specs=(
            P("aperture", None, "beam", None),
            P("aperture", None, None, None),
            P("aperture", "beam", None, None, None),
            P(None, "beam"),
            P("aperture", "beam", None, None, None),
            P(None, "beam"),
            P("aperture", "beam", None),
        ),
        out_specs=P("aperture", "beam", None, None, None),
        check_vma=False,
    )
```

```python
import functools

import jax
import jax.numpy as jnp
from jax import lax
from jax.experimental import pallas as pl
from jax.experimental.pallas import tpu as pltpu
from jax.sharding import PartitionSpec as P

BLK = 32
NW = 10
REACH = 2
OS = 64
MARGIN_BLOCKS = (NW - 2) // 2 + REACH
VMEM_LIMIT = 8 * 1024 * 1024
MOST_VMEM = 53 * 1024 * 1024
ANY = pl.BlockSpec(memory_space=pl.ANY)
VMEM = pl.BlockSpec(memory_space=pltpu.VMEM)
SMEM = pl.BlockSpec(memory_space=pltpu.SMEM)


def params(limit=VMEM_LIMIT):
    return pltpu.CompilerParams(vmem_limit_bytes=limit)


def cost(macs, moved):
    return pl.CostEstimate(flops=2 * macs, bytes_accessed=moved, transcendentals=0)


def trade_edges(first, second):
    count, apertures = lax.axis_size("beam"), lax.axis_size("aperture")
    received = []
    for order, block in enumerate((first, second)):
        route = []
        for aper in range(apertures):
            for place in range(count):
                other = place + 1 if (place - order - aper) % 2 == 0 else place - 1
                if 0 <= other < count:
                    to = aper * count + other
                else:
                    to = (aper ^ 2 if aper ^ 2 < apertures else aper) * count + place
                route.append((aper * count + place, to))
        received.append(lax.ppermute(block, ("aperture", "beam"), route))
    return received


def partner(block, axis, distance):
    count = lax.axis_size(axis)
    route = []
    for low in range(count):
        high = low | 1 << distance
        if high != low and high < count:
            route += [(low, high), (high, low)]
    return lax.ppermute(block, axis, route)


def dot(left, right):
    return jnp.dot(left, right, preferred_element_type=jnp.float32)


def resample_kernel(child_hbm, kernel_hbm, first_ref, second_ref, child, kernel, own, sems):
    aper, beam = lax.axis_index("aperture"), lax.axis_index("beam")
    half, quarter = aper & 1, (aper >> 1) & 1
    even = 1 - ((aper + beam) & 1)
    rows, rng = child.shape[1:]
    piece = rng // 4
    child_copy = pltpu.make_async_copy(child_hbm, child, sems.at[4])
    copies = []
    for place in range(4):
        source = (half ^ (place // 2)) * 2 + (quarter ^ (place % 2))
        copies.append(
            pltpu.make_async_copy(
                kernel_hbm.at[:, :, pl.ds(pl.multiple_of(source * piece, 128), piece)],
                kernel.at[:, :, place * piece : (place + 1) * piece],
                sems.at[place],
            )
        )
    child_copy.start()
    for copy in copies:
        copy.start()
    child_copy.wait()
    real, imag = child[0], child[1]
    margin = first_ref.shape[1]
    tail = pl.ds(pl.multiple_of(even * (rows - margin), BLK), margin)
    head = pl.ds(pl.multiple_of((1 - even) * (rows - margin), BLK), margin)
    for side in range(2):
        columns = slice(side * 2 * piece, (side + 1) * 2 * piece)
        copies[2 * side].wait()
        copies[2 * side + 1].wait()
        k_real, k_imag = kernel[0, :, columns], kernel[1, :, columns]
        own[0, :, columns] = (dot(real, k_real) - dot(imag, k_imag)).astype(jnp.bfloat16)
        own[1, :, columns] = (dot(real, k_imag) + dot(imag, k_real)).astype(jnp.bfloat16)
        for part in range(2):
            first_ref[part, :, columns] = own[part, tail, columns]
            second_ref[part, :, columns] = own[part, head, columns]


def resample(child, kernel, margin):
    rows, rng = child.shape[1:]
    shape = jax.ShapeDtypeStruct((2, margin, rng), jnp.bfloat16)
    return pl.pallas_call(
        resample_kernel,
        out_shape=(shape, shape),
        in_specs=[ANY, ANY],
        out_specs=(VMEM, VMEM),
        scratch_shapes=[
            pltpu.VMEM(child.shape, jnp.bfloat16),
            pltpu.VMEM(kernel.shape, jnp.bfloat16),
            pltpu.VMEM(child.shape, jnp.bfloat16),
            pltpu.SemaphoreType.DMA((5,)),
        ],
        compiler_params=params(MOST_VMEM),
        cost_estimate=cost(4 * rows * rng * rng, 2**21),
        name="resample",
    )(child, kernel)


def complex_window(weights, real, imag):
    beams = weights.shape[0] // 2
    with_real = dot(weights, real)
    with_imag = dot(weights, imag)
    return (
        (with_real[:beams] - with_imag[beams:]).astype(jnp.bfloat16),
        (with_imag[:beams] + with_real[beams:]).astype(jnp.bfloat16),
    )


def place_halos(padded, side_ref, rows, first, second):
    even, lowest, highest = side_ref[0], side_ref[1], side_ref[2]
    margin = first.shape[1]
    far = margin + rows
    padded[:, pl.ds(pl.multiple_of(even * far, BLK), margin), :] = first
    padded[:, pl.ds(pl.multiple_of((1 - even) * far, BLK), margin), :] = second
    zeros = jnp.zeros_like(first)

    @pl.when(lowest == 1)
    def _():
        padded[:, :margin, :] = zeros

    @pl.when(highest == 1)
    def _():
        padded[:, far:, :] = zeros


def first_level_kernel(
    column, rows, starts_ref, side_ref, sent_first_ref, sent_second_ref, first_ref, second_ref,
    weights_ref, out_ref, padded,
):
    sectors, stacked, window = weights_ref.shape
    beams = stacked // 2
    margin = first_ref.shape[1]
    columns = slice(column, column + out_ref.shape[2])
    even = side_ref[0]
    tail = pl.multiple_of(margin + even * (rows - margin), BLK)
    head = pl.multiple_of(margin + (1 - even) * (rows - margin), BLK)
    padded[:, pl.ds(tail, margin), :] = sent_first_ref[:, :, columns]
    padded[:, pl.ds(head, margin), :] = sent_second_ref[:, :, columns]
    place_halos(padded, side_ref, rows, first_ref[:, :, columns], second_ref[:, :, columns])
    for sector in range(sectors):
        place = pl.ds(pl.multiple_of(starts_ref[sector] * BLK, BLK), window)
        parts = complex_window(weights_ref[sector], padded[0, place, :], padded[1, place, :])
        for part in range(2):
            out_ref[part, sector * beams : (sector + 1) * beams, :] = parts[part]


def first_level(column, rows, starts, side, sent, halos, weights):
    sectors, stacked, window = weights.shape
    margin, rng = sent[0].shape[1:]
    assert 2 * margin >= rows
    width = rng // 2
    return pl.pallas_call(
        functools.partial(first_level_kernel, column, rows),
        out_shape=jax.ShapeDtypeStruct((2, sectors * stacked // 2, width), jnp.bfloat16),
        in_specs=[SMEM, SMEM] + [VMEM] * 5,
        out_specs=VMEM,
        scratch_shapes=[pltpu.VMEM((2, rows + 2 * margin, width), jnp.bfloat16)],
        compiler_params=params(),
        cost_estimate=cost(sectors * 2 * stacked * window * width, 2**21),
        name="first_level",
    )(starts, side, *sent, *halos, weights)


def second_level_early_kernel(
    starts_ref, side_ref, sector_ref, own_ref, first_ref, second_ref, weights_ref, send_ref, padded
):
    _, stacked, window = weights_ref.shape
    per = stacked // 2 // OS
    margin, rows = first_ref.shape[1], own_ref.shape[1]
    columns = slice(send_ref.shape[3], 2 * send_ref.shape[3])
    padded[:, margin : margin + rows, :] = own_ref[:, :, columns]
    place_halos(padded, side_ref, rows, first_ref[:, :, columns], second_ref[:, :, columns])
    for place in range(send_ref.shape[0]):
        sector = sector_ref[place] // per
        piece = pl.multiple_of(sector_ref[place] % per * OS, OS)
        window_rows = pl.ds(pl.multiple_of(starts_ref[sector] * BLK, BLK), window)
        weights = jnp.concatenate(
            [
                weights_ref[sector, pl.ds(piece, OS), :],
                weights_ref[sector, pl.ds(pl.multiple_of(piece + stacked // 2, OS), OS), :],
            ]
        )
        parts = complex_window(weights, padded[0, window_rows, :], padded[1, window_rows, :])
        for part in range(2):
            send_ref[place, part] = parts[part]


def second_level_kernel(
    starts_ref, side_ref, own_at_ref, other_at_ref, own_ref, first_ref, second_ref, weights_ref,
    keep_ref, send_ref, padded, send,
):
    sectors, stacked, window = weights_ref.shape
    beams = stacked // 2
    width = keep_ref.shape[3]
    margin, rows = first_ref.shape[1], own_ref.shape[1]
    padded[:, margin : margin + rows, :] = own_ref[...]
    place_halos(padded, side_ref, rows, first_ref[...], second_ref[...])
    per = beams // OS
    for sector in range(sectors):
        place = pl.ds(pl.multiple_of(starts_ref[sector] * BLK, BLK), window)
        parts = complex_window(weights_ref[sector], padded[0, place, :], padded[1, place, :])
        for piece in range(per):
            own_at = own_at_ref[sector * per + piece]
            other_at = other_at_ref[sector * per + piece]
            taken = slice(piece * OS, (piece + 1) * OS)
            for part in range(2):
                keep_ref[own_at, part] = parts[part][taken, :width]
                send[other_at, part] = parts[part][taken, width:]
    send_ref[...] = send[send.shape[0] - send_ref.shape[0] :]


def second_level(starts, side, planned, own, halos, weights, early):
    sectors, stacked, window = weights.shape
    margin, rows, rng = halos[0].shape[1], own.shape[1], own.shape[2]
    count = sectors * stacked // 2 // OS
    block = (2, OS, rng // 2)
    own_at, other_at, other_sector = planned
    early_send = pl.pallas_call(
        second_level_early_kernel,
        out_shape=jax.ShapeDtypeStruct((early,) + block, jnp.bfloat16),
        in_specs=[SMEM] * 3 + [VMEM] * 4,
        out_specs=VMEM,
        scratch_shapes=[pltpu.VMEM((2, rows + 2 * margin, rng // 2), jnp.bfloat16)],
        compiler_params=params(),
        cost_estimate=cost(early * 2 * 2 * OS * window * rng // 2, 2**20),
        name="second_level_early",
    )(starts, side, other_sector, own, *halos, weights)
    shapes = [jax.ShapeDtypeStruct((n,) + block, jnp.bfloat16) for n in (count, count - early)]
    keep, late_send = pl.pallas_call(
        second_level_kernel,
        out_shape=shapes,
        in_specs=[SMEM] * 4 + [VMEM] * 4,
        out_specs=[VMEM] * 2,
        scratch_shapes=[
            pltpu.VMEM((2, rows + 2 * margin, rng), jnp.bfloat16),
            pltpu.VMEM((count,) + block, jnp.bfloat16),
        ],
        compiler_params=params(),
        cost_estimate=cost(sectors * 2 * stacked * window * rng, 2**22),
        name="second_level",
    )(starts, side, own_at, other_at, own, *halos, weights)
    return keep, early_send, late_send


def plan_kernel(
    shift, me_ref, own_ref, other_ref, own_at_ref, other_at_ref, other_sector_ref, target_ref, rank_ref,
    taken, filled,
):
    count = own_ref.shape[0]
    far_bit = taken.shape[0] // 2

    def delay(target):
        distance = target ^ me_ref[0]
        return jnp.where((distance & far_bit) == 0, 2 * count, (distance & 1) * shift)

    for owners_ref, at_ref in ((other_ref, other_at_ref), (own_ref, own_at_ref)):
        for target in range(taken.shape[0]):
            taken[target] = 0
        for bucket in range(filled.shape[0]):
            filled[bucket] = 0
        for sector in range(count):
            target = owners_ref[sector]
            rank = taken[target]
            taken[target] = rank + 1
            bucket = rank + delay(target)
            at_ref[sector] = bucket
            filled[bucket + 1] = filled[bucket + 1] + 1
        for bucket in range(1, filled.shape[0]):
            filled[bucket] = filled[bucket] + filled[bucket - 1]
        for sector in range(count):
            bucket = at_ref[sector]
            place = filled[bucket]
            filled[bucket] = place + 1
            at_ref[sector] = place
            if at_ref is own_at_ref:
                target_ref[place] = owners_ref[sector]
                rank_ref[place] = bucket - delay(owners_ref[sector])
            else:
                other_sector_ref[place] = sector


def plan(shift, me, own, other, beam_count):
    count = own.shape[0]
    shape = jax.ShapeDtypeStruct((count,), jnp.int32)
    return pl.pallas_call(
        functools.partial(plan_kernel, shift),
        out_shape=[shape] * 5,
        in_specs=[SMEM] * 3,
        out_specs=[SMEM] * 5,
        scratch_shapes=[
            pltpu.SMEM((beam_count,), jnp.int32),
            pltpu.SMEM((3 * count + 1,), jnp.int32),
        ],
        compiler_params=params(),
        name="plan",
    )(me, own, other)


def wires_kernel(spans, early, me_ref, target_ref, rank_ref, keep_ref, *refs):
    wires = refs[-1]
    spare = wires.shape[0] - 1
    out_refs = refs[-1 - len(spans) : -1]
    other_ref, *summed_refs = refs[: -1 - len(spans)]
    wires[...] = jnp.zeros_like(wires)
    me = me_ref[0]

    def lay(place, total):
        rank = rank_ref[place]
        distance = target_ref[place] ^ me
        at = spare
        start = 0
        for number, low, high in spans:
            wanted = (distance == number) & (rank >= low) & (rank < high)
            at = jnp.where(wanted, start + rank - low, at)
            start += high - low
        wires[at] = total

    before = 0
    if not early:
        before = summed_refs[0].shape[0]
        for row in range(before):
            lay(row, summed_refs[0][row])
    for row in range(other_ref.shape[0]):
        place = before + row
        total = keep_ref[place].astype(jnp.float32) + other_ref[row].astype(jnp.float32)
        total = total.astype(jnp.bfloat16)
        lay(place, total)
        if early:
            summed_refs[0][row] = total
    start = 0
    for (_, low, high), ref in zip(spans, out_refs):
        ref[...] = wires[start : start + high - low]
        start += high - low


def wires(spans, me, target, rank, keep, other, summed=None):
    block = keep.shape[1:]
    sizes = [high - low for _, low, high in spans]
    inputs = [me, target, rank, keep, other]
    if summed is None:
        sizes = [other.shape[0]] + sizes
    else:
        inputs.append(summed)
    shapes = [jax.ShapeDtypeStruct((size,) + block, jnp.bfloat16) for size in sizes]
    total = sum(high - low for _, low, high in spans)
    return pl.pallas_call(
        functools.partial(wires_kernel, spans, summed is None),
        out_shape=shapes,
        in_specs=[SMEM] * 3 + [VMEM] * (len(inputs) - 3),
        out_specs=[VMEM] * len(shapes),
        scratch_shapes=[pltpu.VMEM((total + 1,) + block, jnp.bfloat16)],
        compiler_params=params(),
        cost_estimate=cost(0, 2**21),
        name="early_wires" if summed is None else "late_wires",
    )(*inputs)


def collect_kernel(spans, capacity, me_ref, *refs):
    sems = refs[-1]
    out_ref = refs[-2]
    copies = []
    for number, (distance, low, high) in enumerate(spans):
        start = (me_ref[0] ^ distance) * capacity + low
        copies.append(
            pltpu.make_async_copy(
                refs[number], out_ref.at[pl.ds(start, high - low)], sems.at[number]
            )
        )
    for copy in copies:
        copy.start()
    for copy in copies:
        copy.wait()


def collect(spans, capacity, beam_count, me, received):
    shape = (beam_count * capacity,) + received[0].shape[1:]
    return pl.pallas_call(
        functools.partial(collect_kernel, spans, capacity),
        out_shape=jax.ShapeDtypeStruct(shape, jnp.bfloat16),
        in_specs=[SMEM] + [ANY] * len(received),
        out_specs=ANY,
        scratch_shapes=[pltpu.SemaphoreType.DMA((len(received),))],
        compiler_params=params(),
        cost_estimate=cost(0, 2**21),
        name="collect",
    )(me, *received)


def spread(spans, group):
    count = lax.axis_size("beam")
    received = []
    for (distance, _, _), wire in zip(spans, group):
        route = [(place, place ^ distance) for place in range(count)]
        received.append(lax.ppermute(wire, "beam", route) if distance else wire)
    return received


def stacked_weights(weights):
    return weights[0].reshape(weights.shape[1], -1, weights.shape[4])


def table_row(table, row_number):
    return lax.dynamic_index_in_dim(table, row_number, 0, keepdims=False)


def local(subimages, range_kernel, weights0, starts0, weights1, starts1, owners):
    aper_index = lax.axis_index("aperture")
    beam_index = lax.axis_index("beam")
    beam_count = lax.axis_size("beam")
    margin = MARGIN_BLOCKS * BLK
    rows = subimages.shape[2]
    local_blocks = rows // BLK
    even = (aper_index + beam_index + 1) % 2
    ends = (beam_index == 0, beam_index == beam_count - 1)
    side = jnp.stack([even] + [end.astype(jnp.int32) for end in ends])
    me = beam_index.reshape(1)

    sector_count = owners.shape[1]
    capacity = max(2, 2 * sector_count // beam_count)
    shorter, longer = max(1, capacity // 4), max(1, capacity // 2)
    far = range(beam_count // 2, beam_count)
    odd = [distance for distance in far if distance % 2]
    others = [distance for distance in far if distance % 2 == 0]
    early = len(odd) * shorter + len(others) * longer
    early_spans = [(distance, 0, shorter) for distance in odd]
    early_spans += [(distance, 0, longer) for distance in others]
    late_spans = [(distance, shorter, capacity) for distance in odd]
    for distance in range(1, beam_count // 2):
        late_spans += [(distance, 0, capacity // 2), (distance, capacity // 2, capacity)]
    late_spans.append((0, 0, capacity))
    last_spans = [(distance, longer, capacity) for distance in others]

    sent = resample(subimages[0], range_kernel[0], margin)
    halos = trade_edges(*sent)
    own_owners = owners[0, :, 0]
    other_owners = partner(owners, "aperture", 1)[0, :, 0]
    planned = plan(longer - shorter, me, own_owners, other_owners, beam_count)
    begin0 = table_row(starts0, aper_index) - (beam_index * local_blocks - MARGIN_BLOCKS)
    halos, planned = lax.optimization_barrier((halos, planned))
    *planned, target, rank = planned
    width = range_kernel.shape[3] // 2
    weights = stacked_weights(weights0)
    send = first_level(width, rows, begin0, side, sent, halos, weights)
    other = partner(send, "aperture", 0)
    keep = first_level(0, rows, begin0, side, sent, halos, weights)
    level_one = (keep.astype(jnp.float32) + other.astype(jnp.float32)).astype(jnp.bfloat16)

    beams = level_one.shape[1]
    first = lax.dynamic_slice_in_dim(level_one, even * (beams - margin), margin, 1)
    second = lax.dynamic_slice_in_dim(level_one, (1 - even) * (beams - margin), margin, 1)
    halos = trade_edges(first, second)
    begin1 = table_row(starts1, aper_index) - (beam_index * 2 * local_blocks - MARGIN_BLOCKS)
    keep, send, late = second_level(
        begin1, side, planned, level_one, halos, stacked_weights(weights1), early
    )
    other = partner(send, "aperture", 1)
    other, late = lax.optimization_barrier((other, late))
    late = partner(late, "aperture", 1)
    summed, *group = wires(early_spans, me, target, rank, keep, other)
    received = spread(early_spans, group)
    from_odd, from_others = received[: len(odd)], received[len(odd) :]
    ready, from_odd = lax.optimization_barrier((late, from_odd))
    group = wires(late_spans, me, target, rank, keep, ready, summed)
    received = from_odd + spread(late_spans, group)
    ready, from_others = lax.optimization_barrier((late, from_others))
    group = wires(last_spans, me, target, rank, keep, ready, summed)
    received += from_others + spread(last_spans, group)
    spans = early_spans[: len(odd)] + late_spans + early_spans[len(odd) :] + last_spans
    return collect(spans, capacity, beam_count, me, received)[None]


def solution(mesh):
    return jax.shard_map(
        local,
        mesh=mesh,
        in_specs=(
            P("aperture", None, "beam", None),
            P("aperture", None, None, None),
            P("aperture", "beam", None, None, None),
            P(None, "beam"),
            P("aperture", "beam", None, None, None),
            P(None, "beam"),
            P("aperture", "beam", None),
        ),
        out_specs=P("aperture", "beam", None, None, None),
        check_vma=False,
    )
```

```python
import functools

import jax
import jax.numpy as jnp
from jax import lax
from jax.experimental import pallas as pl
from jax.experimental.pallas import tpu as pltpu
from jax.sharding import PartitionSpec as P

BLK = 32
NW = 10
REACH = 2
OS = 64
MARGIN_BLOCKS = (NW - 2) // 2 + REACH
VMEM_LIMIT = 8 * 1024 * 1024
MOST_VMEM = 53 * 1024 * 1024
ANY = pl.BlockSpec(memory_space=pl.ANY)
VMEM = pl.BlockSpec(memory_space=pltpu.VMEM)
SMEM = pl.BlockSpec(memory_space=pltpu.SMEM)


def params(limit=VMEM_LIMIT):
    return pltpu.CompilerParams(vmem_limit_bytes=limit)


def cost(macs, moved):
    return pl.CostEstimate(flops=2 * macs, bytes_accessed=moved, transcendentals=0)


def trade_edges(first, second):
    count, apertures = lax.axis_size("beam"), lax.axis_size("aperture")
    received = []
    for order, block in enumerate((first, second)):
        route = []
        for aper in range(apertures):
            for place in range(count):
                other = place + 1 if (place - order) % 2 == 0 else place - 1
                if 0 <= other < count:
                    to = aper * count + other
                else:
                    to = min(aper ^ 1, apertures - 1) * count + place
                route.append((aper * count + place, to))
        received.append(lax.ppermute(block, ("aperture", "beam"), route))
    return received


def partner(block, axis, distance):
    count = lax.axis_size(axis)
    route = []
    for low in range(count):
        high = low | 1 << distance
        if high != low and high < count:
            route += [(low, high), (high, low)]
    return lax.ppermute(block, axis, route)


def dot(left, right):
    return jnp.dot(left, right, preferred_element_type=jnp.float32)


def resample_kernel(child_hbm, kernel_hbm, first_ref, second_ref, child, kernel, own, sems):
    aper, beam = lax.axis_index("aperture"), lax.axis_index("beam")
    half, quarter = aper & 1, (aper >> 1) & 1
    even = 1 - (beam & 1)
    rows, rng = child.shape[1:]
    piece = rng // 4
    child_copy = pltpu.make_async_copy(child_hbm, child, sems.at[4])
    copies = []
    for place in range(4):
        source = (half ^ (place // 2)) * 2 + (quarter ^ (place % 2))
        copies.append(
            pltpu.make_async_copy(
                kernel_hbm.at[:, :, pl.ds(pl.multiple_of(source * piece, 128), piece)],
                kernel.at[:, :, place * piece : (place + 1) * piece],
                sems.at[place],
            )
        )
    child_copy.start()
    for copy in copies:
        copy.start()
    child_copy.wait()
    real, imag = child[0], child[1]
    margin = first_ref.shape[1]
    tail = pl.ds(pl.multiple_of(even * (rows - margin), BLK), margin)
    head = pl.ds(pl.multiple_of((1 - even) * (rows - margin), BLK), margin)
    for side in range(2):
        columns = slice(side * 2 * piece, (side + 1) * 2 * piece)
        copies[2 * side].wait()
        copies[2 * side + 1].wait()
        k_real, k_imag = kernel[0, :, columns], kernel[1, :, columns]
        own[0, :, columns] = (dot(real, k_real) - dot(imag, k_imag)).astype(jnp.bfloat16)
        own[1, :, columns] = (dot(real, k_imag) + dot(imag, k_real)).astype(jnp.bfloat16)
        for part in range(2):
            first_ref[part, :, columns] = own[part, tail, columns]
            second_ref[part, :, columns] = own[part, head, columns]


def resample(child, kernel, margin):
    rows, rng = child.shape[1:]
    shape = jax.ShapeDtypeStruct((2, margin, rng), jnp.bfloat16)
    return pl.pallas_call(
        resample_kernel,
        out_shape=(shape, shape),
        in_specs=[ANY, ANY],
        out_specs=(VMEM, VMEM),
        scratch_shapes=[
            pltpu.VMEM(child.shape, jnp.bfloat16),
            pltpu.VMEM(kernel.shape, jnp.bfloat16),
            pltpu.VMEM(child.shape, jnp.bfloat16),
            pltpu.SemaphoreType.DMA((5,)),
        ],
        compiler_params=params(MOST_VMEM),
        cost_estimate=cost(4 * rows * rng * rng, 2**21),
        name="resample",
    )(child, kernel)


def complex_window(weights, real, imag):
    beams = weights.shape[0] // 2
    with_real = dot(weights, real)
    with_imag = dot(weights, imag)
    return (
        (with_real[:beams] - with_imag[beams:]).astype(jnp.bfloat16),
        (with_imag[:beams] + with_real[beams:]).astype(jnp.bfloat16),
    )


def place_halos(padded, side_ref, rows, first, second):
    even, lowest, highest = side_ref[0], side_ref[1], side_ref[2]
    margin = first.shape[1]
    far = margin + rows
    padded[:, pl.ds(pl.multiple_of(even * far, BLK), margin), :] = first
    padded[:, pl.ds(pl.multiple_of((1 - even) * far, BLK), margin), :] = second
    zeros = jnp.zeros_like(first)

    @pl.when(lowest == 1)
    def _():
        padded[:, :margin, :] = zeros

    @pl.when(highest == 1)
    def _():
        padded[:, far:, :] = zeros


def first_level_kernel(
    column, rows, starts_ref, side_ref, sent_first_ref, sent_second_ref, first_ref, second_ref,
    weights_ref, out_ref, padded,
):
    sectors, stacked, window = weights_ref.shape
    beams = stacked // 2
    margin = first_ref.shape[1]
    columns = slice(column, column + out_ref.shape[2])
    even = side_ref[0]
    tail = pl.multiple_of(margin + even * (rows - margin), BLK)
    head = pl.multiple_of(margin + (1 - even) * (rows - margin), BLK)
    padded[:, pl.ds(tail, margin), :] = sent_first_ref[:, :, columns]
    padded[:, pl.ds(head, margin), :] = sent_second_ref[:, :, columns]
    place_halos(padded, side_ref, rows, first_ref[:, :, columns], second_ref[:, :, columns])
    for sector in range(sectors):
        place = pl.ds(pl.multiple_of(starts_ref[sector] * BLK, BLK), window)
        parts = complex_window(weights_ref[sector], padded[0, place, :], padded[1, place, :])
        for part in range(2):
            out_ref[part, sector * beams : (sector + 1) * beams, :] = parts[part]


def first_level(column, rows, starts, side, sent, halos, weights):
    sectors, stacked, window = weights.shape
    margin, rng = sent[0].shape[1:]
    assert 2 * margin >= rows
    width = rng // 2
    return pl.pallas_call(
        functools.partial(first_level_kernel, column, rows),
        out_shape=jax.ShapeDtypeStruct((2, sectors * stacked // 2, width), jnp.bfloat16),
        in_specs=[SMEM, SMEM] + [VMEM] * 5,
        out_specs=VMEM,
        scratch_shapes=[pltpu.VMEM((2, rows + 2 * margin, width), jnp.bfloat16)],
        compiler_params=params(),
        cost_estimate=cost(sectors * 2 * stacked * window * width, 2**21),
        name="first_level",
    )(starts, side, *sent, *halos, weights)


def second_level_early_kernel(
    starts_ref, side_ref, sector_ref, own_ref, first_ref, second_ref, weights_ref, send_ref, padded
):
    _, stacked, window = weights_ref.shape
    per = stacked // 2 // OS
    margin, rows = first_ref.shape[1], own_ref.shape[1]
    columns = slice(send_ref.shape[3], 2 * send_ref.shape[3])
    padded[:, margin : margin + rows, :] = own_ref[:, :, columns]
    place_halos(padded, side_ref, rows, first_ref[:, :, columns], second_ref[:, :, columns])
    for place in range(send_ref.shape[0]):
        sector = sector_ref[place] // per
        piece = pl.multiple_of(sector_ref[place] % per * OS, OS)
        window_rows = pl.ds(pl.multiple_of(starts_ref[sector] * BLK, BLK), window)
        weights = jnp.concatenate(
            [
                weights_ref[sector, pl.ds(piece, OS), :],
                weights_ref[sector, pl.ds(pl.multiple_of(piece + stacked // 2, OS), OS), :],
            ]
        )
        parts = complex_window(weights, padded[0, window_rows, :], padded[1, window_rows, :])
        for part in range(2):
            send_ref[place, part] = parts[part]


def second_level_kernel(
    starts_ref, side_ref, own_at_ref, other_at_ref, own_ref, first_ref, second_ref, weights_ref,
    keep_ref, send_ref, padded, send,
):
    sectors, stacked, window = weights_ref.shape
    beams = stacked // 2
    width = keep_ref.shape[3]
    margin, rows = first_ref.shape[1], own_ref.shape[1]
    padded[:, margin : margin + rows, :] = own_ref[...]
    place_halos(padded, side_ref, rows, first_ref[...], second_ref[...])
    per = beams // OS
    for sector in range(sectors):
        place = pl.ds(pl.multiple_of(starts_ref[sector] * BLK, BLK), window)
        parts = complex_window(weights_ref[sector], padded[0, place, :], padded[1, place, :])
        for piece in range(per):
            own_at = own_at_ref[sector * per + piece]
            other_at = other_at_ref[sector * per + piece]
            taken = slice(piece * OS, (piece + 1) * OS)
            for part in range(2):
                keep_ref[own_at, part] = parts[part][taken, :width]
                send[other_at, part] = parts[part][taken, width:]
    send_ref[...] = send[send.shape[0] - send_ref.shape[0] :]


def second_level(starts, side, planned, own, halos, weights, early):
    sectors, stacked, window = weights.shape
    margin, rows, rng = halos[0].shape[1], own.shape[1], own.shape[2]
    count = sectors * stacked // 2 // OS
    block = (2, OS, rng // 2)
    own_at, other_at, other_sector = planned
    early_send = pl.pallas_call(
        second_level_early_kernel,
        out_shape=jax.ShapeDtypeStruct((early,) + block, jnp.bfloat16),
        in_specs=[SMEM] * 3 + [VMEM] * 4,
        out_specs=VMEM,
        scratch_shapes=[pltpu.VMEM((2, rows + 2 * margin, rng // 2), jnp.bfloat16)],
        compiler_params=params(),
        cost_estimate=cost(early * 2 * 2 * OS * window * rng // 2, 2**20),
        name="second_level_early",
    )(starts, side, other_sector, own, *halos, weights)
    shapes = [jax.ShapeDtypeStruct((n,) + block, jnp.bfloat16) for n in (count, count - early)]
    keep, late_send = pl.pallas_call(
        second_level_kernel,
        out_shape=shapes,
        in_specs=[SMEM] * 4 + [VMEM] * 4,
        out_specs=[VMEM] * 2,
        scratch_shapes=[
            pltpu.VMEM((2, rows + 2 * margin, rng), jnp.bfloat16),
            pltpu.VMEM((count,) + block, jnp.bfloat16),
        ],
        compiler_params=params(),
        cost_estimate=cost(sectors * 2 * stacked * window * rng, 2**22),
        name="second_level",
    )(starts, side, own_at, other_at, own, *halos, weights)
    return keep, early_send, late_send


def plan_kernel(
    shift, me_ref, own_ref, other_ref, own_at_ref, other_at_ref, other_sector_ref, target_ref, rank_ref,
    taken, filled,
):
    count = own_ref.shape[0]
    far_bit = taken.shape[0] // 2

    def delay(target):
        distance = target ^ me_ref[0]
        return jnp.where((distance & far_bit) == 0, 2 * count, (distance & 1) * shift)

    for owners_ref, at_ref in ((other_ref, other_at_ref), (own_ref, own_at_ref)):
        for target in range(taken.shape[0]):
            taken[target] = 0
        for bucket in range(filled.shape[0]):
            filled[bucket] = 0
        for sector in range(count):
            target = owners_ref[sector]
            rank = taken[target]
            taken[target] = rank + 1
            bucket = rank + delay(target)
            at_ref[sector] = bucket
            filled[bucket + 1] = filled[bucket + 1] + 1
        for bucket in range(1, filled.shape[0]):
            filled[bucket] = filled[bucket] + filled[bucket - 1]
        for sector in range(count):
            bucket = at_ref[sector]
            place = filled[bucket]
            filled[bucket] = place + 1
            at_ref[sector] = place
            if at_ref is own_at_ref:
                target_ref[place] = owners_ref[sector]
                rank_ref[place] = bucket - delay(owners_ref[sector])
            else:
                other_sector_ref[place] = sector


def plan(shift, me, own, other, beam_count):
    count = own.shape[0]
    shape = jax.ShapeDtypeStruct((count,), jnp.int32)
    return pl.pallas_call(
        functools.partial(plan_kernel, shift),
        out_shape=[shape] * 5,
        in_specs=[SMEM] * 3,
        out_specs=[SMEM] * 5,
        scratch_shapes=[
            pltpu.SMEM((beam_count,), jnp.int32),
            pltpu.SMEM((3 * count + 1,), jnp.int32),
        ],
        compiler_params=params(),
        name="plan",
    )(me, own, other)


def wires_kernel(spans, early, me_ref, target_ref, rank_ref, keep_ref, *refs):
    wires = refs[-1]
    spare = wires.shape[0] - 1
    out_refs = refs[-1 - len(spans) : -1]
    other_ref, *summed_refs = refs[: -1 - len(spans)]
    wires[...] = jnp.zeros_like(wires)
    me = me_ref[0]

    def lay(place, total):
        rank = rank_ref[place]
        distance = target_ref[place] ^ me
        at = spare
        start = 0
        for number, low, high in spans:
            wanted = (distance == number) & (rank >= low) & (rank < high)
            at = jnp.where(wanted, start + rank - low, at)
            start += high - low
        wires[at] = total

    before = 0
    if not early:
        before = summed_refs[0].shape[0]
        for row in range(before):
            lay(row, summed_refs[0][row])
    for row in range(other_ref.shape[0]):
        place = before + row
        total = keep_ref[place].astype(jnp.float32) + other_ref[row].astype(jnp.float32)
        total = total.astype(jnp.bfloat16)
        lay(place, total)
        if early:
            summed_refs[0][row] = total
    start = 0
    for (_, low, high), ref in zip(spans, out_refs):
        ref[...] = wires[start : start + high - low]
        start += high - low


def wires(spans, me, target, rank, keep, other, summed=None):
    block = keep.shape[1:]
    sizes = [high - low for _, low, high in spans]
    inputs = [me, target, rank, keep, other]
    if summed is None:
        sizes = [other.shape[0]] + sizes
    else:
        inputs.append(summed)
    shapes = [jax.ShapeDtypeStruct((size,) + block, jnp.bfloat16) for size in sizes]
    total = sum(high - low for _, low, high in spans)
    return pl.pallas_call(
        functools.partial(wires_kernel, spans, summed is None),
        out_shape=shapes,
        in_specs=[SMEM] * 3 + [VMEM] * (len(inputs) - 3),
        out_specs=[VMEM] * len(shapes),
        scratch_shapes=[pltpu.VMEM((total + 1,) + block, jnp.bfloat16)],
        compiler_params=params(),
        cost_estimate=cost(0, 2**21),
        name="early_wires" if summed is None else "late_wires",
    )(*inputs)


def collect_kernel(spans, capacity, me_ref, *refs):
    sems = refs[-1]
    out_ref = refs[-2]
    copies = []
    for number, (distance, low, high) in enumerate(spans):
        start = (me_ref[0] ^ distance) * capacity + low
        copies.append(
            pltpu.make_async_copy(
                refs[number], out_ref.at[pl.ds(start, high - low)], sems.at[number]
            )
        )
    for copy in copies:
        copy.start()
    for copy in copies:
        copy.wait()


def collect(spans, capacity, beam_count, me, received):
    shape = (beam_count * capacity,) + received[0].shape[1:]
    return pl.pallas_call(
        functools.partial(collect_kernel, spans, capacity),
        out_shape=jax.ShapeDtypeStruct(shape, jnp.bfloat16),
        in_specs=[SMEM] + [ANY] * len(received),
        out_specs=ANY,
        scratch_shapes=[pltpu.SemaphoreType.DMA((len(received),))],
        compiler_params=params(),
        cost_estimate=cost(0, 2**21),
        name="collect",
    )(me, *received)


def spread(spans, group):
    count = lax.axis_size("beam")
    received = []
    for (distance, _, _), wire in zip(spans, group):
        route = [(place, place ^ distance) for place in range(count)]
        received.append(lax.ppermute(wire, "beam", route) if distance else wire)
    return received


def stacked_weights(weights):
    return weights[0].reshape(weights.shape[1], -1, weights.shape[4])


def table_row(table, row_number):
    return lax.dynamic_index_in_dim(table, row_number, 0, keepdims=False)


def local(subimages, range_kernel, weights0, starts0, weights1, starts1, owners):
    aper_index = lax.axis_index("aperture")
    beam_index = lax.axis_index("beam")
    beam_count = lax.axis_size("beam")
    margin = MARGIN_BLOCKS * BLK
    rows = subimages.shape[2]
    local_blocks = rows // BLK
    even = (beam_index + 1) % 2
    ends = (beam_index == 0, beam_index == beam_count - 1)
    side = jnp.stack([even] + [end.astype(jnp.int32) for end in ends])
    me = beam_index.reshape(1)

    sector_count = owners.shape[1]
    capacity = max(2, 2 * sector_count // beam_count)
    shorter, longer = max(1, capacity // 4), max(1, capacity // 2)
    far = range(beam_count // 2, beam_count)
    odd = [distance for distance in far if distance % 2]
    others = [distance for distance in far if distance % 2 == 0]
    early = len(odd) * shorter + len(others) * longer
    early_spans = [(distance, 0, shorter) for distance in odd]
    early_spans += [(distance, 0, longer) for distance in others]
    late_spans = [(distance, shorter, capacity) for distance in odd]
    for distance in range(1, beam_count // 2):
        cut = (5 * capacity + 4) // 8
        late_spans += [(distance, 0, cut), (distance, cut, capacity)]
    late_spans.append((0, 0, capacity))
    last_spans = [(distance, longer, capacity) for distance in others]

    sent = resample(subimages[0], range_kernel[0], margin)
    halos = trade_edges(*sent)
    own_owners = owners[0, :, 0]
    other_owners = partner(owners, "aperture", 1)[0, :, 0]
    planned = plan(longer - shorter, me, own_owners, other_owners, beam_count)
    begin0 = table_row(starts0, aper_index) - (beam_index * local_blocks - MARGIN_BLOCKS)
    halos, planned = lax.optimization_barrier((halos, planned))
    *planned, target, rank = planned
    width = range_kernel.shape[3] // 2
    weights = stacked_weights(weights0)
    send = first_level(width, rows, begin0, side, sent, halos, weights)
    other = partner(send, "aperture", 0)
    keep = first_level(0, rows, begin0, side, sent, halos, weights)
    level_one = (keep.astype(jnp.float32) + other.astype(jnp.float32)).astype(jnp.bfloat16)

    beams = level_one.shape[1]
    first = lax.dynamic_slice_in_dim(level_one, even * (beams - margin), margin, 1)
    second = lax.dynamic_slice_in_dim(level_one, (1 - even) * (beams - margin), margin, 1)
    halos = trade_edges(first, second)
    begin1 = table_row(starts1, aper_index) - (beam_index * 2 * local_blocks - MARGIN_BLOCKS)
    keep, send, late = second_level(
        begin1, side, planned, level_one, halos, stacked_weights(weights1), early
    )
    other = partner(send, "aperture", 1)
    other, late = lax.optimization_barrier((other, late))
    late = partner(late, "aperture", 1)
    summed, *group = wires(early_spans, me, target, rank, keep, other)
    received = spread(early_spans, group)
    from_odd, from_others = received[: len(odd)], received[len(odd) :]
    ready, from_odd = lax.optimization_barrier((late, from_odd))
    group = wires(late_spans, me, target, rank, keep, ready, summed)
    received = from_odd + spread(late_spans, group)
    ready, from_others = lax.optimization_barrier((late, from_others))
    group = wires(last_spans, me, target, rank, keep, ready, summed)
    received += from_others + spread(last_spans, group)
    spans = early_spans[: len(odd)] + late_spans + early_spans[len(odd) :] + last_spans
    return collect(spans, capacity, beam_count, me, received)[None]


def solution(mesh):
    return jax.shard_map(
        local,
        mesh=mesh,
        in_specs=(
            P("aperture", None, "beam", None),
            P("aperture", None, None, None),
            P("aperture", "beam", None, None, None),
            P(None, "beam"),
            P("aperture", "beam", None, None, None),
            P(None, "beam"),
            P("aperture", "beam", None),
        ),
        out_specs=P("aperture", "beam", None, None, None),
        check_vma=False,
    )
```

```python
import functools

import jax
import jax.numpy as jnp
from jax import lax
from jax.experimental import pallas as pl
from jax.experimental.pallas import tpu as pltpu
from jax.sharding import PartitionSpec as P

BLK = 32
NW = 10
REACH = 2
OS = 64
MARGIN_BLOCKS = (NW - 2) // 2 + REACH
VMEM_LIMIT = 8 * 1024 * 1024
MOST_VMEM = 53 * 1024 * 1024
ANY = pl.BlockSpec(memory_space=pl.ANY)
VMEM = pl.BlockSpec(memory_space=pltpu.VMEM)
SMEM = pl.BlockSpec(memory_space=pltpu.SMEM)


def params(limit=VMEM_LIMIT):
    return pltpu.CompilerParams(vmem_limit_bytes=limit)


def cost(macs, moved):
    return pl.CostEstimate(flops=2 * macs, bytes_accessed=moved, transcendentals=0)


def trade_edges(first, second):
    count, apertures = lax.axis_size("beam"), lax.axis_size("aperture")
    received = []
    for order, block in enumerate((first, second)):
        route = []
        for aper in range(apertures):
            for place in range(count):
                other = place + 1 if (place - order) % 2 == 0 else place - 1
                if 0 <= other < count:
                    to = aper * count + other
                else:
                    to = min(aper ^ 1, apertures - 1) * count + place
                route.append((aper * count + place, to))
        received.append(lax.ppermute(block, ("aperture", "beam"), route))
    return received


def partner(block, axis, distance):
    count = lax.axis_size(axis)
    route = []
    for low in range(count):
        high = low | 1 << distance
        if high != low and high < count:
            route += [(low, high), (high, low)]
    return lax.ppermute(block, axis, route)


def gathered_partner(block, axis, distance):
    bit = 1 << distance
    count = lax.axis_size(axis)
    pairs = [[low, low | bit] for low in range(count) if not low & bit]
    both = lax.all_gather(block, axis, axis_index_groups=pairs)
    return table_row(both, 1 - (lax.axis_index(axis) >> distance) % 2)


def dot(left, right):
    return jnp.dot(left, right, preferred_element_type=jnp.float32)


def resample_kernel(child_hbm, kernel_hbm, first_ref, second_ref, child, kernel, own, sems):
    aper, beam = lax.axis_index("aperture"), lax.axis_index("beam")
    half, quarter = aper & 1, (aper >> 1) & 1
    even = 1 - (beam & 1)
    rows, rng = child.shape[1:]
    piece = rng // 4
    child_copy = pltpu.make_async_copy(child_hbm, child, sems.at[4])
    copies = []
    for place in range(4):
        source = (half ^ (place // 2)) * 2 + (quarter ^ (place % 2))
        copies.append(
            pltpu.make_async_copy(
                kernel_hbm.at[:, :, pl.ds(pl.multiple_of(source * piece, 128), piece)],
                kernel.at[:, :, place * piece : (place + 1) * piece],
                sems.at[place],
            )
        )
    child_copy.start()
    for copy in copies:
        copy.start()
    child_copy.wait()
    real, imag = child[0], child[1]
    margin = first_ref.shape[1]
    tail = pl.ds(pl.multiple_of(even * (rows - margin), BLK), margin)
    head = pl.ds(pl.multiple_of((1 - even) * (rows - margin), BLK), margin)
    for side in range(2):
        columns = slice(side * 2 * piece, (side + 1) * 2 * piece)
        copies[2 * side].wait()
        copies[2 * side + 1].wait()
        k_real, k_imag = kernel[0, :, columns], kernel[1, :, columns]
        own[0, :, columns] = (dot(real, k_real) - dot(imag, k_imag)).astype(jnp.bfloat16)
        own[1, :, columns] = (dot(real, k_imag) + dot(imag, k_real)).astype(jnp.bfloat16)
        for part in range(2):
            first_ref[part, :, columns] = own[part, tail, columns]
            second_ref[part, :, columns] = own[part, head, columns]


def resample(child, kernel, margin):
    rows, rng = child.shape[1:]
    shape = jax.ShapeDtypeStruct((2, margin, rng), jnp.bfloat16)
    return pl.pallas_call(
        resample_kernel,
        out_shape=(shape, shape),
        in_specs=[ANY, ANY],
        out_specs=(VMEM, VMEM),
        scratch_shapes=[
            pltpu.VMEM(child.shape, jnp.bfloat16),
            pltpu.VMEM(kernel.shape, jnp.bfloat16),
            pltpu.VMEM(child.shape, jnp.bfloat16),
            pltpu.SemaphoreType.DMA((5,)),
        ],
        compiler_params=params(MOST_VMEM),
        cost_estimate=cost(4 * rows * rng * rng, 2**21),
        name="resample",
    )(child, kernel)


def complex_window(weights, real, imag):
    beams = weights.shape[0] // 2
    with_real = dot(weights, real)
    with_imag = dot(weights, imag)
    return (
        (with_real[:beams] - with_imag[beams:]).astype(jnp.bfloat16),
        (with_imag[:beams] + with_real[beams:]).astype(jnp.bfloat16),
    )


def place_halos(padded, side_ref, rows, first, second):
    even, lowest, highest = side_ref[0], side_ref[1], side_ref[2]
    margin = first.shape[1]
    far = margin + rows
    padded[:, pl.ds(pl.multiple_of(even * far, BLK), margin), :] = first
    padded[:, pl.ds(pl.multiple_of((1 - even) * far, BLK), margin), :] = second
    zeros = jnp.zeros_like(first)

    @pl.when(lowest == 1)
    def _():
        padded[:, :margin, :] = zeros

    @pl.when(highest == 1)
    def _():
        padded[:, far:, :] = zeros


def first_level_kernel(
    column, rows, starts_ref, side_ref, sent_first_ref, sent_second_ref, first_ref, second_ref,
    weights_ref, out_ref, padded,
):
    sectors, stacked, window = weights_ref.shape
    beams = stacked // 2
    margin = first_ref.shape[1]
    columns = slice(column, column + out_ref.shape[2])
    even = side_ref[0]
    tail = pl.multiple_of(margin + even * (rows - margin), BLK)
    head = pl.multiple_of(margin + (1 - even) * (rows - margin), BLK)
    padded[:, pl.ds(tail, margin), :] = sent_first_ref[:, :, columns]
    padded[:, pl.ds(head, margin), :] = sent_second_ref[:, :, columns]
    place_halos(padded, side_ref, rows, first_ref[:, :, columns], second_ref[:, :, columns])
    for sector in range(sectors):
        place = pl.ds(pl.multiple_of(starts_ref[sector] * BLK, BLK), window)
        parts = complex_window(weights_ref[sector], padded[0, place, :], padded[1, place, :])
        for part in range(2):
            out_ref[part, sector * beams : (sector + 1) * beams, :] = parts[part]


def first_level(column, rows, starts, side, sent, halos, weights):
    sectors, stacked, window = weights.shape
    margin, rng = sent[0].shape[1:]
    assert 2 * margin >= rows
    width = rng // 2
    return pl.pallas_call(
        functools.partial(first_level_kernel, column, rows),
        out_shape=jax.ShapeDtypeStruct((2, sectors * stacked // 2, width), jnp.bfloat16),
        in_specs=[SMEM, SMEM] + [VMEM] * 5,
        out_specs=VMEM,
        scratch_shapes=[pltpu.VMEM((2, rows + 2 * margin, width), jnp.bfloat16)],
        compiler_params=params(),
        cost_estimate=cost(sectors * 2 * stacked * window * width, 2**21),
        name="first_level",
    )(starts, side, *sent, *halos, weights)


def second_level_early_kernel(
    starts_ref, side_ref, sector_ref, own_ref, first_ref, second_ref, weights_ref, send_ref, padded
):
    _, stacked, window = weights_ref.shape
    per = stacked // 2 // OS
    margin, rows = first_ref.shape[1], own_ref.shape[1]
    columns = slice(send_ref.shape[3], 2 * send_ref.shape[3])
    padded[:, margin : margin + rows, :] = own_ref[:, :, columns]
    place_halos(padded, side_ref, rows, first_ref[:, :, columns], second_ref[:, :, columns])
    for place in range(send_ref.shape[0]):
        sector = sector_ref[place] // per
        piece = pl.multiple_of(sector_ref[place] % per * OS, OS)
        window_rows = pl.ds(pl.multiple_of(starts_ref[sector] * BLK, BLK), window)
        weights = jnp.concatenate(
            [
                weights_ref[sector, pl.ds(piece, OS), :],
                weights_ref[sector, pl.ds(pl.multiple_of(piece + stacked // 2, OS), OS), :],
            ]
        )
        parts = complex_window(weights, padded[0, window_rows, :], padded[1, window_rows, :])
        for part in range(2):
            send_ref[place, part] = parts[part]


def second_level_kernel(
    starts_ref, side_ref, own_at_ref, other_at_ref, own_ref, first_ref, second_ref, weights_ref,
    keep_ref, send_ref, padded, send,
):
    sectors, stacked, window = weights_ref.shape
    beams = stacked // 2
    width = keep_ref.shape[3]
    margin, rows = first_ref.shape[1], own_ref.shape[1]
    padded[:, margin : margin + rows, :] = own_ref[...]
    place_halos(padded, side_ref, rows, first_ref[...], second_ref[...])
    per = beams // OS
    for sector in range(sectors):
        place = pl.ds(pl.multiple_of(starts_ref[sector] * BLK, BLK), window)
        parts = complex_window(weights_ref[sector], padded[0, place, :], padded[1, place, :])
        for piece in range(per):
            own_at = own_at_ref[sector * per + piece]
            other_at = other_at_ref[sector * per + piece]
            taken = slice(piece * OS, (piece + 1) * OS)
            for part in range(2):
                keep_ref[own_at, part] = parts[part][taken, :width]
                send[other_at, part] = parts[part][taken, width:]
    send_ref[...] = send[send.shape[0] - send_ref.shape[0] :]


def second_level(starts, side, planned, own, halos, weights, early):
    sectors, stacked, window = weights.shape
    margin, rows, rng = halos[0].shape[1], own.shape[1], own.shape[2]
    count = sectors * stacked // 2 // OS
    block = (2, OS, rng // 2)
    own_at, other_at, other_sector = planned
    early_send = pl.pallas_call(
        second_level_early_kernel,
        out_shape=jax.ShapeDtypeStruct((early,) + block, jnp.bfloat16),
        in_specs=[SMEM] * 3 + [VMEM] * 4,
        out_specs=VMEM,
        scratch_shapes=[pltpu.VMEM((2, rows + 2 * margin, rng // 2), jnp.bfloat16)],
        compiler_params=params(),
        cost_estimate=cost(early * 2 * 2 * OS * window * rng // 2, 2**20),
        name="second_level_early",
    )(starts, side, other_sector, own, *halos, weights)
    shapes = [jax.ShapeDtypeStruct((n,) + block, jnp.bfloat16) for n in (count, count - early)]
    keep, late_send = pl.pallas_call(
        second_level_kernel,
        out_shape=shapes,
        in_specs=[SMEM] * 4 + [VMEM] * 4,
        out_specs=[VMEM] * 2,
        scratch_shapes=[
            pltpu.VMEM((2, rows + 2 * margin, rng), jnp.bfloat16),
            pltpu.VMEM((count,) + block, jnp.bfloat16),
        ],
        compiler_params=params(),
        cost_estimate=cost(sectors * 2 * stacked * window * rng, 2**22),
        name="second_level",
    )(starts, side, own_at, other_at, own, *halos, weights)
    return keep, early_send, late_send


def plan_kernel(
    shift, me_ref, own_ref, other_ref, own_at_ref, other_at_ref, other_sector_ref, target_ref, rank_ref,
    taken, filled,
):
    count = own_ref.shape[0]
    far_bit = taken.shape[0] // 2

    def delay(target):
        distance = target ^ me_ref[0]
        return jnp.where((distance & far_bit) == 0, 2 * count, (distance & 1) * shift)

    for owners_ref, at_ref in ((other_ref, other_at_ref), (own_ref, own_at_ref)):
        for target in range(taken.shape[0]):
            taken[target] = 0
        for bucket in range(filled.shape[0]):
            filled[bucket] = 0
        for sector in range(count):
            target = owners_ref[sector]
            rank = taken[target]
            taken[target] = rank + 1
            bucket = rank + delay(target)
            at_ref[sector] = bucket
            filled[bucket + 1] = filled[bucket + 1] + 1
        for bucket in range(1, filled.shape[0]):
            filled[bucket] = filled[bucket] + filled[bucket - 1]
        for sector in range(count):
            bucket = at_ref[sector]
            place = filled[bucket]
            filled[bucket] = place + 1
            at_ref[sector] = place
            if at_ref is own_at_ref:
                target_ref[place] = owners_ref[sector]
                rank_ref[place] = bucket - delay(owners_ref[sector])
            else:
                other_sector_ref[place] = sector


def plan(shift, me, own, other, beam_count):
    count = own.shape[0]
    shape = jax.ShapeDtypeStruct((count,), jnp.int32)
    return pl.pallas_call(
        functools.partial(plan_kernel, shift),
        out_shape=[shape] * 5,
        in_specs=[SMEM] * 3,
        out_specs=[SMEM] * 5,
        scratch_shapes=[
            pltpu.SMEM((beam_count,), jnp.int32),
            pltpu.SMEM((3 * count + 1,), jnp.int32),
        ],
        compiler_params=params(),
        name="plan",
    )(me, own, other)


def wires_kernel(spans, early, me_ref, target_ref, rank_ref, keep_ref, *refs):
    wires = refs[-1]
    spare = wires.shape[0] - 1
    out_refs = refs[-1 - len(spans) : -1]
    other_ref, *summed_refs = refs[: -1 - len(spans)]
    wires[...] = jnp.zeros_like(wires)
    me = me_ref[0]

    def lay(place, total):
        rank = rank_ref[place]
        distance = target_ref[place] ^ me
        at = spare
        start = 0
        for number, low, high in spans:
            wanted = (distance == number) & (rank >= low) & (rank < high)
            at = jnp.where(wanted, start + rank - low, at)
            start += high - low
        wires[at] = total

    before = 0
    if not early:
        before = summed_refs[0].shape[0]
        for row in range(before):
            lay(row, summed_refs[0][row])
    for row in range(other_ref.shape[0]):
        place = before + row
        total = keep_ref[place].astype(jnp.float32) + other_ref[row].astype(jnp.float32)
        total = total.astype(jnp.bfloat16)
        lay(place, total)
        if early:
            summed_refs[0][row] = total
    start = 0
    for (_, low, high), ref in zip(spans, out_refs):
        ref[...] = wires[start : start + high - low]
        start += high - low


def wires(spans, me, target, rank, keep, other, summed=None):
    block = keep.shape[1:]
    sizes = [high - low for _, low, high in spans]
    inputs = [me, target, rank, keep, other]
    if summed is None:
        sizes = [other.shape[0]] + sizes
    else:
        inputs.append(summed)
    shapes = [jax.ShapeDtypeStruct((size,) + block, jnp.bfloat16) for size in sizes]
    total = sum(high - low for _, low, high in spans)
    return pl.pallas_call(
        functools.partial(wires_kernel, spans, summed is None),
        out_shape=shapes,
        in_specs=[SMEM] * 3 + [VMEM] * (len(inputs) - 3),
        out_specs=[VMEM] * len(shapes),
        scratch_shapes=[pltpu.VMEM((total + 1,) + block, jnp.bfloat16)],
        compiler_params=params(),
        cost_estimate=cost(0, 2**21),
        name="early_wires" if summed is None else "late_wires",
    )(*inputs)


def collect_kernel(spans, capacity, me_ref, *refs):
    sems = refs[-1]
    out_ref = refs[-2]
    copies = []
    for number, (distance, low, high) in enumerate(spans):
        start = (me_ref[0] ^ distance) * capacity + low
        copies.append(
            pltpu.make_async_copy(
                refs[number], out_ref.at[pl.ds(start, high - low)], sems.at[number]
            )
        )
    for copy in copies:
        copy.start()
    for copy in copies:
        copy.wait()


def collect(spans, capacity, beam_count, me, received):
    shape = (beam_count * capacity,) + received[0].shape[1:]
    return pl.pallas_call(
        functools.partial(collect_kernel, spans, capacity),
        out_shape=jax.ShapeDtypeStruct(shape, jnp.bfloat16),
        in_specs=[SMEM] + [ANY] * len(received),
        out_specs=ANY,
        scratch_shapes=[pltpu.SemaphoreType.DMA((len(received),))],
        compiler_params=params(),
        cost_estimate=cost(0, 2**21),
        name="collect",
    )(me, *received)


def spread(spans, group):
    count = lax.axis_size("beam")
    received = []
    for (distance, _, _), wire in zip(spans, group):
        route = [(place, place ^ distance) for place in range(count)]
        received.append(lax.ppermute(wire, "beam", route) if distance else wire)
    return received


def stacked_weights(weights):
    return weights[0].reshape(weights.shape[1], -1, weights.shape[4])


def table_row(table, row_number):
    return lax.dynamic_index_in_dim(table, row_number, 0, keepdims=False)


def local(subimages, range_kernel, weights0, starts0, weights1, starts1, owners):
    aper_index = lax.axis_index("aperture")
    beam_index = lax.axis_index("beam")
    beam_count = lax.axis_size("beam")
    margin = MARGIN_BLOCKS * BLK
    rows = subimages.shape[2]
    local_blocks = rows // BLK
    even = (beam_index + 1) % 2
    ends = (beam_index == 0, beam_index == beam_count - 1)
    side = jnp.stack([even] + [end.astype(jnp.int32) for end in ends])
    me = beam_index.reshape(1)

    sector_count = owners.shape[1]
    capacity = max(2, 2 * sector_count // beam_count)
    shorter, longer = max(1, capacity // 4), max(1, capacity // 2)
    far = range(beam_count // 2, beam_count)
    odd = [distance for distance in far if distance % 2]
    others = [distance for distance in far if distance % 2 == 0]
    early = len(odd) * shorter + len(others) * longer
    early_spans = [(distance, 0, shorter) for distance in odd]
    early_spans += [(distance, 0, longer) for distance in others]
    late_spans = [(distance, shorter, capacity) for distance in odd]
    for distance in range(1, beam_count // 2):
        cut = (5 * capacity + 4) // 8
        late_spans += [(distance, 0, cut), (distance, cut, capacity)]
    late_spans.append((0, 0, capacity))
    last_spans = [(distance, longer, capacity) for distance in others]

    sent = resample(subimages[0], range_kernel[0], margin)
    halos = trade_edges(*sent)
    own_owners = owners[0, :, 0]
    other_owners = partner(owners, "aperture", 1)[0, :, 0]
    planned = plan(longer - shorter, me, own_owners, other_owners, beam_count)
    begin0 = table_row(starts0, aper_index) - (beam_index * local_blocks - MARGIN_BLOCKS)
    halos, planned = lax.optimization_barrier((halos, planned))
    *planned, target, rank = planned
    width = range_kernel.shape[3] // 2
    weights = stacked_weights(weights0)
    send = first_level(width, rows, begin0, side, sent, halos, weights)
    other = partner(send, "aperture", 0)
    keep = first_level(0, rows, begin0, side, sent, halos, weights)
    level_one = (keep.astype(jnp.float32) + other.astype(jnp.float32)).astype(jnp.bfloat16)

    beams = level_one.shape[1]
    first = lax.dynamic_slice_in_dim(level_one, even * (beams - margin), margin, 1)
    second = lax.dynamic_slice_in_dim(level_one, (1 - even) * (beams - margin), margin, 1)
    halos = trade_edges(first, second)
    begin1 = table_row(starts1, aper_index) - (beam_index * 2 * local_blocks - MARGIN_BLOCKS)
    keep, send, late = second_level(
        begin1, side, planned, level_one, halos, stacked_weights(weights1), early
    )
    other = partner(send, "aperture", 1)
    other, late = lax.optimization_barrier((other, late))
    late = gathered_partner(late, "aperture", 1)
    summed, *group = wires(early_spans, me, target, rank, keep, other)
    received = spread(early_spans, group)
    from_odd, from_others = received[: len(odd)], received[len(odd) :]
    ready, from_odd = lax.optimization_barrier((late, from_odd))
    group = wires(late_spans, me, target, rank, keep, ready, summed)
    received = from_odd + spread(late_spans, group)
    ready, from_others = lax.optimization_barrier((late, from_others))
    group = wires(last_spans, me, target, rank, keep, ready, summed)
    received += from_others + spread(last_spans, group)
    spans = early_spans[: len(odd)] + late_spans + early_spans[len(odd) :] + last_spans
    return collect(spans, capacity, beam_count, me, received)[None]


def solution(mesh):
    return jax.shard_map(
        local,
        mesh=mesh,
        in_specs=(
            P("aperture", None, "beam", None),
            P("aperture", None, None, None),
            P("aperture", "beam", None, None, None),
            P(None, "beam"),
            P("aperture", "beam", None, None, None),
            P(None, "beam"),
            P("aperture", "beam", None),
        ),
        out_specs=P("aperture", "beam", None, None, None),
        check_vma=False,
    )
```

```python
import functools

import jax
import jax.numpy as jnp
from jax import lax
from jax.experimental import pallas as pl
from jax.experimental.pallas import tpu as pltpu
from jax.sharding import PartitionSpec as P

BLK = 32
NW = 10
REACH = 2
OS = 64
MARGIN_BLOCKS = (NW - 2) // 2 + REACH
VMEM_LIMIT = 8 * 1024 * 1024
MOST_VMEM = 53 * 1024 * 1024
ANY = pl.BlockSpec(memory_space=pl.ANY)
VMEM = pl.BlockSpec(memory_space=pltpu.VMEM)
SMEM = pl.BlockSpec(memory_space=pltpu.SMEM)


def params(limit=VMEM_LIMIT):
    return pltpu.CompilerParams(vmem_limit_bytes=limit)


def cost(macs, moved):
    return pl.CostEstimate(flops=2 * macs, bytes_accessed=moved, transcendentals=0)


def trade_edges(first, second):
    count, apertures = lax.axis_size("beam"), lax.axis_size("aperture")
    received = []
    for order, block in enumerate((first, second)):
        route = []
        for aper in range(apertures):
            for place in range(count):
                other = place + 1 if (place - order) % 2 == 0 else place - 1
                if 0 <= other < count:
                    to = aper * count + other
                else:
                    to = min(aper ^ 1, apertures - 1) * count + place
                route.append((aper * count + place, to))
        received.append(lax.ppermute(block, ("aperture", "beam"), route))
    return received


def partner(block, axis, distance):
    count = lax.axis_size(axis)
    route = []
    for low in range(count):
        high = low | 1 << distance
        if high != low and high < count:
            route += [(low, high), (high, low)]
    return lax.ppermute(block, axis, route)


def dot(left, right):
    return jnp.dot(left, right, preferred_element_type=jnp.float32)


def resample_kernel(child_hbm, kernel_hbm, first_ref, second_ref, child, kernel, own, sems):
    aper, beam = lax.axis_index("aperture"), lax.axis_index("beam")
    half, quarter = aper & 1, (aper >> 1) & 1
    even = 1 - (beam & 1)
    rows, rng = child.shape[1:]
    piece = rng // 4
    child_copy = pltpu.make_async_copy(child_hbm, child, sems.at[4])
    copies = []
    for place in range(4):
        source = (half ^ (place // 2)) * 2 + (quarter ^ (place % 2))
        copies.append(
            pltpu.make_async_copy(
                kernel_hbm.at[:, :, pl.ds(pl.multiple_of(source * piece, 128), piece)],
                kernel.at[:, :, place * piece : (place + 1) * piece],
                sems.at[place],
            )
        )
    child_copy.start()
    for copy in copies:
        copy.start()
    child_copy.wait()
    real, imag = child[0], child[1]
    margin = first_ref.shape[1]
    tail = pl.ds(pl.multiple_of(even * (rows - margin), BLK), margin)
    head = pl.ds(pl.multiple_of((1 - even) * (rows - margin), BLK), margin)
    for side in range(2):
        columns = slice(side * 2 * piece, (side + 1) * 2 * piece)
        copies[2 * side].wait()
        copies[2 * side + 1].wait()
        k_real, k_imag = kernel[0, :, columns], kernel[1, :, columns]
        own[0, :, columns] = (dot(real, k_real) - dot(imag, k_imag)).astype(jnp.bfloat16)
        own[1, :, columns] = (dot(real, k_imag) + dot(imag, k_real)).astype(jnp.bfloat16)
        for part in range(2):
            first_ref[part, :, columns] = own[part, tail, columns]
            second_ref[part, :, columns] = own[part, head, columns]


def resample(child, kernel, margin):
    rows, rng = child.shape[1:]
    shape = jax.ShapeDtypeStruct((2, margin, rng), jnp.bfloat16)
    return pl.pallas_call(
        resample_kernel,
        out_shape=(shape, shape),
        in_specs=[ANY, ANY],
        out_specs=(VMEM, VMEM),
        scratch_shapes=[
            pltpu.VMEM(child.shape, jnp.bfloat16),
            pltpu.VMEM(kernel.shape, jnp.bfloat16),
            pltpu.VMEM(child.shape, jnp.bfloat16),
            pltpu.SemaphoreType.DMA((5,)),
        ],
        compiler_params=params(MOST_VMEM),
        cost_estimate=cost(4 * rows * rng * rng, 2**21),
        name="resample",
    )(child, kernel)


def complex_window(weights, real, imag):
    beams = weights.shape[0] // 2
    with_real = dot(weights, real)
    with_imag = dot(weights, imag)
    return (
        (with_real[:beams] - with_imag[beams:]).astype(jnp.bfloat16),
        (with_imag[:beams] + with_real[beams:]).astype(jnp.bfloat16),
    )


def place_halos(padded, side_ref, rows, first, second):
    even, lowest, highest = side_ref[0], side_ref[1], side_ref[2]
    margin = first.shape[1]
    far = margin + rows
    padded[:, pl.ds(pl.multiple_of(even * far, BLK), margin), :] = first
    padded[:, pl.ds(pl.multiple_of((1 - even) * far, BLK), margin), :] = second
    zeros = jnp.zeros_like(first)

    @pl.when(lowest == 1)
    def _():
        padded[:, :margin, :] = zeros

    @pl.when(highest == 1)
    def _():
        padded[:, far:, :] = zeros


def first_level_kernel(
    column, rows, starts_ref, side_ref, sent_first_ref, sent_second_ref, first_ref, second_ref,
    weights_ref, out_ref, padded,
):
    sectors, stacked, window = weights_ref.shape
    beams = stacked // 2
    margin = first_ref.shape[1]
    columns = slice(column, column + out_ref.shape[2])
    even = side_ref[0]
    tail = pl.multiple_of(margin + even * (rows - margin), BLK)
    head = pl.multiple_of(margin + (1 - even) * (rows - margin), BLK)
    padded[:, pl.ds(tail, margin), :] = sent_first_ref[:, :, columns]
    padded[:, pl.ds(head, margin), :] = sent_second_ref[:, :, columns]
    place_halos(padded, side_ref, rows, first_ref[:, :, columns], second_ref[:, :, columns])
    for sector in range(sectors):
        place = pl.ds(pl.multiple_of(starts_ref[sector] * BLK, BLK), window)
        parts = complex_window(weights_ref[sector], padded[0, place, :], padded[1, place, :])
        for part in range(2):
            out_ref[part, sector * beams : (sector + 1) * beams, :] = parts[part]


def first_level(column, rows, starts, side, sent, halos, weights):
    sectors, stacked, window = weights.shape
    margin, rng = sent[0].shape[1:]
    assert 2 * margin >= rows
    width = rng // 2
    return pl.pallas_call(
        functools.partial(first_level_kernel, column, rows),
        out_shape=jax.ShapeDtypeStruct((2, sectors * stacked // 2, width), jnp.bfloat16),
        in_specs=[SMEM, SMEM] + [VMEM] * 5,
        out_specs=VMEM,
        scratch_shapes=[pltpu.VMEM((2, rows + 2 * margin, width), jnp.bfloat16)],
        compiler_params=params(),
        cost_estimate=cost(sectors * 2 * stacked * window * width, 2**21),
        name="first_level",
    )(starts, side, *sent, *halos, weights)


def second_level_early_kernel(
    starts_ref, side_ref, sector_ref, own_ref, first_ref, second_ref, weights_ref, send_ref, padded
):
    _, stacked, window = weights_ref.shape
    per = stacked // 2 // OS
    margin, rows = first_ref.shape[1], own_ref.shape[1]
    columns = slice(send_ref.shape[3], 2 * send_ref.shape[3])
    padded[:, margin : margin + rows, :] = own_ref[:, :, columns]
    place_halos(padded, side_ref, rows, first_ref[:, :, columns], second_ref[:, :, columns])
    for place in range(send_ref.shape[0]):
        sector = sector_ref[place] // per
        piece = pl.multiple_of(sector_ref[place] % per * OS, OS)
        window_rows = pl.ds(pl.multiple_of(starts_ref[sector] * BLK, BLK), window)
        weights = jnp.concatenate(
            [
                weights_ref[sector, pl.ds(piece, OS), :],
                weights_ref[sector, pl.ds(pl.multiple_of(piece + stacked // 2, OS), OS), :],
            ]
        )
        parts = complex_window(weights, padded[0, window_rows, :], padded[1, window_rows, :])
        for part in range(2):
            send_ref[place, part] = parts[part]


def second_level_kernel(
    starts_ref, side_ref, own_at_ref, other_at_ref, own_ref, first_ref, second_ref, weights_ref,
    keep_ref, send_ref, padded, send,
):
    sectors, stacked, window = weights_ref.shape
    beams = stacked // 2
    width = keep_ref.shape[3]
    margin, rows = first_ref.shape[1], own_ref.shape[1]
    padded[:, margin : margin + rows, :] = own_ref[...]
    place_halos(padded, side_ref, rows, first_ref[...], second_ref[...])
    per = beams // OS
    for sector in range(sectors):
        place = pl.ds(pl.multiple_of(starts_ref[sector] * BLK, BLK), window)
        parts = complex_window(weights_ref[sector], padded[0, place, :], padded[1, place, :])
        for piece in range(per):
            own_at = own_at_ref[sector * per + piece]
            other_at = other_at_ref[sector * per + piece]
            taken = slice(piece * OS, (piece + 1) * OS)
            for part in range(2):
                keep_ref[own_at, part] = parts[part][taken, :width]
                send[other_at, part] = parts[part][taken, width:]
    send_ref[...] = send[send.shape[0] - send_ref.shape[0] :]


def second_level(starts, side, planned, own, halos, weights, early):
    sectors, stacked, window = weights.shape
    margin, rows, rng = halos[0].shape[1], own.shape[1], own.shape[2]
    count = sectors * stacked // 2 // OS
    block = (2, OS, rng // 2)
    own_at, other_at, other_sector = planned
    early_send = pl.pallas_call(
        second_level_early_kernel,
        out_shape=jax.ShapeDtypeStruct((early,) + block, jnp.bfloat16),
        in_specs=[SMEM] * 3 + [VMEM] * 4,
        out_specs=VMEM,
        scratch_shapes=[pltpu.VMEM((2, rows + 2 * margin, rng // 2), jnp.bfloat16)],
        compiler_params=params(),
        cost_estimate=cost(early * 2 * 2 * OS * window * rng // 2, 2**20),
        name="second_level_early",
    )(starts, side, other_sector, own, *halos, weights)
    shapes = [jax.ShapeDtypeStruct((n,) + block, jnp.bfloat16) for n in (count, count - early)]
    keep, late_send = pl.pallas_call(
        second_level_kernel,
        out_shape=shapes,
        in_specs=[SMEM] * 4 + [VMEM] * 4,
        out_specs=[VMEM] * 2,
        scratch_shapes=[
            pltpu.VMEM((2, rows + 2 * margin, rng), jnp.bfloat16),
            pltpu.VMEM((count,) + block, jnp.bfloat16),
        ],
        compiler_params=params(),
        cost_estimate=cost(sectors * 2 * stacked * window * rng, 2**22),
        name="second_level",
    )(starts, side, own_at, other_at, own, *halos, weights)
    return keep, early_send, late_send


def plan_kernel(
    shift, me_ref, own_ref, other_ref, own_at_ref, other_at_ref, other_sector_ref, target_ref, rank_ref,
    taken, filled,
):
    count = own_ref.shape[0]
    far_bit = taken.shape[0] // 2

    def delay(target):
        distance = target ^ me_ref[0]
        return jnp.where((distance & far_bit) == 0, 2 * count, (distance & 1) * shift)

    for owners_ref, at_ref in ((other_ref, other_at_ref), (own_ref, own_at_ref)):
        for target in range(taken.shape[0]):
            taken[target] = 0
        for bucket in range(filled.shape[0]):
            filled[bucket] = 0
        for sector in range(count):
            target = owners_ref[sector]
            rank = taken[target]
            taken[target] = rank + 1
            bucket = rank + delay(target)
            at_ref[sector] = bucket
            filled[bucket + 1] = filled[bucket + 1] + 1
        for bucket in range(1, filled.shape[0]):
            filled[bucket] = filled[bucket] + filled[bucket - 1]
        for sector in range(count):
            bucket = at_ref[sector]
            place = filled[bucket]
            filled[bucket] = place + 1
            at_ref[sector] = place
            if at_ref is own_at_ref:
                target_ref[place] = owners_ref[sector]
                rank_ref[place] = bucket - delay(owners_ref[sector])
            else:
                other_sector_ref[place] = sector


def plan(shift, me, own, other, beam_count):
    count = own.shape[0]
    shape = jax.ShapeDtypeStruct((count,), jnp.int32)
    return pl.pallas_call(
        functools.partial(plan_kernel, shift),
        out_shape=[shape] * 5,
        in_specs=[SMEM] * 3,
        out_specs=[SMEM] * 5,
        scratch_shapes=[
            pltpu.SMEM((beam_count,), jnp.int32),
            pltpu.SMEM((3 * count + 1,), jnp.int32),
        ],
        compiler_params=params(),
        name="plan",
    )(me, own, other)


def wires_kernel(spans, early, me_ref, target_ref, rank_ref, keep_ref, *refs):
    wires = refs[-1]
    spare = wires.shape[0] - 1
    out_refs = refs[-1 - len(spans) : -1]
    other_ref, *summed_refs = refs[: -1 - len(spans)]
    wires[...] = jnp.zeros_like(wires)
    me = me_ref[0]

    def lay(place, total):
        rank = rank_ref[place]
        distance = target_ref[place] ^ me
        at = spare
        start = 0
        for number, low, high in spans:
            wanted = (distance == number) & (rank >= low) & (rank < high)
            at = jnp.where(wanted, start + rank - low, at)
            start += high - low
        wires[at] = total

    before = 0
    if not early:
        before = summed_refs[0].shape[0]
        for row in range(before):
            lay(row, summed_refs[0][row])
    for row in range(other_ref.shape[0]):
        place = before + row
        total = keep_ref[place].astype(jnp.float32) + other_ref[row].astype(jnp.float32)
        total = total.astype(jnp.bfloat16)
        lay(place, total)
        if early:
            summed_refs[0][row] = total
    start = 0
    for (_, low, high), ref in zip(spans, out_refs):
        ref[...] = wires[start : start + high - low]
        start += high - low


def wires(spans, me, target, rank, keep, other, summed=None):
    block = keep.shape[1:]
    sizes = [high - low for _, low, high in spans]
    inputs = [me, target, rank, keep, other]
    if summed is None:
        sizes = [other.shape[0]] + sizes
    else:
        inputs.append(summed)
    shapes = [jax.ShapeDtypeStruct((size,) + block, jnp.bfloat16) for size in sizes]
    total = sum(high - low for _, low, high in spans)
    return pl.pallas_call(
        functools.partial(wires_kernel, spans, summed is None),
        out_shape=shapes,
        in_specs=[SMEM] * 3 + [VMEM] * (len(inputs) - 3),
        out_specs=[VMEM] * len(shapes),
        scratch_shapes=[pltpu.VMEM((total + 1,) + block, jnp.bfloat16)],
        compiler_params=params(),
        cost_estimate=cost(0, 2**21),
        name="early_wires" if summed is None else "late_wires",
    )(*inputs)


def collect_kernel(spans, capacity, me_ref, *refs):
    sems = refs[-1]
    out_ref = refs[-2]
    copies = []
    for number, (distance, low, high) in enumerate(spans):
        start = (me_ref[0] ^ distance) * capacity + low
        copies.append(
            pltpu.make_async_copy(
                refs[number], out_ref.at[pl.ds(start, high - low)], sems.at[number]
            )
        )
    for copy in copies:
        copy.start()
    for copy in copies:
        copy.wait()


def collect(spans, capacity, beam_count, me, received):
    shape = (beam_count * capacity,) + received[0].shape[1:]
    return pl.pallas_call(
        functools.partial(collect_kernel, spans, capacity),
        out_shape=jax.ShapeDtypeStruct(shape, jnp.bfloat16),
        in_specs=[SMEM] + [ANY] * len(received),
        out_specs=ANY,
        scratch_shapes=[pltpu.SemaphoreType.DMA((len(received),))],
        compiler_params=params(),
        cost_estimate=cost(0, 2**21),
        name="collect",
    )(me, *received)


def spread(spans, group):
    count = lax.axis_size("beam")
    received = []
    for (distance, _, _), wire in zip(spans, group):
        route = [(place, place ^ distance) for place in range(count)]
        received.append(lax.ppermute(wire, "beam", route) if distance else wire)
    return received


def choose_tail(own_owners, common):
    count, beam = lax.axis_size("beam"), lax.axis_index("beam")
    targets = jnp.arange(count, dtype=jnp.int32)
    sectors = jnp.sum((own_owners[:, None] == targets[None, :]).astype(jnp.int32), axis=0)
    is_far = ((targets ^ beam) & (count // 2)) != 0
    full = jnp.where((sectors > common) & is_far, 1, 0).astype(jnp.int32)
    full = lax.pmax(full, ("aperture", "beam"))
    return jnp.where(jnp.sum(full) > 1, count, jnp.argmax(full).astype(jnp.int32))


def spread_tail(spans, branch, group):
    count, apertures = lax.axis_size("beam"), lax.axis_size("aperture")

    def only(target, wires_out):
        received = []
        for (distance, _, _), wire in zip(spans, wires_out):
            pair = (target, target ^ distance)
            route = []
            for aper in range(apertures):
                for place in range(count):
                    if place in pair:
                        to = aper * count + (place ^ distance)
                    else:
                        to = min(aper ^ 1, apertures - 1) * count + place
                    route.append((aper * count + place, to))
            received.append(lax.ppermute(wire, ("aperture", "beam"), route))
        return received

    branches = [functools.partial(only, target) for target in range(count)]
    branches.append(functools.partial(spread, spans))
    return lax.switch(branch, branches, group)


def stacked_weights(weights):
    return weights[0].reshape(weights.shape[1], -1, weights.shape[4])


def table_row(table, row_number):
    return lax.dynamic_index_in_dim(table, row_number, 0, keepdims=False)


def local(subimages, range_kernel, weights0, starts0, weights1, starts1, owners):
    aper_index = lax.axis_index("aperture")
    beam_index = lax.axis_index("beam")
    beam_count = lax.axis_size("beam")
    margin = MARGIN_BLOCKS * BLK
    rows = subimages.shape[2]
    local_blocks = rows // BLK
    even = (beam_index + 1) % 2
    ends = (beam_index == 0, beam_index == beam_count - 1)
    side = jnp.stack([even] + [end.astype(jnp.int32) for end in ends])
    me = beam_index.reshape(1)

    sector_count = owners.shape[1]
    capacity = max(2, 2 * sector_count // beam_count)
    common = (5 * capacity + 7) // 8
    far = range(beam_count // 2, beam_count)
    early_spans = [(distance, 0, common) for distance in far if distance % 2 == 0]
    late_spans = [(distance, 0, common) for distance in far if distance % 2]
    for distance in range(1, beam_count // 2):
        late_spans += [(distance, 0, capacity // 2), (distance, capacity // 2, capacity)]
    late_spans.append((0, 0, capacity))
    tail_spans = [(distance, common, capacity) for distance in far if common < capacity]
    early = common * len(early_spans)

    sent = resample(subimages[0], range_kernel[0], margin)
    halos = trade_edges(*sent)
    own_owners = owners[0, :, 0]
    other_owners = partner(owners, "aperture", 1)[0, :, 0]
    planned = plan(common, me, own_owners, other_owners, beam_count)
    begin0 = table_row(starts0, aper_index) - (beam_index * local_blocks - MARGIN_BLOCKS)
    branch = choose_tail(own_owners, common) if tail_spans else me
    halos, planned, branch = lax.optimization_barrier((halos, planned, branch))
    *planned, target, rank = planned
    width = range_kernel.shape[3] // 2
    weights = stacked_weights(weights0)
    send = first_level(width, rows, begin0, side, sent, halos, weights)
    other = partner(send, "aperture", 0)
    keep = first_level(0, rows, begin0, side, sent, halos, weights)
    level_one = (keep.astype(jnp.float32) + other.astype(jnp.float32)).astype(jnp.bfloat16)

    beams = level_one.shape[1]
    first = lax.dynamic_slice_in_dim(level_one, even * (beams - margin), margin, 1)
    second = lax.dynamic_slice_in_dim(level_one, (1 - even) * (beams - margin), margin, 1)
    halos = trade_edges(first, second)
    begin1 = table_row(starts1, aper_index) - (beam_index * 2 * local_blocks - MARGIN_BLOCKS)
    keep, send, late = second_level(
        begin1, side, planned, level_one, halos, stacked_weights(weights1), early
    )
    other = partner(send, "aperture", 1)
    other, late = lax.optimization_barrier((other, late))
    late = partner(late, "aperture", 1)
    summed, *group = wires(early_spans, me, target, rank, keep, other)
    received = spread(early_spans, group)
    ready, received = lax.optimization_barrier((late, received))
    group = wires(late_spans + tail_spans, me, target, rank, keep, ready, summed)
    received += spread(late_spans, group[: len(late_spans)])
    if tail_spans:
        received += spread_tail(tail_spans, branch, group[len(late_spans) :])
    spans = early_spans + late_spans + tail_spans
    return collect(spans, capacity, beam_count, me, received)[None]


def solution(mesh):
    return jax.shard_map(
        local,
        mesh=mesh,
        in_specs=(
            P("aperture", None, "beam", None),
            P("aperture", None, None, None),
            P("aperture", "beam", None, None, None),
            P(None, "beam"),
            P("aperture", "beam", None, None, None),
            P(None, "beam"),
            P("aperture", "beam", None),
        ),
        out_specs=P("aperture", "beam", None, None, None),
        check_vma=False,
    )
```

```python
import functools

import jax
import jax.numpy as jnp
from jax import lax
from jax.experimental import pallas as pl
from jax.experimental.pallas import tpu as pltpu
from jax.sharding import PartitionSpec as P

BLK = 32
NW = 10
REACH = 2
OS = 64
MARGIN_BLOCKS = (NW - 2) // 2 + REACH
VMEM_LIMIT = 8 * 1024 * 1024
MOST_VMEM = 53 * 1024 * 1024
ANY = pl.BlockSpec(memory_space=pl.ANY)
VMEM = pl.BlockSpec(memory_space=pltpu.VMEM)
SMEM = pl.BlockSpec(memory_space=pltpu.SMEM)


def params(limit=VMEM_LIMIT):
    return pltpu.CompilerParams(vmem_limit_bytes=limit)


def cost(macs, moved):
    return pl.CostEstimate(flops=2 * macs, bytes_accessed=moved, transcendentals=0)


def trade_edges(first, second):
    count, apertures = lax.axis_size("beam"), lax.axis_size("aperture")
    received = []
    for order, block in enumerate((first, second)):
        route = []
        for aper in range(apertures):
            for place in range(count):
                other = place + 1 if (place - order) % 2 == 0 else place - 1
                if 0 <= other < count:
                    to = aper * count + other
                else:
                    to = min(aper ^ 1, apertures - 1) * count + place
                route.append((aper * count + place, to))
        received.append(lax.ppermute(block, ("aperture", "beam"), route))
    return received


def partner(block, axis, distance):
    count = lax.axis_size(axis)
    route = []
    for low in range(count):
        high = low | 1 << distance
        if high != low and high < count:
            route += [(low, high), (high, low)]
    return lax.ppermute(block, axis, route)


def dot(left, right):
    return jnp.dot(left, right, preferred_element_type=jnp.float32)


def resample_kernel(child_hbm, kernel_hbm, first_ref, second_ref, child, kernel, own, sems):
    aper, beam = lax.axis_index("aperture"), lax.axis_index("beam")
    half, quarter = aper & 1, (aper >> 1) & 1
    even = 1 - (beam & 1)
    rows, rng = child.shape[1:]
    piece = rng // 4
    child_copy = pltpu.make_async_copy(child_hbm, child, sems.at[4])
    copies = []
    for place in range(4):
        source = (half ^ (place // 2)) * 2 + (quarter ^ (place % 2))
        copies.append(
            pltpu.make_async_copy(
                kernel_hbm.at[:, :, pl.ds(pl.multiple_of(source * piece, 128), piece)],
                kernel.at[:, :, place * piece : (place + 1) * piece],
                sems.at[place],
            )
        )
    child_copy.start()
    for copy in copies:
        copy.start()
    child_copy.wait()
    real, imag = child[0], child[1]
    margin = first_ref.shape[1]
    tail = pl.ds(pl.multiple_of(even * (rows - margin), BLK), margin)
    head = pl.ds(pl.multiple_of((1 - even) * (rows - margin), BLK), margin)
    for side in range(2):
        columns = slice(side * 2 * piece, (side + 1) * 2 * piece)
        copies[2 * side].wait()
        copies[2 * side + 1].wait()
        k_real, k_imag = kernel[0, :, columns], kernel[1, :, columns]
        own[0, :, columns] = (dot(real, k_real) - dot(imag, k_imag)).astype(jnp.bfloat16)
        own[1, :, columns] = (dot(real, k_imag) + dot(imag, k_real)).astype(jnp.bfloat16)
        for part in range(2):
            first_ref[part, :, columns] = own[part, tail, columns]
            second_ref[part, :, columns] = own[part, head, columns]


def resample(child, kernel, margin):
    rows, rng = child.shape[1:]
    shape = jax.ShapeDtypeStruct((2, margin, rng), jnp.bfloat16)
    return pl.pallas_call(
        resample_kernel,
        out_shape=(shape, shape),
        in_specs=[ANY, ANY],
        out_specs=(VMEM, VMEM),
        scratch_shapes=[
            pltpu.VMEM(child.shape, jnp.bfloat16),
            pltpu.VMEM(kernel.shape, jnp.bfloat16),
            pltpu.VMEM(child.shape, jnp.bfloat16),
            pltpu.SemaphoreType.DMA((5,)),
        ],
        compiler_params=params(MOST_VMEM),
        cost_estimate=cost(4 * rows * rng * rng, 2**21),
        name="resample",
    )(child, kernel)


def complex_window(weights, window):
    beams, width = weights.shape[0] // 2, window.shape[1] // 2
    product = dot(weights, window)
    return (
        (product[:beams, :width] - product[beams:, width:]).astype(jnp.bfloat16),
        (product[:beams, width:] + product[beams:, :width]).astype(jnp.bfloat16),
    )


def place_rows(padded, start, source, columns):
    width = padded.shape[1] // 2
    for part in range(2):
        target = slice(part * width, (part + 1) * width)
        padded[pl.ds(start, source.shape[1]), target] = source[part, :, columns]


def place_halos(padded, side_ref, rows, first_ref, second_ref, columns):
    even, lowest, highest = side_ref[0], side_ref[1], side_ref[2]
    margin = first_ref.shape[1]
    far = margin + rows
    place_rows(padded, pl.multiple_of(even * far, BLK), first_ref, columns)
    place_rows(padded, pl.multiple_of((1 - even) * far, BLK), second_ref, columns)
    zeros = jnp.zeros((margin, padded.shape[1]), padded.dtype)

    @pl.when(lowest == 1)
    def _():
        padded[:margin, :] = zeros

    @pl.when(highest == 1)
    def _():
        padded[far:, :] = zeros


def first_level_kernel(
    column, rows, starts_ref, side_ref, sent_first_ref, sent_second_ref, first_ref, second_ref,
    weights_ref, out_ref, padded,
):
    sectors, stacked, window = weights_ref.shape
    beams = stacked // 2
    margin = first_ref.shape[1]
    columns = slice(column, column + out_ref.shape[2])
    even = side_ref[0]
    tail = pl.multiple_of(margin + even * (rows - margin), BLK)
    head = pl.multiple_of(margin + (1 - even) * (rows - margin), BLK)
    place_rows(padded, tail, sent_first_ref, columns)
    place_rows(padded, head, sent_second_ref, columns)
    place_halos(padded, side_ref, rows, first_ref, second_ref, columns)
    for sector in range(sectors):
        place = pl.ds(pl.multiple_of(starts_ref[sector] * BLK, BLK), window)
        parts = complex_window(weights_ref[sector], padded[place, :])
        for part in range(2):
            out_ref[part, sector * beams : (sector + 1) * beams, :] = parts[part]


def first_level(column, rows, starts, side, sent, halos, weights):
    sectors, stacked, window = weights.shape
    margin, rng = sent[0].shape[1:]
    assert 2 * margin >= rows
    width = rng // 2
    return pl.pallas_call(
        functools.partial(first_level_kernel, column, rows),
        out_shape=jax.ShapeDtypeStruct((2, sectors * stacked // 2, width), jnp.bfloat16),
        in_specs=[SMEM, SMEM] + [VMEM] * 5,
        out_specs=VMEM,
        scratch_shapes=[pltpu.VMEM((rows + 2 * margin, 2 * width), jnp.bfloat16)],
        compiler_params=params(),
        cost_estimate=cost(sectors * 2 * stacked * window * width, 2**21),
        name="first_level",
    )(starts, side, *sent, *halos, weights)


def second_level_early_kernel(
    starts_ref, side_ref, sector_ref, own_ref, first_ref, second_ref, weights_ref, send_ref, padded
):
    _, stacked, window = weights_ref.shape
    per = stacked // 2 // OS
    margin, rows = first_ref.shape[1], own_ref.shape[1]
    columns = slice(send_ref.shape[3], 2 * send_ref.shape[3])
    place_rows(padded, margin, own_ref, columns)
    place_halos(padded, side_ref, rows, first_ref, second_ref, columns)
    for place in range(send_ref.shape[0]):
        sector = sector_ref[place] // per
        piece = pl.multiple_of(sector_ref[place] % per * OS, OS)
        window_rows = pl.ds(pl.multiple_of(starts_ref[sector] * BLK, BLK), window)
        weights = jnp.concatenate(
            [
                weights_ref[sector, pl.ds(piece, OS), :],
                weights_ref[sector, pl.ds(pl.multiple_of(piece + stacked // 2, OS), OS), :],
            ]
        )
        parts = complex_window(weights, padded[window_rows, :])
        for part in range(2):
            send_ref[place, part] = parts[part]


def second_level_kernel(
    starts_ref, side_ref, own_at_ref, other_at_ref, own_ref, first_ref, second_ref, weights_ref,
    keep_ref, send_ref, padded, send,
):
    sectors, stacked, window = weights_ref.shape
    beams = stacked // 2
    width = keep_ref.shape[3]
    margin, rows = first_ref.shape[1], own_ref.shape[1]
    columns = slice(0, 2 * width)
    place_rows(padded, margin, own_ref, columns)
    place_halos(padded, side_ref, rows, first_ref, second_ref, columns)
    per = beams // OS
    for sector in range(sectors):
        place = pl.ds(pl.multiple_of(starts_ref[sector] * BLK, BLK), window)
        parts = complex_window(weights_ref[sector], padded[place, :])
        for piece in range(per):
            own_at = own_at_ref[sector * per + piece]
            other_at = other_at_ref[sector * per + piece]
            taken = slice(piece * OS, (piece + 1) * OS)
            for part in range(2):
                keep_ref[own_at, part] = parts[part][taken, :width]
                send[other_at, part] = parts[part][taken, width:]
    send_ref[...] = send[send.shape[0] - send_ref.shape[0] :]


def second_level(starts, side, planned, own, halos, weights, early):
    sectors, stacked, window = weights.shape
    margin, rows, rng = halos[0].shape[1], own.shape[1], own.shape[2]
    count = sectors * stacked // 2 // OS
    block = (2, OS, rng // 2)
    own_at, other_at, other_sector = planned
    early_send = pl.pallas_call(
        second_level_early_kernel,
        out_shape=jax.ShapeDtypeStruct((early,) + block, jnp.bfloat16),
        in_specs=[SMEM] * 3 + [VMEM] * 4,
        out_specs=VMEM,
        scratch_shapes=[pltpu.VMEM((rows + 2 * margin, rng), jnp.bfloat16)],
        compiler_params=params(),
        cost_estimate=cost(early * 2 * 2 * OS * window * rng // 2, 2**20),
        name="second_level_early",
    )(starts, side, other_sector, own, *halos, weights)
    shapes = [jax.ShapeDtypeStruct((n,) + block, jnp.bfloat16) for n in (count, count - early)]
    keep, late_send = pl.pallas_call(
        second_level_kernel,
        out_shape=shapes,
        in_specs=[SMEM] * 4 + [VMEM] * 4,
        out_specs=[VMEM] * 2,
        scratch_shapes=[
            pltpu.VMEM((rows + 2 * margin, 2 * rng), jnp.bfloat16),
            pltpu.VMEM((count,) + block, jnp.bfloat16),
        ],
        compiler_params=params(),
        cost_estimate=cost(sectors * 2 * stacked * window * rng, 2**22),
        name="second_level",
    )(starts, side, own_at, other_at, own, *halos, weights)
    return keep, early_send, late_send


def plan_kernel(
    shift, me_ref, own_ref, other_ref, own_at_ref, other_at_ref, other_sector_ref, target_ref, rank_ref,
    taken, filled,
):
    count = own_ref.shape[0]
    far_bit = taken.shape[0] // 2

    def delay(target):
        distance = target ^ me_ref[0]
        return jnp.where((distance & far_bit) == 0, 2 * count, (distance & 1) * shift)

    for owners_ref, at_ref in ((other_ref, other_at_ref), (own_ref, own_at_ref)):
        for target in range(taken.shape[0]):
            taken[target] = 0
        for bucket in range(filled.shape[0]):
            filled[bucket] = 0
        for sector in range(count):
            target = owners_ref[sector]
            rank = taken[target]
            taken[target] = rank + 1
            bucket = rank + delay(target)
            at_ref[sector] = bucket
            filled[bucket + 1] = filled[bucket + 1] + 1
        for bucket in range(1, filled.shape[0]):
            filled[bucket] = filled[bucket] + filled[bucket - 1]
        for sector in range(count):
            bucket = at_ref[sector]
            place = filled[bucket]
            filled[bucket] = place + 1
            at_ref[sector] = place
            if at_ref is own_at_ref:
                target_ref[place] = owners_ref[sector]
                rank_ref[place] = bucket - delay(owners_ref[sector])
            else:
                other_sector_ref[place] = sector


def plan(shift, me, own, other, beam_count):
    count = own.shape[0]
    shape = jax.ShapeDtypeStruct((count,), jnp.int32)
    return pl.pallas_call(
        functools.partial(plan_kernel, shift),
        out_shape=[shape] * 5,
        in_specs=[SMEM] * 3,
        out_specs=[SMEM] * 5,
        scratch_shapes=[
            pltpu.SMEM((beam_count,), jnp.int32),
            pltpu.SMEM((3 * count + 1,), jnp.int32),
        ],
        compiler_params=params(),
        name="plan",
    )(me, own, other)


def wires_kernel(spans, early, me_ref, target_ref, rank_ref, keep_ref, *refs):
    wires = refs[-1]
    spare = wires.shape[0] - 1
    out_refs = refs[-1 - len(spans) : -1]
    other_ref, *summed_refs = refs[: -1 - len(spans)]
    wires[...] = jnp.zeros_like(wires)
    me = me_ref[0]

    def lay(place, total):
        rank = rank_ref[place]
        distance = target_ref[place] ^ me
        at = spare
        start = 0
        for number, low, high in spans:
            wanted = (distance == number) & (rank >= low) & (rank < high)
            at = jnp.where(wanted, start + rank - low, at)
            start += high - low
        wires[at] = total

    before = 0
    if not early:
        before = summed_refs[0].shape[0]
        for row in range(before):
            lay(row, summed_refs[0][row])
    for row in range(other_ref.shape[0]):
        place = before + row
        total = keep_ref[place].astype(jnp.float32) + other_ref[row].astype(jnp.float32)
        total = total.astype(jnp.bfloat16)
        lay(place, total)
        if early:
            summed_refs[0][row] = total
    start = 0
    for (_, low, high), ref in zip(spans, out_refs):
        ref[...] = wires[start : start + high - low]
        start += high - low


def wires(spans, me, target, rank, keep, other, summed=None):
    block = keep.shape[1:]
    sizes = [high - low for _, low, high in spans]
    inputs = [me, target, rank, keep, other]
    if summed is None:
        sizes = [other.shape[0]] + sizes
    else:
        inputs.append(summed)
    shapes = [jax.ShapeDtypeStruct((size,) + block, jnp.bfloat16) for size in sizes]
    total = sum(high - low for _, low, high in spans)
    return pl.pallas_call(
        functools.partial(wires_kernel, spans, summed is None),
        out_shape=shapes,
        in_specs=[SMEM] * 3 + [VMEM] * (len(inputs) - 3),
        out_specs=[VMEM] * len(shapes),
        scratch_shapes=[pltpu.VMEM((total + 1,) + block, jnp.bfloat16)],
        compiler_params=params(),
        cost_estimate=cost(0, 2**21),
        name="early_wires" if summed is None else "late_wires",
    )(*inputs)


def collect_kernel(spans, capacity, me_ref, *refs):
    sems = refs[-1]
    out_ref = refs[-2]
    copies = []
    for number, (distance, low, high) in enumerate(spans):
        start = (me_ref[0] ^ distance) * capacity + low
        copies.append(
            pltpu.make_async_copy(
                refs[number], out_ref.at[pl.ds(start, high - low)], sems.at[number]
            )
        )
    for copy in copies:
        copy.start()
    for copy in copies:
        copy.wait()


def collect(spans, capacity, beam_count, me, received):
    shape = (beam_count * capacity,) + received[0].shape[1:]
    return pl.pallas_call(
        functools.partial(collect_kernel, spans, capacity),
        out_shape=jax.ShapeDtypeStruct(shape, jnp.bfloat16),
        in_specs=[SMEM] + [ANY] * len(received),
        out_specs=ANY,
        scratch_shapes=[pltpu.SemaphoreType.DMA((len(received),))],
        compiler_params=params(),
        cost_estimate=cost(0, 2**21),
        name="collect",
    )(me, *received)


def spread(spans, group):
    count = lax.axis_size("beam")
    received = []
    for (distance, _, _), wire in zip(spans, group):
        route = [(place, place ^ distance) for place in range(count)]
        received.append(lax.ppermute(wire, "beam", route) if distance else wire)
    return received


def stacked_weights(weights):
    return weights[0].reshape(weights.shape[1], -1, weights.shape[4])


def table_row(table, row_number):
    return lax.dynamic_index_in_dim(table, row_number, 0, keepdims=False)


def local(subimages, range_kernel, weights0, starts0, weights1, starts1, owners):
    aper_index = lax.axis_index("aperture")
    beam_index = lax.axis_index("beam")
    beam_count = lax.axis_size("beam")
    margin = MARGIN_BLOCKS * BLK
    rows = subimages.shape[2]
    local_blocks = rows // BLK
    even = (beam_index + 1) % 2
    ends = (beam_index == 0, beam_index == beam_count - 1)
    side = jnp.stack([even] + [end.astype(jnp.int32) for end in ends])
    me = beam_index.reshape(1)

    sector_count = owners.shape[1]
    capacity = max(2, 2 * sector_count // beam_count)
    shorter, longer = max(1, capacity // 4), max(1, capacity // 2)
    far = range(beam_count // 2, beam_count)
    odd = [distance for distance in far if distance % 2]
    others = [distance for distance in far if distance % 2 == 0]
    early = len(odd) * shorter + len(others) * longer
    early_spans = [(distance, 0, shorter) for distance in odd]
    early_spans += [(distance, 0, longer) for distance in others]
    late_spans = [(distance, shorter, capacity) for distance in odd]
    for distance in range(1, beam_count // 2):
        cut = (5 * capacity + 4) // 8
        late_spans += [(distance, 0, cut), (distance, cut, capacity)]
    late_spans.append((0, 0, capacity))
    last_spans = [(distance, longer, capacity) for distance in others]

    sent = resample(subimages[0], range_kernel[0], margin)
    halos = trade_edges(*sent)
    own_owners = owners[0, :, 0]
    other_owners = partner(owners, "aperture", 1)[0, :, 0]
    planned = plan(longer - shorter, me, own_owners, other_owners, beam_count)
    begin0 = table_row(starts0, aper_index) - (beam_index * local_blocks - MARGIN_BLOCKS)
    halos, planned = lax.optimization_barrier((halos, planned))
    *planned, target, rank = planned
    width = range_kernel.shape[3] // 2
    weights = stacked_weights(weights0)
    send = first_level(width, rows, begin0, side, sent, halos, weights)
    other = partner(send, "aperture", 0)
    keep = first_level(0, rows, begin0, side, sent, halos, weights)
    level_one = (keep.astype(jnp.float32) + other.astype(jnp.float32)).astype(jnp.bfloat16)

    beams = level_one.shape[1]
    first = lax.dynamic_slice_in_dim(level_one, even * (beams - margin), margin, 1)
    second = lax.dynamic_slice_in_dim(level_one, (1 - even) * (beams - margin), margin, 1)
    halos = trade_edges(first, second)
    begin1 = table_row(starts1, aper_index) - (beam_index * 2 * local_blocks - MARGIN_BLOCKS)
    keep, send, late = second_level(
        begin1, side, planned, level_one, halos, stacked_weights(weights1), early
    )
    other = partner(send, "aperture", 1)
    other, late = lax.optimization_barrier((other, late))
    late = partner(late, "aperture", 1)
    summed, *group = wires(early_spans, me, target, rank, keep, other)
    received = spread(early_spans, group)
    from_odd, from_others = received[: len(odd)], received[len(odd) :]
    ready, from_odd = lax.optimization_barrier((late, from_odd))
    group = wires(late_spans, me, target, rank, keep, ready, summed)
    received = from_odd + spread(late_spans, group)
    ready, from_others = lax.optimization_barrier((late, from_others))
    group = wires(last_spans, me, target, rank, keep, ready, summed)
    received += from_others + spread(last_spans, group)
    spans = early_spans[: len(odd)] + late_spans + early_spans[len(odd) :] + last_spans
    return collect(spans, capacity, beam_count, me, received)[None]


def solution(mesh):
    return jax.shard_map(
        local,
        mesh=mesh,
        in_specs=(
            P("aperture", None, "beam", None),
            P("aperture", None, None, None),
            P("aperture", "beam", None, None, None),
            P(None, "beam"),
            P("aperture", "beam", None, None, None),
            P(None, "beam"),
            P("aperture", "beam", None),
        ),
        out_specs=P("aperture", "beam", None, None, None),
        check_vma=False,
    )
```

```python
import functools

import jax
import jax.numpy as jnp
from jax import lax
from jax.experimental import pallas as pl
from jax.experimental.pallas import tpu as pltpu
from jax.sharding import PartitionSpec as P

BLK = 32
NW = 10
REACH = 2
OS = 64
MARGIN_BLOCKS = (NW - 2) // 2 + REACH
VMEM_LIMIT = 8 * 1024 * 1024
MOST_VMEM = 53 * 1024 * 1024
ANY = pl.BlockSpec(memory_space=pl.ANY)
VMEM = pl.BlockSpec(memory_space=pltpu.VMEM)
SMEM = pl.BlockSpec(memory_space=pltpu.SMEM)


def params(limit=VMEM_LIMIT):
    return pltpu.CompilerParams(vmem_limit_bytes=limit)


def cost(macs, moved):
    return pl.CostEstimate(flops=2 * macs, bytes_accessed=moved, transcendentals=0)


def trade_edges(first, second, inner):
    count, apertures = lax.axis_size("beam"), lax.axis_size("aperture")
    received = []
    for order, block in enumerate((first, second)):
        route = []
        for aper in range(apertures):
            for place in range(count):
                other = place + 1 if (place - order - inner) % 2 == 0 else place - 1
                if 0 <= other < count:
                    to = aper * count + other
                else:
                    to = min(aper ^ 1, apertures - 1) * count + place
                route.append((aper * count + place, to))
        received.append(lax.ppermute(block, ("aperture", "beam"), route))
    return received


def partner(block, axis, distance):
    count = lax.axis_size(axis)
    route = []
    for low in range(count):
        high = low | 1 << distance
        if high != low and high < count:
            route += [(low, high), (high, low)]
    return lax.ppermute(block, axis, route)


def dot(left, right):
    return jnp.dot(left, right, preferred_element_type=jnp.float32)


def resample_kernel(child_hbm, kernel_hbm, first_ref, second_ref, child, kernel, own, sems):
    aper, beam = lax.axis_index("aperture"), lax.axis_index("beam")
    half, quarter = aper & 1, (aper >> 1) & 1
    even = beam & 1
    rows, rng = child.shape[1:]
    piece = rng // 4
    child_copy = pltpu.make_async_copy(child_hbm, child, sems.at[4])
    copies = []
    for place in range(4):
        source = (half ^ (place // 2)) * 2 + (quarter ^ (place % 2))
        copies.append(
            pltpu.make_async_copy(
                kernel_hbm.at[:, :, pl.ds(pl.multiple_of(source * piece, 128), piece)],
                kernel.at[:, :, place * piece : (place + 1) * piece],
                sems.at[place],
            )
        )
    child_copy.start()
    for copy in copies:
        copy.start()
    child_copy.wait()
    real, imag = child[0], child[1]
    margin = first_ref.shape[1]
    tail = pl.ds(pl.multiple_of(even * (rows - margin), BLK), margin)
    head = pl.ds(pl.multiple_of((1 - even) * (rows - margin), BLK), margin)
    for side in range(2):
        columns = slice(side * 2 * piece, (side + 1) * 2 * piece)
        copies[2 * side].wait()
        copies[2 * side + 1].wait()
        k_real, k_imag = kernel[0, :, columns], kernel[1, :, columns]
        own[0, :, columns] = (dot(real, k_real) - dot(imag, k_imag)).astype(jnp.bfloat16)
        own[1, :, columns] = (dot(real, k_imag) + dot(imag, k_real)).astype(jnp.bfloat16)
        for part in range(2):
            first_ref[part, :, columns] = own[part, tail, columns]
            second_ref[part, :, columns] = own[part, head, columns]


def resample(child, kernel, margin):
    rows, rng = child.shape[1:]
    shape = jax.ShapeDtypeStruct((2, margin, rng), jnp.bfloat16)
    return pl.pallas_call(
        resample_kernel,
        out_shape=(shape, shape),
        in_specs=[ANY, ANY],
        out_specs=(VMEM, VMEM),
        scratch_shapes=[
            pltpu.VMEM(child.shape, jnp.bfloat16),
            pltpu.VMEM(kernel.shape, jnp.bfloat16),
            pltpu.VMEM(child.shape, jnp.bfloat16),
            pltpu.SemaphoreType.DMA((5,)),
        ],
        compiler_params=params(MOST_VMEM),
        cost_estimate=cost(4 * rows * rng * rng, 2**21),
        name="resample",
    )(child, kernel)


def complex_window(weights, window):
    beams, width = weights.shape[0] // 2, window.shape[1] // 2
    product = dot(weights, window)
    return (
        (product[:beams, :width] - product[beams:, width:]).astype(jnp.bfloat16),
        (product[:beams, width:] + product[beams:, :width]).astype(jnp.bfloat16),
    )


def place_rows(padded, start, source, columns):
    width = padded.shape[1] // 2
    for part in range(2):
        target = slice(part * width, (part + 1) * width)
        padded[pl.ds(start, source.shape[1]), target] = source[part, :, columns]


def place_halos(padded, side_ref, rows, first_ref, second_ref, columns):
    even, lowest, highest = side_ref[0], side_ref[1], side_ref[2]
    margin = first_ref.shape[1]
    far = margin + rows
    place_rows(padded, pl.multiple_of(even * far, BLK), first_ref, columns)
    place_rows(padded, pl.multiple_of((1 - even) * far, BLK), second_ref, columns)
    zeros = jnp.zeros((margin, padded.shape[1]), padded.dtype)

    @pl.when(lowest == 1)
    def _():
        padded[:margin, :] = zeros

    @pl.when(highest == 1)
    def _():
        padded[far:, :] = zeros


def first_level_kernel(
    column, rows, starts_ref, side_ref, sent_first_ref, sent_second_ref, first_ref, second_ref,
    weights_ref, out_ref, padded,
):
    sectors, stacked, window = weights_ref.shape
    beams = stacked // 2
    margin = first_ref.shape[1]
    columns = slice(column, column + out_ref.shape[2])
    even = side_ref[0]
    tail = pl.multiple_of(margin + even * (rows - margin), BLK)
    head = pl.multiple_of(margin + (1 - even) * (rows - margin), BLK)
    place_rows(padded, tail, sent_first_ref, columns)
    place_rows(padded, head, sent_second_ref, columns)
    place_halos(padded, side_ref, rows, first_ref, second_ref, columns)
    for sector in range(sectors):
        place = pl.ds(pl.multiple_of(starts_ref[sector] * BLK, BLK), window)
        parts = complex_window(weights_ref[sector], padded[place, :])
        for part in range(2):
            out_ref[part, sector * beams : (sector + 1) * beams, :] = parts[part]


def first_level(column, rows, starts, side, sent, halos, weights):
    sectors, stacked, window = weights.shape
    margin, rng = sent[0].shape[1:]
    assert 2 * margin >= rows
    width = rng // 2
    return pl.pallas_call(
        functools.partial(first_level_kernel, column, rows),
        out_shape=jax.ShapeDtypeStruct((2, sectors * stacked // 2, width), jnp.bfloat16),
        in_specs=[SMEM, SMEM] + [VMEM] * 5,
        out_specs=VMEM,
        scratch_shapes=[pltpu.VMEM((rows + 2 * margin, 2 * width), jnp.bfloat16)],
        compiler_params=params(),
        cost_estimate=cost(sectors * 2 * stacked * window * width, 2**21),
        name="first_level",
    )(starts, side, *sent, *halos, weights)


def second_level_early_kernel(
    starts_ref, side_ref, sector_ref, own_ref, first_ref, second_ref, weights_ref, send_ref, padded
):
    _, stacked, window = weights_ref.shape
    per = stacked // 2 // OS
    margin, rows = first_ref.shape[1], own_ref.shape[1]
    columns = slice(send_ref.shape[3], 2 * send_ref.shape[3])
    place_rows(padded, margin, own_ref, columns)
    place_halos(padded, side_ref, rows, first_ref, second_ref, columns)
    for place in range(send_ref.shape[0]):
        sector = sector_ref[place] // per
        piece = pl.multiple_of(sector_ref[place] % per * OS, OS)
        window_rows = pl.ds(pl.multiple_of(starts_ref[sector] * BLK, BLK), window)
        weights = jnp.concatenate(
            [
                weights_ref[sector, pl.ds(piece, OS), :],
                weights_ref[sector, pl.ds(pl.multiple_of(piece + stacked // 2, OS), OS), :],
            ]
        )
        parts = complex_window(weights, padded[window_rows, :])
        for part in range(2):
            send_ref[place, part] = parts[part]


def second_level_kernel(
    starts_ref, side_ref, own_at_ref, other_at_ref, own_ref, first_ref, second_ref, weights_ref,
    keep_ref, send_ref, padded, send,
):
    sectors, stacked, window = weights_ref.shape
    beams = stacked // 2
    width = keep_ref.shape[3]
    margin, rows = first_ref.shape[1], own_ref.shape[1]
    columns = slice(0, 2 * width)
    place_rows(padded, margin, own_ref, columns)
    place_halos(padded, side_ref, rows, first_ref, second_ref, columns)
    per = beams // OS
    for sector in range(sectors):
        place = pl.ds(pl.multiple_of(starts_ref[sector] * BLK, BLK), window)
        parts = complex_window(weights_ref[sector], padded[place, :])
        for piece in range(per):
            own_at = own_at_ref[sector * per + piece]
            other_at = other_at_ref[sector * per + piece]
            taken = slice(piece * OS, (piece + 1) * OS)
            for part in range(2):
                keep_ref[own_at, part] = parts[part][taken, :width]
                send[other_at, part] = parts[part][taken, width:]
    send_ref[...] = send[send.shape[0] - send_ref.shape[0] :]


def second_level(starts, side, planned, own, halos, weights, early):
    sectors, stacked, window = weights.shape
    margin, rows, rng = halos[0].shape[1], own.shape[1], own.shape[2]
    count = sectors * stacked // 2 // OS
    block = (2, OS, rng // 2)
    own_at, other_at, other_sector = planned
    early_send = pl.pallas_call(
        second_level_early_kernel,
        out_shape=jax.ShapeDtypeStruct((early,) + block, jnp.bfloat16),
        in_specs=[SMEM] * 3 + [VMEM] * 4,
        out_specs=VMEM,
        scratch_shapes=[pltpu.VMEM((rows + 2 * margin, rng), jnp.bfloat16)],
        compiler_params=params(),
        cost_estimate=cost(early * 2 * 2 * OS * window * rng // 2, 2**20),
        name="second_level_early",
    )(starts, side, other_sector, own, *halos, weights)
    shapes = [jax.ShapeDtypeStruct((n,) + block, jnp.bfloat16) for n in (count, count - early)]
    keep, late_send = pl.pallas_call(
        second_level_kernel,
        out_shape=shapes,
        in_specs=[SMEM] * 4 + [VMEM] * 4,
        out_specs=[VMEM] * 2,
        scratch_shapes=[
            pltpu.VMEM((rows + 2 * margin, 2 * rng), jnp.bfloat16),
            pltpu.VMEM((count,) + block, jnp.bfloat16),
        ],
        compiler_params=params(),
        cost_estimate=cost(sectors * 2 * stacked * window * rng, 2**22),
        name="second_level",
    )(starts, side, own_at, other_at, own, *halos, weights)
    return keep, early_send, late_send


def plan_kernel(
    shift, me_ref, own_ref, other_ref, own_at_ref, other_at_ref, other_sector_ref, target_ref, rank_ref,
    taken, filled,
):
    count = own_ref.shape[0]
    far_bit = taken.shape[0] // 2

    def delay(target):
        distance = target ^ me_ref[0]
        return jnp.where((distance & far_bit) == 0, 2 * count, (distance & 1) * shift)

    for owners_ref, at_ref in ((other_ref, other_at_ref), (own_ref, own_at_ref)):
        for target in range(taken.shape[0]):
            taken[target] = 0
        for bucket in range(filled.shape[0]):
            filled[bucket] = 0
        for sector in range(count):
            target = owners_ref[sector]
            rank = taken[target]
            taken[target] = rank + 1
            bucket = rank + delay(target)
            at_ref[sector] = bucket
            filled[bucket + 1] = filled[bucket + 1] + 1
        for bucket in range(1, filled.shape[0]):
            filled[bucket] = filled[bucket] + filled[bucket - 1]
        for sector in range(count):
            bucket = at_ref[sector]
            place = filled[bucket]
            filled[bucket] = place + 1
            at_ref[sector] = place
            if at_ref is own_at_ref:
                target_ref[place] = owners_ref[sector]
                rank_ref[place] = bucket - delay(owners_ref[sector])
            else:
                other_sector_ref[place] = sector


def plan(shift, me, own, other, beam_count):
    count = own.shape[0]
    shape = jax.ShapeDtypeStruct((count,), jnp.int32)
    return pl.pallas_call(
        functools.partial(plan_kernel, shift),
        out_shape=[shape] * 5,
        in_specs=[SMEM] * 3,
        out_specs=[SMEM] * 5,
        scratch_shapes=[
            pltpu.SMEM((beam_count,), jnp.int32),
            pltpu.SMEM((3 * count + 1,), jnp.int32),
        ],
        compiler_params=params(),
        name="plan",
    )(me, own, other)


def wires_kernel(spans, early, me_ref, target_ref, rank_ref, keep_ref, *refs):
    wires = refs[-1]
    spare = wires.shape[0] - 1
    out_refs = refs[-1 - len(spans) : -1]
    other_ref, *summed_refs = refs[: -1 - len(spans)]
    wires[...] = jnp.zeros_like(wires)
    me = me_ref[0]

    def lay(place, total):
        rank = rank_ref[place]
        distance = target_ref[place] ^ me
        at = spare
        start = 0
        for number, low, high in spans:
            wanted = (distance == number) & (rank >= low) & (rank < high)
            at = jnp.where(wanted, start + rank - low, at)
            start += high - low
        wires[at] = total

    before = 0
    if not early:
        before = summed_refs[0].shape[0]
        for row in range(before):
            lay(row, summed_refs[0][row])
    for row in range(other_ref.shape[0]):
        place = before + row
        total = keep_ref[place].astype(jnp.float32) + other_ref[row].astype(jnp.float32)
        total = total.astype(jnp.bfloat16)
        lay(place, total)
        if early:
            summed_refs[0][row] = total
    start = 0
    for (_, low, high), ref in zip(spans, out_refs):
        ref[...] = wires[start : start + high - low]
        start += high - low


def wires(spans, me, target, rank, keep, other, summed=None):
    block = keep.shape[1:]
    sizes = [high - low for _, low, high in spans]
    inputs = [me, target, rank, keep, other]
    if summed is None:
        sizes = [other.shape[0]] + sizes
    else:
        inputs.append(summed)
    shapes = [jax.ShapeDtypeStruct((size,) + block, jnp.bfloat16) for size in sizes]
    total = sum(high - low for _, low, high in spans)
    return pl.pallas_call(
        functools.partial(wires_kernel, spans, summed is None),
        out_shape=shapes,
        in_specs=[SMEM] * 3 + [VMEM] * (len(inputs) - 3),
        out_specs=[VMEM] * len(shapes),
        scratch_shapes=[pltpu.VMEM((total + 1,) + block, jnp.bfloat16)],
        compiler_params=params(),
        cost_estimate=cost(0, 2**21),
        name="early_wires" if summed is None else "late_wires",
    )(*inputs)


def collect_kernel(spans, capacity, me_ref, *refs):
    sems = refs[-1]
    out_ref = refs[-2]
    copies = []
    for number, (distance, low, high) in enumerate(spans):
        start = (me_ref[0] ^ distance) * capacity + low
        copies.append(
            pltpu.make_async_copy(
                refs[number], out_ref.at[pl.ds(start, high - low)], sems.at[number]
            )
        )
    for copy in copies:
        copy.start()
    for copy in copies:
        copy.wait()


def collect(spans, capacity, beam_count, me, received):
    shape = (beam_count * capacity,) + received[0].shape[1:]
    return pl.pallas_call(
        functools.partial(collect_kernel, spans, capacity),
        out_shape=jax.ShapeDtypeStruct(shape, jnp.bfloat16),
        in_specs=[SMEM] + [ANY] * len(received),
        out_specs=ANY,
        scratch_shapes=[pltpu.SemaphoreType.DMA((len(received),))],
        compiler_params=params(),
        cost_estimate=cost(0, 2**21),
        name="collect",
    )(me, *received)


def spread(spans, group):
    count = lax.axis_size("beam")
    received = []
    for (distance, _, _), wire in zip(spans, group):
        route = [(place, place ^ distance) for place in range(count)]
        received.append(lax.ppermute(wire, "beam", route) if distance else wire)
    return received


def stacked_weights(weights):
    return weights[0].reshape(weights.shape[1], -1, weights.shape[4])


def table_row(table, row_number):
    return lax.dynamic_index_in_dim(table, row_number, 0, keepdims=False)


def local(subimages, range_kernel, weights0, starts0, weights1, starts1, owners):
    aper_index = lax.axis_index("aperture")
    beam_index = lax.axis_index("beam")
    beam_count = lax.axis_size("beam")
    margin = MARGIN_BLOCKS * BLK
    rows = subimages.shape[2]
    local_blocks = rows // BLK
    even = (beam_index + 1) % 2
    ends = (beam_index == 0, beam_index == beam_count - 1)
    ends = [end.astype(jnp.int32) for end in ends]
    inner_side, side = jnp.stack([1 - even] + ends), jnp.stack([even] + ends)
    me = beam_index.reshape(1)

    sector_count = owners.shape[1]
    capacity = max(2, 2 * sector_count // beam_count)
    shorter, longer = max(1, capacity // 4), max(1, capacity // 2)
    far = range(beam_count // 2, beam_count)
    odd = [distance for distance in far if distance % 2]
    others = [distance for distance in far if distance % 2 == 0]
    early = len(odd) * shorter + len(others) * longer
    early_spans = [(distance, 0, shorter) for distance in odd]
    early_spans += [(distance, 0, longer) for distance in others]
    late_spans = [(distance, shorter, capacity) for distance in odd]
    for distance in range(1, beam_count // 2):
        cut = (5 * capacity + 4) // 8
        late_spans += [(distance, 0, cut), (distance, cut, capacity)]
    late_spans.append((0, 0, capacity))
    last_spans = [(distance, longer, capacity) for distance in others]

    sent = resample(subimages[0], range_kernel[0], margin)
    halos = trade_edges(*sent, 1)
    own_owners = owners[0, :, 0]
    other_owners = partner(owners, "aperture", 1)[0, :, 0]
    planned = plan(longer - shorter, me, own_owners, other_owners, beam_count)
    begin0 = table_row(starts0, aper_index) - (beam_index * local_blocks - MARGIN_BLOCKS)
    halos, planned = lax.optimization_barrier((halos, planned))
    *planned, target, rank = planned
    width = range_kernel.shape[3] // 2
    weights = stacked_weights(weights0)
    send = first_level(width, rows, begin0, inner_side, sent, halos, weights)
    other = partner(send, "aperture", 0)
    keep = first_level(0, rows, begin0, inner_side, sent, halos, weights)
    level_one = (keep.astype(jnp.float32) + other.astype(jnp.float32)).astype(jnp.bfloat16)

    beams = level_one.shape[1]
    first = lax.dynamic_slice_in_dim(level_one, even * (beams - margin), margin, 1)
    second = lax.dynamic_slice_in_dim(level_one, (1 - even) * (beams - margin), margin, 1)
    halos = trade_edges(first, second, 0)
    begin1 = table_row(starts1, aper_index) - (beam_index * 2 * local_blocks - MARGIN_BLOCKS)
    keep, send, late = second_level(
        begin1, side, planned, level_one, halos, stacked_weights(weights1), early
    )
    other = partner(send, "aperture", 1)
    other, late = lax.optimization_barrier((other, late))
    late = partner(late, "aperture", 1)
    summed, *group = wires(early_spans, me, target, rank, keep, other)
    received = spread(early_spans, group)
    from_odd, from_others = received[: len(odd)], received[len(odd) :]
    ready, from_odd = lax.optimization_barrier((late, from_odd))
    group = wires(late_spans, me, target, rank, keep, ready, summed)
    received = from_odd + spread(late_spans, group)
    ready, from_others = lax.optimization_barrier((late, from_others))
    group = wires(last_spans, me, target, rank, keep, ready, summed)
    received += from_others + spread(last_spans, group)
    spans = early_spans[: len(odd)] + late_spans + early_spans[len(odd) :] + last_spans
    return collect(spans, capacity, beam_count, me, received)[None]


def solution(mesh):
    return jax.shard_map(
        local,
        mesh=mesh,
        in_specs=(
            P("aperture", None, "beam", None),
            P("aperture", None, None, None),
            P("aperture", "beam", None, None, None),
            P(None, "beam"),
            P("aperture", "beam", None, None, None),
            P(None, "beam"),
            P("aperture", "beam", None),
        ),
        out_specs=P("aperture", "beam", None, None, None),
        check_vma=False,
    )
```

```python
import functools

import jax
import jax.numpy as jnp
from jax import lax
from jax.experimental import pallas as pl
from jax.experimental.pallas import tpu as pltpu
from jax.sharding import PartitionSpec as P

BLK = 32
NW = 10
REACH = 2
OS = 64
MARGIN_BLOCKS = (NW - 2) // 2 + REACH
VMEM_LIMIT = 8 * 1024 * 1024
MOST_VMEM = 53 * 1024 * 1024
ANY = pl.BlockSpec(memory_space=pl.ANY)
VMEM = pl.BlockSpec(memory_space=pltpu.VMEM)
SMEM = pl.BlockSpec(memory_space=pltpu.SMEM)


def params(limit=VMEM_LIMIT):
    return pltpu.CompilerParams(vmem_limit_bytes=limit)


def cost(macs, moved):
    return pl.CostEstimate(flops=2 * macs, bytes_accessed=moved, transcendentals=0)


def trade_edges(first, second, inner):
    count, apertures = lax.axis_size("beam"), lax.axis_size("aperture")
    received = []
    for order, block in enumerate((first, second)):
        route = []
        for aper in range(apertures):
            for place in range(count):
                other = place + 1 if (place - order - inner) % 2 == 0 else place - 1
                if 0 <= other < count:
                    to = aper * count + other
                else:
                    to = min(aper ^ 1, apertures - 1) * count + place
                route.append((aper * count + place, to))
        received.append(lax.ppermute(block, ("aperture", "beam"), route))
    return received


def partner(block, axis, distance):
    count = lax.axis_size(axis)
    route = []
    for low in range(count):
        high = low | 1 << distance
        if high != low and high < count:
            route += [(low, high), (high, low)]
    return lax.ppermute(block, axis, route)


def dot(left, right):
    return jnp.dot(left, right, preferred_element_type=jnp.float32)


def resample_kernel(child_hbm, kernel_hbm, first_ref, second_ref, child, kernel, own, sems):
    aper, beam = lax.axis_index("aperture"), lax.axis_index("beam")
    half, quarter = aper & 1, (aper >> 1) & 1
    even = beam & 1
    rows, rng = child.shape[1:]
    piece = rng // 4
    child_copy = pltpu.make_async_copy(child_hbm, child, sems.at[4])
    copies = []
    for place in range(4):
        source = (half ^ (place // 2)) * 2 + (quarter ^ (place % 2))
        copies.append(
            pltpu.make_async_copy(
                kernel_hbm.at[:, :, pl.ds(pl.multiple_of(source * piece, 128), piece)],
                kernel.at[:, :, place * piece : (place + 1) * piece],
                sems.at[place],
            )
        )
    child_copy.start()
    for copy in copies:
        copy.start()
    child_copy.wait()
    real, imag = child[0], child[1]
    margin = first_ref.shape[1]
    tail = pl.ds(pl.multiple_of(even * (rows - margin), BLK), margin)
    head = pl.ds(pl.multiple_of((1 - even) * (rows - margin), BLK), margin)
    for side in range(2):
        columns = slice(side * 2 * piece, (side + 1) * 2 * piece)
        copies[2 * side].wait()
        copies[2 * side + 1].wait()
        k_real, k_imag = kernel[0, :, columns], kernel[1, :, columns]
        own[0, :, columns] = (dot(real, k_real) - dot(imag, k_imag)).astype(jnp.bfloat16)
        own[1, :, columns] = (dot(real, k_imag) + dot(imag, k_real)).astype(jnp.bfloat16)
        for part in range(2):
            first_ref[part, :, columns] = own[part, tail, columns]
            second_ref[part, :, columns] = own[part, head, columns]


def resample(child, kernel, margin):
    rows, rng = child.shape[1:]
    shape = jax.ShapeDtypeStruct((2, margin, rng), jnp.bfloat16)
    return pl.pallas_call(
        resample_kernel,
        out_shape=(shape, shape),
        in_specs=[ANY, ANY],
        out_specs=(VMEM, VMEM),
        scratch_shapes=[
            pltpu.VMEM(child.shape, jnp.bfloat16),
            pltpu.VMEM(kernel.shape, jnp.bfloat16),
            pltpu.VMEM(child.shape, jnp.bfloat16),
            pltpu.SemaphoreType.DMA((5,)),
        ],
        compiler_params=params(MOST_VMEM),
        cost_estimate=cost(4 * rows * rng * rng, 2**21),
        name="resample",
    )(child, kernel)


def complex_window(weights, window):
    beams, width = weights.shape[0] // 2, window.shape[1] // 2
    product = dot(weights, window)
    return (
        (product[:beams, :width] - product[beams:, width:]).astype(jnp.bfloat16),
        (product[:beams, width:] + product[beams:, :width]).astype(jnp.bfloat16),
    )


def place_rows(padded, start, source, columns):
    width = padded.shape[1] // 2
    for part in range(2):
        target = slice(part * width, (part + 1) * width)
        padded[pl.ds(start, source.shape[1]), target] = source[part, :, columns]


def place_halos(padded, side_ref, rows, first_ref, second_ref, columns):
    even, lowest, highest = side_ref[0], side_ref[1], side_ref[2]
    margin = first_ref.shape[1]
    far = margin + rows
    place_rows(padded, pl.multiple_of(even * far, BLK), first_ref, columns)
    place_rows(padded, pl.multiple_of((1 - even) * far, BLK), second_ref, columns)
    zeros = jnp.zeros((margin, padded.shape[1]), padded.dtype)

    @pl.when(lowest == 1)
    def _():
        padded[:margin, :] = zeros

    @pl.when(highest == 1)
    def _():
        padded[far:, :] = zeros


def first_level_kernel(
    column, rows, starts_ref, side_ref, sent_first_ref, sent_second_ref, first_ref, second_ref,
    weights_ref, out_ref, padded,
):
    sectors, stacked, window = weights_ref.shape
    beams = stacked // 2
    margin = first_ref.shape[1]
    columns = slice(column, column + out_ref.shape[2])
    even = side_ref[0]
    tail = pl.multiple_of(margin + even * (rows - margin), BLK)
    head = pl.multiple_of(margin + (1 - even) * (rows - margin), BLK)
    place_rows(padded, tail, sent_first_ref, columns)
    place_rows(padded, head, sent_second_ref, columns)
    place_halos(padded, side_ref, rows, first_ref, second_ref, columns)
    for sector in range(sectors):
        place = pl.ds(pl.multiple_of(starts_ref[sector] * BLK, BLK), window)
        parts = complex_window(weights_ref[sector], padded[place, :])
        for part in range(2):
            out_ref[part, sector * beams : (sector + 1) * beams, :] = parts[part]


def first_level(column, rows, starts, side, sent, halos, weights):
    sectors, stacked, window = weights.shape
    margin, rng = sent[0].shape[1:]
    assert 2 * margin >= rows
    width = rng // 2
    return pl.pallas_call(
        functools.partial(first_level_kernel, column, rows),
        out_shape=jax.ShapeDtypeStruct((2, sectors * stacked // 2, width), jnp.bfloat16),
        in_specs=[SMEM, SMEM] + [VMEM] * 5,
        out_specs=VMEM,
        scratch_shapes=[pltpu.VMEM((rows + 2 * margin, 2 * width), jnp.bfloat16)],
        compiler_params=params(),
        cost_estimate=cost(sectors * 2 * stacked * window * width, 2**21),
        name="first_level",
    )(starts, side, *sent, *halos, weights)


def second_level_early_kernel(
    starts_ref, side_ref, sector_ref, own_ref, first_ref, second_ref, weights_ref, send_ref, padded
):
    _, stacked, window = weights_ref.shape
    per = stacked // 2 // OS
    margin, rows = first_ref.shape[1], own_ref.shape[1]
    columns = slice(send_ref.shape[3], 2 * send_ref.shape[3])
    place_rows(padded, margin, own_ref, columns)
    place_halos(padded, side_ref, rows, first_ref, second_ref, columns)
    for place in range(send_ref.shape[0]):
        sector = sector_ref[place] // per
        piece = pl.multiple_of(sector_ref[place] % per * OS, OS)
        window_rows = pl.ds(pl.multiple_of(starts_ref[sector] * BLK, BLK), window)
        weights = jnp.concatenate(
            [
                weights_ref[sector, pl.ds(piece, OS), :],
                weights_ref[sector, pl.ds(pl.multiple_of(piece + stacked // 2, OS), OS), :],
            ]
        )
        parts = complex_window(weights, padded[window_rows, :])
        for part in range(2):
            send_ref[place, part] = parts[part]


def second_level_kernel(
    starts_ref, side_ref, own_at_ref, other_at_ref, own_ref, first_ref, second_ref, weights_ref,
    keep_ref, send_ref, padded, send,
):
    sectors, stacked, window = weights_ref.shape
    beams = stacked // 2
    width = keep_ref.shape[3]
    margin, rows = first_ref.shape[1], own_ref.shape[1]
    columns = slice(0, 2 * width)
    place_rows(padded, margin, own_ref, columns)
    place_halos(padded, side_ref, rows, first_ref, second_ref, columns)
    per = beams // OS
    for sector in range(sectors):
        place = pl.ds(pl.multiple_of(starts_ref[sector] * BLK, BLK), window)
        parts = complex_window(weights_ref[sector], padded[place, :])
        for piece in range(per):
            own_at = own_at_ref[sector * per + piece]
            other_at = other_at_ref[sector * per + piece]
            taken = slice(piece * OS, (piece + 1) * OS)
            for part in range(2):
                keep_ref[own_at, part] = parts[part][taken, :width]
                send[other_at, part] = parts[part][taken, width:]
    send_ref[...] = send[send.shape[0] - send_ref.shape[0] :]


def second_level(starts, side, planned, own, halos, weights, early):
    sectors, stacked, window = weights.shape
    margin, rows, rng = halos[0].shape[1], own.shape[1], own.shape[2]
    count = sectors * stacked // 2 // OS
    block = (2, OS, rng // 2)
    own_at, other_at, other_sector = planned
    early_send = pl.pallas_call(
        second_level_early_kernel,
        out_shape=jax.ShapeDtypeStruct((early,) + block, jnp.bfloat16),
        in_specs=[SMEM] * 3 + [VMEM] * 4,
        out_specs=VMEM,
        scratch_shapes=[pltpu.VMEM((rows + 2 * margin, rng), jnp.bfloat16)],
        compiler_params=params(),
        cost_estimate=cost(early * 2 * 2 * OS * window * rng // 2, 2**20),
        name="second_level_early",
    )(starts, side, other_sector, own, *halos, weights)
    shapes = [jax.ShapeDtypeStruct((n,) + block, jnp.bfloat16) for n in (count, count - early)]
    keep, late_send = pl.pallas_call(
        second_level_kernel,
        out_shape=shapes,
        in_specs=[SMEM] * 4 + [VMEM] * 4,
        out_specs=[VMEM] * 2,
        scratch_shapes=[
            pltpu.VMEM((rows + 2 * margin, 2 * rng), jnp.bfloat16),
            pltpu.VMEM((count,) + block, jnp.bfloat16),
        ],
        compiler_params=params(),
        cost_estimate=cost(sectors * 2 * stacked * window * rng, 2**22),
        name="second_level",
    )(starts, side, own_at, other_at, own, *halos, weights)
    return keep, early_send, late_send


def plan_kernel(
    shift, me_ref, own_ref, other_ref, own_at_ref, other_at_ref, other_sector_ref, target_ref, rank_ref,
    taken, filled,
):
    count = own_ref.shape[0]
    far_bit = taken.shape[0] // 2

    def delay(target):
        distance = target ^ me_ref[0]
        return jnp.where((distance & far_bit) == 0, 2 * count, (distance & 1) * shift)

    for owners_ref, at_ref in ((other_ref, other_at_ref), (own_ref, own_at_ref)):
        for target in range(taken.shape[0]):
            taken[target] = 0
        for bucket in range(filled.shape[0]):
            filled[bucket] = 0
        for sector in range(count):
            target = owners_ref[sector]
            rank = taken[target]
            taken[target] = rank + 1
            bucket = rank + delay(target)
            at_ref[sector] = bucket
            filled[bucket + 1] = filled[bucket + 1] + 1
        for bucket in range(1, filled.shape[0]):
            filled[bucket] = filled[bucket] + filled[bucket - 1]
        for sector in range(count):
            bucket = at_ref[sector]
            place = filled[bucket]
            filled[bucket] = place + 1
            at_ref[sector] = place
            if at_ref is own_at_ref:
                target_ref[place] = owners_ref[sector]
                rank_ref[place] = bucket - delay(owners_ref[sector])
            else:
                other_sector_ref[place] = sector


def plan(shift, me, own, other, beam_count):
    count = own.shape[0]
    shape = jax.ShapeDtypeStruct((count,), jnp.int32)
    return pl.pallas_call(
        functools.partial(plan_kernel, shift),
        out_shape=[shape] * 5,
        in_specs=[SMEM] * 3,
        out_specs=[SMEM] * 5,
        scratch_shapes=[
            pltpu.SMEM((beam_count,), jnp.int32),
            pltpu.SMEM((3 * count + 1,), jnp.int32),
        ],
        compiler_params=params(),
        name="plan",
    )(me, own, other)


def wires_kernel(spans, early, me_ref, target_ref, rank_ref, keep_ref, *refs):
    wires = refs[-1]
    spare = wires.shape[0] - 1
    out_refs = refs[-1 - len(spans) : -1]
    other_ref, *summed_refs = refs[: -1 - len(spans)]
    wires[...] = jnp.zeros_like(wires)
    me = me_ref[0]

    def lay(place, total):
        rank = rank_ref[place]
        distance = target_ref[place] ^ me
        at = spare
        start = 0
        for number, low, high in spans:
            wanted = (distance == number) & (rank >= low) & (rank < high)
            at = jnp.where(wanted, start + rank - low, at)
            start += high - low
        wires[at] = total

    before = 0
    if not early:
        before = summed_refs[0].shape[0]
        for row in range(before):
            lay(row, summed_refs[0][row])
    for row in range(other_ref.shape[0]):
        place = before + row
        total = keep_ref[place].astype(jnp.float32) + other_ref[row].astype(jnp.float32)
        total = total.astype(jnp.bfloat16)
        lay(place, total)
        if early:
            summed_refs[0][row] = total
    start = 0
    for (_, low, high), ref in zip(spans, out_refs):
        ref[...] = wires[start : start + high - low]
        start += high - low


def wires(spans, me, target, rank, keep, other, summed=None):
    block = keep.shape[1:]
    sizes = [high - low for _, low, high in spans]
    inputs = [me, target, rank, keep, other]
    if summed is None:
        sizes = [other.shape[0]] + sizes
    else:
        inputs.append(summed)
    shapes = [jax.ShapeDtypeStruct((size,) + block, jnp.bfloat16) for size in sizes]
    total = sum(high - low for _, low, high in spans)
    return pl.pallas_call(
        functools.partial(wires_kernel, spans, summed is None),
        out_shape=shapes,
        in_specs=[SMEM] * 3 + [VMEM] * (len(inputs) - 3),
        out_specs=[VMEM] * len(shapes),
        scratch_shapes=[pltpu.VMEM((total + 1,) + block, jnp.bfloat16)],
        compiler_params=params(),
        cost_estimate=cost(0, 2**21),
        name="early_wires" if summed is None else "late_wires",
    )(*inputs)


def collect_kernel(spans, capacity, me_ref, *refs):
    sems = refs[-1]
    out_ref = refs[-2]
    copies = []
    for number, (distance, low, high) in enumerate(spans):
        start = (me_ref[0] ^ distance) * capacity + low
        copies.append(
            pltpu.make_async_copy(
                refs[number], out_ref.at[pl.ds(start, high - low)], sems.at[number]
            )
        )
    for copy in copies:
        copy.start()
    for copy in copies:
        copy.wait()


def collect(spans, capacity, beam_count, me, received):
    shape = (beam_count * capacity,) + received[0].shape[1:]
    return pl.pallas_call(
        functools.partial(collect_kernel, spans, capacity),
        out_shape=jax.ShapeDtypeStruct(shape, jnp.bfloat16),
        in_specs=[SMEM] + [ANY] * len(received),
        out_specs=ANY,
        scratch_shapes=[pltpu.SemaphoreType.DMA((len(received),))],
        compiler_params=params(),
        cost_estimate=cost(0, 2**21),
        name="collect",
    )(me, *received)


def spread(spans, group):
    count = lax.axis_size("beam")
    received = []
    for (distance, _, _), wire in zip(spans, group):
        route = [(place, place ^ distance) for place in range(count)]
        received.append(lax.ppermute(wire, "beam", route) if distance else wire)
    return received


def stacked_weights(weights):
    return weights[0].reshape(weights.shape[1], -1, weights.shape[4])


def table_row(table, row_number):
    return lax.dynamic_index_in_dim(table, row_number, 0, keepdims=False)


def local(subimages, range_kernel, weights0, starts0, weights1, starts1, owners):
    aper_index = lax.axis_index("aperture")
    beam_index = lax.axis_index("beam")
    beam_count = lax.axis_size("beam")
    margin = MARGIN_BLOCKS * BLK
    rows = subimages.shape[2]
    local_blocks = rows // BLK
    even = (beam_index + 1) % 2
    ends = (beam_index == 0, beam_index == beam_count - 1)
    ends = [end.astype(jnp.int32) for end in ends]
    inner_side, side = jnp.stack([1 - even] + ends), jnp.stack([even] + ends)
    me = beam_index.reshape(1)

    sector_count = owners.shape[1]
    capacity = max(2, 2 * sector_count // beam_count)
    shorter, longer = max(1, capacity // 4), max(1, capacity // 2)
    far = range(beam_count // 2, beam_count)
    odd = [distance for distance in far if distance % 2]
    others = [distance for distance in far if distance % 2 == 0]
    early = len(odd) * shorter + len(others) * longer
    early_spans = [(distance, 0, shorter) for distance in odd]
    early_spans += [(distance, 0, longer) for distance in others]
    late_spans = [(distance, shorter, capacity) for distance in odd]
    for distance in range(1, beam_count // 2):
        cut = (5 * capacity + 4) // 8
        late_spans += [(distance, 0, cut), (distance, cut, capacity)]
    late_spans.append((0, 0, capacity))
    last_spans = [(distance, longer, capacity) for distance in others]

    sent = resample(subimages[0], range_kernel[0], margin)
    halos = trade_edges(*sent, 1)
    own_owners = owners[0, :, 0]
    other_owners = partner(owners, "aperture", 1)[0, :, 0]
    planned = plan(longer - shorter, me, own_owners, other_owners, beam_count)
    begin0 = table_row(starts0, aper_index) - (beam_index * local_blocks - MARGIN_BLOCKS)
    halos, planned = lax.optimization_barrier((halos, planned))
    *planned, target, rank = planned
    width = range_kernel.shape[3] // 2
    weights = stacked_weights(weights0)
    send = first_level(width, rows, begin0, inner_side, sent, halos, weights)
    other = partner(send, "aperture", 0)
    keep = first_level(0, rows, begin0, inner_side, sent, halos, weights)
    level_one = (keep.astype(jnp.float32) + other.astype(jnp.float32)).astype(jnp.bfloat16)

    level_one, weights1 = lax.optimization_barrier((level_one, weights1))
    beams = level_one.shape[1]
    first = lax.dynamic_slice_in_dim(level_one, even * (beams - margin), margin, 1)
    second = lax.dynamic_slice_in_dim(level_one, (1 - even) * (beams - margin), margin, 1)
    halos = trade_edges(first, second, 0)
    begin1 = table_row(starts1, aper_index) - (beam_index * 2 * local_blocks - MARGIN_BLOCKS)
    keep, send, late = second_level(
        begin1, side, planned, level_one, halos, stacked_weights(weights1), early
    )
    other = partner(send, "aperture", 1)
    other, late = lax.optimization_barrier((other, late))
    late = partner(late, "aperture", 1)
    summed, *group = wires(early_spans, me, target, rank, keep, other)
    received = spread(early_spans, group)
    from_odd, from_others = received[: len(odd)], received[len(odd) :]
    ready, from_odd = lax.optimization_barrier((late, from_odd))
    group = wires(late_spans, me, target, rank, keep, ready, summed)
    received = from_odd + spread(late_spans, group)
    ready, from_others = lax.optimization_barrier((late, from_others))
    group = wires(last_spans, me, target, rank, keep, ready, summed)
    received += from_others + spread(last_spans, group)
    spans = early_spans[: len(odd)] + late_spans + early_spans[len(odd) :] + last_spans
    return collect(spans, capacity, beam_count, me, received)[None]


def solution(mesh):
    return jax.shard_map(
        local,
        mesh=mesh,
        in_specs=(
            P("aperture", None, "beam", None),
            P("aperture", None, None, None),
            P("aperture", "beam", None, None, None),
            P(None, "beam"),
            P("aperture", "beam", None, None, None),
            P(None, "beam"),
            P("aperture", "beam", None),
        ),
        out_specs=P("aperture", "beam", None, None, None),
        check_vma=False,
    )
```

```python
import functools

import jax
import jax.numpy as jnp
from jax import lax
from jax.experimental import pallas as pl
from jax.experimental.pallas import tpu as pltpu
from jax.sharding import PartitionSpec as P

BLK = 32
NW = 10
REACH = 2
OS = 64
MARGIN_BLOCKS = (NW - 2) // 2 + REACH
VMEM_LIMIT = 8 * 1024 * 1024
MOST_VMEM = 53 * 1024 * 1024
ANY = pl.BlockSpec(memory_space=pl.ANY)
VMEM = pl.BlockSpec(memory_space=pltpu.VMEM)
SMEM = pl.BlockSpec(memory_space=pltpu.SMEM)


def params(limit=VMEM_LIMIT):
    return pltpu.CompilerParams(vmem_limit_bytes=limit)


def cost(macs, moved):
    return pl.CostEstimate(flops=2 * macs, bytes_accessed=moved, transcendentals=0)


def trade_edges(first, second):
    count, apertures = lax.axis_size("beam"), lax.axis_size("aperture")
    received = []
    for order, block in enumerate((first, second)):
        route = []
        for aper in range(apertures):
            for place in range(count):
                other = place + 1 if (place - order) % 2 == 1 else place - 1
                if 0 <= other < count:
                    to = aper * count + other
                else:
                    to = min(aper ^ 1, apertures - 1) * count + place
                route.append((aper * count + place, to))
        received.append(lax.ppermute(block, ("aperture", "beam"), route))
    return received


def partner(block, axis, distance):
    count = lax.axis_size(axis)
    route = []
    for low in range(count):
        high = low | 1 << distance
        if high != low and high < count:
            route += [(low, high), (high, low)]
    return lax.ppermute(block, axis, route)


def dot(left, right):
    return jnp.dot(left, right, preferred_element_type=jnp.float32)


def resample_kernel(child_hbm, kernel_hbm, first_ref, second_ref, child, kernel, own, sems):
    aper, beam = lax.axis_index("aperture"), lax.axis_index("beam")
    half, quarter = aper & 1, (aper >> 1) & 1
    odd = beam & 1
    rows, rng = child.shape[1:]
    piece = rng // 4
    child_copy = pltpu.make_async_copy(child_hbm, child, sems.at[4])
    copies = []
    for place in range(4):
        source = (half ^ (place // 2)) * 2 + (quarter ^ (place % 2))
        copies.append(
            pltpu.make_async_copy(
                kernel_hbm.at[:, :, pl.ds(pl.multiple_of(source * piece, 128), piece)],
                kernel.at[:, :, place * piece : (place + 1) * piece],
                sems.at[place],
            )
        )
    child_copy.start()
    for copy in copies:
        copy.start()
    child_copy.wait()
    real, imag = child[0], child[1]
    margin = first_ref.shape[1]
    tail = pl.ds(pl.multiple_of(odd * (rows - margin), BLK), margin)
    head = pl.ds(pl.multiple_of((1 - odd) * (rows - margin), BLK), margin)
    for side in range(2):
        columns = slice(side * 2 * piece, (side + 1) * 2 * piece)
        copies[2 * side].wait()
        copies[2 * side + 1].wait()
        k_real, k_imag = kernel[0, :, columns], kernel[1, :, columns]
        own[0, :, columns] = (dot(real, k_real) - dot(imag, k_imag)).astype(jnp.bfloat16)
        own[1, :, columns] = (dot(real, k_imag) + dot(imag, k_real)).astype(jnp.bfloat16)
        for part in range(2):
            first_ref[part, :, columns] = own[part, tail, columns]
            second_ref[part, :, columns] = own[part, head, columns]


def resample(child, kernel, margin):
    rows, rng = child.shape[1:]
    shape = jax.ShapeDtypeStruct((2, margin, rng), jnp.bfloat16)
    return pl.pallas_call(
        resample_kernel,
        out_shape=(shape, shape),
        in_specs=[ANY, ANY],
        out_specs=(VMEM, VMEM),
        scratch_shapes=[
            pltpu.VMEM(child.shape, jnp.bfloat16),
            pltpu.VMEM(kernel.shape, jnp.bfloat16),
            pltpu.VMEM(child.shape, jnp.bfloat16),
            pltpu.SemaphoreType.DMA((5,)),
        ],
        compiler_params=params(MOST_VMEM),
        cost_estimate=cost(4 * rows * rng * rng, 2**21),
        name="resample",
    )(child, kernel)


def complex_window(weights, window):
    beams, width = weights.shape[0] // 2, window.shape[1] // 2
    product = dot(weights, window)
    return (
        (product[:beams, :width] - product[beams:, width:]).astype(jnp.bfloat16),
        (product[:beams, width:] + product[beams:, :width]).astype(jnp.bfloat16),
    )


def place_rows(padded, start, source, columns):
    width = padded.shape[1] // 2
    for part in range(2):
        target = slice(part * width, (part + 1) * width)
        padded[pl.ds(start, source.shape[1]), target] = source[part, :, columns]


def place_halos(padded, side_ref, rows, first_ref, second_ref, columns):
    odd, lowest, highest = side_ref[0], side_ref[1], side_ref[2]
    margin = first_ref.shape[1]
    far = margin + rows
    place_rows(padded, pl.multiple_of(odd * far, BLK), first_ref, columns)
    place_rows(padded, pl.multiple_of((1 - odd) * far, BLK), second_ref, columns)
    zeros = jnp.zeros((margin, padded.shape[1]), padded.dtype)

    @pl.when(lowest == 1)
    def _():
        padded[:margin, :] = zeros

    @pl.when(highest == 1)
    def _():
        padded[far:, :] = zeros


def first_level_kernel(
    column, rows, starts_ref, side_ref, sent_first_ref, sent_second_ref, first_ref, second_ref,
    weights_ref, out_ref, padded,
):
    sectors, stacked, window = weights_ref.shape
    beams = stacked // 2
    margin = first_ref.shape[1]
    columns = slice(column, column + out_ref.shape[2])
    odd = side_ref[0]
    tail = pl.multiple_of(margin + odd * (rows - margin), BLK)
    head = pl.multiple_of(margin + (1 - odd) * (rows - margin), BLK)
    place_rows(padded, tail, sent_first_ref, columns)
    place_rows(padded, head, sent_second_ref, columns)
    place_halos(padded, side_ref, rows, first_ref, second_ref, columns)
    for sector in range(sectors):
        place = pl.ds(pl.multiple_of(starts_ref[sector] * BLK, BLK), window)
        parts = complex_window(weights_ref[sector], padded[place, :])
        for part in range(2):
            out_ref[part, sector * beams : (sector + 1) * beams, :] = parts[part]


def first_level(column, rows, starts, side, sent, halos, weights):
    sectors, stacked, window = weights.shape
    margin, rng = sent[0].shape[1:]
    assert 2 * margin >= rows
    width = rng // 2
    return pl.pallas_call(
        functools.partial(first_level_kernel, column, rows),
        out_shape=jax.ShapeDtypeStruct((2, sectors * stacked // 2, width), jnp.bfloat16),
        in_specs=[SMEM, SMEM] + [VMEM] * 5,
        out_specs=VMEM,
        scratch_shapes=[pltpu.VMEM((rows + 2 * margin, 2 * width), jnp.bfloat16)],
        compiler_params=params(),
        cost_estimate=cost(sectors * 2 * stacked * window * width, 2**21),
        name="first_level",
    )(starts, side, *sent, *halos, weights)


def second_level_early_kernel(
    starts_ref, side_ref, sector_ref, own_ref, first_ref, second_ref, weights_ref, send_ref, padded
):
    _, stacked, window = weights_ref.shape
    per = stacked // 2 // OS
    margin, rows = first_ref.shape[1], own_ref.shape[1]
    columns = slice(send_ref.shape[3], 2 * send_ref.shape[3])
    place_rows(padded, margin, own_ref, columns)
    place_halos(padded, side_ref, rows, first_ref, second_ref, columns)
    for place in range(send_ref.shape[0]):
        sector = sector_ref[place] // per
        piece = pl.multiple_of(sector_ref[place] % per * OS, OS)
        window_rows = pl.ds(pl.multiple_of(starts_ref[sector] * BLK, BLK), window)
        weights = jnp.concatenate(
            [
                weights_ref[sector, pl.ds(piece, OS), :],
                weights_ref[sector, pl.ds(pl.multiple_of(piece + stacked // 2, OS), OS), :],
            ]
        )
        parts = complex_window(weights, padded[window_rows, :])
        for part in range(2):
            send_ref[place, part] = parts[part]


def second_level_kernel(
    starts_ref, side_ref, own_at_ref, other_at_ref, own_ref, first_ref, second_ref, weights_ref,
    keep_ref, send_ref, padded, send,
):
    sectors, stacked, window = weights_ref.shape
    beams = stacked // 2
    width = keep_ref.shape[3]
    margin, rows = first_ref.shape[1], own_ref.shape[1]
    columns = slice(0, 2 * width)
    place_rows(padded, margin, own_ref, columns)
    place_halos(padded, side_ref, rows, first_ref, second_ref, columns)
    per = beams // OS
    for sector in range(sectors):
        place = pl.ds(pl.multiple_of(starts_ref[sector] * BLK, BLK), window)
        parts = complex_window(weights_ref[sector], padded[place, :])
        for piece in range(per):
            own_at = own_at_ref[sector * per + piece]
            other_at = other_at_ref[sector * per + piece]
            taken = slice(piece * OS, (piece + 1) * OS)
            for part in range(2):
                keep_ref[own_at, part] = parts[part][taken, :width]
                send[other_at, part] = parts[part][taken, width:]
    send_ref[...] = send[send.shape[0] - send_ref.shape[0] :]


def second_level(starts, side, planned, own, halos, weights, early):
    sectors, stacked, window = weights.shape
    margin, rows, rng = halos[0].shape[1], own.shape[1], own.shape[2]
    count = sectors * stacked // 2 // OS
    block = (2, OS, rng // 2)
    own_at, other_at, other_sector = planned
    early_send = pl.pallas_call(
        second_level_early_kernel,
        out_shape=jax.ShapeDtypeStruct((early,) + block, jnp.bfloat16),
        in_specs=[SMEM] * 3 + [VMEM] * 4,
        out_specs=VMEM,
        scratch_shapes=[pltpu.VMEM((rows + 2 * margin, rng), jnp.bfloat16)],
        compiler_params=params(),
        cost_estimate=cost(early * 2 * 2 * OS * window * rng // 2, 2**20),
        name="second_level_early",
    )(starts, side, other_sector, own, *halos, weights)
    shapes = [jax.ShapeDtypeStruct((n,) + block, jnp.bfloat16) for n in (count, count - early)]
    keep, late_send = pl.pallas_call(
        second_level_kernel,
        out_shape=shapes,
        in_specs=[SMEM] * 4 + [VMEM] * 4,
        out_specs=[VMEM] * 2,
        scratch_shapes=[
            pltpu.VMEM((rows + 2 * margin, 2 * rng), jnp.bfloat16),
            pltpu.VMEM((count,) + block, jnp.bfloat16),
        ],
        compiler_params=params(),
        cost_estimate=cost(sectors * 2 * stacked * window * rng, 2**22),
        name="second_level",
    )(starts, side, own_at, other_at, own, *halos, weights)
    return keep, early_send, late_send


def plan_kernel(
    shift, me_ref, own_ref, other_ref, own_at_ref, other_at_ref, other_sector_ref, target_ref, rank_ref,
    taken, filled,
):
    count = own_ref.shape[0]
    far_bit = taken.shape[0] // 2

    def delay(target):
        distance = target ^ me_ref[0]
        return jnp.where((distance & far_bit) == 0, 2 * count, (distance & 1) * shift)

    for owners_ref, at_ref in ((other_ref, other_at_ref), (own_ref, own_at_ref)):
        for target in range(taken.shape[0]):
            taken[target] = 0
        for bucket in range(filled.shape[0]):
            filled[bucket] = 0
        for sector in range(count):
            target = owners_ref[sector]
            rank = taken[target]
            taken[target] = rank + 1
            bucket = rank + delay(target)
            at_ref[sector] = bucket
            filled[bucket + 1] = filled[bucket + 1] + 1
        for bucket in range(1, filled.shape[0]):
            filled[bucket] = filled[bucket] + filled[bucket - 1]
        for sector in range(count):
            bucket = at_ref[sector]
            place = filled[bucket]
            filled[bucket] = place + 1
            at_ref[sector] = place
            if at_ref is own_at_ref:
                target_ref[place] = owners_ref[sector]
                rank_ref[place] = bucket - delay(owners_ref[sector])
            else:
                other_sector_ref[place] = sector


def plan(shift, me, own, other, beam_count):
    count = own.shape[0]
    shape = jax.ShapeDtypeStruct((count,), jnp.int32)
    return pl.pallas_call(
        functools.partial(plan_kernel, shift),
        out_shape=[shape] * 5,
        in_specs=[SMEM] * 3,
        out_specs=[SMEM] * 5,
        scratch_shapes=[
            pltpu.SMEM((beam_count,), jnp.int32),
            pltpu.SMEM((3 * count + 1,), jnp.int32),
        ],
        compiler_params=params(),
        name="plan",
    )(me, own, other)


def wires_kernel(spans, early, me_ref, target_ref, rank_ref, keep_ref, *refs):
    wires = refs[-1]
    spare = wires.shape[0] - 1
    out_refs = refs[-1 - len(spans) : -1]
    other_ref, *summed_refs = refs[: -1 - len(spans)]
    wires[...] = jnp.zeros_like(wires)
    me = me_ref[0]

    def lay(place, total):
        rank = rank_ref[place]
        distance = target_ref[place] ^ me
        at = spare
        start = 0
        for number, low, high in spans:
            wanted = (distance == number) & (rank >= low) & (rank < high)
            at = jnp.where(wanted, start + rank - low, at)
            start += high - low
        wires[at] = total

    before = 0
    if not early:
        before = summed_refs[0].shape[0]
        for row in range(before):
            lay(row, summed_refs[0][row])
    for row in range(other_ref.shape[0]):
        place = before + row
        total = keep_ref[place].astype(jnp.float32) + other_ref[row].astype(jnp.float32)
        total = total.astype(jnp.bfloat16)
        lay(place, total)
        if early:
            summed_refs[0][row] = total
    start = 0
    for (_, low, high), ref in zip(spans, out_refs):
        ref[...] = wires[start : start + high - low]
        start += high - low


def wires(spans, me, target, rank, keep, other, summed=None):
    block = keep.shape[1:]
    sizes = [high - low for _, low, high in spans]
    inputs = [me, target, rank, keep, other]
    if summed is None:
        sizes = [other.shape[0]] + sizes
    else:
        inputs.append(summed)
    shapes = [jax.ShapeDtypeStruct((size,) + block, jnp.bfloat16) for size in sizes]
    total = sum(high - low for _, low, high in spans)
    return pl.pallas_call(
        functools.partial(wires_kernel, spans, summed is None),
        out_shape=shapes,
        in_specs=[SMEM] * 3 + [VMEM] * (len(inputs) - 3),
        out_specs=[VMEM] * len(shapes),
        scratch_shapes=[pltpu.VMEM((total + 1,) + block, jnp.bfloat16)],
        compiler_params=params(),
        cost_estimate=cost(0, 2**21),
        name="early_wires" if summed is None else "late_wires",
    )(*inputs)


def collect_kernel(spans, capacity, me_ref, *refs):
    sems = refs[-1]
    out_ref = refs[-2]
    copies = []
    for number, (distance, low, high) in enumerate(spans):
        start = (me_ref[0] ^ distance) * capacity + low
        copies.append(
            pltpu.make_async_copy(
                refs[number], out_ref.at[pl.ds(start, high - low)], sems.at[number]
            )
        )
    for copy in copies:
        copy.start()
    for copy in copies:
        copy.wait()


def collect(spans, capacity, beam_count, me, received):
    shape = (beam_count * capacity,) + received[0].shape[1:]
    return pl.pallas_call(
        functools.partial(collect_kernel, spans, capacity),
        out_shape=jax.ShapeDtypeStruct(shape, jnp.bfloat16),
        in_specs=[SMEM] + [ANY] * len(received),
        out_specs=ANY,
        scratch_shapes=[pltpu.SemaphoreType.DMA((len(received),))],
        compiler_params=params(),
        cost_estimate=cost(0, 2**21),
        name="collect",
    )(me, *received)


def spread(spans, group):
    count = lax.axis_size("beam")
    received = []
    for (distance, _, _), wire in zip(spans, group):
        route = [(place, place ^ distance) for place in range(count)]
        received.append(lax.ppermute(wire, "beam", route) if distance else wire)
    return received


def stacked_weights(weights):
    return weights[0].reshape(weights.shape[1], -1, weights.shape[4])


def table_row(table, row_number):
    return lax.dynamic_index_in_dim(table, row_number, 0, keepdims=False)


def local(subimages, range_kernel, weights0, starts0, weights1, starts1, owners):
    aper_index = lax.axis_index("aperture")
    beam_index = lax.axis_index("beam")
    beam_count = lax.axis_size("beam")
    margin = MARGIN_BLOCKS * BLK
    rows = subimages.shape[2]
    local_blocks = rows // BLK
    upper = beam_index % 2
    ends = (beam_index == 0, beam_index == beam_count - 1)
    ends = [end.astype(jnp.int32) for end in ends]
    side = jnp.stack([upper] + ends)
    me = beam_index.reshape(1)

    sector_count = owners.shape[1]
    capacity = max(2, 2 * sector_count // beam_count)
    shorter, longer = max(1, capacity // 4), max(1, capacity // 2)
    far = range(beam_count // 2, beam_count)
    odd = [distance for distance in far if distance % 2]
    others = [distance for distance in far if distance % 2 == 0]
    early = len(odd) * shorter + len(others) * longer
    early_spans = [(distance, 0, shorter) for distance in odd]
    early_spans += [(distance, 0, longer) for distance in others]
    late_spans = [(distance, shorter, capacity) for distance in odd]
    for distance in range(1, beam_count // 2):
        cut = (5 * capacity + 4) // 8
        late_spans += [(distance, 0, cut), (distance, cut, capacity)]
    late_spans.append((0, 0, capacity))
    last_spans = [(distance, longer, capacity) for distance in others]

    sent = resample(subimages[0], range_kernel[0], margin)
    halos = trade_edges(*sent)
    own_owners = owners[0, :, 0]
    other_owners = partner(owners, "aperture", 1)[0, :, 0]
    planned = plan(longer - shorter, me, own_owners, other_owners, beam_count)
    begin0 = table_row(starts0, aper_index) - (beam_index * local_blocks - MARGIN_BLOCKS)
    halos, planned = lax.optimization_barrier((halos, planned))
    *planned, target, rank = planned
    width = range_kernel.shape[3] // 2
    weights = stacked_weights(weights0)
    send = first_level(width, rows, begin0, side, sent, halos, weights)
    other = partner(send, "aperture", 0)
    keep = first_level(0, rows, begin0, side, sent, halos, weights)
    level_one = (keep.astype(jnp.float32) + other.astype(jnp.float32)).astype(jnp.bfloat16)

    level_one, weights1 = lax.optimization_barrier((level_one, weights1))
    beams = level_one.shape[1]
    first = lax.dynamic_slice_in_dim(level_one, upper * (beams - margin), margin, 1)
    second = lax.dynamic_slice_in_dim(level_one, (1 - upper) * (beams - margin), margin, 1)
    halos = trade_edges(first, second)
    begin1 = table_row(starts1, aper_index) - (beam_index * 2 * local_blocks - MARGIN_BLOCKS)
    keep, send, late = second_level(
        begin1, side, planned, level_one, halos, stacked_weights(weights1), early
    )
    other = partner(send, "aperture", 1)
    other, late = lax.optimization_barrier((other, late))
    late = partner(late, "aperture", 1)
    summed, *group = wires(early_spans, me, target, rank, keep, other)
    received = spread(early_spans, group)
    from_odd, from_others = received[: len(odd)], received[len(odd) :]
    ready, from_odd = lax.optimization_barrier((late, from_odd))
    group = wires(late_spans, me, target, rank, keep, ready, summed)
    received = from_odd + spread(late_spans, group)
    ready, from_others = lax.optimization_barrier((late, from_others))
    group = wires(last_spans, me, target, rank, keep, ready, summed)
    received += from_others + spread(last_spans, group)
    spans = early_spans[: len(odd)] + late_spans + early_spans[len(odd) :] + last_spans
    return collect(spans, capacity, beam_count, me, received)[None]


def solution(mesh):
    return jax.shard_map(
        local,
        mesh=mesh,
        in_specs=(
            P("aperture", None, "beam", None),
            P("aperture", None, None, None),
            P("aperture", "beam", None, None, None),
            P(None, "beam"),
            P("aperture", "beam", None, None, None),
            P(None, "beam"),
            P("aperture", "beam", None),
        ),
        out_specs=P("aperture", "beam", None, None, None),
        check_vma=False,
    )
```

```python
import functools

import jax
import jax.numpy as jnp
from jax import lax
from jax.experimental import pallas as pl
from jax.experimental.pallas import tpu as pltpu
from jax.sharding import PartitionSpec as P

BLK = 32
NW = 10
REACH = 2
OS = 64
MARGIN_BLOCKS = (NW - 2) // 2 + REACH
VMEM_LIMIT = 8 * 1024 * 1024
MOST_VMEM = 53 * 1024 * 1024
ANY = pl.BlockSpec(memory_space=pl.ANY)
VMEM = pl.BlockSpec(memory_space=pltpu.VMEM)
SMEM = pl.BlockSpec(memory_space=pltpu.SMEM)


def params(limit=VMEM_LIMIT):
    return pltpu.CompilerParams(vmem_limit_bytes=limit)


def cost(macs, moved):
    return pl.CostEstimate(flops=2 * macs, bytes_accessed=moved, transcendentals=0)


def trade_edges(first, second):
    count, apertures = lax.axis_size("beam"), lax.axis_size("aperture")
    received = []
    for order, block in enumerate((first, second)):
        route = []
        for aper in range(apertures):
            for place in range(count):
                other = place + 1 if (place - order) % 2 == 0 else place - 1
                if 0 <= other < count:
                    to = aper * count + other
                else:
                    to = min(aper ^ 1, apertures - 1) * count + place
                route.append((aper * count + place, to))
        received.append(lax.ppermute(block, ("aperture", "beam"), route))
    return received


def partner(block, axis, distance):
    count = lax.axis_size(axis)
    route = []
    for low in range(count):
        high = low | 1 << distance
        if high != low and high < count:
            route += [(low, high), (high, low)]
    return lax.ppermute(block, axis, route)


def dot(left, right):
    return jnp.dot(left, right, preferred_element_type=jnp.float32)


def resample_kernel(child_hbm, kernel_hbm, first_ref, second_ref, child, kernel, own, sems):
    aper, beam = lax.axis_index("aperture"), lax.axis_index("beam")
    half, quarter = aper & 1, (aper >> 1) & 1
    even = 1 - (beam & 1)
    rows, rng = child.shape[1:]
    piece = rng // 4
    child_copy = pltpu.make_async_copy(child_hbm, child, sems.at[4])
    copies = []
    for place in range(4):
        source = (half ^ (place // 2)) * 2 + (quarter ^ (place % 2))
        copies.append(
            pltpu.make_async_copy(
                kernel_hbm.at[:, :, pl.ds(pl.multiple_of(source * piece, 128), piece)],
                kernel.at[:, :, place * piece : (place + 1) * piece],
                sems.at[place],
            )
        )
    child_copy.start()
    for copy in copies:
        copy.start()
    child_copy.wait()
    real, imag = child[0], child[1]
    margin = first_ref.shape[1]
    tail = pl.ds(pl.multiple_of(even * (rows - margin), BLK), margin)
    head = pl.ds(pl.multiple_of((1 - even) * (rows - margin), BLK), margin)
    for side in range(2):
        columns = slice(side * 2 * piece, (side + 1) * 2 * piece)
        copies[2 * side].wait()
        copies[2 * side + 1].wait()
        k_real, k_imag = kernel[0, :, columns], kernel[1, :, columns]
        own[0, :, columns] = (dot(real, k_real) - dot(imag, k_imag)).astype(jnp.bfloat16)
        own[1, :, columns] = (dot(real, k_imag) + dot(imag, k_real)).astype(jnp.bfloat16)
        for part in range(2):
            first_ref[part, :, columns] = own[part, tail, columns]
            second_ref[part, :, columns] = own[part, head, columns]


def resample(child, kernel, margin):
    rows, rng = child.shape[1:]
    shape = jax.ShapeDtypeStruct((2, margin, rng), jnp.bfloat16)
    return pl.pallas_call(
        resample_kernel,
        out_shape=(shape, shape),
        in_specs=[ANY, ANY],
        out_specs=(VMEM, VMEM),
        scratch_shapes=[
            pltpu.VMEM(child.shape, jnp.bfloat16),
            pltpu.VMEM(kernel.shape, jnp.bfloat16),
            pltpu.VMEM(child.shape, jnp.bfloat16),
            pltpu.SemaphoreType.DMA((5,)),
        ],
        compiler_params=params(MOST_VMEM),
        cost_estimate=cost(4 * rows * rng * rng, 2**21),
        name="resample",
    )(child, kernel)


def complex_window(weights, window):
    beams, width = weights.shape[0] // 2, window.shape[1] // 2
    product = dot(weights, window)
    return (
        (product[:beams, :width] - product[beams:, width:]).astype(jnp.bfloat16),
        (product[:beams, width:] + product[beams:, :width]).astype(jnp.bfloat16),
    )


def place_rows(padded, start, source, columns):
    width = padded.shape[1] // 2
    for part in range(2):
        target = slice(part * width, (part + 1) * width)
        padded[pl.ds(start, source.shape[1]), target] = source[part, :, columns]


def place_halos(padded, side_ref, rows, first_ref, second_ref, columns):
    even, lowest, highest = side_ref[0], side_ref[1], side_ref[2]
    margin = first_ref.shape[1]
    far = margin + rows
    place_rows(padded, pl.multiple_of(even * far, BLK), first_ref, columns)
    place_rows(padded, pl.multiple_of((1 - even) * far, BLK), second_ref, columns)
    zeros = jnp.zeros((margin, padded.shape[1]), padded.dtype)

    @pl.when(lowest == 1)
    def _():
        padded[:margin, :] = zeros

    @pl.when(highest == 1)
    def _():
        padded[far:, :] = zeros


def first_level_kernel(
    column, rows, starts_ref, side_ref, sent_first_ref, sent_second_ref, first_ref, second_ref,
    weights_ref, out_ref, padded,
):
    sectors, stacked, window = weights_ref.shape
    beams = stacked // 2
    margin = first_ref.shape[1]
    columns = slice(column, column + out_ref.shape[2])
    even = side_ref[0]
    tail = pl.multiple_of(margin + even * (rows - margin), BLK)
    head = pl.multiple_of(margin + (1 - even) * (rows - margin), BLK)
    place_rows(padded, tail, sent_first_ref, columns)
    place_rows(padded, head, sent_second_ref, columns)
    place_halos(padded, side_ref, rows, first_ref, second_ref, columns)
    for sector in range(sectors):
        place = pl.ds(pl.multiple_of(starts_ref[sector] * BLK, BLK), window)
        parts = complex_window(weights_ref[sector], padded[place, :])
        for part in range(2):
            out_ref[part, sector * beams : (sector + 1) * beams, :] = parts[part]


def first_level(column, rows, starts, side, sent, halos, weights):
    sectors, stacked, window = weights.shape
    margin, rng = sent[0].shape[1:]
    assert 2 * margin >= rows
    width = rng // 2
    return pl.pallas_call(
        functools.partial(first_level_kernel, column, rows),
        out_shape=jax.ShapeDtypeStruct((2, sectors * stacked // 2, width), jnp.bfloat16),
        in_specs=[SMEM, SMEM] + [VMEM] * 5,
        out_specs=VMEM,
        scratch_shapes=[pltpu.VMEM((rows + 2 * margin, 2 * width), jnp.bfloat16)],
        compiler_params=params(),
        cost_estimate=cost(sectors * 2 * stacked * window * width, 2**21),
        name="first_level",
    )(starts, side, *sent, *halos, weights)


def second_level_early_kernel(
    starts_ref, side_ref, sector_ref, own_ref, first_ref, second_ref, weights_ref, send_ref, padded
):
    _, stacked, window = weights_ref.shape
    per = stacked // 2 // OS
    margin, rows = first_ref.shape[1], own_ref.shape[1]
    columns = slice(send_ref.shape[3], 2 * send_ref.shape[3])
    place_rows(padded, margin, own_ref, columns)
    place_halos(padded, side_ref, rows, first_ref, second_ref, columns)
    for place in range(send_ref.shape[0]):
        sector = sector_ref[place] // per
        piece = pl.multiple_of(sector_ref[place] % per * OS, OS)
        window_rows = pl.ds(pl.multiple_of(starts_ref[sector] * BLK, BLK), window)
        weights = jnp.concatenate(
            [
                weights_ref[sector, pl.ds(piece, OS), :],
                weights_ref[sector, pl.ds(pl.multiple_of(piece + stacked // 2, OS), OS), :],
            ]
        )
        parts = complex_window(weights, padded[window_rows, :])
        for part in range(2):
            send_ref[place, part] = parts[part]


def second_level_kernel(
    starts_ref, side_ref, own_at_ref, other_at_ref, own_ref, first_ref, second_ref, weights_ref,
    keep_ref, send_ref, padded, send,
):
    sectors, stacked, window = weights_ref.shape
    beams = stacked // 2
    width = keep_ref.shape[3]
    margin, rows = first_ref.shape[1], own_ref.shape[1]
    columns = slice(0, 2 * width)
    place_rows(padded, margin, own_ref, columns)
    place_halos(padded, side_ref, rows, first_ref, second_ref, columns)
    per = beams // OS
    for sector in range(sectors):
        place = pl.ds(pl.multiple_of(starts_ref[sector] * BLK, BLK), window)
        parts = complex_window(weights_ref[sector], padded[place, :])
        for piece in range(per):
            own_at = own_at_ref[sector * per + piece]
            other_at = other_at_ref[sector * per + piece]
            taken = slice(piece * OS, (piece + 1) * OS)
            for part in range(2):
                keep_ref[own_at, part] = parts[part][taken, :width]
                send[other_at, part] = parts[part][taken, width:]
    send_ref[...] = send[send.shape[0] - send_ref.shape[0] :]


def second_level(starts, side, planned, own, halos, weights, early):
    sectors, stacked, window = weights.shape
    margin, rows, rng = halos[0].shape[1], own.shape[1], own.shape[2]
    count = sectors * stacked // 2 // OS
    block = (2, OS, rng // 2)
    own_at, other_at, other_sector = planned
    early_send = pl.pallas_call(
        second_level_early_kernel,
        out_shape=jax.ShapeDtypeStruct((early,) + block, jnp.bfloat16),
        in_specs=[SMEM] * 3 + [VMEM] * 4,
        out_specs=VMEM,
        scratch_shapes=[pltpu.VMEM((rows + 2 * margin, rng), jnp.bfloat16)],
        compiler_params=params(),
        cost_estimate=cost(early * 2 * 2 * OS * window * rng // 2, 2**20),
        name="second_level_early",
    )(starts, side, other_sector, own, *halos, weights)
    shapes = [jax.ShapeDtypeStruct((n,) + block, jnp.bfloat16) for n in (count, count - early)]
    keep, late_send = pl.pallas_call(
        second_level_kernel,
        out_shape=shapes,
        in_specs=[SMEM] * 4 + [VMEM] * 4,
        out_specs=[VMEM] * 2,
        scratch_shapes=[
            pltpu.VMEM((rows + 2 * margin, 2 * rng), jnp.bfloat16),
            pltpu.VMEM((count,) + block, jnp.bfloat16),
        ],
        compiler_params=params(),
        cost_estimate=cost(sectors * 2 * stacked * window * rng, 2**22),
        name="second_level",
    )(starts, side, own_at, other_at, own, *halos, weights)
    return keep, early_send, late_send


def plan_kernel(
    shift, me_ref, own_ref, other_ref, own_at_ref, other_at_ref, other_sector_ref, target_ref, rank_ref,
    taken, filled,
):
    count = own_ref.shape[0]
    far_bit = taken.shape[0] // 2

    def delay(target):
        distance = target ^ me_ref[0]
        return jnp.where((distance & far_bit) == 0, 2 * count, (distance & 1) * shift)

    for owners_ref, at_ref in ((other_ref, other_at_ref), (own_ref, own_at_ref)):
        for target in range(taken.shape[0]):
            taken[target] = 0
        for bucket in range(filled.shape[0]):
            filled[bucket] = 0
        for sector in range(count):
            target = owners_ref[sector]
            rank = taken[target]
            taken[target] = rank + 1
            bucket = rank + delay(target)
            at_ref[sector] = bucket
            filled[bucket + 1] = filled[bucket + 1] + 1
        for bucket in range(1, filled.shape[0]):
            filled[bucket] = filled[bucket] + filled[bucket - 1]
        for sector in range(count):
            bucket = at_ref[sector]
            place = filled[bucket]
            filled[bucket] = place + 1
            at_ref[sector] = place
            if at_ref is own_at_ref:
                target_ref[place] = owners_ref[sector]
                rank_ref[place] = bucket - delay(owners_ref[sector])
            else:
                other_sector_ref[place] = sector


def plan(shift, me, own, other, beam_count):
    count = own.shape[0]
    shape = jax.ShapeDtypeStruct((count,), jnp.int32)
    return pl.pallas_call(
        functools.partial(plan_kernel, shift),
        out_shape=[shape] * 5,
        in_specs=[SMEM] * 3,
        out_specs=[SMEM] * 5,
        scratch_shapes=[
            pltpu.SMEM((beam_count,), jnp.int32),
            pltpu.SMEM((3 * count + 1,), jnp.int32),
        ],
        compiler_params=params(),
        name="plan",
    )(me, own, other)


def wires_kernel(spans, early, me_ref, target_ref, rank_ref, keep_ref, *refs):
    wires = refs[-1]
    spare = wires.shape[0] - 1
    out_refs = refs[-1 - len(spans) : -1]
    other_ref, *summed_refs = refs[: -1 - len(spans)]
    wires[...] = jnp.zeros_like(wires)
    me = me_ref[0]

    def lay(place, total):
        rank = rank_ref[place]
        distance = target_ref[place] ^ me
        at = spare
        start = 0
        for number, low, high in spans:
            wanted = (distance == number) & (rank >= low) & (rank < high)
            at = jnp.where(wanted, start + rank - low, at)
            start += high - low
        wires[at] = total

    before = 0
    if not early:
        before = summed_refs[0].shape[0]
        for row in range(before):
            lay(row, summed_refs[0][row])
    for row in range(other_ref.shape[0]):
        place = before + row
        total = keep_ref[place].astype(jnp.float32) + other_ref[row].astype(jnp.float32)
        total = total.astype(jnp.bfloat16)
        lay(place, total)
        if early:
            summed_refs[0][row] = total
    start = 0
    for (_, low, high), ref in zip(spans, out_refs):
        ref[...] = wires[start : start + high - low]
        start += high - low


def wires(spans, me, target, rank, keep, other, summed=None):
    block = keep.shape[1:]
    sizes = [high - low for _, low, high in spans]
    inputs = [me, target, rank, keep, other]
    if summed is None:
        sizes = [other.shape[0]] + sizes
    else:
        inputs.append(summed)
    shapes = [jax.ShapeDtypeStruct((size,) + block, jnp.bfloat16) for size in sizes]
    total = sum(high - low for _, low, high in spans)
    return pl.pallas_call(
        functools.partial(wires_kernel, spans, summed is None),
        out_shape=shapes,
        in_specs=[SMEM] * 3 + [VMEM] * (len(inputs) - 3),
        out_specs=[VMEM] * len(shapes),
        scratch_shapes=[pltpu.VMEM((total + 1,) + block, jnp.bfloat16)],
        compiler_params=params(),
        cost_estimate=cost(0, 2**21),
        name="early_wires" if summed is None else "late_wires",
    )(*inputs)


def collect_kernel(spans, capacity, me_ref, *refs):
    sems = refs[-1]
    out_ref = refs[-2]
    copies = []
    for number, (distance, low, high) in enumerate(spans):
        start = (me_ref[0] ^ distance) * capacity + low
        copies.append(
            pltpu.make_async_copy(
                refs[number], out_ref.at[pl.ds(start, high - low)], sems.at[number]
            )
        )
    for copy in copies:
        copy.start()
    for copy in copies:
        copy.wait()


def collect(spans, capacity, beam_count, me, received):
    shape = (beam_count * capacity,) + received[0].shape[1:]
    return pl.pallas_call(
        functools.partial(collect_kernel, spans, capacity),
        out_shape=jax.ShapeDtypeStruct(shape, jnp.bfloat16),
        in_specs=[SMEM] + [ANY] * len(received),
        out_specs=ANY,
        scratch_shapes=[pltpu.SemaphoreType.DMA((len(received),))],
        compiler_params=params(),
        cost_estimate=cost(0, 2**21),
        name="collect",
    )(me, *received)


def spread(spans, group):
    count = lax.axis_size("beam")
    received = []
    for (distance, _, _), wire in zip(spans, group):
        route = [(place, place ^ distance) for place in range(count)]
        received.append(lax.ppermute(wire, "beam", route) if distance else wire)
    return received


def stacked_weights(weights):
    return weights[0].reshape(weights.shape[1], -1, weights.shape[4])


def table_row(table, row_number):
    return lax.dynamic_index_in_dim(table, row_number, 0, keepdims=False)


def local(subimages, range_kernel, weights0, starts0, weights1, starts1, owners):
    aper_index = lax.axis_index("aperture")
    beam_index = lax.axis_index("beam")
    beam_count = lax.axis_size("beam")
    margin = MARGIN_BLOCKS * BLK
    rows = subimages.shape[2]
    local_blocks = rows // BLK
    even = (beam_index + 1) % 2
    ends = (beam_index == 0, beam_index == beam_count - 1)
    side = jnp.stack([even] + [end.astype(jnp.int32) for end in ends])
    me = beam_index.reshape(1)

    sector_count = owners.shape[1]
    capacity = max(2, 2 * sector_count // beam_count)
    shorter, longer = max(1, capacity // 4), max(1, capacity // 2)
    far = range(beam_count // 2, beam_count)
    odd = [distance for distance in far if distance % 2]
    others = [distance for distance in far if distance % 2 == 0]
    early = len(odd) * shorter + len(others) * longer
    early_spans = [(distance, 0, shorter) for distance in odd]
    early_spans += [(distance, 0, longer) for distance in others]
    late_spans = [(distance, shorter, capacity) for distance in odd]
    last_spans = [(distance, longer, capacity) for distance in others]
    third = (3 * capacity + 7) // 8
    for distance in range(1, beam_count // 2):
        cuts = sorted({0, min(third, capacity), min(2 * third, capacity), capacity})
        last_spans += [(distance, low, high) for low, high in zip(cuts, cuts[1:])]
    last_spans.append((0, 0, capacity))

    sent = resample(subimages[0], range_kernel[0], margin)
    halos = trade_edges(*sent)
    own_owners = owners[0, :, 0]
    other_owners = partner(owners, "aperture", 1)[0, :, 0]
    planned = plan(longer - shorter, me, own_owners, other_owners, beam_count)
    begin0 = table_row(starts0, aper_index) - (beam_index * local_blocks - MARGIN_BLOCKS)
    halos, planned = lax.optimization_barrier((halos, planned))
    *planned, target, rank = planned
    width = range_kernel.shape[3] // 2
    weights = stacked_weights(weights0)
    send = first_level(width, rows, begin0, side, sent, halos, weights)
    other = partner(send, "aperture", 0)
    keep = first_level(0, rows, begin0, side, sent, halos, weights)
    level_one = (keep.astype(jnp.float32) + other.astype(jnp.float32)).astype(jnp.bfloat16)

    beams = level_one.shape[1]
    first = lax.dynamic_slice_in_dim(level_one, even * (beams - margin), margin, 1)
    second = lax.dynamic_slice_in_dim(level_one, (1 - even) * (beams - margin), margin, 1)
    halos = trade_edges(first, second)
    begin1 = table_row(starts1, aper_index) - (beam_index * 2 * local_blocks - MARGIN_BLOCKS)
    keep, send, late = second_level(
        begin1, side, planned, level_one, halos, stacked_weights(weights1), early
    )
    other = partner(send, "aperture", 1)
    other, late = lax.optimization_barrier((other, late))
    late = partner(late, "aperture", 1)
    summed, *group = wires(early_spans, me, target, rank, keep, other)
    received = spread(early_spans, group)
    from_odd, from_others = received[: len(odd)], received[len(odd) :]
    ready, from_odd = lax.optimization_barrier((late, from_odd))
    group = wires(late_spans, me, target, rank, keep, ready, summed)
    received = from_odd + spread(late_spans, group)
    ready, from_others = lax.optimization_barrier((late, from_others))
    group = wires(last_spans, me, target, rank, keep, ready, summed)
    received += from_others + spread(last_spans, group)
    spans = early_spans[: len(odd)] + late_spans + early_spans[len(odd) :] + last_spans
    return collect(spans, capacity, beam_count, me, received)[None]


def solution(mesh):
    return jax.shard_map(
        local,
        mesh=mesh,
        in_specs=(
            P("aperture", None, "beam", None),
            P("aperture", None, None, None),
            P("aperture", "beam", None, None, None),
            P(None, "beam"),
            P("aperture", "beam", None, None, None),
            P(None, "beam"),
            P("aperture", "beam", None),
        ),
        out_specs=P("aperture", "beam", None, None, None),
        check_vma=False,
    )
```

```python
import functools

import jax
import jax.numpy as jnp
from jax import lax
from jax.experimental import pallas as pl
from jax.experimental.pallas import tpu as pltpu
from jax.sharding import PartitionSpec as P

BLK = 32
NW = 10
REACH = 2
OS = 64
MARGIN_BLOCKS = (NW - 2) // 2 + REACH
VMEM_LIMIT = 8 * 1024 * 1024
MOST_VMEM = 53 * 1024 * 1024
ANY = pl.BlockSpec(memory_space=pl.ANY)
VMEM = pl.BlockSpec(memory_space=pltpu.VMEM)
SMEM = pl.BlockSpec(memory_space=pltpu.SMEM)


def params(limit=VMEM_LIMIT):
    return pltpu.CompilerParams(vmem_limit_bytes=limit)


def cost(macs, moved):
    return pl.CostEstimate(flops=2 * macs, bytes_accessed=moved, transcendentals=0)


def trade_edges(first, second):
    count, apertures = lax.axis_size("beam"), lax.axis_size("aperture")
    received = []
    for order, block in enumerate((first, second)):
        route = []
        for aper in range(apertures):
            for place in range(count):
                other = place + 1 if (place - order) % 2 == 0 else place - 1
                if 0 <= other < count:
                    to = aper * count + other
                else:
                    to = min(aper ^ 1, apertures - 1) * count + place
                route.append((aper * count + place, to))
        received.append(lax.ppermute(block, ("aperture", "beam"), route))
    return received


def partner(block, axis, distance):
    count = lax.axis_size(axis)
    route = []
    for low in range(count):
        high = low | 1 << distance
        if high != low and high < count:
            route += [(low, high), (high, low)]
    return lax.ppermute(block, axis, route)


def dot(left, right):
    return jnp.dot(left, right, preferred_element_type=jnp.float32)


def resample_kernel(child_hbm, kernel_hbm, first_ref, second_ref, child, kernel, own, sems):
    aper, beam = lax.axis_index("aperture"), lax.axis_index("beam")
    half, quarter = aper & 1, (aper >> 1) & 1
    even = 1 - (beam & 1)
    rows, rng = child.shape[1:]
    piece = rng // 4
    child_copy = pltpu.make_async_copy(child_hbm, child, sems.at[4])
    copies = []
    for place in range(4):
        source = (half ^ (place // 2)) * 2 + (quarter ^ (place % 2))
        copies.append(
            pltpu.make_async_copy(
                kernel_hbm.at[:, :, pl.ds(pl.multiple_of(source * piece, 128), piece)],
                kernel.at[:, :, place * piece : (place + 1) * piece],
                sems.at[place],
            )
        )
    child_copy.start()
    for copy in copies:
        copy.start()
    child_copy.wait()
    real, imag = child[0], child[1]
    margin = first_ref.shape[1]
    tail = pl.ds(pl.multiple_of(even * (rows - margin), BLK), margin)
    head = pl.ds(pl.multiple_of((1 - even) * (rows - margin), BLK), margin)
    for side in range(2):
        columns = slice(side * 2 * piece, (side + 1) * 2 * piece)
        copies[2 * side].wait()
        copies[2 * side + 1].wait()
        k_real, k_imag = kernel[0, :, columns], kernel[1, :, columns]
        own[0, :, columns] = (dot(real, k_real) - dot(imag, k_imag)).astype(jnp.bfloat16)
        own[1, :, columns] = (dot(real, k_imag) + dot(imag, k_real)).astype(jnp.bfloat16)
        for part in range(2):
            first_ref[part, :, columns] = own[part, tail, columns]
            second_ref[part, :, columns] = own[part, head, columns]


def resample(child, kernel, margin):
    rows, rng = child.shape[1:]
    shape = jax.ShapeDtypeStruct((2, margin, rng), jnp.bfloat16)
    return pl.pallas_call(
        resample_kernel,
        out_shape=(shape, shape),
        in_specs=[ANY, ANY],
        out_specs=(VMEM, VMEM),
        scratch_shapes=[
            pltpu.VMEM(child.shape, jnp.bfloat16),
            pltpu.VMEM(kernel.shape, jnp.bfloat16),
            pltpu.VMEM(child.shape, jnp.bfloat16),
            pltpu.SemaphoreType.DMA((5,)),
        ],
        compiler_params=params(MOST_VMEM),
        cost_estimate=cost(4 * rows * rng * rng, 2**21),
        name="resample",
    )(child, kernel)


def complex_window(weights, window):
    beams, width = weights.shape[0] // 2, window.shape[1] // 2
    product = dot(weights, window)
    return (
        (product[:beams, :width] - product[beams:, width:]).astype(jnp.bfloat16),
        (product[:beams, width:] + product[beams:, :width]).astype(jnp.bfloat16),
    )


def place_rows(padded, start, source, columns):
    width = padded.shape[1] // 2
    for part in range(2):
        target = slice(part * width, (part + 1) * width)
        padded[pl.ds(start, source.shape[1]), target] = source[part, :, columns]


def place_halos(padded, side_ref, rows, first_ref, second_ref, columns):
    even, lowest, highest = side_ref[0], side_ref[1], side_ref[2]
    margin = first_ref.shape[1]
    far = margin + rows
    place_rows(padded, pl.multiple_of(even * far, BLK), first_ref, columns)
    place_rows(padded, pl.multiple_of((1 - even) * far, BLK), second_ref, columns)
    zeros = jnp.zeros((margin, padded.shape[1]), padded.dtype)

    @pl.when(lowest == 1)
    def _():
        padded[:margin, :] = zeros

    @pl.when(highest == 1)
    def _():
        padded[far:, :] = zeros


def first_level_kernel(
    column, rows, starts_ref, side_ref, sent_first_ref, sent_second_ref, first_ref, second_ref,
    weights_ref, out_ref, padded,
):
    sectors, stacked, window = weights_ref.shape
    beams = stacked // 2
    margin = first_ref.shape[1]
    columns = slice(column, column + out_ref.shape[2])
    even = side_ref[0]
    tail = pl.multiple_of(margin + even * (rows - margin), BLK)
    head = pl.multiple_of(margin + (1 - even) * (rows - margin), BLK)
    place_rows(padded, tail, sent_first_ref, columns)
    place_rows(padded, head, sent_second_ref, columns)
    place_halos(padded, side_ref, rows, first_ref, second_ref, columns)
    for sector in range(sectors):
        place = pl.ds(pl.multiple_of(starts_ref[sector] * BLK, BLK), window)
        parts = complex_window(weights_ref[sector], padded[place, :])
        for part in range(2):
            out_ref[part, sector * beams : (sector + 1) * beams, :] = parts[part]


def first_level(column, rows, starts, side, sent, halos, weights):
    sectors, stacked, window = weights.shape
    margin, rng = sent[0].shape[1:]
    assert 2 * margin >= rows
    width = rng // 2
    return pl.pallas_call(
        functools.partial(first_level_kernel, column, rows),
        out_shape=jax.ShapeDtypeStruct((2, sectors * stacked // 2, width), jnp.bfloat16),
        in_specs=[SMEM, SMEM] + [VMEM] * 5,
        out_specs=VMEM,
        scratch_shapes=[pltpu.VMEM((rows + 2 * margin, 2 * width), jnp.bfloat16)],
        compiler_params=params(),
        cost_estimate=cost(sectors * 2 * stacked * window * width, 2**21),
        name="first_level",
    )(starts, side, *sent, *halos, weights)


def second_level_early_kernel(
    starts_ref, side_ref, sector_ref, own_ref, first_ref, second_ref, weights_ref, send_ref, padded
):
    _, stacked, window = weights_ref.shape
    per = stacked // 2 // OS
    margin, rows = first_ref.shape[1], own_ref.shape[1]
    columns = slice(send_ref.shape[3], 2 * send_ref.shape[3])
    place_rows(padded, margin, own_ref, columns)
    place_halos(padded, side_ref, rows, first_ref, second_ref, columns)
    for place in range(send_ref.shape[0]):
        sector = sector_ref[place] // per
        piece = pl.multiple_of(sector_ref[place] % per * OS, OS)
        window_rows = pl.ds(pl.multiple_of(starts_ref[sector] * BLK, BLK), window)
        weights = jnp.concatenate(
            [
                weights_ref[sector, pl.ds(piece, OS), :],
                weights_ref[sector, pl.ds(pl.multiple_of(piece + stacked // 2, OS), OS), :],
            ]
        )
        parts = complex_window(weights, padded[window_rows, :])
        for part in range(2):
            send_ref[place, part] = parts[part]


def second_level_kernel(
    starts_ref, side_ref, own_at_ref, other_at_ref, own_ref, first_ref, second_ref, weights_ref,
    keep_ref, send_ref, padded, send,
):
    sectors, stacked, window = weights_ref.shape
    beams = stacked // 2
    width = keep_ref.shape[3]
    margin, rows = first_ref.shape[1], own_ref.shape[1]
    columns = slice(0, 2 * width)
    place_rows(padded, margin, own_ref, columns)
    place_halos(padded, side_ref, rows, first_ref, second_ref, columns)
    per = beams // OS
    for sector in range(sectors):
        place = pl.ds(pl.multiple_of(starts_ref[sector] * BLK, BLK), window)
        parts = complex_window(weights_ref[sector], padded[place, :])
        for piece in range(per):
            own_at = own_at_ref[sector * per + piece]
            other_at = other_at_ref[sector * per + piece]
            taken = slice(piece * OS, (piece + 1) * OS)
            for part in range(2):
                keep_ref[own_at, part] = parts[part][taken, :width]
                send[other_at, part] = parts[part][taken, width:]
    send_ref[...] = send[send.shape[0] - send_ref.shape[0] :]


def second_level(starts, side, planned, own, halos, weights, early):
    sectors, stacked, window = weights.shape
    margin, rows, rng = halos[0].shape[1], own.shape[1], own.shape[2]
    count = sectors * stacked // 2 // OS
    block = (2, OS, rng // 2)
    own_at, other_at, other_sector = planned
    early_send = pl.pallas_call(
        second_level_early_kernel,
        out_shape=jax.ShapeDtypeStruct((early,) + block, jnp.bfloat16),
        in_specs=[SMEM] * 3 + [VMEM] * 4,
        out_specs=VMEM,
        scratch_shapes=[pltpu.VMEM((rows + 2 * margin, rng), jnp.bfloat16)],
        compiler_params=params(),
        cost_estimate=cost(early * 2 * 2 * OS * window * rng // 2, 2**20),
        name="second_level_early",
    )(starts, side, other_sector, own, *halos, weights)
    shapes = [jax.ShapeDtypeStruct((n,) + block, jnp.bfloat16) for n in (count, count - early)]
    keep, late_send = pl.pallas_call(
        second_level_kernel,
        out_shape=shapes,
        in_specs=[SMEM] * 4 + [VMEM] * 4,
        out_specs=[VMEM] * 2,
        scratch_shapes=[
            pltpu.VMEM((rows + 2 * margin, 2 * rng), jnp.bfloat16),
            pltpu.VMEM((count,) + block, jnp.bfloat16),
        ],
        compiler_params=params(),
        cost_estimate=cost(sectors * 2 * stacked * window * rng, 2**22),
        name="second_level",
    )(starts, side, own_at, other_at, own, *halos, weights)
    return keep, early_send, late_send


def plan_kernel(
    shift, me_ref, own_ref, other_ref, own_at_ref, other_at_ref, other_sector_ref, target_ref, rank_ref,
    taken, filled,
):
    count = own_ref.shape[0]
    far_bit = taken.shape[0] // 2

    def delay(target):
        distance = target ^ me_ref[0]
        return jnp.where((distance & far_bit) == 0, 2 * count, (distance & 1) * shift)

    for owners_ref, at_ref in ((other_ref, other_at_ref), (own_ref, own_at_ref)):
        for target in range(taken.shape[0]):
            taken[target] = 0
        for bucket in range(filled.shape[0]):
            filled[bucket] = 0
        for sector in range(count):
            target = owners_ref[sector]
            rank = taken[target]
            taken[target] = rank + 1
            bucket = rank + delay(target)
            at_ref[sector] = bucket
            filled[bucket + 1] = filled[bucket + 1] + 1
        for bucket in range(1, filled.shape[0]):
            filled[bucket] = filled[bucket] + filled[bucket - 1]
        for sector in range(count):
            bucket = at_ref[sector]
            place = filled[bucket]
            filled[bucket] = place + 1
            at_ref[sector] = place
            if at_ref is own_at_ref:
                target_ref[place] = owners_ref[sector]
                rank_ref[place] = bucket - delay(owners_ref[sector])
            else:
                other_sector_ref[place] = sector


def plan(shift, me, own, other, beam_count):
    count = own.shape[0]
    shape = jax.ShapeDtypeStruct((count,), jnp.int32)
    return pl.pallas_call(
        functools.partial(plan_kernel, shift),
        out_shape=[shape] * 5,
        in_specs=[SMEM] * 3,
        out_specs=[SMEM] * 5,
        scratch_shapes=[
            pltpu.SMEM((beam_count,), jnp.int32),
            pltpu.SMEM((3 * count + 1,), jnp.int32),
        ],
        compiler_params=params(),
        name="plan",
    )(me, own, other)


def wires_kernel(spans, early, me_ref, target_ref, rank_ref, keep_ref, *refs):
    wires = refs[-1]
    spare = wires.shape[0] - 1
    out_refs = refs[-1 - len(spans) : -1]
    other_ref, *summed_refs = refs[: -1 - len(spans)]
    wires[...] = jnp.zeros_like(wires)
    me = me_ref[0]

    def lay(place, total):
        rank = rank_ref[place]
        distance = target_ref[place] ^ me
        at = spare
        start = 0
        for number, low, high in spans:
            wanted = (distance == number) & (rank >= low) & (rank < high)
            at = jnp.where(wanted, start + rank - low, at)
            start += high - low
        wires[at] = total

    before = 0
    if not early:
        before = summed_refs[0].shape[0]
        for row in range(before):
            lay(row, summed_refs[0][row])
    for row in range(other_ref.shape[0]):
        place = before + row
        total = keep_ref[place].astype(jnp.float32) + other_ref[row].astype(jnp.float32)
        total = total.astype(jnp.bfloat16)
        lay(place, total)
        if early:
            summed_refs[0][row] = total
    start = 0
    for (_, low, high), ref in zip(spans, out_refs):
        ref[...] = wires[start : start + high - low]
        start += high - low


def wires(spans, me, target, rank, keep, other, summed=None):
    block = keep.shape[1:]
    sizes = [high - low for _, low, high in spans]
    inputs = [me, target, rank, keep, other]
    if summed is None:
        sizes = [other.shape[0]] + sizes
    else:
        inputs.append(summed)
    shapes = [jax.ShapeDtypeStruct((size,) + block, jnp.bfloat16) for size in sizes]
    total = sum(high - low for _, low, high in spans)
    return pl.pallas_call(
        functools.partial(wires_kernel, spans, summed is None),
        out_shape=shapes,
        in_specs=[SMEM] * 3 + [VMEM] * (len(inputs) - 3),
        out_specs=[VMEM] * len(shapes),
        scratch_shapes=[pltpu.VMEM((total + 1,) + block, jnp.bfloat16)],
        compiler_params=params(),
        cost_estimate=cost(0, 2**21),
        name="early_wires" if summed is None else "late_wires",
    )(*inputs)


def collect_kernel(spans, capacity, me_ref, *refs):
    sems = refs[-1]
    out_ref = refs[-2]
    copies = []
    for number, (distance, low, high) in enumerate(spans):
        start = (me_ref[0] ^ distance) * capacity + low
        copies.append(
            pltpu.make_async_copy(
                refs[number], out_ref.at[pl.ds(start, high - low)], sems.at[number]
            )
        )
    for copy in copies:
        copy.start()
    for copy in copies:
        copy.wait()


def collect(spans, capacity, beam_count, me, received):
    shape = (beam_count * capacity,) + received[0].shape[1:]
    return pl.pallas_call(
        functools.partial(collect_kernel, spans, capacity),
        out_shape=jax.ShapeDtypeStruct(shape, jnp.bfloat16),
        in_specs=[SMEM] + [ANY] * len(received),
        out_specs=ANY,
        scratch_shapes=[pltpu.SemaphoreType.DMA((len(received),))],
        compiler_params=params(),
        cost_estimate=cost(0, 2**21),
        name="collect",
    )(me, *received)


def spread(spans, group):
    count = lax.axis_size("beam")
    received = []
    for (distance, _, _), wire in zip(spans, group):
        route = [(place, place ^ distance) for place in range(count)]
        received.append(lax.ppermute(wire, "beam", route) if distance else wire)
    return received


def stacked_weights(weights):
    return weights[0].reshape(weights.shape[1], -1, weights.shape[4])


def table_row(table, row_number):
    return lax.dynamic_index_in_dim(table, row_number, 0, keepdims=False)


def local(subimages, range_kernel, weights0, starts0, weights1, starts1, owners):
    aper_index = lax.axis_index("aperture")
    beam_index = lax.axis_index("beam")
    beam_count = lax.axis_size("beam")
    margin = MARGIN_BLOCKS * BLK
    rows = subimages.shape[2]
    local_blocks = rows // BLK
    even = (beam_index + 1) % 2
    ends = (beam_index == 0, beam_index == beam_count - 1)
    side = jnp.stack([even] + [end.astype(jnp.int32) for end in ends])
    me = beam_index.reshape(1)

    sector_count = owners.shape[1]
    capacity = max(2, 2 * sector_count // beam_count)
    shorter, longer = max(1, capacity // 4), max(1, capacity // 2)
    far = range(beam_count // 2, beam_count)
    odd = [distance for distance in far if distance % 2]
    others = [distance for distance in far if distance % 2 == 0]
    early = len(odd) * shorter + len(others) * longer
    early_spans = [(distance, 0, shorter) for distance in odd]
    early_spans += [(distance, 0, longer) for distance in others]
    late_spans = [(distance, shorter, capacity) for distance in odd]
    for distance in range(1, beam_count // 2):
        cuts = sorted({cut * capacity // 8 for cut in (0, 3, 6, 8)})
        late_spans += [(distance, low, high) for low, high in zip(cuts, cuts[1:])]
    late_spans.append((0, 0, capacity))
    last_spans = [(distance, longer, capacity) for distance in others]

    sent = resample(subimages[0], range_kernel[0], margin)
    halos = trade_edges(*sent)
    own_owners = owners[0, :, 0]
    other_owners = partner(owners, "aperture", 1)[0, :, 0]
    planned = plan(longer - shorter, me, own_owners, other_owners, beam_count)
    begin0 = table_row(starts0, aper_index) - (beam_index * local_blocks - MARGIN_BLOCKS)
    halos, planned = lax.optimization_barrier((halos, planned))
    *planned, target, rank = planned
    width = range_kernel.shape[3] // 2
    weights = stacked_weights(weights0)
    send = first_level(width, rows, begin0, side, sent, halos, weights)
    other = partner(send, "aperture", 0)
    keep = first_level(0, rows, begin0, side, sent, halos, weights)
    level_one = (keep.astype(jnp.float32) + other.astype(jnp.float32)).astype(jnp.bfloat16)

    beams = level_one.shape[1]
    first = lax.dynamic_slice_in_dim(level_one, even * (beams - margin), margin, 1)
    second = lax.dynamic_slice_in_dim(level_one, (1 - even) * (beams - margin), margin, 1)
    halos = trade_edges(first, second)
    begin1 = table_row(starts1, aper_index) - (beam_index * 2 * local_blocks - MARGIN_BLOCKS)
    keep, send, late = second_level(
        begin1, side, planned, level_one, halos, stacked_weights(weights1), early
    )
    other = partner(send, "aperture", 1)
    other, late = lax.optimization_barrier((other, late))
    late = partner(late, "aperture", 1)
    summed, *group = wires(early_spans, me, target, rank, keep, other)
    received = spread(early_spans, group)
    from_odd, from_others = received[: len(odd)], received[len(odd) :]
    ready, from_odd = lax.optimization_barrier((late, from_odd))
    group = wires(late_spans, me, target, rank, keep, ready, summed)
    received = from_odd + spread(late_spans, group)
    ready, from_others = lax.optimization_barrier((late, from_others))
    group = wires(last_spans, me, target, rank, keep, ready, summed)
    received += from_others + spread(last_spans, group)
    spans = early_spans[: len(odd)] + late_spans + early_spans[len(odd) :] + last_spans
    return collect(spans, capacity, beam_count, me, received)[None]


def solution(mesh):
    return jax.shard_map(
        local,
        mesh=mesh,
        in_specs=(
            P("aperture", None, "beam", None),
            P("aperture", None, None, None),
            P("aperture", "beam", None, None, None),
            P(None, "beam"),
            P("aperture", "beam", None, None, None),
            P(None, "beam"),
            P("aperture", "beam", None),
        ),
        out_specs=P("aperture", "beam", None, None, None),
        check_vma=False,
    )
```

```python
import functools

import jax
import jax.numpy as jnp
from jax import lax
from jax.experimental import pallas as pl
from jax.experimental.pallas import tpu as pltpu
from jax.sharding import PartitionSpec as P

BLK = 32
NW = 10
REACH = 2
OS = 64
MARGIN_BLOCKS = (NW - 2) // 2 + REACH
VMEM_LIMIT = 8 * 1024 * 1024
MOST_VMEM = 53 * 1024 * 1024
ANY = pl.BlockSpec(memory_space=pl.ANY)
VMEM = pl.BlockSpec(memory_space=pltpu.VMEM)
SMEM = pl.BlockSpec(memory_space=pltpu.SMEM)


def params(limit=VMEM_LIMIT):
    return pltpu.CompilerParams(vmem_limit_bytes=limit)


def cost(macs, moved):
    return pl.CostEstimate(flops=2 * macs, bytes_accessed=moved, transcendentals=0)


def trade_edges(first, second):
    count, apertures = lax.axis_size("beam"), lax.axis_size("aperture")
    received = []
    for order, block in enumerate((first, second)):
        route = []
        for aper in range(apertures):
            for place in range(count):
                other = place + 1 if (place - order) % 2 == 0 else place - 1
                if 0 <= other < count:
                    to = aper * count + other
                else:
                    to = min(aper ^ 1, apertures - 1) * count + place
                route.append((aper * count + place, to))
        received.append(lax.ppermute(block, ("aperture", "beam"), route))
    return received


def partner(block, axis, distance):
    count = lax.axis_size(axis)
    route = []
    for low in range(count):
        high = low | 1 << distance
        if high != low and high < count:
            route += [(low, high), (high, low)]
    return lax.ppermute(block, axis, route)


def dot(left, right):
    return jnp.dot(left, right, preferred_element_type=jnp.float32)


def resample_kernel(child_hbm, kernel_hbm, first_ref, second_ref, child, kernel, own, sems):
    aper, beam = lax.axis_index("aperture"), lax.axis_index("beam")
    half, quarter = aper & 1, (aper >> 1) & 1
    even = 1 - (beam & 1)
    rows, rng = child.shape[1:]
    piece = rng // 4
    child_copy = pltpu.make_async_copy(child_hbm, child, sems.at[4])
    copies = []
    for place in range(4):
        source = (half ^ (place // 2)) * 2 + (quarter ^ (place % 2))
        copies.append(
            pltpu.make_async_copy(
                kernel_hbm.at[:, :, pl.ds(pl.multiple_of(source * piece, 128), piece)],
                kernel.at[:, :, place * piece : (place + 1) * piece],
                sems.at[place],
            )
        )
    child_copy.start()
    for copy in copies:
        copy.start()
    child_copy.wait()
    real, imag = child[0], child[1]
    margin = first_ref.shape[1]
    tail = pl.ds(pl.multiple_of(even * (rows - margin), BLK), margin)
    head = pl.ds(pl.multiple_of((1 - even) * (rows - margin), BLK), margin)
    for side in range(2):
        columns = slice(side * 2 * piece, (side + 1) * 2 * piece)
        copies[2 * side].wait()
        copies[2 * side + 1].wait()
        k_real, k_imag = kernel[0, :, columns], kernel[1, :, columns]
        own[0, :, columns] = (dot(real, k_real) - dot(imag, k_imag)).astype(jnp.bfloat16)
        own[1, :, columns] = (dot(real, k_imag) + dot(imag, k_real)).astype(jnp.bfloat16)
        for part in range(2):
            first_ref[part, :, columns] = own[part, tail, columns]
            second_ref[part, :, columns] = own[part, head, columns]


def resample(child, kernel, margin):
    rows, rng = child.shape[1:]
    shape = jax.ShapeDtypeStruct((2, margin, rng), jnp.bfloat16)
    return pl.pallas_call(
        resample_kernel,
        out_shape=(shape, shape),
        in_specs=[ANY, ANY],
        out_specs=(VMEM, VMEM),
        scratch_shapes=[
            pltpu.VMEM(child.shape, jnp.bfloat16),
            pltpu.VMEM(kernel.shape, jnp.bfloat16),
            pltpu.VMEM(child.shape, jnp.bfloat16),
            pltpu.SemaphoreType.DMA((5,)),
        ],
        compiler_params=params(MOST_VMEM),
        cost_estimate=cost(4 * rows * rng * rng, 2**21),
        name="resample",
    )(child, kernel)


def complex_window(weights, window):
    beams, width = weights.shape[0] // 2, window.shape[1] // 2
    product = dot(weights, window)
    return (
        (product[:beams, :width] - product[beams:, width:]).astype(jnp.bfloat16),
        (product[:beams, width:] + product[beams:, :width]).astype(jnp.bfloat16),
    )


def place_rows(padded, start, source, columns):
    width = padded.shape[1] // 2
    for part in range(2):
        target = slice(part * width, (part + 1) * width)
        padded[pl.ds(start, source.shape[1]), target] = source[part, :, columns]


def place_halos(padded, side_ref, rows, first_ref, second_ref, columns):
    even, lowest, highest = side_ref[0], side_ref[1], side_ref[2]
    margin = first_ref.shape[1]
    far = margin + rows
    place_rows(padded, pl.multiple_of(even * far, BLK), first_ref, columns)
    place_rows(padded, pl.multiple_of((1 - even) * far, BLK), second_ref, columns)
    zeros = jnp.zeros((margin, padded.shape[1]), padded.dtype)

    @pl.when(lowest == 1)
    def _():
        padded[:margin, :] = zeros

    @pl.when(highest == 1)
    def _():
        padded[far:, :] = zeros


def first_level_kernel(
    column, rows, starts_ref, side_ref, sent_first_ref, sent_second_ref, first_ref, second_ref,
    weights_ref, out_ref, padded,
):
    sectors, stacked, window = weights_ref.shape
    window //= 2
    beams = stacked // 2
    margin = first_ref.shape[1]
    columns = slice(column, column + out_ref.shape[2])
    even = side_ref[0]
    tail = pl.multiple_of(margin + even * (rows - margin), BLK)
    head = pl.multiple_of(margin + (1 - even) * (rows - margin), BLK)
    place_rows(padded, tail, sent_first_ref, columns)
    place_rows(padded, head, sent_second_ref, columns)
    place_halos(padded, side_ref, rows, first_ref, second_ref, columns)
    for sector in range(sectors):
        place = pl.ds(pl.multiple_of(starts_ref[sector] * BLK, BLK), window)
        width = out_ref.shape[2]
        both = jnp.concatenate([padded[place, :width], padded[place, width:]])
        parts = dot(weights_ref[sector], both).astype(jnp.bfloat16)
        for part in range(2):
            out_ref[part, sector * beams : (sector + 1) * beams, :] = parts[
                part * beams : (part + 1) * beams
            ]


def first_level(column, rows, starts, side, sent, halos, weights):
    sectors, stacked, window = weights.shape
    margin, rng = sent[0].shape[1:]
    assert 2 * margin >= rows
    width = rng // 2
    return pl.pallas_call(
        functools.partial(first_level_kernel, column, rows),
        out_shape=jax.ShapeDtypeStruct((2, sectors * stacked // 2, width), jnp.bfloat16),
        in_specs=[SMEM, SMEM] + [VMEM] * 5,
        out_specs=VMEM,
        scratch_shapes=[pltpu.VMEM((rows + 2 * margin, 2 * width), jnp.bfloat16)],
        compiler_params=params(),
        cost_estimate=cost(sectors * stacked * window * width, 2**21),
        name="first_level",
    )(starts, side, *sent, *halos, weights)


def second_level_early_kernel(
    starts_ref, side_ref, sector_ref, own_ref, first_ref, second_ref, weights_ref, send_ref, padded
):
    _, stacked, window = weights_ref.shape
    per = stacked // 2 // OS
    margin, rows = first_ref.shape[1], own_ref.shape[1]
    columns = slice(send_ref.shape[3], 2 * send_ref.shape[3])
    place_rows(padded, margin, own_ref, columns)
    place_halos(padded, side_ref, rows, first_ref, second_ref, columns)
    for place in range(send_ref.shape[0]):
        sector = sector_ref[place] // per
        piece = pl.multiple_of(sector_ref[place] % per * OS, OS)
        window_rows = pl.ds(pl.multiple_of(starts_ref[sector] * BLK, BLK), window)
        weights = jnp.concatenate(
            [
                weights_ref[sector, pl.ds(piece, OS), :],
                weights_ref[sector, pl.ds(pl.multiple_of(piece + stacked // 2, OS), OS), :],
            ]
        )
        parts = complex_window(weights, padded[window_rows, :])
        for part in range(2):
            send_ref[place, part] = parts[part]


def second_level_kernel(
    starts_ref, side_ref, own_at_ref, other_at_ref, own_ref, first_ref, second_ref, weights_ref,
    keep_ref, send_ref, padded, send,
):
    sectors, stacked, window = weights_ref.shape
    beams = stacked // 2
    width = keep_ref.shape[3]
    margin, rows = first_ref.shape[1], own_ref.shape[1]
    columns = slice(0, 2 * width)
    place_rows(padded, margin, own_ref, columns)
    place_halos(padded, side_ref, rows, first_ref, second_ref, columns)
    per = beams // OS
    for sector in range(sectors):
        place = pl.ds(pl.multiple_of(starts_ref[sector] * BLK, BLK), window)
        parts = complex_window(weights_ref[sector], padded[place, :])
        for piece in range(per):
            own_at = own_at_ref[sector * per + piece]
            other_at = other_at_ref[sector * per + piece]
            taken = slice(piece * OS, (piece + 1) * OS)
            for part in range(2):
                keep_ref[own_at, part] = parts[part][taken, :width]
                send[other_at, part] = parts[part][taken, width:]
    send_ref[...] = send[send.shape[0] - send_ref.shape[0] :]


def second_level(starts, side, planned, own, halos, weights, early):
    sectors, stacked, window = weights.shape
    margin, rows, rng = halos[0].shape[1], own.shape[1], own.shape[2]
    count = sectors * stacked // 2 // OS
    block = (2, OS, rng // 2)
    own_at, other_at, other_sector = planned
    early_send = pl.pallas_call(
        second_level_early_kernel,
        out_shape=jax.ShapeDtypeStruct((early,) + block, jnp.bfloat16),
        in_specs=[SMEM] * 3 + [VMEM] * 4,
        out_specs=VMEM,
        scratch_shapes=[pltpu.VMEM((rows + 2 * margin, rng), jnp.bfloat16)],
        compiler_params=params(),
        cost_estimate=cost(early * 2 * 2 * OS * window * rng // 2, 2**20),
        name="second_level_early",
    )(starts, side, other_sector, own, *halos, weights)
    shapes = [jax.ShapeDtypeStruct((n,) + block, jnp.bfloat16) for n in (count, count - early)]
    keep, late_send = pl.pallas_call(
        second_level_kernel,
        out_shape=shapes,
        in_specs=[SMEM] * 4 + [VMEM] * 4,
        out_specs=[VMEM] * 2,
        scratch_shapes=[
            pltpu.VMEM((rows + 2 * margin, 2 * rng), jnp.bfloat16),
            pltpu.VMEM((count,) + block, jnp.bfloat16),
        ],
        compiler_params=params(),
        cost_estimate=cost(sectors * 2 * stacked * window * rng, 2**22),
        name="second_level",
    )(starts, side, own_at, other_at, own, *halos, weights)
    return keep, early_send, late_send


def plan_kernel(
    shift, me_ref, own_ref, other_ref, own_at_ref, other_at_ref, other_sector_ref, target_ref, rank_ref,
    taken, filled,
):
    count = own_ref.shape[0]
    far_bit = taken.shape[0] // 2

    def delay(target):
        distance = target ^ me_ref[0]
        return jnp.where((distance & far_bit) == 0, 2 * count, (distance & 1) * shift)

    for owners_ref, at_ref in ((other_ref, other_at_ref), (own_ref, own_at_ref)):
        for target in range(taken.shape[0]):
            taken[target] = 0
        for bucket in range(filled.shape[0]):
            filled[bucket] = 0
        for sector in range(count):
            target = owners_ref[sector]
            rank = taken[target]
            taken[target] = rank + 1
            bucket = rank + delay(target)
            at_ref[sector] = bucket
            filled[bucket + 1] = filled[bucket + 1] + 1
        for bucket in range(1, filled.shape[0]):
            filled[bucket] = filled[bucket] + filled[bucket - 1]
        for sector in range(count):
            bucket = at_ref[sector]
            place = filled[bucket]
            filled[bucket] = place + 1
            at_ref[sector] = place
            if at_ref is own_at_ref:
                target_ref[place] = owners_ref[sector]
                rank_ref[place] = bucket - delay(owners_ref[sector])
            else:
                other_sector_ref[place] = sector


def plan(shift, me, own, other, beam_count):
    count = own.shape[0]
    shape = jax.ShapeDtypeStruct((count,), jnp.int32)
    return pl.pallas_call(
        functools.partial(plan_kernel, shift),
        out_shape=[shape] * 5,
        in_specs=[SMEM] * 3,
        out_specs=[SMEM] * 5,
        scratch_shapes=[
            pltpu.SMEM((beam_count,), jnp.int32),
            pltpu.SMEM((3 * count + 1,), jnp.int32),
        ],
        compiler_params=params(),
        name="plan",
    )(me, own, other)


def wires_kernel(spans, early, me_ref, target_ref, rank_ref, keep_ref, *refs):
    wires = refs[-1]
    spare = wires.shape[0] - 1
    out_refs = refs[-1 - len(spans) : -1]
    other_ref, *summed_refs = refs[: -1 - len(spans)]
    wires[...] = jnp.zeros_like(wires)
    me = me_ref[0]

    def lay(place, total):
        rank = rank_ref[place]
        distance = target_ref[place] ^ me
        at = spare
        start = 0
        for number, low, high in spans:
            wanted = (distance == number) & (rank >= low) & (rank < high)
            at = jnp.where(wanted, start + rank - low, at)
            start += high - low
        wires[at] = total

    before = 0
    if not early:
        before = summed_refs[0].shape[0]
        for row in range(before):
            lay(row, summed_refs[0][row])
    for row in range(other_ref.shape[0]):
        place = before + row
        total = keep_ref[place].astype(jnp.float32) + other_ref[row].astype(jnp.float32)
        total = total.astype(jnp.bfloat16)
        lay(place, total)
        if early:
            summed_refs[0][row] = total
    start = 0
    for (_, low, high), ref in zip(spans, out_refs):
        ref[...] = wires[start : start + high - low]
        start += high - low


def wires(spans, me, target, rank, keep, other, summed=None):
    block = keep.shape[1:]
    sizes = [high - low for _, low, high in spans]
    inputs = [me, target, rank, keep, other]
    if summed is None:
        sizes = [other.shape[0]] + sizes
    else:
        inputs.append(summed)
    shapes = [jax.ShapeDtypeStruct((size,) + block, jnp.bfloat16) for size in sizes]
    total = sum(high - low for _, low, high in spans)
    return pl.pallas_call(
        functools.partial(wires_kernel, spans, summed is None),
        out_shape=shapes,
        in_specs=[SMEM] * 3 + [VMEM] * (len(inputs) - 3),
        out_specs=[VMEM] * len(shapes),
        scratch_shapes=[pltpu.VMEM((total + 1,) + block, jnp.bfloat16)],
        compiler_params=params(),
        cost_estimate=cost(0, 2**21),
        name="early_wires" if summed is None else "late_wires",
    )(*inputs)


def collect_kernel(spans, capacity, me_ref, *refs):
    sems = refs[-1]
    out_ref = refs[-2]
    copies = []
    for number, (distance, low, high) in enumerate(spans):
        start = (me_ref[0] ^ distance) * capacity + low
        copies.append(
            pltpu.make_async_copy(
                refs[number], out_ref.at[pl.ds(start, high - low)], sems.at[number]
            )
        )
    for copy in copies:
        copy.start()
    for copy in copies:
        copy.wait()


def collect(spans, capacity, beam_count, me, received):
    shape = (beam_count * capacity,) + received[0].shape[1:]
    return pl.pallas_call(
        functools.partial(collect_kernel, spans, capacity),
        out_shape=jax.ShapeDtypeStruct(shape, jnp.bfloat16),
        in_specs=[SMEM] + [ANY] * len(received),
        out_specs=ANY,
        scratch_shapes=[pltpu.SemaphoreType.DMA((len(received),))],
        compiler_params=params(),
        cost_estimate=cost(0, 2**21),
        name="collect",
    )(me, *received)


def spread(spans, group):
    count = lax.axis_size("beam")
    received = []
    for (distance, _, _), wire in zip(spans, group):
        route = [(place, place ^ distance) for place in range(count)]
        received.append(lax.ppermute(wire, "beam", route) if distance else wire)
    return received


def real_form(weights):
    real, imag = weights[0, :, 0], weights[0, :, 1]
    upper = jnp.concatenate([real, -imag], axis=-1)
    lower = jnp.concatenate([imag, real], axis=-1)
    return jnp.concatenate([upper, lower], axis=1)


def stacked_weights(weights):
    return weights[0].reshape(weights.shape[1], -1, weights.shape[4])


def table_row(table, row_number):
    return lax.dynamic_index_in_dim(table, row_number, 0, keepdims=False)


def local(subimages, range_kernel, weights0, starts0, weights1, starts1, owners):
    aper_index = lax.axis_index("aperture")
    beam_index = lax.axis_index("beam")
    beam_count = lax.axis_size("beam")
    margin = MARGIN_BLOCKS * BLK
    rows = subimages.shape[2]
    local_blocks = rows // BLK
    even = (beam_index + 1) % 2
    ends = (beam_index == 0, beam_index == beam_count - 1)
    side = jnp.stack([even] + [end.astype(jnp.int32) for end in ends])
    me = beam_index.reshape(1)

    sector_count = owners.shape[1]
    capacity = max(2, 2 * sector_count // beam_count)
    shorter, longer = max(1, capacity // 4), max(1, capacity // 2)
    far = range(beam_count // 2, beam_count)
    odd = [distance for distance in far if distance % 2]
    others = [distance for distance in far if distance % 2 == 0]
    early = len(odd) * shorter + len(others) * longer
    early_spans = [(distance, 0, shorter) for distance in odd]
    early_spans += [(distance, 0, longer) for distance in others]
    late_spans = [(distance, shorter, capacity) for distance in odd]
    for distance in range(1, beam_count // 2):
        cut = (5 * capacity + 4) // 8
        late_spans += [(distance, 0, cut), (distance, cut, capacity)]
    late_spans.append((0, 0, capacity))
    last_spans = [(distance, longer, capacity) for distance in others]

    sent = resample(subimages[0], range_kernel[0], margin)
    sent, weights0 = lax.optimization_barrier((sent, weights0))
    weights, owners = lax.optimization_barrier((real_form(weights0), owners))
    halos = trade_edges(*sent)
    own_owners = owners[0, :, 0]
    other_owners = partner(owners, "aperture", 1)[0, :, 0]
    planned = plan(longer - shorter, me, own_owners, other_owners, beam_count)
    begin0 = table_row(starts0, aper_index) - (beam_index * local_blocks - MARGIN_BLOCKS)
    halos, planned = lax.optimization_barrier((halos, planned))
    *planned, target, rank = planned
    width = range_kernel.shape[3] // 2
    send = first_level(width, rows, begin0, side, sent, halos, weights)
    other = partner(send, "aperture", 0)
    keep = first_level(0, rows, begin0, side, sent, halos, weights)
    level_one = (keep.astype(jnp.float32) + other.astype(jnp.float32)).astype(jnp.bfloat16)

    beams = level_one.shape[1]
    first = lax.dynamic_slice_in_dim(level_one, even * (beams - margin), margin, 1)
    second = lax.dynamic_slice_in_dim(level_one, (1 - even) * (beams - margin), margin, 1)
    halos = trade_edges(first, second)
    begin1 = table_row(starts1, aper_index) - (beam_index * 2 * local_blocks - MARGIN_BLOCKS)
    keep, send, late = second_level(
        begin1, side, planned, level_one, halos, stacked_weights(weights1), early
    )
    other = partner(send, "aperture", 1)
    other, late = lax.optimization_barrier((other, late))
    late = partner(late, "aperture", 1)
    summed, *group = wires(early_spans, me, target, rank, keep, other)
    received = spread(early_spans, group)
    from_odd, from_others = received[: len(odd)], received[len(odd) :]
    ready, from_odd = lax.optimization_barrier((late, from_odd))
    group = wires(late_spans, me, target, rank, keep, ready, summed)
    received = from_odd + spread(late_spans, group)
    ready, from_others = lax.optimization_barrier((late, from_others))
    group = wires(last_spans, me, target, rank, keep, ready, summed)
    received += from_others + spread(last_spans, group)
    spans = early_spans[: len(odd)] + late_spans + early_spans[len(odd) :] + last_spans
    return collect(spans, capacity, beam_count, me, received)[None]


def solution(mesh):
    return jax.shard_map(
        local,
        mesh=mesh,
        in_specs=(
            P("aperture", None, "beam", None),
            P("aperture", None, None, None),
            P("aperture", "beam", None, None, None),
            P(None, "beam"),
            P("aperture", "beam", None, None, None),
            P(None, "beam"),
            P("aperture", "beam", None),
        ),
        out_specs=P("aperture", "beam", None, None, None),
        check_vma=False,
    )
```

```python
import functools

import jax
import jax.numpy as jnp
from jax import lax
from jax.experimental import pallas as pl
from jax.experimental.pallas import tpu as pltpu
from jax.sharding import PartitionSpec as P

BLK = 32
NW = 10
REACH = 2
OS = 64
MARGIN_BLOCKS = (NW - 2) // 2 + REACH
VMEM_LIMIT = 4 * 1024 * 1024
MOST_VMEM = 53 * 1024 * 1024
ANY = pl.BlockSpec(memory_space=pl.ANY)
VMEM = pl.BlockSpec(memory_space=pltpu.VMEM)
SMEM = pl.BlockSpec(memory_space=pltpu.SMEM)


def params(limit=VMEM_LIMIT):
    return pltpu.CompilerParams(vmem_limit_bytes=limit)


def cost(macs, moved):
    return pl.CostEstimate(flops=2 * macs, bytes_accessed=moved, transcendentals=0)


def trade_edges(first, second):
    count, apertures = lax.axis_size("beam"), lax.axis_size("aperture")
    received = []
    for order, block in enumerate((first, second)):
        route = []
        for aper in range(apertures):
            for place in range(count):
                other = place + 1 if (place - order) % 2 == 0 else place - 1
                if 0 <= other < count:
                    to = aper * count + other
                else:
                    to = min(aper ^ 1, apertures - 1) * count + place
                route.append((aper * count + place, to))
        received.append(lax.ppermute(block, ("aperture", "beam"), route))
    return received


def partner(block, axis, distance):
    count = lax.axis_size(axis)
    route = []
    for low in range(count):
        high = low | 1 << distance
        if high != low and high < count:
            route += [(low, high), (high, low)]
    return lax.ppermute(block, axis, route)


def dot(left, right):
    return jnp.dot(left, right, preferred_element_type=jnp.float32)


def resample_kernel(child_hbm, kernel_hbm, first_ref, second_ref, child, kernel, own, sems):
    aper, beam = lax.axis_index("aperture"), lax.axis_index("beam")
    half, quarter = aper & 1, (aper >> 1) & 1
    even = 1 - (beam & 1)
    rows, rng = child.shape[1:]
    piece = rng // 4
    child_copy = pltpu.make_async_copy(child_hbm, child, sems.at[4])
    copies = []
    for place in range(4):
        source = (half ^ (place // 2)) * 2 + (quarter ^ (place % 2))
        copies.append(
            pltpu.make_async_copy(
                kernel_hbm.at[:, :, pl.ds(pl.multiple_of(source * piece, 128), piece)],
                kernel.at[:, :, place * piece : (place + 1) * piece],
                sems.at[place],
            )
        )
    child_copy.start()
    for copy in copies:
        copy.start()
    child_copy.wait()
    real, imag = child[0], child[1]
    margin = first_ref.shape[1]
    tail = pl.ds(pl.multiple_of(even * (rows - margin), BLK), margin)
    head = pl.ds(pl.multiple_of((1 - even) * (rows - margin), BLK), margin)
    for side in range(2):
        columns = slice(side * 2 * piece, (side + 1) * 2 * piece)
        copies[2 * side].wait()
        copies[2 * side + 1].wait()
        k_real, k_imag = kernel[0, :, columns], kernel[1, :, columns]
        own[0, :, columns] = (dot(real, k_real) - dot(imag, k_imag)).astype(jnp.bfloat16)
        own[1, :, columns] = (dot(real, k_imag) + dot(imag, k_real)).astype(jnp.bfloat16)
        for part in range(2):
            first_ref[part, :, columns] = own[part, tail, columns]
            second_ref[part, :, columns] = own[part, head, columns]


def resample(child, kernel, margin):
    rows, rng = child.shape[1:]
    shape = jax.ShapeDtypeStruct((2, margin, rng), jnp.bfloat16)
    return pl.pallas_call(
        resample_kernel,
        out_shape=(shape, shape),
        in_specs=[ANY, ANY],
        out_specs=(VMEM, VMEM),
        scratch_shapes=[
            pltpu.VMEM(child.shape, jnp.bfloat16),
            pltpu.VMEM(kernel.shape, jnp.bfloat16),
            pltpu.VMEM(child.shape, jnp.bfloat16),
            pltpu.SemaphoreType.DMA((5,)),
        ],
        compiler_params=params(MOST_VMEM),
        cost_estimate=cost(4 * rows * rng * rng, 2**21),
        name="resample",
    )(child, kernel)


def complex_window(weights, window):
    beams, width = weights.shape[0] // 2, window.shape[1] // 2
    product = dot(weights, window)
    return (
        (product[:beams, :width] - product[beams:, width:]).astype(jnp.bfloat16),
        (product[:beams, width:] + product[beams:, :width]).astype(jnp.bfloat16),
    )


def place_rows(padded, start, source, columns):
    width = padded.shape[1] // 2
    for part in range(2):
        target = slice(part * width, (part + 1) * width)
        padded[pl.ds(start, source.shape[1]), target] = source[part, :, columns]


def place_halos(padded, side_ref, rows, first_ref, second_ref, columns):
    even, lowest, highest = side_ref[0], side_ref[1], side_ref[2]
    margin = first_ref.shape[1]
    far = margin + rows
    place_rows(padded, pl.multiple_of(even * far, BLK), first_ref, columns)
    place_rows(padded, pl.multiple_of((1 - even) * far, BLK), second_ref, columns)
    zeros = jnp.zeros((margin, padded.shape[1]), padded.dtype)

    @pl.when(lowest == 1)
    def _():
        padded[:margin, :] = zeros

    @pl.when(highest == 1)
    def _():
        padded[far:, :] = zeros


def first_level_kernel(
    column, rows, starts_ref, side_ref, sent_first_ref, sent_second_ref, first_ref, second_ref,
    weights_ref, out_ref, padded,
):
    sectors, stacked, window = weights_ref.shape
    window //= 2
    beams = stacked // 2
    margin = first_ref.shape[1]
    columns = slice(column, column + out_ref.shape[2])
    even = side_ref[0]
    tail = pl.multiple_of(margin + even * (rows - margin), BLK)
    head = pl.multiple_of(margin + (1 - even) * (rows - margin), BLK)
    place_rows(padded, tail, sent_first_ref, columns)
    place_rows(padded, head, sent_second_ref, columns)
    place_halos(padded, side_ref, rows, first_ref, second_ref, columns)
    for sector in range(sectors):
        place = pl.ds(pl.multiple_of(starts_ref[sector] * BLK, BLK), window)
        width = out_ref.shape[2]
        both = jnp.concatenate([padded[place, :width], padded[place, width:]])
        parts = dot(weights_ref[sector], both).astype(jnp.bfloat16)
        for part in range(2):
            out_ref[part, sector * beams : (sector + 1) * beams, :] = parts[
                part * beams : (part + 1) * beams
            ]


def first_level(column, rows, starts, side, sent, halos, weights):
    sectors, stacked, window = weights.shape
    margin, rng = sent[0].shape[1:]
    assert 2 * margin >= rows
    width = rng // 2
    return pl.pallas_call(
        functools.partial(first_level_kernel, column, rows),
        out_shape=jax.ShapeDtypeStruct((2, sectors * stacked // 2, width), jnp.bfloat16),
        in_specs=[SMEM, SMEM] + [VMEM] * 5,
        out_specs=VMEM,
        scratch_shapes=[pltpu.VMEM((rows + 2 * margin, 2 * width), jnp.bfloat16)],
        compiler_params=params(),
        cost_estimate=cost(sectors * stacked * window * width, 2**21),
        name="first_level",
    )(starts, side, *sent, *halos, weights)


def second_level_early_kernel(
    starts_ref, side_ref, sector_ref, own_ref, first_ref, second_ref, weights_ref, send_ref, padded
):
    _, stacked, window = weights_ref.shape
    per = stacked // 2 // OS
    margin, rows = first_ref.shape[1], own_ref.shape[1]
    columns = slice(send_ref.shape[3], 2 * send_ref.shape[3])
    place_rows(padded, margin, own_ref, columns)
    place_halos(padded, side_ref, rows, first_ref, second_ref, columns)
    for place in range(send_ref.shape[0]):
        sector = sector_ref[place] // per
        piece = pl.multiple_of(sector_ref[place] % per * OS, OS)
        window_rows = pl.ds(pl.multiple_of(starts_ref[sector] * BLK, BLK), window)
        weights = jnp.concatenate(
            [
                weights_ref[sector, pl.ds(piece, OS), :],
                weights_ref[sector, pl.ds(pl.multiple_of(piece + stacked // 2, OS), OS), :],
            ]
        )
        parts = complex_window(weights, padded[window_rows, :])
        for part in range(2):
            send_ref[place, part] = parts[part]


def second_level_kernel(
    starts_ref, side_ref, own_at_ref, other_at_ref, own_ref, first_ref, second_ref, weights_ref,
    keep_ref, send_ref, padded, send,
):
    sectors, stacked, window = weights_ref.shape
    beams = stacked // 2
    width = keep_ref.shape[3]
    margin, rows = first_ref.shape[1], own_ref.shape[1]
    columns = slice(0, 2 * width)
    place_rows(padded, margin, own_ref, columns)
    place_halos(padded, side_ref, rows, first_ref, second_ref, columns)
    per = beams // OS
    for sector in range(sectors):
        place = pl.ds(pl.multiple_of(starts_ref[sector] * BLK, BLK), window)
        parts = complex_window(weights_ref[sector], padded[place, :])
        for piece in range(per):
            own_at = own_at_ref[sector * per + piece]
            other_at = other_at_ref[sector * per + piece]
            taken = slice(piece * OS, (piece + 1) * OS)
            for part in range(2):
                keep_ref[own_at, part] = parts[part][taken, :width]
                send[other_at, part] = parts[part][taken, width:]
    send_ref[...] = send[send.shape[0] - send_ref.shape[0] :]


def second_level(starts, side, planned, own, halos, weights, early):
    sectors, stacked, window = weights.shape
    margin, rows, rng = halos[0].shape[1], own.shape[1], own.shape[2]
    count = sectors * stacked // 2 // OS
    block = (2, OS, rng // 2)
    own_at, other_at, other_sector = planned
    early_send = pl.pallas_call(
        second_level_early_kernel,
        out_shape=jax.ShapeDtypeStruct((early,) + block, jnp.bfloat16),
        in_specs=[SMEM] * 3 + [VMEM] * 4,
        out_specs=VMEM,
        scratch_shapes=[pltpu.VMEM((rows + 2 * margin, rng), jnp.bfloat16)],
        compiler_params=params(),
        cost_estimate=cost(early * 2 * 2 * OS * window * rng // 2, 2**20),
        name="second_level_early",
    )(starts, side, other_sector, own, *halos, weights)
    shapes = [jax.ShapeDtypeStruct((n,) + block, jnp.bfloat16) for n in (count, count - early)]
    keep, late_send = pl.pallas_call(
        second_level_kernel,
        out_shape=shapes,
        in_specs=[SMEM] * 4 + [VMEM] * 4,
        out_specs=[VMEM] * 2,
        scratch_shapes=[
            pltpu.VMEM((rows + 2 * margin, 2 * rng), jnp.bfloat16),
            pltpu.VMEM((count,) + block, jnp.bfloat16),
        ],
        compiler_params=params(),
        cost_estimate=cost(sectors * 2 * stacked * window * rng, 2**22),
        name="second_level",
    )(starts, side, own_at, other_at, own, *halos, weights)
    return keep, early_send, late_send


def plan_kernel(
    shift, me_ref, own_ref, other_ref, own_at_ref, other_at_ref, other_sector_ref, target_ref, rank_ref,
    taken, filled,
):
    count = own_ref.shape[0]
    far_bit = taken.shape[0] // 2

    def delay(target):
        distance = target ^ me_ref[0]
        return jnp.where((distance & far_bit) == 0, 2 * count, (distance & 1) * shift)

    for owners_ref, at_ref in ((other_ref, other_at_ref), (own_ref, own_at_ref)):
        for target in range(taken.shape[0]):
            taken[target] = 0
        for bucket in range(filled.shape[0]):
            filled[bucket] = 0
        for sector in range(count):
            target = owners_ref[sector]
            rank = taken[target]
            taken[target] = rank + 1
            bucket = rank + delay(target)
            at_ref[sector] = bucket
            filled[bucket + 1] = filled[bucket + 1] + 1
        for bucket in range(1, filled.shape[0]):
            filled[bucket] = filled[bucket] + filled[bucket - 1]
        for sector in range(count):
            bucket = at_ref[sector]
            place = filled[bucket]
            filled[bucket] = place + 1
            at_ref[sector] = place
            if at_ref is own_at_ref:
                target_ref[place] = owners_ref[sector]
                rank_ref[place] = bucket - delay(owners_ref[sector])
            else:
                other_sector_ref[place] = sector


def plan(shift, me, own, other, beam_count):
    count = own.shape[0]
    shape = jax.ShapeDtypeStruct((count,), jnp.int32)
    return pl.pallas_call(
        functools.partial(plan_kernel, shift),
        out_shape=[shape] * 5,
        in_specs=[SMEM] * 3,
        out_specs=[SMEM] * 5,
        scratch_shapes=[
            pltpu.SMEM((beam_count,), jnp.int32),
            pltpu.SMEM((3 * count + 1,), jnp.int32),
        ],
        compiler_params=params(),
        name="plan",
    )(me, own, other)


def wires_kernel(spans, early, me_ref, target_ref, rank_ref, keep_ref, *refs):
    wires = refs[-1]
    spare = wires.shape[0] - 1
    out_refs = refs[-1 - len(spans) : -1]
    other_ref, *summed_refs = refs[: -1 - len(spans)]
    wires[...] = jnp.zeros_like(wires)
    me = me_ref[0]

    def lay(place, total):
        rank = rank_ref[place]
        distance = target_ref[place] ^ me
        at = spare
        start = 0
        for number, low, high in spans:
            wanted = (distance == number) & (rank >= low) & (rank < high)
            at = jnp.where(wanted, start + rank - low, at)
            start += high - low
        wires[at] = total

    before = 0
    if not early:
        before = summed_refs[0].shape[0]
        for row in range(before):
            lay(row, summed_refs[0][row])
    for row in range(other_ref.shape[0]):
        place = before + row
        total = keep_ref[place].astype(jnp.float32) + other_ref[row].astype(jnp.float32)
        total = total.astype(jnp.bfloat16)
        lay(place, total)
        if early:
            summed_refs[0][row] = total
    start = 0
    for (_, low, high), ref in zip(spans, out_refs):
        ref[...] = wires[start : start + high - low]
        start += high - low


def wires(spans, me, target, rank, keep, other, summed=None):
    block = keep.shape[1:]
    sizes = [high - low for _, low, high in spans]
    inputs = [me, target, rank, keep, other]
    if summed is None:
        sizes = [other.shape[0]] + sizes
    else:
        inputs.append(summed)
    shapes = [jax.ShapeDtypeStruct((size,) + block, jnp.bfloat16) for size in sizes]
    total = sum(high - low for _, low, high in spans)
    return pl.pallas_call(
        functools.partial(wires_kernel, spans, summed is None),
        out_shape=shapes,
        in_specs=[SMEM] * 3 + [VMEM] * (len(inputs) - 3),
        out_specs=[VMEM] * len(shapes),
        scratch_shapes=[pltpu.VMEM((total + 1,) + block, jnp.bfloat16)],
        compiler_params=params(),
        cost_estimate=cost(0, 2**21),
        name="early_wires" if summed is None else "late_wires",
    )(*inputs)


def collect_kernel(spans, capacity, me_ref, *refs):
    sems = refs[-1]
    out_ref = refs[-2]
    copies = []
    for number, (distance, low, high) in enumerate(spans):
        start = (me_ref[0] ^ distance) * capacity + low
        copies.append(
            pltpu.make_async_copy(
                refs[number], out_ref.at[pl.ds(start, high - low)], sems.at[number]
            )
        )
    for copy in copies:
        copy.start()
    for copy in copies:
        copy.wait()


def collect(spans, capacity, beam_count, me, received):
    shape = (beam_count * capacity,) + received[0].shape[1:]
    return pl.pallas_call(
        functools.partial(collect_kernel, spans, capacity),
        out_shape=jax.ShapeDtypeStruct(shape, jnp.bfloat16),
        in_specs=[SMEM] + [ANY] * len(received),
        out_specs=ANY,
        scratch_shapes=[pltpu.SemaphoreType.DMA((len(received),))],
        compiler_params=params(),
        cost_estimate=cost(0, 2**21),
        name="collect",
    )(me, *received)


def spread(spans, group):
    count = lax.axis_size("beam")
    received = []
    for (distance, _, _), wire in zip(spans, group):
        route = [(place, place ^ distance) for place in range(count)]
        received.append(lax.ppermute(wire, "beam", route) if distance else wire)
    return received


def real_form(weights):
    real, imag = weights[0, :, 0], weights[0, :, 1]
    upper = jnp.concatenate([real, -imag], axis=-1)
    lower = jnp.concatenate([imag, real], axis=-1)
    return jnp.concatenate([upper, lower], axis=1)


def stacked_weights(weights):
    return weights[0].reshape(weights.shape[1], -1, weights.shape[4])


def table_row(table, row_number):
    return lax.dynamic_index_in_dim(table, row_number, 0, keepdims=False)


def local(subimages, range_kernel, weights0, starts0, weights1, starts1, owners):
    aper_index = lax.axis_index("aperture")
    beam_index = lax.axis_index("beam")
    beam_count = lax.axis_size("beam")
    margin = MARGIN_BLOCKS * BLK
    rows = subimages.shape[2]
    local_blocks = rows // BLK
    even = (beam_index + 1) % 2
    ends = (beam_index == 0, beam_index == beam_count - 1)
    side = jnp.stack([even] + [end.astype(jnp.int32) for end in ends])
    me = beam_index.reshape(1)

    sector_count = owners.shape[1]
    capacity = max(2, 2 * sector_count // beam_count)
    shorter, longer = max(1, capacity // 4), max(1, capacity // 2)
    far = range(beam_count // 2, beam_count)
    odd = [distance for distance in far if distance % 2]
    others = [distance for distance in far if distance % 2 == 0]
    early = len(odd) * shorter + len(others) * longer
    early_spans = [(distance, 0, shorter) for distance in odd]
    early_spans += [(distance, 0, longer) for distance in others]
    late_spans = [(distance, shorter, capacity) for distance in odd]
    for distance in range(1, beam_count // 2):
        cut = (5 * capacity + 4) // 8
        late_spans += [(distance, 0, cut), (distance, cut, capacity)]
    late_spans.append((0, 0, capacity))
    last_spans = [(distance, longer, capacity) for distance in others]

    sent = resample(subimages[0], range_kernel[0], margin)
    sent, weights0 = lax.optimization_barrier((sent, weights0))
    weights, owners = lax.optimization_barrier((real_form(weights0), owners))
    halos = trade_edges(*sent)
    own_owners = owners[0, :, 0]
    other_owners = partner(owners, "aperture", 1)[0, :, 0]
    planned = plan(longer - shorter, me, own_owners, other_owners, beam_count)
    begin0 = table_row(starts0, aper_index) - (beam_index * local_blocks - MARGIN_BLOCKS)
    halos, planned = lax.optimization_barrier((halos, planned))
    *planned, target, rank = planned
    width = range_kernel.shape[3] // 2
    send = first_level(width, rows, begin0, side, sent, halos, weights)
    other = partner(send, "aperture", 0)
    keep = first_level(0, rows, begin0, side, sent, halos, weights)
    level_one = (keep.astype(jnp.float32) + other.astype(jnp.float32)).astype(jnp.bfloat16)

    beams = level_one.shape[1]
    first = lax.dynamic_slice_in_dim(level_one, even * (beams - margin), margin, 1)
    second = lax.dynamic_slice_in_dim(level_one, (1 - even) * (beams - margin), margin, 1)
    halos = trade_edges(first, second)
    begin1 = table_row(starts1, aper_index) - (beam_index * 2 * local_blocks - MARGIN_BLOCKS)
    keep, send, late = second_level(
        begin1, side, planned, level_one, halos, stacked_weights(weights1), early
    )
    other = partner(send, "aperture", 1)
    other, late = lax.optimization_barrier((other, late))
    late = partner(late, "aperture", 1)
    summed, *group = wires(early_spans, me, target, rank, keep, other)
    received = spread(early_spans, group)
    from_odd, from_others = received[: len(odd)], received[len(odd) :]
    ready, from_odd = lax.optimization_barrier((late, from_odd))
    group = wires(late_spans, me, target, rank, keep, ready, summed)
    received = from_odd + spread(late_spans, group)
    ready, from_others = lax.optimization_barrier((late, from_others))
    group = wires(last_spans, me, target, rank, keep, ready, summed)
    received += from_others + spread(last_spans, group)
    spans = early_spans[: len(odd)] + late_spans + early_spans[len(odd) :] + last_spans
    return collect(spans, capacity, beam_count, me, received)[None]


def solution(mesh):
    return jax.shard_map(
        local,
        mesh=mesh,
        in_specs=(
            P("aperture", None, "beam", None),
            P("aperture", None, None, None),
            P("aperture", "beam", None, None, None),
            P(None, "beam"),
            P("aperture", "beam", None, None, None),
            P(None, "beam"),
            P("aperture", "beam", None),
        ),
        out_specs=P("aperture", "beam", None, None, None),
        check_vma=False,
    )
```

```python
import functools

import jax
import jax.numpy as jnp
from jax import lax
from jax.experimental import pallas as pl
from jax.experimental.pallas import tpu as pltpu
from jax.sharding import PartitionSpec as P

BLK = 32
NW = 10
REACH = 2
OS = 64
MARGIN_BLOCKS = (NW - 2) // 2 + REACH
VMEM_LIMIT = 8 * 1024 * 1024
MOST_VMEM = 53 * 1024 * 1024
ANY = pl.BlockSpec(memory_space=pl.ANY)
VMEM = pl.BlockSpec(memory_space=pltpu.VMEM)
SMEM = pl.BlockSpec(memory_space=pltpu.SMEM)


def params(limit=VMEM_LIMIT):
    return pltpu.CompilerParams(vmem_limit_bytes=limit)


def cost(macs, moved):
    return pl.CostEstimate(flops=2 * macs, bytes_accessed=moved, transcendentals=0)


def trade_edges(first, second):
    count, apertures = lax.axis_size("beam"), lax.axis_size("aperture")
    received = []
    for order, block in enumerate((first, second)):
        route = []
        for aper in range(apertures):
            for place in range(count):
                other = place + 1 if (place - order) % 2 == 0 else place - 1
                if 0 <= other < count:
                    to = aper * count + other
                else:
                    to = min(aper ^ 1, apertures - 1) * count + place
                route.append((aper * count + place, to))
        received.append(lax.ppermute(block, ("aperture", "beam"), route))
    return received


def partner(block, axis, distance):
    count = lax.axis_size(axis)
    route = []
    for low in range(count):
        high = low | 1 << distance
        if high != low and high < count:
            route += [(low, high), (high, low)]
    return lax.ppermute(block, axis, route)


def dot(left, right):
    return jnp.dot(left, right, preferred_element_type=jnp.float32)


def resample_kernel(child_hbm, kernel_hbm, first_ref, second_ref, child, kernel, own, sems):
    aper, beam = lax.axis_index("aperture"), lax.axis_index("beam")
    half, quarter = aper & 1, (aper >> 1) & 1
    even = 1 - (beam & 1)
    rows, rng = child.shape[1:]
    piece = rng // 4
    child_copy = pltpu.make_async_copy(child_hbm, child, sems.at[4])
    copies = []
    for place in range(4):
        source = (half ^ (place // 2)) * 2 + (quarter ^ (place % 2))
        copies.append(
            pltpu.make_async_copy(
                kernel_hbm.at[:, :, pl.ds(pl.multiple_of(source * piece, 128), piece)],
                kernel.at[:, :, place * piece : (place + 1) * piece],
                sems.at[place],
            )
        )
    child_copy.start()
    for copy in copies:
        copy.start()
    child_copy.wait()
    real, imag = child[0], child[1]
    margin = first_ref.shape[1]
    tail = pl.ds(pl.multiple_of(even * (rows - margin), BLK), margin)
    head = pl.ds(pl.multiple_of((1 - even) * (rows - margin), BLK), margin)
    for side in range(2):
        columns = slice(side * 2 * piece, (side + 1) * 2 * piece)
        copies[2 * side].wait()
        copies[2 * side + 1].wait()
        k_real, k_imag = kernel[0, :, columns], kernel[1, :, columns]
        own[0, :, columns] = (dot(real, k_real) - dot(imag, k_imag)).astype(jnp.bfloat16)
        own[1, :, columns] = (dot(real, k_imag) + dot(imag, k_real)).astype(jnp.bfloat16)
        for part in range(2):
            first_ref[part, :, columns] = own[part, tail, columns]
            second_ref[part, :, columns] = own[part, head, columns]


def resample(child, kernel, margin):
    rows, rng = child.shape[1:]
    shape = jax.ShapeDtypeStruct((2, margin, rng), jnp.bfloat16)
    return pl.pallas_call(
        resample_kernel,
        out_shape=(shape, shape),
        in_specs=[ANY, ANY],
        out_specs=(VMEM, VMEM),
        scratch_shapes=[
            pltpu.VMEM(child.shape, jnp.bfloat16),
            pltpu.VMEM(kernel.shape, jnp.bfloat16),
            pltpu.VMEM(child.shape, jnp.bfloat16),
            pltpu.SemaphoreType.DMA((5,)),
        ],
        compiler_params=params(MOST_VMEM),
        cost_estimate=cost(4 * rows * rng * rng, 2**21),
        name="resample",
    )(child, kernel)


def complex_window(weights, window):
    beams, width = weights.shape[0] // 2, window.shape[1] // 2
    product = dot(weights, window)
    return (
        (product[:beams, :width] - product[beams:, width:]).astype(jnp.bfloat16),
        (product[:beams, width:] + product[beams:, :width]).astype(jnp.bfloat16),
    )


def place_rows(padded, start, source, columns):
    width = padded.shape[1] // 2
    for part in range(2):
        target = slice(part * width, (part + 1) * width)
        padded[pl.ds(start, source.shape[1]), target] = source[part, :, columns]


def place_halos(padded, side_ref, rows, first_ref, second_ref, columns):
    even, lowest, highest = side_ref[0], side_ref[1], side_ref[2]
    margin = first_ref.shape[1]
    far = margin + rows
    place_rows(padded, pl.multiple_of(even * far, BLK), first_ref, columns)
    place_rows(padded, pl.multiple_of((1 - even) * far, BLK), second_ref, columns)
    zeros = jnp.zeros((margin, padded.shape[1]), padded.dtype)

    @pl.when(lowest == 1)
    def _():
        padded[:margin, :] = zeros

    @pl.when(highest == 1)
    def _():
        padded[far:, :] = zeros


def first_level_kernel(
    column, rows, starts_ref, side_ref, sent_first_ref, sent_second_ref, first_ref, second_ref,
    weights_ref, out_ref, padded,
):
    sectors, stacked, window = weights_ref.shape
    one_product = column > 0
    window = window // 2 if one_product else window
    beams = stacked // 2
    margin = first_ref.shape[1]
    columns = slice(column, column + out_ref.shape[2])
    even = side_ref[0]
    tail = pl.multiple_of(margin + even * (rows - margin), BLK)
    head = pl.multiple_of(margin + (1 - even) * (rows - margin), BLK)
    place_rows(padded, tail, sent_first_ref, columns)
    place_rows(padded, head, sent_second_ref, columns)
    place_halos(padded, side_ref, rows, first_ref, second_ref, columns)
    for sector in range(sectors):
        place = pl.ds(pl.multiple_of(starts_ref[sector] * BLK, BLK), window)
        width = out_ref.shape[2]
        if one_product:
            both = jnp.concatenate([padded[place, :width], padded[place, width:]])
            product = dot(weights_ref[sector], both).astype(jnp.bfloat16)
            parts = (product[:beams], product[beams:])
        else:
            parts = complex_window(weights_ref[sector], padded[place, :])
        for part in range(2):
            out_ref[part, sector * beams : (sector + 1) * beams, :] = parts[part]


def first_level(column, rows, starts, side, sent, halos, weights):
    sectors, stacked, window = weights.shape
    margin, rng = sent[0].shape[1:]
    assert 2 * margin >= rows
    width = rng // 2
    return pl.pallas_call(
        functools.partial(first_level_kernel, column, rows),
        out_shape=jax.ShapeDtypeStruct((2, sectors * stacked // 2, width), jnp.bfloat16),
        in_specs=[SMEM, SMEM] + [VMEM] * 5,
        out_specs=VMEM,
        scratch_shapes=[pltpu.VMEM((rows + 2 * margin, 2 * width), jnp.bfloat16)],
        compiler_params=params(),
        cost_estimate=cost(sectors * stacked * window * width, 2**21),
        name="first_level",
    )(starts, side, *sent, *halos, weights)


def second_level_early_kernel(
    starts_ref, side_ref, sector_ref, own_ref, first_ref, second_ref, weights_ref, send_ref, padded
):
    _, stacked, window = weights_ref.shape
    per = stacked // 2 // OS
    margin, rows = first_ref.shape[1], own_ref.shape[1]
    columns = slice(send_ref.shape[3], 2 * send_ref.shape[3])
    place_rows(padded, margin, own_ref, columns)
    place_halos(padded, side_ref, rows, first_ref, second_ref, columns)
    for place in range(send_ref.shape[0]):
        sector = sector_ref[place] // per
        piece = pl.multiple_of(sector_ref[place] % per * OS, OS)
        window_rows = pl.ds(pl.multiple_of(starts_ref[sector] * BLK, BLK), window)
        weights = jnp.concatenate(
            [
                weights_ref[sector, pl.ds(piece, OS), :],
                weights_ref[sector, pl.ds(pl.multiple_of(piece + stacked // 2, OS), OS), :],
            ]
        )
        parts = complex_window(weights, padded[window_rows, :])
        for part in range(2):
            send_ref[place, part] = parts[part]


def second_level_kernel(
    starts_ref, side_ref, own_at_ref, other_at_ref, own_ref, first_ref, second_ref, weights_ref,
    keep_ref, send_ref, padded, send,
):
    sectors, stacked, window = weights_ref.shape
    beams = stacked // 2
    width = keep_ref.shape[3]
    margin, rows = first_ref.shape[1], own_ref.shape[1]
    columns = slice(0, 2 * width)
    place_rows(padded, margin, own_ref, columns)
    place_halos(padded, side_ref, rows, first_ref, second_ref, columns)
    per = beams // OS
    for sector in range(sectors):
        place = pl.ds(pl.multiple_of(starts_ref[sector] * BLK, BLK), window)
        parts = complex_window(weights_ref[sector], padded[place, :])
        for piece in range(per):
            own_at = own_at_ref[sector * per + piece]
            other_at = other_at_ref[sector * per + piece]
            taken = slice(piece * OS, (piece + 1) * OS)
            for part in range(2):
                keep_ref[own_at, part] = parts[part][taken, :width]
                send[other_at, part] = parts[part][taken, width:]
    send_ref[...] = send[send.shape[0] - send_ref.shape[0] :]


def second_level(starts, side, planned, own, halos, weights, early):
    sectors, stacked, window = weights.shape
    margin, rows, rng = halos[0].shape[1], own.shape[1], own.shape[2]
    count = sectors * stacked // 2 // OS
    block = (2, OS, rng // 2)
    own_at, other_at, other_sector = planned
    early_send = pl.pallas_call(
        second_level_early_kernel,
        out_shape=jax.ShapeDtypeStruct((early,) + block, jnp.bfloat16),
        in_specs=[SMEM] * 3 + [VMEM] * 4,
        out_specs=VMEM,
        scratch_shapes=[pltpu.VMEM((rows + 2 * margin, rng), jnp.bfloat16)],
        compiler_params=params(),
        cost_estimate=cost(early * 2 * 2 * OS * window * rng // 2, 2**20),
        name="second_level_early",
    )(starts, side, other_sector, own, *halos, weights)
    shapes = [jax.ShapeDtypeStruct((n,) + block, jnp.bfloat16) for n in (count, count - early)]
    keep, late_send = pl.pallas_call(
        second_level_kernel,
        out_shape=shapes,
        in_specs=[SMEM] * 4 + [VMEM] * 4,
        out_specs=[VMEM] * 2,
        scratch_shapes=[
            pltpu.VMEM((rows + 2 * margin, 2 * rng), jnp.bfloat16),
            pltpu.VMEM((count,) + block, jnp.bfloat16),
        ],
        compiler_params=params(),
        cost_estimate=cost(sectors * 2 * stacked * window * rng, 2**22),
        name="second_level",
    )(starts, side, own_at, other_at, own, *halos, weights)
    return keep, early_send, late_send


def plan_kernel(
    shift, me_ref, own_ref, other_ref, own_at_ref, other_at_ref, other_sector_ref, target_ref, rank_ref,
    taken, filled,
):
    count = own_ref.shape[0]
    far_bit = taken.shape[0] // 2

    def delay(target):
        distance = target ^ me_ref[0]
        return jnp.where((distance & far_bit) == 0, 2 * count, (distance & 1) * shift)

    for owners_ref, at_ref in ((other_ref, other_at_ref), (own_ref, own_at_ref)):
        for target in range(taken.shape[0]):
            taken[target] = 0
        for bucket in range(filled.shape[0]):
            filled[bucket] = 0
        for sector in range(count):
            target = owners_ref[sector]
            rank = taken[target]
            taken[target] = rank + 1
            bucket = rank + delay(target)
            at_ref[sector] = bucket
            filled[bucket + 1] = filled[bucket + 1] + 1
        for bucket in range(1, filled.shape[0]):
            filled[bucket] = filled[bucket] + filled[bucket - 1]
        for sector in range(count):
            bucket = at_ref[sector]
            place = filled[bucket]
            filled[bucket] = place + 1
            at_ref[sector] = place
            if at_ref is own_at_ref:
                target_ref[place] = owners_ref[sector]
                rank_ref[place] = bucket - delay(owners_ref[sector])
            else:
                other_sector_ref[place] = sector


def plan(shift, me, own, other, beam_count):
    count = own.shape[0]
    shape = jax.ShapeDtypeStruct((count,), jnp.int32)
    return pl.pallas_call(
        functools.partial(plan_kernel, shift),
        out_shape=[shape] * 5,
        in_specs=[SMEM] * 3,
        out_specs=[SMEM] * 5,
        scratch_shapes=[
            pltpu.SMEM((beam_count,), jnp.int32),
            pltpu.SMEM((3 * count + 1,), jnp.int32),
        ],
        compiler_params=params(),
        name="plan",
    )(me, own, other)


def wires_kernel(spans, early, me_ref, target_ref, rank_ref, keep_ref, *refs):
    wires = refs[-1]
    spare = wires.shape[0] - 1
    out_refs = refs[-1 - len(spans) : -1]
    other_ref, *summed_refs = refs[: -1 - len(spans)]
    wires[...] = jnp.zeros_like(wires)
    me = me_ref[0]

    def lay(place, total):
        rank = rank_ref[place]
        distance = target_ref[place] ^ me
        at = spare
        start = 0
        for number, low, high in spans:
            wanted = (distance == number) & (rank >= low) & (rank < high)
            at = jnp.where(wanted, start + rank - low, at)
            start += high - low
        wires[at] = total

    before = 0
    if not early:
        before = summed_refs[0].shape[0]
        for row in range(before):
            lay(row, summed_refs[0][row])
    for row in range(other_ref.shape[0]):
        place = before + row
        total = keep_ref[place].astype(jnp.float32) + other_ref[row].astype(jnp.float32)
        total = total.astype(jnp.bfloat16)
        lay(place, total)
        if early:
            summed_refs[0][row] = total
    start = 0
    for (_, low, high), ref in zip(spans, out_refs):
        ref[...] = wires[start : start + high - low]
        start += high - low


def wires(spans, me, target, rank, keep, other, summed=None):
    block = keep.shape[1:]
    sizes = [high - low for _, low, high in spans]
    inputs = [me, target, rank, keep, other]
    if summed is None:
        sizes = [other.shape[0]] + sizes
    else:
        inputs.append(summed)
    shapes = [jax.ShapeDtypeStruct((size,) + block, jnp.bfloat16) for size in sizes]
    total = sum(high - low for _, low, high in spans)
    return pl.pallas_call(
        functools.partial(wires_kernel, spans, summed is None),
        out_shape=shapes,
        in_specs=[SMEM] * 3 + [VMEM] * (len(inputs) - 3),
        out_specs=[VMEM] * len(shapes),
        scratch_shapes=[pltpu.VMEM((total + 1,) + block, jnp.bfloat16)],
        compiler_params=params(),
        cost_estimate=cost(0, 2**21),
        name="early_wires" if summed is None else "late_wires",
    )(*inputs)


def collect_kernel(spans, capacity, me_ref, *refs):
    sems = refs[-1]
    out_ref = refs[-2]
    copies = []
    for number, (distance, low, high) in enumerate(spans):
        start = (me_ref[0] ^ distance) * capacity + low
        copies.append(
            pltpu.make_async_copy(
                refs[number], out_ref.at[pl.ds(start, high - low)], sems.at[number]
            )
        )
    for copy in copies:
        copy.start()
    for copy in copies:
        copy.wait()


def collect(spans, capacity, beam_count, me, received):
    shape = (beam_count * capacity,) + received[0].shape[1:]
    return pl.pallas_call(
        functools.partial(collect_kernel, spans, capacity),
        out_shape=jax.ShapeDtypeStruct(shape, jnp.bfloat16),
        in_specs=[SMEM] + [ANY] * len(received),
        out_specs=ANY,
        scratch_shapes=[pltpu.SemaphoreType.DMA((len(received),))],
        compiler_params=params(),
        cost_estimate=cost(0, 2**21),
        name="collect",
    )(me, *received)


def spread(spans, group):
    count = lax.axis_size("beam")
    received = []
    for (distance, _, _), wire in zip(spans, group):
        route = [(place, place ^ distance) for place in range(count)]
        received.append(lax.ppermute(wire, "beam", route) if distance else wire)
    return received


def real_form(weights):
    real, imag = weights[0, :, 0], weights[0, :, 1]
    upper = jnp.concatenate([real, -imag], axis=-1)
    lower = jnp.concatenate([imag, real], axis=-1)
    return jnp.concatenate([upper, lower], axis=1)


def stacked_weights(weights):
    return weights[0].reshape(weights.shape[1], -1, weights.shape[4])


def table_row(table, row_number):
    return lax.dynamic_index_in_dim(table, row_number, 0, keepdims=False)


def local(subimages, range_kernel, weights0, starts0, weights1, starts1, owners):
    aper_index = lax.axis_index("aperture")
    beam_index = lax.axis_index("beam")
    beam_count = lax.axis_size("beam")
    margin = MARGIN_BLOCKS * BLK
    rows = subimages.shape[2]
    local_blocks = rows // BLK
    even = (beam_index + 1) % 2
    ends = (beam_index == 0, beam_index == beam_count - 1)
    side = jnp.stack([even] + [end.astype(jnp.int32) for end in ends])
    me = beam_index.reshape(1)

    sector_count = owners.shape[1]
    capacity = max(2, 2 * sector_count // beam_count)
    shorter, longer = max(1, capacity // 4), max(1, capacity // 2)
    far = range(beam_count // 2, beam_count)
    odd = [distance for distance in far if distance % 2]
    others = [distance for distance in far if distance % 2 == 0]
    early = len(odd) * shorter + len(others) * longer
    early_spans = [(distance, 0, shorter) for distance in odd]
    early_spans += [(distance, 0, longer) for distance in others]
    late_spans = [(distance, shorter, capacity) for distance in odd]
    for distance in range(1, beam_count // 2):
        cut = (5 * capacity + 4) // 8
        late_spans += [(distance, 0, cut), (distance, cut, capacity)]
    late_spans.append((0, 0, capacity))
    last_spans = [(distance, longer, capacity) for distance in others]

    sent = resample(subimages[0], range_kernel[0], margin)
    sent, weights0 = lax.optimization_barrier((sent, weights0))
    weights, owners = lax.optimization_barrier((real_form(weights0), owners))
    halos = trade_edges(*sent)
    own_owners = owners[0, :, 0]
    other_owners = partner(owners, "aperture", 1)[0, :, 0]
    planned = plan(longer - shorter, me, own_owners, other_owners, beam_count)
    begin0 = table_row(starts0, aper_index) - (beam_index * local_blocks - MARGIN_BLOCKS)
    halos, planned = lax.optimization_barrier((halos, planned))
    *planned, target, rank = planned
    width = range_kernel.shape[3] // 2
    send = first_level(width, rows, begin0, side, sent, halos, weights)
    other = partner(send, "aperture", 0)
    keep = first_level(0, rows, begin0, side, sent, halos, stacked_weights(weights0))
    level_one = (keep.astype(jnp.float32) + other.astype(jnp.float32)).astype(jnp.bfloat16)

    beams = level_one.shape[1]
    first = lax.dynamic_slice_in_dim(level_one, even * (beams - margin), margin, 1)
    second = lax.dynamic_slice_in_dim(level_one, (1 - even) * (beams - margin), margin, 1)
    halos = trade_edges(first, second)
    begin1 = table_row(starts1, aper_index) - (beam_index * 2 * local_blocks - MARGIN_BLOCKS)
    keep, send, late = second_level(
        begin1, side, planned, level_one, halos, stacked_weights(weights1), early
    )
    other = partner(send, "aperture", 1)
    other, late = lax.optimization_barrier((other, late))
    late = partner(late, "aperture", 1)
    summed, *group = wires(early_spans, me, target, rank, keep, other)
    received = spread(early_spans, group)
    from_odd, from_others = received[: len(odd)], received[len(odd) :]
    ready, from_odd = lax.optimization_barrier((late, from_odd))
    group = wires(late_spans, me, target, rank, keep, ready, summed)
    received = from_odd + spread(late_spans, group)
    ready, from_others = lax.optimization_barrier((late, from_others))
    group = wires(last_spans, me, target, rank, keep, ready, summed)
    received += from_others + spread(last_spans, group)
    spans = early_spans[: len(odd)] + late_spans + early_spans[len(odd) :] + last_spans
    return collect(spans, capacity, beam_count, me, received)[None]


def solution(mesh):
    return jax.shard_map(
        local,
        mesh=mesh,
        in_specs=(
            P("aperture", None, "beam", None),
            P("aperture", None, None, None),
            P("aperture", "beam", None, None, None),
            P(None, "beam"),
            P("aperture", "beam", None, None, None),
            P(None, "beam"),
            P("aperture", "beam", None),
        ),
        out_specs=P("aperture", "beam", None, None, None),
        check_vma=False,
    )
```
